32 devices in a mesh: recon: 2 (over y), blk: 4 (over z), probe: 4 (over x, core).
Axes of the slice: x: 2, y: 2, z: 4, core: 2. Of those that a mesh axis runs over, the one named last changes fastest.
Arguments:
- tiles: bfloat16 [8, 2, 512, 512], P(('recon', 'blk')), parts along dimension 0, may hold values from -5 to 5
- eigenprobes: bfloat16 [12, 2, 256, 256], P('recon'), parts along dimension 0, may hold values from -6 to 6
- coefficients: float32 [320, 6], P(('recon', 'blk', 'probe')), parts along dimension 0, may hold values from -2.4 to 2.4
- tile_list: int32 [320, 2], P(('recon', 'blk', 'probe')), parts along dimension 0, may hold values from 0 to 3, as said below
- offsets: int32 [320, 4], P(('recon', 'blk', 'probe')), parts along dimension 0, may hold values from 0 to 256
- amplitudes: bfloat16 [320, 256, 256], P(('recon', 'blk', 'probe')), parts along dimension 0, may hold values from 0 to 2
- group_counts: int32 [8], P(('recon', 'blk')), parts along dimension 0, may hold values from 10 to 40, as said below
Outputs:
- object_grad: float32 [8, 2, 512, 512], P(('recon', 'blk'), None, 'probe'), parts along dimension 0
- eigen_grad: float32 [12, 2, 256, 256], P('recon', None, 'probe'), parts along dimension 0
- coef_grad: float32 [320, 6], P(('recon', 'blk', 'probe')), parts along dimension 0
The draws below stay inside these ranges and needn't reach their ends.
There are 2 independent parts, one for each index of `recon`. The reference program is written for one: setup_inputs(seed, part) draws one part's arguments, and reference() takes and returns one part's arrays. A program takes and returns all parts, laid end to end along the dimension named above; each array names one. Nothing has to cross between parts.
Inputs may be any that keep to these rules, and one draw needn't show every extreme that they name: `tile_list`: A position of group g lists two different tiles among (g + r) mod 4 for r from 0 to 2. `group_counts`: some group is full in every draw.
All inputs are finite; a program needn't handle non-finite values.
Results may differ from the reference program's by a relative error of at most 0.0034.
Values may be sent and summed in bfloat16 or wider, within the bound.
No kernel may reach another device: no remote copies, remote signals or barrier semaphores. Data moves between devices by JAX's collectives and lax.ppermute only.
A program may use at most 64 MiB of HBM per device.

```python
import math
import jax
import jax.numpy as jnp
from jax import lax

TILE = 512
PSZ = 256
MODES = 6
REACH = 3
NB = 4
GROUP_SLOTS = 40
POSITIONS = 160


def draw_tile_list(key, part):
    key = jax.random.fold_in(key, 11)
    first_key, second_key = jax.random.split(key)
    position = jnp.arange(POSITIONS, dtype=jnp.int32)
    group_id = position // GROUP_SLOTS
    first_reach = jax.random.randint(first_key, (POSITIONS,), 0, REACH)
    stride = jax.random.randint(second_key, (POSITIONS,), 1, REACH)
    second_reach = (first_reach + stride) % REACH
    return jnp.stack([(group_id + first_reach) % NB, (group_id + second_reach) % NB], 1).astype(jnp.int32)


def draw_group_counts(key, part):
    key = jax.random.fold_in(key, 23)
    count_key, full_key = jax.random.split(key)
    counts = jax.random.randint(count_key, (NB,), GROUP_SLOTS // 4, GROUP_SLOTS + 1)
    full_group = jax.random.randint(full_key, (), 0, NB)
    return jnp.where(jnp.arange(NB) == full_group, GROUP_SLOTS, counts).astype(jnp.int32)


def touch_ends(values, stream_key, low, top_value):
    dims = values.shape
    spot = [jax.random.randint(jax.random.fold_in(stream_key, axis), (), 0, dims[axis]) for axis in range(len(dims))]
    values = values.at[tuple(spot)].set(low)
    longest = dims.index(max(dims))
    spot[longest] = (spot[longest] + 1) % dims[longest]
    return values.at[tuple(spot)].set(top_value)


def levels(own_key, extent, cuts, smallest, high):
    level = 1.0
    for dim, shards_of in cuts:
        heights = jax.random.uniform(jax.random.fold_in(jax.random.fold_in(own_key, 6), dim), (shards_of,), jnp.float32, smallest / len(cuts), high / len(cuts))
        level = level * jnp.repeat(jnp.exp(heights), extent[dim] // shards_of).reshape((-1,) + (1,) * (len(extent) - 1 - dim))
    return level


def normal_values(key, shape, scale, limit, shards=(), kind=jnp.bfloat16):
    entries = jax.random.normal(key, shape, jnp.float32) * scale
    if len(shards) > 0:
        entries = levels(key, shape, shards, -0.22, 0.18) * entries
    return jnp.clip(entries, min=-limit, max=limit).astype(kind)


def setup_inputs(seed: int = 0, part: int = 0) -> dict:
    splits = jax.random.split(jax.random.key(seed), 8)
    part_splits = jax.random.split(jax.random.fold_in(splits[7], part), 8)
    return {
        "tiles": normal_values(part_splits[0], (NB, 2, TILE, TILE), 0.7, 5.0, ((0, 4),)),
        "eigenprobes": normal_values(part_splits[1], (MODES, 2, PSZ, PSZ), 1.0, 6.0),
        "coefficients": normal_values(part_splits[2], (POSITIONS, MODES), 0.4, 2.4, ((0, 16),), jnp.float32),
        "tile_list": draw_tile_list(jax.random.fold_in(jax.random.fold_in(splits[7], part), 71), part),
        "offsets": touch_ends(jax.random.randint(part_splits[4], (POSITIONS, 4), 0, TILE - PSZ + 1), jax.random.fold_in(part_splits[4], 1), 0, TILE - PSZ).astype(jnp.int32),
        "amplitudes": jnp.clip(2.0 * jax.random.uniform(part_splits[5], (POSITIONS, PSZ, PSZ), jnp.float32) ** levels(part_splits[5], (POSITIONS, PSZ, PSZ), ((0, 16),), -0.2, 0.2), 0.0, 2.0).astype(jnp.bfloat16),
        "group_counts": draw_group_counts(jax.random.fold_in(jax.random.fold_in(splits[7], part), 71), part),
    }


def tables(frame):
    indices = jnp.arange(frame, dtype=jnp.int32)
    product = indices[:, None] * indices[None, :] % frame
    angle = product.astype(jnp.float32) * (2.0 * math.pi / frame)
    cos_part = jnp.cos(angle) / math.sqrt(frame)
    sin_part = -jnp.sin(angle) / math.sqrt(frame)
    forward = jnp.concatenate([jnp.concatenate([cos_part, sin_part], 1), jnp.concatenate([-sin_part, cos_part], 1)], 0)
    backward = jnp.concatenate([jnp.concatenate([cos_part, -sin_part], 1), jnp.concatenate([sin_part, cos_part], 1)], 0)
    return (forward.astype(jnp.bfloat16), backward.astype(jnp.bfloat16))

def transform(in_real, in_imag, dft_table):
    width_n = in_real.shape[0]
    section_one = jnp.dot(jnp.concatenate([in_real, in_imag], 1), dft_table, preferred_element_type=jnp.float32).astype(jnp.bfloat16)
    joined = jnp.concatenate([section_one[:, :width_n].T, section_one[:, width_n:].T], 1)
    second = jnp.dot(joined, dft_table, preferred_element_type=jnp.float32)
    return (second[:, :width_n].T, second[:, width_n:].T)

def position_terms(obj_re, obj_im, probe_re, probe_im, measured, living, forward, backward):
    exit_re = (probe_re * obj_re - probe_im * obj_im).astype(jnp.bfloat16)
    exit_im = (probe_re * obj_im + probe_im * obj_re).astype(jnp.bfloat16)
    far_re, far_im = transform(exit_re, exit_im, forward)
    modulus = jnp.sqrt(far_re * far_re + far_im * far_im + 1.0)
    factor = (1.0 - measured / modulus) * living
    back_re, back_im = transform((far_re * factor).astype(jnp.bfloat16), (far_im * factor).astype(jnp.bfloat16), backward)
    grad_obj = jnp.stack([probe_re * back_re + probe_im * back_im, probe_re * back_im - probe_im * back_re])
    grad_probe = jnp.stack([obj_re * back_re + obj_im * back_im, obj_re * back_im - obj_im * back_re])
    return (grad_obj, grad_probe)

def take_block(source, which, row_at, col_at, frame):
    start_at = (jnp.asarray(which).astype(jnp.int32), jnp.int32(0), jnp.asarray(row_at).astype(jnp.int32), jnp.asarray(col_at).astype(jnp.int32))
    return lax.dynamic_slice(source, start_at, (1, 2, frame, frame))[0].astype(jnp.float32)

def add_block(target, which, row_at, col_at, piece):
    frame = piece.shape[1]
    start_at = (jnp.asarray(which).astype(jnp.int32), jnp.int32(0), jnp.asarray(row_at).astype(jnp.int32), jnp.asarray(col_at).astype(jnp.int32))
    present = lax.dynamic_slice(target, start_at, (1, 2, frame, frame))
    return lax.dynamic_update_slice(target, present + piece[None], start_at)

def reference(tiles, eigenprobes, coefficients, tile_list, offsets, amplitudes, group_counts):
    forward, backward = tables(PSZ)
    probes_wide = eigenprobes.astype(jnp.float32)
    tile_list = tile_list.astype(jnp.int32)
    offsets = offsets.astype(jnp.int32)
    group_counts = group_counts.astype(jnp.int32)

    def visit(carried, position):
        grad_tiles, eigen_acc = carried
        group_id = position // GROUP_SLOTS
        slot_id = position % GROUP_SLOTS
        living = (slot_id < group_counts[group_id]).astype(jnp.float32)
        tile_ids = tile_list[position]
        corner = offsets[position]
        obj_patch = 0.5 * (take_block(tiles, tile_ids[0], corner[0], corner[1], PSZ) + take_block(tiles, tile_ids[1], corner[2], corner[3], PSZ))
        weights = coefficients[position]
        probe_now = jnp.einsum('k,kcxy->cxy', weights, probes_wide, precision=lax.Precision.HIGHEST)
        grad_obj, grad_probe = position_terms(obj_patch[0], obj_patch[1], probe_now[0], probe_now[1], amplitudes[position].astype(jnp.float32), living, forward, backward)
        grad_tiles = add_block(grad_tiles, tile_ids[0], corner[0], corner[1], 0.5 * grad_obj)
        grad_tiles = add_block(grad_tiles, tile_ids[1], corner[2], corner[3], 0.5 * grad_obj)
        eigen_acc = eigen_acc + weights[:, None, None, None] * grad_probe[None]
        coef_row = jnp.einsum('kcxy,cxy->k', probes_wide, grad_probe, precision=lax.Precision.HIGHEST) / PSZ
        return ((grad_tiles, eigen_acc), coef_row)
    start = (jnp.zeros((NB, 2, TILE, TILE), jnp.float32), jnp.zeros((MODES, 2, PSZ, PSZ), jnp.float32))
    (grad_tiles, eigen_acc), coef_rows = lax.scan(visit, start, jnp.arange(POSITIONS, dtype=jnp.int32))
    return (grad_tiles, eigen_acc * POSITIONS ** (-0.5), coef_rows)
```

```python
import functools
import math

import jax
import jax.numpy as jnp
import ml_dtypes
import numpy as np
from jax import lax
from jax.experimental import pallas as pl
from jax.experimental.pallas import tpu as pltpu
from jax.sharding import PartitionSpec as P

REACH = 3
LANES = 128
STRIP = 16
KRON = 32
VMEM = pltpu.MemorySpace.VMEM
SMEM = pltpu.MemorySpace.SMEM
VMEM_LIMIT = 56 * 1024 * 1024


def tables(frame):
    indices = np.arange(frame)
    angle = (indices[:, None] * indices[None, :] % frame) * (2.0 * math.pi / frame)
    cos_part = np.cos(angle) / math.sqrt(frame)
    sin_part = -np.sin(angle) / math.sqrt(frame)
    forward = np.block([[cos_part, sin_part], [-sin_part, cos_part]])
    forward = forward.astype(np.float32).astype(ml_dtypes.bfloat16)
    return jnp.asarray(forward), jnp.asarray(np.ascontiguousarray(forward.T))


def shift(array, axis, by):
    peers = lax.axis_size(axis)
    return lax.ppermute(array, axis, [(i, (i + by) % peers) for i in range(peers)])


def swap(array, axis, bit):
    peers = lax.axis_size(axis)
    return lax.ppermute(array, axis, [(i, i ^ bit) for i in range(peers)])


def synth_kernel(coef, eig, out):
    modes = eig.shape[0]
    pos_dev = out.shape[0]
    wide = [[eig[k, c].astype(jnp.float32) for k in range(modes)] for c in range(2)]
    for j in range(pos_dev):
        for c in range(2):
            total = coef[j, 0] * wide[c][0]
            for k in range(1, modes):
                total += coef[j, k] * wide[c][k]
            out[j, c] = total


def synth(coefficients, eigenprobes):
    modes, _, frame, _ = eigenprobes.shape
    pos_dev = coefficients.shape[0]
    return pl.pallas_call(
        synth_kernel,
        grid=(frame // STRIP,),
        in_specs=[
            pl.BlockSpec(memory_space=SMEM),
            pl.BlockSpec((modes, 2, STRIP, frame), lambda i: (0, 0, i, 0)),
        ],
        out_specs=pl.BlockSpec((pos_dev, 2, STRIP, frame), lambda i: (0, 0, i, 0)),
        out_shape=jax.ShapeDtypeStruct((pos_dev, 2, frame, frame), jnp.float32),
        name="probe_synthesis",
    )(coefficients, eigenprobes)


def position_kernel(offs, info, *refs):
    pieces = refs[: 1 + 2 * len(offs)]
    (fwd, bwd, probe, amps, keep, send, dprobe, obj, acc, ex, mid, far, patch) = refs[len(pieces):]
    j = pl.program_id(0)
    pos_dev = pl.num_programs(0)
    frame = probe.shape[2]
    side = pieces[0].shape[2]
    blocks = side // LANES
    shares = len(offs)
    slab = side // shares
    alive = info[0, 6]
    member = info[0, 7]

    @pl.when(j == 0)
    def _():
        for section in range(REACH):
            for i in range(1 if section == 0 else shares):
                if section == 0:
                    piece, start, rows = pieces[0], 0, side
                else:
                    piece = pieces[1 + (section - 1) * shares + i]
                    start, rows = pl.multiple_of((member ^ offs[i]) * slab, slab), slab
                for c in range(2):
                    for b in range(blocks):
                        obj[section, c, b, pl.ds(start, rows), :] = piece[
                            c, :, b * LANES:(b + 1) * LANES
                        ].astype(jnp.float32)
        acc[...] = jnp.zeros_like(acc)

    @pl.when(j >= alive)
    def _():
        dprobe[...] = jnp.zeros_like(dprobe)

    @pl.when(j < alive)
    def _():
        lane = lax.broadcasted_iota(jnp.int32, (STRIP, LANES), 1)
        where = []
        for m in range(2):
            row, col = info[j, 2 + 2 * m], info[j, 3 + 2 * m]
            where.append((info[j, m], row, col // LANES, col % LANES))
        strips = range(frame // STRIP)
        for i in strips:
            rows = slice(i * STRIP, (i + 1) * STRIP)
            parts = []
            for c in range(2):
                total = None
                for section, row, cb, s in where:
                    back_by = (LANES - s) % LANES
                    keep_lane = lane < LANES - s
                    rolled = [
                        pltpu.roll(obj[section, c, cb + b, pl.ds(row + i * STRIP, STRIP), :], back_by, 1)
                        for b in range(3)
                    ]
                    block = [jnp.where(keep_lane, rolled[b], rolled[b + 1]) for b in range(2)]
                    total = block if total is None else [x + y for x, y in zip(total, block)]
                parts.append([0.5 * x for x in total])
            for b in range(2):
                cols = slice(b * LANES, (b + 1) * LANES)
                o_re, o_im = parts[0][b], parts[1][b]
                p_re, p_im = probe[0, 0, rows, cols], probe[0, 1, rows, cols]
                patch[0, rows, cols] = o_re
                patch[1, rows, cols] = o_im
                ex[rows, b * LANES:(b + 1) * LANES] = (p_re * o_re - p_im * o_im).astype(jnp.bfloat16)
                ex[rows, frame + b * LANES:frame + (b + 1) * LANES] = (
                    p_re * o_im + p_im * o_re
                ).astype(jnp.bfloat16)

        def transform(table, table_t):
            half = jnp.dot(ex[...], table[...], preferred_element_type=jnp.float32)
            mid[:frame] = half[:, :frame].astype(jnp.bfloat16)
            mid[frame:] = half[:, frame:].astype(jnp.bfloat16)
            far[...] = jnp.dot(table_t[...], mid[...], preferred_element_type=jnp.float32)

        transform(fwd, bwd)
        for i in strips:
            rows = slice(i * STRIP, (i + 1) * STRIP)
            lower = slice(frame + i * STRIP, frame + (i + 1) * STRIP)
            f_re, f_im = far[rows], far[lower]
            factor = 1.0 - amps[0, rows].astype(jnp.float32) * lax.rsqrt(f_re * f_re + f_im * f_im + 1.0)
            ex[rows, :frame] = (f_re * factor).astype(jnp.bfloat16)
            ex[rows, frame:] = (f_im * factor).astype(jnp.bfloat16)
        transform(bwd, fwd)
        for i in strips:
            rows = slice(i * STRIP, (i + 1) * STRIP)
            lower = slice(frame + i * STRIP, frame + (i + 1) * STRIP)
            grads = [[], []]
            for b in range(2):
                cols = slice(b * LANES, (b + 1) * LANES)
                b_re, b_im = far[rows, cols], far[lower, cols]
                o_re, o_im = patch[0, rows, cols], patch[1, rows, cols]
                p_re, p_im = probe[0, 0, rows, cols], probe[0, 1, rows, cols]
                dprobe[0, 0, rows, cols] = (o_re * b_re + o_im * b_im).astype(jnp.bfloat16)
                dprobe[0, 1, rows, cols] = (o_re * b_im - o_im * b_re).astype(jnp.bfloat16)
                grads[0].append(0.5 * (p_re * b_re + p_im * b_im))
                grads[1].append(0.5 * (p_re * b_im - p_im * b_re))
            for section, row, cb, s in where:
                inside = lane >= s
                for c in range(2):
                    low = pltpu.roll(grads[c][0], s, 1)
                    high = pltpu.roll(grads[c][1], s, 1)
                    for b, value in enumerate(
                        (
                            jnp.where(inside, low, 0.0),
                            jnp.where(inside, high, low),
                            jnp.where(inside, 0.0, high),
                        )
                    ):
                        at = (section, c, cb + b, pl.ds(row + i * STRIP, STRIP), slice(None))
                        acc[at] = acc[at] + value

    @pl.when(j == pos_dev - 1)
    def _():
        core = member % 2
        for section in range(REACH):
            for h in range(shares // 2):
                mine = pl.multiple_of((2 * h + core) * slab, slab)
                other = pl.multiple_of((2 * h + 1 - core) * slab, slab)
                for c in range(2):
                    for b in range(blocks):
                        cols = slice(b * LANES, (b + 1) * LANES)
                        keep[section, h, c, :, cols] = acc[section, c, b, pl.ds(mine, slab), :]
                        send[section, h, c, :, cols] = acc[section, c, b, pl.ds(other, slab), :].astype(
                            jnp.bfloat16
                        )


def positions(offs, info, pieces, fwd, bwd, probe, amps):
    pos_dev, _, frame, _ = probe.shape
    side = pieces[0].shape[2]
    shares = len(offs)
    slab = side // shares
    blocks = side // LANES
    whole = pl.BlockSpec(memory_space=VMEM)
    per_pos = lambda j, info: (j, 0, 0, 0)
    half_shape = (REACH, shares // 2, 2, slab, side)
    return pl.pallas_call(
        functools.partial(position_kernel, offs),
        grid_spec=pltpu.PrefetchScalarGridSpec(
            num_scalar_prefetch=1,
            grid=(pos_dev,),
            in_specs=[whole] * (len(pieces) + 2)
            + [
                pl.BlockSpec((1, 2, frame, frame), per_pos),
                pl.BlockSpec((1, frame, frame), lambda j, info: (j, 0, 0)),
            ],
            out_specs=[whole, whole, pl.BlockSpec((1, 2, frame, frame), per_pos)],
            scratch_shapes=[
                pltpu.VMEM((REACH, 2, blocks + 1, side, LANES), jnp.float32),
                pltpu.VMEM((REACH, 2, blocks + 1, side, LANES), jnp.float32),
                pltpu.VMEM((frame, 2 * frame), jnp.bfloat16),
                pltpu.VMEM((2 * frame, frame), jnp.bfloat16),
                pltpu.VMEM((2 * frame, frame), jnp.float32),
                pltpu.VMEM((2, frame, frame), jnp.float32),
            ],
        ),
        out_shape=[
            jax.ShapeDtypeStruct(half_shape, jnp.float32),
            jax.ShapeDtypeStruct(half_shape, jnp.bfloat16),
            jax.ShapeDtypeStruct((pos_dev, 2, frame, frame), jnp.bfloat16),
        ],
        compiler_params=pltpu.CompilerParams(vmem_limit_bytes=VMEM_LIMIT),
        name="positions",
    )(info, *pieces, fwd, bwd, probe, amps)


def eigen_kernel(scale, weights, dprobe, eig, out, cross):
    modes = eig.shape[0]
    pos_dev = dprobe.shape[0]
    frame = eig.shape[3]
    width = pos_dev * KRON

    @pl.when(pl.program_id(0) == 0)
    def _():
        cross[...] = jnp.zeros_like(cross)

    for c in range(2):
        d = dprobe[:, c].reshape(width, frame)
        e = eig[:, c].reshape(modes * KRON, frame)
        grad = jnp.dot(weights[0], d, preferred_element_type=jnp.float32)
        grad += jnp.dot(weights[1], d, preferred_element_type=jnp.float32)
        out[:, c] = (scale * grad).reshape(modes, KRON, frame)
        cross[...] += lax.dot_general(d, e, (((1,), (1,)), ((), ())), preferred_element_type=jnp.float32)


def eigen_terms(scale, weights, dprobe, eigenprobes):
    modes, _, frame, _ = eigenprobes.shape
    pos_dev = dprobe.shape[0]
    return pl.pallas_call(
        functools.partial(eigen_kernel, scale),
        grid=(frame // KRON,),
        in_specs=[
            pl.BlockSpec(memory_space=VMEM),
            pl.BlockSpec((pos_dev, 2, KRON, frame), lambda i: (0, 0, i, 0)),
            pl.BlockSpec((modes, 2, KRON, frame), lambda i: (0, 0, i, 0)),
        ],
        out_specs=[
            pl.BlockSpec((modes, 2, KRON, frame), lambda i: (0, 0, i, 0)),
            pl.BlockSpec((pos_dev * KRON, modes * KRON), lambda i: (0, 0)),
        ],
        out_shape=[
            jax.ShapeDtypeStruct((modes, 2, frame, frame), jnp.float32),
            jax.ShapeDtypeStruct((pos_dev * KRON, modes * KRON), jnp.float32),
        ],
        compiler_params=pltpu.CompilerParams(vmem_limit_bytes=VMEM_LIMIT),
        name="eigen_terms",
    )(weights, dprobe, eigenprobes)


def halve(keep, send, member, shares):
    total = keep + swap(send, "probe", 1).astype(jnp.float32)
    rest = member // 2
    bit = 2
    while bit < shares:
        pairs = total.reshape((total.shape[0] // 2, 2) + total.shape[1:])
        mine = rest % 2
        keep = lax.dynamic_index_in_dim(pairs, mine, 1, False)
        send = lax.dynamic_index_in_dim(pairs, 1 - mine, 1, False).astype(jnp.bfloat16)
        total = keep + swap(send, "probe", bit).astype(jnp.float32)
        rest = rest // 2
        bit *= 2
    return total[0]


def on_device(tiles, eigenprobes, coefficients, tile_list, offsets, amplitudes, group_counts):
    modes, _, frame, _ = eigenprobes.shape
    side = tiles.shape[2]
    pos_dev = coefficients.shape[0]
    blocks = lax.axis_size("blk")
    shares = lax.axis_size("probe")
    my_block = lax.axis_index("blk")
    member = lax.axis_index("probe")
    slab = side // shares
    bits = [1 << i for i in range(shares.bit_length() - 1)]
    forward, backward = tables(frame)

    moving = lax.dynamic_slice_in_dim(tiles[0], member * slab, slab, 1)
    pieces = [tiles[0]]
    offs = [0]
    for bit in reversed(bits):
        offs = offs + [o ^ bit for o in offs]
    for section in range(1, REACH):
        moving = shift(moving, "blk", -1)
        held = [moving]
        for bit in reversed(bits):
            held = held + [swap(piece, "probe", bit) for piece in held]
        pieces += held

    alive = jnp.clip(group_counts[0] - member * pos_dev, 0, pos_dev)
    info = jnp.concatenate(
        [
            (tile_list - my_block) % blocks,
            offsets,
            jnp.broadcast_to(alive, (pos_dev, 1)).astype(jnp.int32),
            jnp.broadcast_to(member, (pos_dev, 1)).astype(jnp.int32),
        ],
        1,
    )
    eye = jnp.eye(KRON, dtype=jnp.float32)
    spread = (coefficients.T[:, None, :, None] * eye[None, :, None, :]).reshape(
        modes * KRON, pos_dev * KRON
    )
    spread_high = spread.astype(jnp.bfloat16)
    weights = jnp.stack([spread_high, (spread - spread_high.astype(jnp.float32)).astype(jnp.bfloat16)])

    probe = synth(coefficients, eigenprobes)
    keep, send, dprobe = positions(offs, info, pieces, forward, backward, probe, amplitudes)

    returned = None
    for section in range(REACH - 1, -1, -1):
        mine = halve(keep[section], send[section], member, shares)
        if returned is None:
            returned = mine
        else:
            returned = shift(returned.astype(jnp.bfloat16), "blk", 1).astype(jnp.float32) + mine

    scale = (pos_dev * blocks * shares) ** (-0.5)
    eigen, cross = eigen_terms(scale, weights, dprobe, eigenprobes)
    slabs = eigen.reshape(modes, 2, shares // 2, 2, frame // shares, frame)
    core = member % 2
    eigen_keep = jnp.moveaxis(lax.dynamic_index_in_dim(slabs, core, 3, False), 2, 0)
    eigen_send = jnp.moveaxis(lax.dynamic_index_in_dim(slabs, 1 - core, 3, False), 2, 0).astype(jnp.bfloat16)
    eigen_mine = halve(eigen_keep, eigen_send, member, shares)
    eigen_share = lax.psum(eigen_mine, "blk")
    coef_rows = jnp.einsum("jrkr->jk", cross.reshape(pos_dev, KRON, modes, KRON)) / frame
    return (returned[None], eigen_share, coef_rows)


def solution(mesh):
    in_specs = (
        P(("recon", "blk"), None, None, None),
        P("recon", None, None, None),
        P(("recon", "blk", "probe"), None),
        P(("recon", "blk", "probe"), None),
        P(("recon", "blk", "probe"), None),
        P(("recon", "blk", "probe"), None, None),
        P(("recon", "blk")),
    )
    out_specs = (
        P(("recon", "blk"), None, "probe", None),
        P("recon", None, "probe", None),
        P(("recon", "blk", "probe"), None),
    )
    return jax.shard_map(
        on_device, mesh=mesh, in_specs=in_specs, out_specs=out_specs, check_vma=False
    )
```

```python
import functools
import math

import jax
import jax.numpy as jnp
import ml_dtypes
import numpy as np
from jax import lax
from jax.experimental import pallas as pl
from jax.experimental.pallas import tpu as pltpu
from jax.sharding import PartitionSpec as P

REACH = 3
LANES = 128
STRIP = 16
VMEM = pltpu.MemorySpace.VMEM
SMEM = pltpu.MemorySpace.SMEM
VMEM_LIMIT = 36 * 1024 * 1024


def tables(frame):
    indices = np.arange(frame)
    angle = (indices[:, None] * indices[None, :] % frame) * (2.0 * math.pi / frame)
    cos_part = np.cos(angle) / math.sqrt(frame)
    sin_part = -np.sin(angle) / math.sqrt(frame)
    forward = np.block([[cos_part, sin_part], [-sin_part, cos_part]])
    forward = forward.astype(np.float32).astype(ml_dtypes.bfloat16)
    return jnp.asarray(np.stack([forward, forward.T]))


def shift(array, axis, by):
    peers = lax.axis_size(axis)
    return lax.ppermute(array, axis, [(i, (i + by) % peers) for i in range(peers)])


def swap(array, axis, bit):
    peers = lax.axis_size(axis)
    return lax.ppermute(array, axis, [(i, i ^ bit) for i in range(peers)])


def slabs_of(member, h):
    pair, core = member >> 1, member & 1
    mine = 2 * (pair ^ h) + core
    return mine, mine ^ 1


def turned(groups, peers):
    return groups // peers if groups % peers == 0 else 0


def coordinates(tile_list, offsets, group_counts, pos_dev):
    blocks = lax.axis_size("blk")
    my_block, member = lax.axis_index("blk"), lax.axis_index("probe")
    alive = jnp.clip(group_counts[0] - member * pos_dev, 0, pos_dev)

    def place(j, m):
        section = lax.rem(tile_list[m, j] - my_block + blocks, blocks)
        return section, offsets[2 * m, j], offsets[2 * m + 1, j]

    return my_block, member, alive, place


def one_hot(shape, axis):
    return (
        lax.broadcasted_iota(jnp.int32, shape, axis) // STRIP == lax.broadcasted_iota(jnp.int32, shape, 1 - axis)
    ).astype(jnp.float32)


def diagonals(array):
    row = lax.broadcasted_iota(jnp.int32, array.shape, 0)
    col = lax.broadcasted_iota(jnp.int32, array.shape, 1)
    return jnp.where(row % STRIP == col % STRIP, array, 0.0)


def exact(left, right):
    return jnp.dot(left, right, precision=lax.Precision.HIGHEST, preferred_element_type=jnp.float32)


def two_terms(array):
    high = array.astype(jnp.bfloat16)
    return high, (array - high.astype(jnp.float32)).astype(jnp.bfloat16)


def position_kernel(offs, scale, tile_list, offsets, group_counts, *refs):
    shares = len(offs)
    pieces = refs[: 1 + (REACH - 1) * shares]
    tables_in, amps_in, eig, coef_in = refs[len(pieces):len(pieces) + 4]
    eigen_send, eigen_keep, grads_out, coef = refs[len(pieces) + 4:len(pieces) + 8]
    (staged, table, probe, amps, obj, ex, mid, far, patch, d_high, d_low, eigen, out_eigen, cross,
     weights, weights_t, piece_sem, table_sem, amps_sem, grad_sem, out_sem) = refs[len(pieces) + 8:]
    pos_dev, _, frame, _ = probe.shape
    modes = eig.shape[0]
    side = staged.shape[2]
    blocks = side // LANES
    slab = side // shares
    my_block, member, alive, place = coordinates(tile_list, offsets, group_counts, pos_dev)
    strips = range(frame // STRIP)

    copies = [pltpu.make_async_copy(pieces[0], staged.at[0], piece_sem.at[0])]
    for section in range(1, REACH):
        for i in range(shares):
            start = pl.multiple_of((member ^ offs[i]) * slab, slab)
            at = 1 + (section - 1) * shares + i
            copies.append(
                pltpu.make_async_copy(
                    pieces[at], staged.at[section, :, pl.ds(start, slab), :], piece_sem.at[at]
                )
            )
    table_copy = pltpu.make_async_copy(tables_in, table, table_sem)
    amps_copy = pltpu.make_async_copy(amps_in, amps, amps_sem)
    for copy in copies + [table_copy, amps_copy]:
        copy.start()

    by_position = (pos_dev * STRIP, pos_dev)
    by_mode = (modes * STRIP, modes)
    tall_t = exact(exact(one_hot(by_mode, 0), coef_in[...]), one_hot(by_position[::-1], 1))
    high, low = two_terms(diagonals(tall_t))
    weights_t[...] = jnp.concatenate([high, low], 0)
    spread = lax.dot_general(
        one_hot(by_position, 0), coef_in[...], (((1,), (1,)), ((), ())),
        precision=lax.Precision.HIGHEST, preferred_element_type=jnp.float32,
    )
    high, low = two_terms(diagonals(exact(spread, one_hot(by_mode[::-1], 1))))
    weights[...] = jnp.concatenate([high, low], 1)

    def synth(i, carry):
        rows = pl.ds(pl.multiple_of(i * STRIP, STRIP), STRIP)
        for c in range(2):
            e = eig[:, c, rows, :].reshape(modes * STRIP, frame)
            made = jnp.dot(
                weights[...], jnp.concatenate([e, e], 0), preferred_element_type=jnp.float32
            )
            probe[:, c, rows, :] = made.reshape(pos_dev, STRIP, frame)
        return carry

    lax.fori_loop(0, frame // STRIP, synth, 0, unroll=4)
    for copy in copies:
        copy.wait()

    def widen(i, carry):
        rows = pl.ds(pl.multiple_of(i * LANES, LANES), LANES)
        for section in range(REACH):
            for c in range(2):
                for b in range(blocks):
                    obj[section, c, b, rows, :] = staged[
                        section, c, rows, b * LANES:(b + 1) * LANES
                    ].astype(jnp.float32)
        return carry

    lax.fori_loop(0, side // LANES, widen, 0)
    table_copy.wait()
    amps_copy.wait()

    lane = lax.broadcasted_iota(jnp.int32, (STRIP, LANES), 1)

    def enter(j, slot):
        where = []
        for m in range(2):
            section, row, col = place(j, m)
            s = col % LANES
            where.append((section, row, col // LANES, (LANES - s) % LANES, lane < LANES - s))
        for i in strips:
            rows = slice(i * STRIP, (i + 1) * STRIP)
            parts = []
            for c in range(2):
                total = None
                for section, row, cb, back_by, keep_lane in where:
                    rolled = [
                        pltpu.roll(obj[section, c, cb + b, pl.ds(row + i * STRIP, STRIP), :], back_by, 1)
                        for b in range(3)
                    ]
                    block = [jnp.where(keep_lane, rolled[b], rolled[b + 1]) for b in range(2)]
                    total = block if total is None else [x + y for x, y in zip(total, block)]
                parts.append([0.5 * x for x in total])
            for b in range(2):
                cols = slice(b * LANES, (b + 1) * LANES)
                o_re, o_im = parts[0][b], parts[1][b]
                p_re, p_im = probe[j, 0, rows, cols], probe[j, 1, rows, cols]
                patch[slot, 0, rows, cols] = o_re
                patch[slot, 1, rows, cols] = o_im
                ex[slot, rows, b * LANES:(b + 1) * LANES] = (p_re * o_re - p_im * o_im).astype(jnp.bfloat16)
                ex[slot, rows, frame + b * LANES:frame + (b + 1) * LANES] = (
                    p_re * o_im + p_im * o_re
                ).astype(jnp.bfloat16)

    def transform(slot, way):
        half = jnp.dot(ex[slot], table[way], preferred_element_type=jnp.float32)
        mid[slot, :frame] = half[:, :frame].astype(jnp.bfloat16)
        mid[slot, frame:] = half[:, frame:].astype(jnp.bfloat16)
        far[slot] = jnp.dot(table[1 - way], mid[slot], preferred_element_type=jnp.float32)

    def residual(j, slot, living):
        for i in strips:
            rows = slice(i * STRIP, (i + 1) * STRIP)
            lower = slice(frame + i * STRIP, frame + (i + 1) * STRIP)
            f_re, f_im = far[slot, rows], far[slot, lower]
            factor = 1.0 - amps[j, rows].astype(jnp.float32) * lax.rsqrt(f_re * f_re + f_im * f_im + 1.0)
            if living is not None:
                factor = factor * living
            ex[slot, rows, :frame] = (f_re * factor).astype(jnp.bfloat16)
            ex[slot, rows, frame:] = (f_im * factor).astype(jnp.bfloat16)

    def leave(j, slot):
        for i in strips:
            rows = slice(i * STRIP, (i + 1) * STRIP)
            lower = slice(frame + i * STRIP, frame + (i + 1) * STRIP)
            b_re, b_im = far[slot, rows], far[slot, lower]
            o_re, o_im = patch[slot, 0, rows], patch[slot, 1, rows]
            p_re, p_im = probe[j, 0, rows], probe[j, 1, rows]
            for c, d in enumerate((o_re * b_re + o_im * b_im, o_re * b_im - o_im * b_re)):
                high = d.astype(jnp.bfloat16)
                d_high[j, c, rows] = high
                d_low[j, c, rows] = (d - high.astype(jnp.float32)).astype(jnp.bfloat16)
            probe[j, 0, rows] = 0.5 * (p_re * b_re + p_im * b_im)
            probe[j, 1, rows] = 0.5 * (p_re * b_im - p_im * b_re)

    def grad_copy(j):
        return pltpu.make_async_copy(probe.at[j], grads_out.at[j], grad_sem.at[j])

    def visit(pair, carry):
        first, second = 2 * pair, 2 * pair + 1
        enter(first, 0)
        transform(0, 0)
        enter(second, 1)
        transform(1, 0)
        residual(first, 0, None)
        transform(0, 1)
        residual(second, 1, jnp.where(second < alive, 1.0, 0.0))
        transform(1, 1)
        leave(first, 0)
        leave(second, 1)
        grad_copy(first).start()
        grad_copy(second).start()
        return carry

    pairs = (alive + 1) // 2
    lax.fori_loop(0, pairs, visit, 0)

    def skip(j, carry):
        d_high[j] = jnp.zeros((2, frame, frame), jnp.bfloat16)
        d_low[j] = jnp.zeros((2, frame, frame), jnp.bfloat16)
        return carry

    lax.fori_loop(2 * pairs, pos_dev, skip, 0)

    cross[...] = jnp.zeros_like(cross)
    rows_q = frame // shares
    groups = 2 * modes
    turn = my_block * turned(groups, lax.axis_size("blk"))

    def eigen_strip(i, carry):
        rows = pl.ds(pl.multiple_of(i * STRIP, STRIP), STRIP)
        q = i // (rows_q // STRIP)
        inner = pl.ds(pl.multiple_of(i % (rows_q // STRIP) * STRIP, STRIP), STRIP)
        for c in range(2):
            high = d_high[:, c, rows, :].reshape(pos_dev * STRIP, frame)
            low = d_low[:, c, rows, :].reshape(pos_dev * STRIP, frame)
            e = eig[:, c, rows, :].reshape(modes * STRIP, frame)
            both = jnp.dot(weights_t[...], high, preferred_element_type=jnp.float32)
            rest = jnp.dot(weights_t[:modes * STRIP], low, preferred_element_type=jnp.float32)
            grad = (both[:modes * STRIP] + both[modes * STRIP:] + rest) * scale
            for k in range(modes):
                group = lax.rem(2 * k + c + groups - turn, groups)
                eigen[q, group, inner, :] = grad[k * STRIP:(k + 1) * STRIP]
            cross[...] += lax.dot_general(
                high, e, (((1,), (1,)), ((), ())), preferred_element_type=jnp.float32
            )
        return carry

    lax.fori_loop(0, frame // STRIP, eigen_strip, 0, unroll=4)
    pending = []

    def start(source, target):
        copy = pltpu.make_async_copy(source, target, out_sem.at[len(pending)])
        copy.start()
        pending.append(copy)

    for h in range(shares // 2):
        mine, other = slabs_of(member, h)
        out_eigen[h] = eigen[other].astype(jnp.bfloat16)
        start(eigen.at[mine], eigen_keep.at[h])
    start(out_eigen, eigen_send)

    total = exact(one_hot(by_position[::-1], 1), diagonals(cross[...]))
    coef[...] = lax.dot_general(
        one_hot(by_mode[::-1], 1), total, (((1,), (1,)), ((), ())),
        precision=lax.Precision.HIGHEST, preferred_element_type=jnp.float32,
    ) * (1.0 / frame)

    def drain(j, carry):
        grad_copy(j).wait()
        return carry

    lax.fori_loop(0, 2 * pairs, drain, 0)
    for copy in pending:
        copy.wait()


def positions(offs, scale, indices, pieces, table, amps, eigenprobes, coefficients):
    modes, _, frame, _ = eigenprobes.shape
    pos_dev = amps.shape[0]
    side = pieces[0].shape[2]
    shares = len(offs)
    blocks = side // LANES
    smem = pl.BlockSpec(memory_space=SMEM)
    whole = pl.BlockSpec(memory_space=VMEM)
    anywhere = pl.BlockSpec(memory_space=pl.ANY)
    eigen_half = (shares // 2, 2 * modes, frame // shares, frame)
    grads = (pos_dev, 2, frame, frame)
    return pl.pallas_call(
        functools.partial(position_kernel, offs, scale),
        in_specs=[smem] * 3 + [anywhere] * (len(pieces) + 2) + [whole] * 2,
        out_specs=[anywhere] * 3 + [whole],
        scratch_shapes=[
            pltpu.VMEM((REACH, 2, side, side), jnp.bfloat16),
            pltpu.VMEM(table.shape, jnp.bfloat16),
            pltpu.VMEM(grads, jnp.float32),
            pltpu.VMEM(amps.shape, jnp.bfloat16),
            pltpu.VMEM((REACH, 2, blocks + 1, side, LANES), jnp.float32),
            pltpu.VMEM((2, frame, 2 * frame), jnp.bfloat16),
            pltpu.VMEM((2, 2 * frame, frame), jnp.bfloat16),
            pltpu.VMEM((2, 2 * frame, frame), jnp.float32),
            pltpu.VMEM((2, 2, frame, frame), jnp.float32),
            pltpu.VMEM(grads, jnp.bfloat16),
            pltpu.VMEM(grads, jnp.bfloat16),
            pltpu.VMEM((shares, 2 * modes, frame // shares, frame), jnp.float32),
            pltpu.VMEM(eigen_half, jnp.bfloat16),
            pltpu.VMEM((pos_dev * STRIP, modes * STRIP), jnp.float32),
            pltpu.VMEM((pos_dev * STRIP, 2 * modes * STRIP), jnp.bfloat16),
            pltpu.VMEM((2 * modes * STRIP, pos_dev * STRIP), jnp.bfloat16),
            pltpu.SemaphoreType.DMA((len(pieces),)),
            pltpu.SemaphoreType.DMA,
            pltpu.SemaphoreType.DMA,
            pltpu.SemaphoreType.DMA((pos_dev,)),
            pltpu.SemaphoreType.DMA((shares // 2 + 1,)),
        ],
        out_shape=[
            jax.ShapeDtypeStruct(eigen_half, jnp.bfloat16),
            jax.ShapeDtypeStruct(eigen_half, jnp.float32),
            jax.ShapeDtypeStruct(grads, jnp.float32),
            jax.ShapeDtypeStruct((modes, pos_dev), jnp.float32),
        ],
        compiler_params=pltpu.CompilerParams(vmem_limit_bytes=VMEM_LIMIT),
        name="positions",
    )(*indices, *pieces, table, amps, eigenprobes, coefficients.T)


def scatter_kernel(shares, tile_list, offsets, group_counts, grads_in, *refs):
    send, keep = refs[:REACH], refs[REACH:2 * REACH]
    grads, acc, out_send, grad_sem, out_sem = refs[2 * REACH:]
    pos_dev, _, frame, _ = grads.shape
    blocks, side = acc.shape[2] - 1, acc.shape[3]
    slab = side // shares
    _, member, alive, place = coordinates(tile_list, offsets, group_counts, pos_dev)

    def grad_copy(j):
        return pltpu.make_async_copy(grads_in.at[j], grads.at[j], grad_sem.at[j])

    def begin(j, carry):
        grad_copy(j).start()
        return carry

    lax.fori_loop(0, alive, begin, 0)

    def clear(i, carry):
        rows = pl.ds(pl.multiple_of(i * LANES, LANES), LANES)
        for section in range(REACH):
            for c in range(2):
                for b in range(blocks + 1):
                    acc[section, c, b, rows, :] = jnp.zeros((LANES, LANES), jnp.float32)
        return carry

    lax.fori_loop(0, side // LANES, clear, 0)
    lane = lax.broadcasted_iota(jnp.int32, (STRIP, LANES), 1)

    def add(j, carry):
        grad_copy(j).wait()
        for m in range(2):
            section, row, col = place(j, m)
            cb, s = col // LANES, col % LANES
            inside = lane >= s
            for i in range(frame // STRIP):
                for c in range(2):
                    low, high = (
                        pltpu.roll(grads[j, c, i * STRIP:(i + 1) * STRIP, b * LANES:(b + 1) * LANES], s, 1)
                        for b in range(2)
                    )
                    for b, value in enumerate(
                        (
                            jnp.where(inside, low, 0.0),
                            jnp.where(inside, high, low),
                            jnp.where(inside, 0.0, high),
                        )
                    ):
                        at = (section, c, cb + b, pl.ds(row + i * STRIP, STRIP), slice(None))
                        acc[at] = acc[at] + value
        return carry

    lax.fori_loop(0, alive, add, 0)
    pending = []

    def start(source, target):
        copy = pltpu.make_async_copy(source, target, out_sem.at[len(pending)])
        copy.start()
        pending.append(copy)

    for section in range(REACH - 1, -1, -1):
        for h in range(shares // 2):
            mine, other = (pl.multiple_of(at * slab, slab) for at in slabs_of(member, h))
            start(acc.at[section, :, pl.ds(0, blocks), pl.ds(mine, slab), :], keep[section].at[h])
            for c in range(2):
                for b in range(blocks):
                    out_send[section, h, c, b] = acc[section, c, b, pl.ds(other, slab), :].astype(jnp.bfloat16)
        start(out_send.at[section], send[section])
    for copy in pending:
        copy.wait()


def scatter(shares, side, indices, grads):
    blocks = side // LANES
    anywhere = pl.BlockSpec(memory_space=pl.ANY)
    half = (shares // 2, 2, blocks, side // shares, LANES)
    return pl.pallas_call(
        functools.partial(scatter_kernel, shares),
        in_specs=[pl.BlockSpec(memory_space=SMEM)] * 3 + [anywhere],
        out_specs=[anywhere] * (2 * REACH),
        scratch_shapes=[
            pltpu.VMEM(grads.shape, jnp.float32),
            pltpu.VMEM((REACH, 2, blocks + 1, side, LANES), jnp.float32),
            pltpu.VMEM((REACH,) + half, jnp.bfloat16),
            pltpu.SemaphoreType.DMA((grads.shape[0],)),
            pltpu.SemaphoreType.DMA((REACH * (shares // 2 + 1),)),
        ],
        out_shape=[jax.ShapeDtypeStruct(half, jnp.bfloat16)] * REACH
        + [jax.ShapeDtypeStruct(half, jnp.float32)] * REACH,
        compiler_params=pltpu.CompilerParams(vmem_limit_bytes=20 * 1024 * 1024),
        cost_estimate=pl.CostEstimate(flops=1 << 24, bytes_accessed=16 << 20, transcendentals=0),
        name="scatter",
    )(*indices, grads)


def after(array, *others):
    return lax.optimization_barrier((array,) + others)[0]


def halve(keep, send, before_core=(), before_cross=()):
    arrived = swap(after(send, *before_core), "probe", 1)
    terms = [keep, after(arrived, *before_cross)]
    bit = 2
    leaving = send
    while keep.shape[0] * 2 > bit:
        pick = lambda term, which: term.reshape((term.shape[0] // 2, 2) + term.shape[1:])[:, which]
        sending = sum(pick(term, 1).astype(jnp.float32) for term in terms).astype(jnp.bfloat16)
        if bit == 2:
            leaving = sending
        arrived = swap(sending, "probe", bit)
        terms = [pick(term, 0) for term in terms] + [arrived]
        bit *= 2
    return sum(term[0].astype(jnp.float32) for term in terms), leaving, arrived


def place_kernel(me, *refs):
    pieces, out = refs[:-1], refs[-1]
    peers = len(pieces)
    for by, piece in enumerate(pieces):
        out[(me[0] + peers - by) % peers] = piece[...].astype(jnp.float32)


def sum_over(axis, value, turned):
    peers = lax.axis_size(axis)
    me = lax.axis_index(axis)
    rows = value.shape[0] // peers

    def chunk(by):
        if turned:
            return value[by * rows:(by + 1) * rows]
        return lax.dynamic_slice_in_dim(value, (me + by) % peers * rows, rows, 0)

    total = chunk(0)
    for by in range(1, peers):
        total += shift(chunk(by).astype(jnp.bfloat16), axis, by).astype(jnp.float32)
    total = total.astype(jnp.bfloat16)
    return [total] + [shift(total, axis, by) for by in range(1, peers)]


def place(axis, held):
    peers, (rows, lanes) = len(held), held[0].shape
    return pl.pallas_call(
        place_kernel,
        in_specs=[pl.BlockSpec(memory_space=SMEM)] + [pl.BlockSpec(memory_space=VMEM)] * peers,
        out_specs=pl.BlockSpec(memory_space=VMEM),
        out_shape=jax.ShapeDtypeStruct((peers, rows, lanes), jnp.float32),
        compiler_params=pltpu.CompilerParams(vmem_limit_bytes=8 * 1024 * 1024),
        name="place",
    )(lax.axis_index(axis).reshape(1).astype(jnp.int32), *held)


def finish_kernel(first, second, out):
    blocks = first.shape[1]
    for c in range(2):
        for b in range(blocks):
            out[c, :, b * LANES:(b + 1) * LANES] = first[c, b] + second[c, b].astype(jnp.float32)


def finish(first, second):
    _, blocks, slab, lanes = first.shape
    return pl.pallas_call(
        finish_kernel,
        in_specs=[pl.BlockSpec(memory_space=VMEM)] * 2,
        out_specs=pl.BlockSpec(memory_space=VMEM),
        out_shape=jax.ShapeDtypeStruct((2, slab, blocks * lanes), jnp.float32),
        compiler_params=pltpu.CompilerParams(vmem_limit_bytes=8 * 1024 * 1024),
        name="finish",
    )(first, second)


def on_device(tiles, eigenprobes, coefficients, tile_list, offsets, amplitudes, group_counts):
    modes, _, frame, _ = eigenprobes.shape
    side = tiles.shape[2]
    pos_dev = coefficients.shape[0]
    blocks = lax.axis_size("blk")
    shares = lax.axis_size("probe")
    member = lax.axis_index("probe")
    slab = side // shares
    bits = [1 << i for i in range(shares.bit_length() - 1)]
    table = tables(frame)

    own = lax.dynamic_slice_in_dim(tiles[0], member * slab, slab, 1)
    pieces = [tiles[0]]
    offs = [0]
    for bit in reversed(bits):
        offs = offs + [o ^ bit for o in offs]
    moving = own
    for section in range(1, REACH):
        moving = shift(moving, "blk", -1)
        held = [moving]
        for bit in reversed(bits):
            held = held + [swap(piece, "probe", bit) for piece in held]
        pieces += held

    indices = (tile_list.T, offsets.T, group_counts)
    scale = (pos_dev * blocks * shares) ** (-0.5)
    eigen_send, eigen_keep, grads, coef_rows = positions(
        tuple(offs), scale, indices, pieces, table, amplitudes, eigenprobes, coefficients
    )

    eigen, leaving, crossed = halve(eigen_keep, eigen_send)
    out = scatter(shares, side, indices, after(grads, leaving))
    send, keep = out[:REACH], out[REACH:]
    last = REACH - 1
    mine, leaving, crossed = halve(keep[last], send[last], before_core=(crossed,))
    eigen = after(eigen, leaving)
    held = sum_over("blk", eigen.reshape(-1, frame), turned(2 * modes, blocks) > 0)
    moving = mine.astype(jnp.bfloat16)
    gate = moving
    for section in range(last - 1, -1, -1):
        mine, _, _ = halve(keep[section], send[section], before_cross=(gate,))
        gate = arrived = shift(moving, "blk", 1)
        if section > 0:
            moving = (arrived.astype(jnp.float32) + mine).astype(jnp.bfloat16)
    eigen_share = place("blk", [after(held[0], moving)] + held[1:])
    eigen_share = eigen_share.reshape(modes, 2, frame // shares, frame)
    summed = finish(mine, arrived)
    return (summed[None], eigen_share, coef_rows.T)


def solution(mesh):
    in_specs = (
        P(("recon", "blk"), None, None, None),
        P("recon", None, None, None),
        P(("recon", "blk", "probe"), None),
        P(("recon", "blk", "probe"), None),
        P(("recon", "blk", "probe"), None),
        P(("recon", "blk", "probe"), None, None),
        P(("recon", "blk")),
    )
    out_specs = (
        P(("recon", "blk"), None, "probe", None),
        P("recon", None, "probe", None),
        P(("recon", "blk", "probe"), None),
    )
    return jax.shard_map(
        on_device, mesh=mesh, in_specs=in_specs, out_specs=out_specs, check_vma=False
    )
```

```python
import functools
import math

import jax
import jax.numpy as jnp
import ml_dtypes
import numpy as np
from jax import lax
from jax.experimental import pallas as pl
from jax.experimental.pallas import tpu as pltpu
from jax.sharding import PartitionSpec as P

REACH = 3
LANES = 128
STRIP = 16
VMEM = pltpu.MemorySpace.VMEM
SMEM = pltpu.MemorySpace.SMEM
VMEM_LIMIT = 36 * 1024 * 1024


def tables(frame):
    indices = np.arange(frame)
    angle = (indices[:, None] * indices[None, :] % frame) * (2.0 * math.pi / frame)
    cos_part = np.cos(angle) / math.sqrt(frame)
    sin_part = -np.sin(angle) / math.sqrt(frame)
    forward = np.block([[cos_part, sin_part], [-sin_part, cos_part]])
    forward = forward.astype(np.float32).astype(ml_dtypes.bfloat16)
    return jnp.asarray(np.stack([forward, forward.T]))


def shift(array, axis, by):
    peers = lax.axis_size(axis)
    return lax.ppermute(array, axis, [(i, (i + by) % peers) for i in range(peers)])


def swap(array, axis, bit):
    peers = lax.axis_size(axis)
    return lax.ppermute(array, axis, [(i, i ^ bit) for i in range(peers)])


def slabs_of(member, h):
    pair, core = member >> 1, member & 1
    mine = 2 * (pair ^ h) + core
    return mine, mine ^ 1


def share_of(groups, peers):
    return groups // peers if groups % peers == 0 else 0


def coordinates(tile_list, offsets, group_counts, pos_dev):
    blocks = lax.axis_size("blk")
    my_block, member = lax.axis_index("blk"), lax.axis_index("probe")
    alive = jnp.clip(group_counts[0] - member * pos_dev, 0, pos_dev)

    def place(j, m):
        section = lax.rem(tile_list[m, j] - my_block + blocks, blocks)
        return section, offsets[2 * m, j], offsets[2 * m + 1, j]

    return my_block, member, alive, place


def one_hot(shape, axis):
    return (
        lax.broadcasted_iota(jnp.int32, shape, axis) // STRIP == lax.broadcasted_iota(jnp.int32, shape, 1 - axis)
    ).astype(jnp.float32)


def diagonals(array):
    row = lax.broadcasted_iota(jnp.int32, array.shape, 0)
    col = lax.broadcasted_iota(jnp.int32, array.shape, 1)
    return jnp.where(row % STRIP == col % STRIP, array, 0.0)


def exact(left, right):
    return jnp.dot(left, right, precision=lax.Precision.HIGHEST, preferred_element_type=jnp.float32)


def two_terms(array):
    high = array.astype(jnp.bfloat16)
    return high, (array - high.astype(jnp.float32)).astype(jnp.bfloat16)


def stage_kernel(*refs):
    count = len(refs) // 2
    sem = refs[-1]
    copies = [
        pltpu.make_async_copy(source, target, sem.at[i])
        for i, (source, target) in enumerate(zip(refs[:count], refs[count:2 * count]))
    ]
    for copy in copies:
        copy.start()
    for copy in copies:
        copy.wait()


def stage(*arrays):
    anywhere = pl.BlockSpec(memory_space=pl.ANY)
    return pl.pallas_call(
        stage_kernel,
        in_specs=[anywhere] * len(arrays),
        out_specs=[anywhere] * len(arrays),
        scratch_shapes=[pltpu.SemaphoreType.DMA((len(arrays),))],
        out_shape=[jax.ShapeDtypeStruct(x.shape, x.dtype) for x in arrays],
        compiler_params=pltpu.CompilerParams(vmem_limit_bytes=1024 * 1024),
        name="stage",
    )(*arrays)


def position_kernel(offs, scale, tile_list, offsets, group_counts, *refs):
    shares = len(offs)
    pieces = refs[: 1 + (REACH - 1) * shares]
    eig_in, amps_in, tables_in, coef_in = refs[len(pieces):len(pieces) + 4]
    eigen_send, eigen_keep, grads_out, coef = refs[len(pieces) + 4:len(pieces) + 8]
    (staged, table, probe, amps, eig, obj, ex, mid, far, patch, d_high, d_low, eigen, out_eigen, cross,
     weights, weights_t, piece_sem, table_sem, amps_sem, eig_sem, grad_sem, out_sem) = refs[len(pieces) + 8:]
    pos_dev, _, frame, _ = probe.shape
    modes = eig.shape[0]
    side = staged.shape[2]
    blocks = side // LANES
    slab = side // shares
    my_block, member, alive, place = coordinates(tile_list, offsets, group_counts, pos_dev)
    strips = range(frame // STRIP)

    copies = [pltpu.make_async_copy(pieces[0], staged.at[0], piece_sem.at[0])]
    for section in range(1, REACH):
        for i in range(shares):
            start = pl.multiple_of((member ^ offs[i]) * slab, slab)
            at = 1 + (section - 1) * shares + i
            copies.append(
                pltpu.make_async_copy(
                    pieces[at], staged.at[section, :, pl.ds(start, slab), :], piece_sem.at[at]
                )
            )
    table_copy = pltpu.make_async_copy(tables_in, table, table_sem)
    amps_copy = pltpu.make_async_copy(amps_in, amps, amps_sem)
    eig_copy = pltpu.make_async_copy(eig_in, eig, eig_sem)
    for copy in [eig_copy] + copies + [table_copy, amps_copy]:
        copy.start()

    by_position = (pos_dev * STRIP, pos_dev)
    by_mode = (modes * STRIP, modes)
    tall_t = exact(exact(one_hot(by_mode, 0), coef_in[...]), one_hot(by_position[::-1], 1))
    high, low = two_terms(diagonals(tall_t))
    weights_t[...] = jnp.concatenate([high, low], 0)
    spread = lax.dot_general(
        one_hot(by_position, 0), coef_in[...], (((1,), (1,)), ((), ())),
        precision=lax.Precision.HIGHEST, preferred_element_type=jnp.float32,
    )
    high, low = two_terms(diagonals(exact(spread, one_hot(by_mode[::-1], 1))))
    weights[...] = jnp.concatenate([high, low], 1)
    eig_copy.wait()

    def synth(i, carry):
        rows = pl.ds(pl.multiple_of(i * STRIP, STRIP), STRIP)
        for c in range(2):
            e = eig[:, c, rows, :].reshape(modes * STRIP, frame)
            made = jnp.dot(
                weights[...], jnp.concatenate([e, e], 0), preferred_element_type=jnp.float32
            )
            probe[:, c, rows, :] = made.reshape(pos_dev, STRIP, frame)
        return carry

    lax.fori_loop(0, frame // STRIP, synth, 0, unroll=4)
    for copy in copies:
        copy.wait()

    def widen(i, carry):
        rows = pl.ds(pl.multiple_of(i * LANES, LANES), LANES)
        for section in range(REACH):
            for c in range(2):
                for b in range(blocks):
                    obj[section, c, b, rows, :] = staged[
                        section, c, rows, b * LANES:(b + 1) * LANES
                    ].astype(jnp.float32)
        return carry

    lax.fori_loop(0, side // LANES, widen, 0)
    table_copy.wait()
    amps_copy.wait()

    lane = lax.broadcasted_iota(jnp.int32, (STRIP, LANES), 1)

    def enter(j, slot):
        where = []
        for m in range(2):
            section, row, col = place(j, m)
            s = col % LANES
            where.append((section, row, col // LANES, (LANES - s) % LANES, lane < LANES - s))
        for i in strips:
            rows = slice(i * STRIP, (i + 1) * STRIP)
            parts = []
            for c in range(2):
                total = None
                for section, row, cb, back_by, keep_lane in where:
                    rolled = [
                        pltpu.roll(obj[section, c, cb + b, pl.ds(row + i * STRIP, STRIP), :], back_by, 1)
                        for b in range(3)
                    ]
                    block = [jnp.where(keep_lane, rolled[b], rolled[b + 1]) for b in range(2)]
                    total = block if total is None else [x + y for x, y in zip(total, block)]
                parts.append([0.5 * x for x in total])
            for b in range(2):
                cols = slice(b * LANES, (b + 1) * LANES)
                o_re, o_im = parts[0][b], parts[1][b]
                p_re, p_im = probe[j, 0, rows, cols], probe[j, 1, rows, cols]
                patch[slot, 0, rows, cols] = o_re
                patch[slot, 1, rows, cols] = o_im
                ex[slot, rows, b * LANES:(b + 1) * LANES] = (p_re * o_re - p_im * o_im).astype(jnp.bfloat16)
                ex[slot, rows, frame + b * LANES:frame + (b + 1) * LANES] = (
                    p_re * o_im + p_im * o_re
                ).astype(jnp.bfloat16)

    def transform(slot, way):
        half = jnp.dot(ex[slot], table[way], preferred_element_type=jnp.float32)
        mid[slot, :frame] = half[:, :frame].astype(jnp.bfloat16)
        mid[slot, frame:] = half[:, frame:].astype(jnp.bfloat16)
        far[slot] = jnp.dot(table[1 - way], mid[slot], preferred_element_type=jnp.float32)

    def residual(j, slot, living):
        for i in strips:
            rows = slice(i * STRIP, (i + 1) * STRIP)
            lower = slice(frame + i * STRIP, frame + (i + 1) * STRIP)
            f_re, f_im = far[slot, rows], far[slot, lower]
            factor = 1.0 - amps[j, rows].astype(jnp.float32) * lax.rsqrt(f_re * f_re + f_im * f_im + 1.0)
            if living is not None:
                factor = factor * living
            ex[slot, rows, :frame] = (f_re * factor).astype(jnp.bfloat16)
            ex[slot, rows, frame:] = (f_im * factor).astype(jnp.bfloat16)

    def leave(j, slot):
        for i in strips:
            rows = slice(i * STRIP, (i + 1) * STRIP)
            lower = slice(frame + i * STRIP, frame + (i + 1) * STRIP)
            b_re, b_im = far[slot, rows], far[slot, lower]
            o_re, o_im = patch[slot, 0, rows], patch[slot, 1, rows]
            p_re, p_im = probe[j, 0, rows], probe[j, 1, rows]
            for c, d in enumerate((o_re * b_re + o_im * b_im, o_re * b_im - o_im * b_re)):
                high = d.astype(jnp.bfloat16)
                d_high[j, c, rows] = high
                d_low[j, c, rows] = (d - high.astype(jnp.float32)).astype(jnp.bfloat16)
            probe[j, 0, rows] = 0.5 * (p_re * b_re + p_im * b_im)
            probe[j, 1, rows] = 0.5 * (p_re * b_im - p_im * b_re)

    def grad_copy(j):
        return pltpu.make_async_copy(probe.at[j], grads_out.at[j], grad_sem.at[j])

    def visit(pair, carry):
        first, second = 2 * pair, 2 * pair + 1
        enter(first, 0)
        transform(0, 0)
        enter(second, 1)
        transform(1, 0)
        residual(first, 0, None)
        transform(0, 1)
        residual(second, 1, jnp.where(second < alive, 1.0, 0.0))
        transform(1, 1)
        leave(first, 0)
        leave(second, 1)
        grad_copy(first).start()
        grad_copy(second).start()
        return carry

    pairs = (alive + 1) // 2
    lax.fori_loop(0, pairs, visit, 0)

    def skip(j, carry):
        d_high[j] = jnp.zeros((2, frame, frame), jnp.bfloat16)
        d_low[j] = jnp.zeros((2, frame, frame), jnp.bfloat16)
        return carry

    lax.fori_loop(2 * pairs, pos_dev, skip, 0)

    cross[...] = jnp.zeros_like(cross)
    rows_q = frame // shares
    groups = 2 * modes
    share = share_of(groups, lax.axis_size("blk"))

    def eigen_strip(i, carry):
        rows = pl.ds(pl.multiple_of(i * STRIP, STRIP), STRIP)
        q = i // (rows_q // STRIP)
        inner = pl.ds(pl.multiple_of(i % (rows_q // STRIP) * STRIP, STRIP), STRIP)
        for c in range(2):
            high = d_high[:, c, rows, :].reshape(pos_dev * STRIP, frame)
            low = d_low[:, c, rows, :].reshape(pos_dev * STRIP, frame)
            e = eig[:, c, rows, :].reshape(modes * STRIP, frame)
            both = jnp.dot(weights_t[...], high, preferred_element_type=jnp.float32)
            rest = jnp.dot(weights_t[:modes * STRIP], low, preferred_element_type=jnp.float32)
            grad = (both[:modes * STRIP] + both[modes * STRIP:] + rest) * scale
            for k in range(modes):
                group = 2 * k + c
                if share:
                    group = (group // share ^ my_block) * share + group % share
                eigen[q, group, inner, :] = grad[k * STRIP:(k + 1) * STRIP]
            cross[...] += lax.dot_general(
                high, e, (((1,), (1,)), ((), ())), preferred_element_type=jnp.float32
            )
        return carry

    lax.fori_loop(0, frame // STRIP, eigen_strip, 0, unroll=4)
    pending = []

    def start(source, target):
        copy = pltpu.make_async_copy(source, target, out_sem.at[len(pending)])
        copy.start()
        pending.append(copy)

    for h in range(shares // 2):
        mine, other = slabs_of(member, h)
        out_eigen[h] = eigen[other].astype(jnp.bfloat16)
        start(eigen.at[mine], eigen_keep.at[h])
    start(out_eigen, eigen_send)

    total = exact(one_hot(by_position[::-1], 1), diagonals(cross[...]))
    coef[...] = lax.dot_general(
        one_hot(by_mode[::-1], 1), total, (((1,), (1,)), ((), ())),
        precision=lax.Precision.HIGHEST, preferred_element_type=jnp.float32,
    ) * (1.0 / frame)

    def drain(j, carry):
        grad_copy(j).wait()
        return carry

    lax.fori_loop(0, 2 * pairs, drain, 0)
    for copy in pending:
        copy.wait()


def positions(offs, scale, indices, pieces, eigenprobes, amps, table, coef_t):
    modes, _, frame, _ = eigenprobes.shape
    pos_dev = amps.shape[0]
    side = pieces[0].shape[2]
    shares = len(offs)
    blocks = side // LANES
    smem = pl.BlockSpec(memory_space=SMEM)
    whole = pl.BlockSpec(memory_space=VMEM)
    anywhere = pl.BlockSpec(memory_space=pl.ANY)
    eigen_half = (shares // 2, 2 * modes, frame // shares, frame)
    grads = (pos_dev, 2, frame, frame)
    return pl.pallas_call(
        functools.partial(position_kernel, offs, scale),
        in_specs=[smem] * 3 + [anywhere] * (len(pieces) + 3) + [whole],
        out_specs=[anywhere] * 3 + [whole],
        scratch_shapes=[
            pltpu.VMEM((REACH, 2, side, side), jnp.bfloat16),
            pltpu.VMEM(table.shape, jnp.bfloat16),
            pltpu.VMEM(grads, jnp.float32),
            pltpu.VMEM(amps.shape, jnp.bfloat16),
            pltpu.VMEM(eigenprobes.shape, jnp.bfloat16),
            pltpu.VMEM((REACH, 2, blocks + 1, side, LANES), jnp.float32),
            pltpu.VMEM((2, frame, 2 * frame), jnp.bfloat16),
            pltpu.VMEM((2, 2 * frame, frame), jnp.bfloat16),
            pltpu.VMEM((2, 2 * frame, frame), jnp.float32),
            pltpu.VMEM((2, 2, frame, frame), jnp.float32),
            pltpu.VMEM(grads, jnp.bfloat16),
            pltpu.VMEM(grads, jnp.bfloat16),
            pltpu.VMEM((shares, 2 * modes, frame // shares, frame), jnp.float32),
            pltpu.VMEM(eigen_half, jnp.bfloat16),
            pltpu.VMEM((pos_dev * STRIP, modes * STRIP), jnp.float32),
            pltpu.VMEM((pos_dev * STRIP, 2 * modes * STRIP), jnp.bfloat16),
            pltpu.VMEM((2 * modes * STRIP, pos_dev * STRIP), jnp.bfloat16),
            pltpu.SemaphoreType.DMA((len(pieces),)),
            pltpu.SemaphoreType.DMA,
            pltpu.SemaphoreType.DMA,
            pltpu.SemaphoreType.DMA,
            pltpu.SemaphoreType.DMA((pos_dev,)),
            pltpu.SemaphoreType.DMA((shares // 2 + 1,)),
        ],
        out_shape=[
            jax.ShapeDtypeStruct(eigen_half, jnp.bfloat16),
            jax.ShapeDtypeStruct(eigen_half, jnp.float32),
            jax.ShapeDtypeStruct(grads, jnp.float32),
            jax.ShapeDtypeStruct((modes, pos_dev), jnp.float32),
        ],
        compiler_params=pltpu.CompilerParams(vmem_limit_bytes=VMEM_LIMIT),
        name="positions",
    )(*indices, *pieces, eigenprobes, amps, table, coef_t)


def scatter_kernel(shares, tile_list, offsets, group_counts, grads_in, *refs):
    send, keep = refs[:REACH], refs[REACH:2 * REACH]
    grads, acc, out_send, grad_sem, out_sem = refs[2 * REACH:]
    pos_dev, _, frame, _ = grads.shape
    blocks, side = acc.shape[2] - 1, acc.shape[3]
    slab = side // shares
    _, member, alive, place = coordinates(tile_list, offsets, group_counts, pos_dev)

    def grad_copy(j):
        return pltpu.make_async_copy(grads_in.at[j], grads.at[j], grad_sem.at[j])

    def begin(j, carry):
        grad_copy(j).start()
        return carry

    lax.fori_loop(0, alive, begin, 0)

    def clear(i, carry):
        rows = pl.ds(pl.multiple_of(i * LANES, LANES), LANES)
        for section in range(REACH):
            for c in range(2):
                for b in range(blocks + 1):
                    acc[section, c, b, rows, :] = jnp.zeros((LANES, LANES), jnp.float32)
        return carry

    lax.fori_loop(0, side // LANES, clear, 0)
    lane = lax.broadcasted_iota(jnp.int32, (STRIP, LANES), 1)

    def add(j, carry):
        grad_copy(j).wait()
        for m in range(2):
            section, row, col = place(j, m)
            cb, s = col // LANES, col % LANES
            inside = lane >= s
            for i in range(frame // STRIP):
                for c in range(2):
                    low, high = (
                        pltpu.roll(grads[j, c, i * STRIP:(i + 1) * STRIP, b * LANES:(b + 1) * LANES], s, 1)
                        for b in range(2)
                    )
                    for b, value in enumerate(
                        (
                            jnp.where(inside, low, 0.0),
                            jnp.where(inside, high, low),
                            jnp.where(inside, 0.0, high),
                        )
                    ):
                        at = (section, c, cb + b, pl.ds(row + i * STRIP, STRIP), slice(None))
                        acc[at] = acc[at] + value
        return carry

    lax.fori_loop(0, alive, add, 0)
    pending = []

    def start(source, target):
        copy = pltpu.make_async_copy(source, target, out_sem.at[len(pending)])
        copy.start()
        pending.append(copy)

    for section in range(REACH - 1, -1, -1):
        for h in range(shares // 2):
            mine, other = (pl.multiple_of(at * slab, slab) for at in slabs_of(member, h))
            start(acc.at[section, :, pl.ds(0, blocks), pl.ds(mine, slab), :], keep[section].at[h])
            for c in range(2):
                for b in range(blocks):
                    out_send[section, h, c, b] = acc[section, c, b, pl.ds(other, slab), :].astype(jnp.bfloat16)
        start(out_send.at[section], send[section])
    for copy in pending:
        copy.wait()


def scatter(shares, side, indices, grads):
    blocks = side // LANES
    anywhere = pl.BlockSpec(memory_space=pl.ANY)
    half = (shares // 2, 2, blocks, side // shares, LANES)
    return pl.pallas_call(
        functools.partial(scatter_kernel, shares),
        in_specs=[pl.BlockSpec(memory_space=SMEM)] * 3 + [anywhere],
        out_specs=[anywhere] * (2 * REACH),
        scratch_shapes=[
            pltpu.VMEM(grads.shape, jnp.float32),
            pltpu.VMEM((REACH, 2, blocks + 1, side, LANES), jnp.float32),
            pltpu.VMEM((REACH,) + half, jnp.bfloat16),
            pltpu.SemaphoreType.DMA((grads.shape[0],)),
            pltpu.SemaphoreType.DMA((REACH * (shares // 2 + 1),)),
        ],
        out_shape=[jax.ShapeDtypeStruct(half, jnp.bfloat16)] * REACH
        + [jax.ShapeDtypeStruct(half, jnp.float32)] * REACH,
        compiler_params=pltpu.CompilerParams(vmem_limit_bytes=20 * 1024 * 1024),
        cost_estimate=pl.CostEstimate(flops=1 << 24, bytes_accessed=16 << 20, transcendentals=0),
        name="scatter",
    )(*indices, grads)


def after(array, *others):
    return lax.optimization_barrier((array,) + others)[0]


def after_all(arrays, *others):
    return lax.optimization_barrier(tuple(arrays) + others)[:len(arrays)]


def halve(keep, send, before_core=(), before_cross=()):
    arrived = swap(after(send, *before_core), "probe", 1)
    terms = [keep, after(arrived, *before_cross)]
    bit = 2
    leaving = send
    while keep.shape[0] * 2 > bit:
        pick = lambda term, which: term.reshape((term.shape[0] // 2, 2) + term.shape[1:])[:, which]
        sending = sum(pick(term, 1).astype(jnp.float32) for term in terms).astype(jnp.bfloat16)
        if bit == 2:
            leaving = sending
        arrived = swap(sending, "probe", bit)
        terms = [pick(term, 0) for term in terms] + [arrived]
        bit *= 2
    return sum(term[0].astype(jnp.float32) for term in terms), leaving, arrived


def next_tiles(own, axis):
    peers = lax.axis_size(axis)
    near = lax.ppermute(own, axis, [(i, i - 1) for i in range(1, peers)])
    around = lax.ppermute(own, axis, [(0, peers - 1)])
    far_around = lax.ppermute(own, axis, [(0, peers - 2), (1, peers - 1)])
    far = lax.ppermute(near, axis, [(i, i - 1) for i in range(1, peers - 1)])
    return near + around, far + far_around


def scatter_rows(axis, value):
    me = lax.axis_index(axis)
    total = lax.dynamic_index_in_dim(value, me, 0, False)
    sent = []
    for i in range(1, lax.axis_size(axis)):
        sent.append(lax.dynamic_index_in_dim(value, me ^ i, 0, False).astype(jnp.bfloat16))
        total += swap(sent[-1], axis, i).astype(jnp.float32)
    return total.astype(jnp.bfloat16), sent


def scatter_sum(axis, value):
    terms = [value]
    sent = []
    bit = 1
    while bit < lax.axis_size(axis):
        pick = lambda term, which: term.reshape((term.shape[0] // 2, 2) + term.shape[1:])[:, which]
        sent.append(sum(pick(term, 1).astype(jnp.float32) for term in terms).astype(jnp.bfloat16))
        terms = [pick(term, 0) for term in terms] + [swap(sent[-1], axis, bit)]
        bit *= 2
    return sum(term[0].astype(jnp.float32) for term in terms).astype(jnp.bfloat16), sent


def gather_shares(axis, total):
    held = {0: total}
    bit = lax.axis_size(axis) // 2
    while bit:
        held.update({i ^ bit: swap(piece, axis, bit) for i, piece in held.items()})
        bit //= 2
    return [held[i] for i in range(lax.axis_size(axis))]


def place_kernel(axis, *refs):
    pieces, out = refs[:-1], refs[-1]
    me = lax.axis_index(axis)
    for i, piece in enumerate(pieces):
        out[me ^ i] = piece[...].astype(jnp.float32)


def place(axis, held):
    return pl.pallas_call(
        functools.partial(place_kernel, axis),
        in_specs=[pl.BlockSpec(memory_space=VMEM)] * len(held),
        out_specs=pl.BlockSpec(memory_space=VMEM),
        out_shape=jax.ShapeDtypeStruct((len(held),) + held[0].shape, jnp.float32),
        compiler_params=pltpu.CompilerParams(vmem_limit_bytes=8 * 1024 * 1024),
        name="place",
    )(*held)


def finish_kernel(first, second, out):
    blocks = first.shape[1]
    for c in range(2):
        for b in range(blocks):
            out[c, :, b * LANES:(b + 1) * LANES] = first[c, b] + second[c, b].astype(jnp.float32)


def finish(first, second):
    _, blocks, slab, lanes = first.shape
    return pl.pallas_call(
        finish_kernel,
        in_specs=[pl.BlockSpec(memory_space=VMEM)] * 2,
        out_specs=pl.BlockSpec(memory_space=VMEM),
        out_shape=jax.ShapeDtypeStruct((2, slab, blocks * lanes), jnp.float32),
        compiler_params=pltpu.CompilerParams(vmem_limit_bytes=8 * 1024 * 1024),
        name="finish",
    )(first, second)


def on_device(tiles, eigenprobes, coefficients, tile_list, offsets, amplitudes, group_counts):
    modes, _, frame, _ = eigenprobes.shape
    side = tiles.shape[2]
    pos_dev = coefficients.shape[0]
    blocks = lax.axis_size("blk")
    shares = lax.axis_size("probe")
    member = lax.axis_index("probe")
    slab = side // shares
    bits = [1 << i for i in range(shares.bit_length() - 1)]

    offs = [0]
    for bit in reversed(bits):
        offs = offs + [o ^ bit for o in offs]
    quarter = lax.dynamic_slice_in_dim(tiles[0], member * slab, slab, 1)
    near, far = next_tiles(quarter, "blk")
    held = [[near], [far]]
    eig, amps = stage(*after_all((eigenprobes, amplitudes), near))
    held[1][0] = after(held[1][0], eig)
    table, tile, coef_t, lists, corners = stage(
        *after_all((tables(frame), tiles[0], coefficients.T, tile_list.T, offsets.T), held[1][0])
    )
    for bit in reversed(bits):
        for part in held:
            arrived = [swap(piece, "probe", bit) for piece in part]
            if bit > 1:
                arrived[0] = after(arrived[0], eig if part is held[0] else table)
            part += arrived

    indices = (lists, corners, group_counts)
    scale = (pos_dev * blocks * shares) ** (-0.5)
    eigen_send, eigen_keep, grads, coef_rows = positions(
        tuple(offs), scale, indices, [tile] + held[0] + held[1], eig, amps, table, coef_t
    )

    eigen, leaving, crossed = halve(eigen_keep, eigen_send)
    out = scatter(shares, side, indices, after(grads, leaving))
    send, keep = out[:REACH], out[REACH:]
    last = REACH - 1
    share = share_of(2 * modes, blocks)
    if share:
        total, sent = scatter_sum("blk", eigen.reshape((blocks, share) + eigen.shape[1:]))
    else:
        total, sent = scatter_rows("blk", eigen.reshape(blocks, -1, frame))
    mine, leaving, _ = halve(keep[last], send[last], before_core=(crossed,), before_cross=sent[:1])
    moving = after(mine.astype(jnp.bfloat16), *sent[1:])
    for section in range(last - 1, -1, -1):
        mine, leaving, _ = halve(keep[section], send[section], before_cross=(moving,))
        if section == last - 1:
            total = after(total, leaving)
        arrived = shift(moving, "blk", 1)
        if section > 0:
            moving = (arrived.astype(jnp.float32) + mine).astype(jnp.bfloat16)
    shares_of_eigen = gather_shares("blk", total)
    shares_of_eigen[0] = after(shares_of_eigen[0], leaving)
    eigen_share = place("blk", shares_of_eigen).reshape(modes, 2, frame // shares, frame)
    summed = finish(mine, arrived)
    return (summed[None], eigen_share, coef_rows.T)


def solution(mesh):
    in_specs = (
        P(("recon", "blk"), None, None, None),
        P("recon", None, None, None),
        P(("recon", "blk", "probe"), None),
        P(("recon", "blk", "probe"), None),
        P(("recon", "blk", "probe"), None),
        P(("recon", "blk", "probe"), None, None),
        P(("recon", "blk")),
    )
    out_specs = (
        P(("recon", "blk"), None, "probe", None),
        P("recon", None, "probe", None),
        P(("recon", "blk", "probe"), None),
    )
    return jax.shard_map(
        on_device, mesh=mesh, in_specs=in_specs, out_specs=out_specs, check_vma=False
    )
```

```python
import functools
import math

import jax
import jax.numpy as jnp
import ml_dtypes
import numpy as np
from jax import lax
from jax.experimental import pallas as pl
from jax.experimental.pallas import tpu as pltpu
from jax.sharding import PartitionSpec as P

REACH = 3
LANES = 128
STRIP = 16
VMEM = pltpu.MemorySpace.VMEM
SMEM = pltpu.MemorySpace.SMEM
VMEM_LIMIT = 36 * 1024 * 1024


def tables(frame):
    indices = np.arange(frame)
    angle = (indices[:, None] * indices[None, :] % frame) * (2.0 * math.pi / frame)
    cos_part = np.cos(angle) / math.sqrt(frame)
    sin_part = -np.sin(angle) / math.sqrt(frame)
    forward = np.block([[cos_part, sin_part], [-sin_part, cos_part]])
    forward = forward.astype(np.float32).astype(ml_dtypes.bfloat16)
    return jnp.asarray(np.stack([forward, forward.T]))


def shift(array, axis, by):
    peers = lax.axis_size(axis)
    return lax.ppermute(array, axis, [(i, (i + by) % peers) for i in range(peers)])


def swap(array, axis, bit):
    peers = lax.axis_size(axis)
    return lax.ppermute(array, axis, [(i, i ^ bit) for i in range(peers)])


def slabs_of(member, h):
    pair, core = member >> 1, member & 1
    mine = 2 * (pair ^ h) + core
    return mine, mine ^ 1


def far_first(shares):
    return [*range(1, shares // 2, 2), *range(0, shares // 2, 2)]


def share_of(groups, peers):
    return groups // peers if groups % peers == 0 else 0


def coordinates(tile_list, offsets, group_counts, pos_dev):
    blocks = lax.axis_size("blk")
    my_block, member = lax.axis_index("blk"), lax.axis_index("probe")
    alive = jnp.clip(group_counts[0] - member * pos_dev, 0, pos_dev)

    def place(j, m):
        section = lax.rem(tile_list[m, j] - my_block + blocks, blocks)
        return section, offsets[2 * m, j], offsets[2 * m + 1, j]

    return my_block, member, alive, place


def one_hot(shape, axis):
    return (
        lax.broadcasted_iota(jnp.int32, shape, axis) // STRIP == lax.broadcasted_iota(jnp.int32, shape, 1 - axis)
    ).astype(jnp.float32)


def diagonals(array):
    row = lax.broadcasted_iota(jnp.int32, array.shape, 0)
    col = lax.broadcasted_iota(jnp.int32, array.shape, 1)
    return jnp.where(row % STRIP == col % STRIP, array, 0.0)


def exact(left, right):
    return jnp.dot(left, right, precision=lax.Precision.HIGHEST, preferred_element_type=jnp.float32)


def two_terms(array):
    high = array.astype(jnp.bfloat16)
    return high, (array - high.astype(jnp.float32)).astype(jnp.bfloat16)


def stage_kernel(*refs):
    count = len(refs) // 2
    sem = refs[-1]
    copies = [
        pltpu.make_async_copy(source, target, sem.at[i])
        for i, (source, target) in enumerate(zip(refs[:count], refs[count:2 * count]))
    ]
    for copy in copies:
        copy.start()
    for copy in copies:
        copy.wait()


def stage(*arrays):
    anywhere = pl.BlockSpec(memory_space=pl.ANY)
    return pl.pallas_call(
        stage_kernel,
        in_specs=[anywhere] * len(arrays),
        out_specs=[anywhere] * len(arrays),
        scratch_shapes=[pltpu.SemaphoreType.DMA((len(arrays),))],
        out_shape=[jax.ShapeDtypeStruct(x.shape, x.dtype) for x in arrays],
        compiler_params=pltpu.CompilerParams(vmem_limit_bytes=1024 * 1024),
        name="stage",
    )(*arrays)


def position_kernel(offs, scale, tile_list, offsets, group_counts, *refs):
    shares = len(offs)
    pieces = refs[: 1 + (REACH - 1) * shares]
    eig_in, amps_in, tables_in, coef_in = refs[len(pieces):len(pieces) + 4]
    eigen_send, eigen_keep = refs[len(pieces) + 4:len(pieces) + 6], refs[len(pieces) + 6:len(pieces) + 8]
    grads_out, coef = refs[len(pieces) + 8:len(pieces) + 10]
    (staged, table, probe, amps, eig, obj, ex, mid, far, patch, d_high, d_low, eigen, out_eigen, cross,
     weights, weights_t, piece_sem, table_sem, amps_sem, eig_sem, grad_sem, out_sem) = refs[len(pieces) + 10:]
    pos_dev, _, frame, _ = probe.shape
    modes = eig.shape[0]
    side = staged.shape[2]
    blocks = side // LANES
    slab = side // shares
    my_block, member, alive, place = coordinates(tile_list, offsets, group_counts, pos_dev)
    strips = range(frame // STRIP)

    copies = [pltpu.make_async_copy(pieces[0], staged.at[0], piece_sem.at[0])]
    for section in range(1, REACH):
        for i in range(shares):
            start = pl.multiple_of((member ^ offs[i]) * slab, slab)
            at = 1 + (section - 1) * shares + i
            copies.append(
                pltpu.make_async_copy(
                    pieces[at], staged.at[section, :, pl.ds(start, slab), :], piece_sem.at[at]
                )
            )
    table_copy = pltpu.make_async_copy(tables_in, table, table_sem)
    amps_copy = pltpu.make_async_copy(amps_in, amps, amps_sem)
    eig_copy = pltpu.make_async_copy(eig_in, eig, eig_sem)
    for copy in [eig_copy] + copies + [table_copy, amps_copy]:
        copy.start()

    by_position = (pos_dev * STRIP, pos_dev)
    by_mode = (modes * STRIP, modes)
    tall_t = exact(exact(one_hot(by_mode, 0), coef_in[...]), one_hot(by_position[::-1], 1))
    high, low = two_terms(diagonals(tall_t))
    weights_t[...] = jnp.concatenate([high, low], 0)
    spread = lax.dot_general(
        one_hot(by_position, 0), coef_in[...], (((1,), (1,)), ((), ())),
        precision=lax.Precision.HIGHEST, preferred_element_type=jnp.float32,
    )
    high, low = two_terms(diagonals(exact(spread, one_hot(by_mode[::-1], 1))))
    weights[...] = jnp.concatenate([high, low], 1)
    eig_copy.wait()

    def synth(i, carry):
        rows = pl.ds(pl.multiple_of(i * STRIP, STRIP), STRIP)
        for c in range(2):
            e = eig[:, c, rows, :].reshape(modes * STRIP, frame)
            made = jnp.dot(
                weights[...], jnp.concatenate([e, e], 0), preferred_element_type=jnp.float32
            )
            probe[:, c, rows, :] = made.reshape(pos_dev, STRIP, frame)
        return carry

    lax.fori_loop(0, frame // STRIP, synth, 0, unroll=4)
    for copy in copies:
        copy.wait()

    def widen(i, carry):
        rows = pl.ds(pl.multiple_of(i * LANES, LANES), LANES)
        for section in range(REACH):
            for c in range(2):
                for b in range(blocks):
                    obj[section, c, b, rows, :] = staged[
                        section, c, rows, b * LANES:(b + 1) * LANES
                    ].astype(jnp.float32)
        return carry

    lax.fori_loop(0, side // LANES, widen, 0)
    table_copy.wait()
    amps_copy.wait()

    lane = lax.broadcasted_iota(jnp.int32, (STRIP, LANES), 1)

    def enter(j, slot):
        where = []
        for m in range(2):
            section, row, col = place(j, m)
            s = col % LANES
            where.append((section, row, col // LANES, (LANES - s) % LANES, lane < LANES - s))
        for i in strips:
            rows = slice(i * STRIP, (i + 1) * STRIP)
            parts = []
            for c in range(2):
                total = None
                for section, row, cb, back_by, keep_lane in where:
                    rolled = [
                        pltpu.roll(obj[section, c, cb + b, pl.ds(row + i * STRIP, STRIP), :], back_by, 1)
                        for b in range(3)
                    ]
                    block = [jnp.where(keep_lane, rolled[b], rolled[b + 1]) for b in range(2)]
                    total = block if total is None else [x + y for x, y in zip(total, block)]
                parts.append([0.5 * x for x in total])
            for b in range(2):
                cols = slice(b * LANES, (b + 1) * LANES)
                o_re, o_im = parts[0][b], parts[1][b]
                p_re, p_im = probe[j, 0, rows, cols], probe[j, 1, rows, cols]
                patch[slot, 0, rows, cols] = o_re
                patch[slot, 1, rows, cols] = o_im
                ex[slot, rows, b * LANES:(b + 1) * LANES] = (p_re * o_re - p_im * o_im).astype(jnp.bfloat16)
                ex[slot, rows, frame + b * LANES:frame + (b + 1) * LANES] = (
                    p_re * o_im + p_im * o_re
                ).astype(jnp.bfloat16)

    def transform(slot, way):
        half = jnp.dot(ex[slot], table[way], preferred_element_type=jnp.float32)
        mid[slot, :frame] = half[:, :frame].astype(jnp.bfloat16)
        mid[slot, frame:] = half[:, frame:].astype(jnp.bfloat16)
        far[slot] = jnp.dot(table[1 - way], mid[slot], preferred_element_type=jnp.float32)

    def residual(j, slot, living):
        for i in strips:
            rows = slice(i * STRIP, (i + 1) * STRIP)
            lower = slice(frame + i * STRIP, frame + (i + 1) * STRIP)
            f_re, f_im = far[slot, rows], far[slot, lower]
            factor = 1.0 - amps[j, rows].astype(jnp.float32) * lax.rsqrt(f_re * f_re + f_im * f_im + 1.0)
            if living is not None:
                factor = factor * living
            ex[slot, rows, :frame] = (f_re * factor).astype(jnp.bfloat16)
            ex[slot, rows, frame:] = (f_im * factor).astype(jnp.bfloat16)

    def leave(j, slot):
        for i in strips:
            rows = slice(i * STRIP, (i + 1) * STRIP)
            lower = slice(frame + i * STRIP, frame + (i + 1) * STRIP)
            b_re, b_im = far[slot, rows], far[slot, lower]
            o_re, o_im = patch[slot, 0, rows], patch[slot, 1, rows]
            p_re, p_im = probe[j, 0, rows], probe[j, 1, rows]
            for c, d in enumerate((o_re * b_re + o_im * b_im, o_re * b_im - o_im * b_re)):
                high = d.astype(jnp.bfloat16)
                d_high[j, c, rows] = high
                d_low[j, c, rows] = (d - high.astype(jnp.float32)).astype(jnp.bfloat16)
            probe[j, 0, rows] = 0.5 * (p_re * b_re + p_im * b_im)
            probe[j, 1, rows] = 0.5 * (p_re * b_im - p_im * b_re)

    def grad_copy(j):
        return pltpu.make_async_copy(probe.at[j], grads_out.at[j], grad_sem.at[j])

    def visit(pair, carry):
        first, second = 2 * pair, 2 * pair + 1
        enter(first, 0)
        transform(0, 0)
        enter(second, 1)
        transform(1, 0)
        residual(first, 0, None)
        transform(0, 1)
        residual(second, 1, jnp.where(second < alive, 1.0, 0.0))
        transform(1, 1)
        leave(first, 0)
        leave(second, 1)
        grad_copy(first).start()
        grad_copy(second).start()
        return carry

    pairs = (alive + 1) // 2
    lax.fori_loop(0, pairs, visit, 0)

    def skip(j, carry):
        d_high[j] = jnp.zeros((2, frame, frame), jnp.bfloat16)
        d_low[j] = jnp.zeros((2, frame, frame), jnp.bfloat16)
        return carry

    lax.fori_loop(2 * pairs, pos_dev, skip, 0)

    cross[...] = jnp.zeros_like(cross)
    rows_q = frame // shares
    groups = 2 * modes
    share = share_of(groups, lax.axis_size("blk"))

    def eigen_strip(i, carry):
        rows = pl.ds(pl.multiple_of(i * STRIP, STRIP), STRIP)
        q = i // (rows_q // STRIP)
        inner = pl.ds(pl.multiple_of(i % (rows_q // STRIP) * STRIP, STRIP), STRIP)
        for c in range(2):
            high = d_high[:, c, rows, :].reshape(pos_dev * STRIP, frame)
            low = d_low[:, c, rows, :].reshape(pos_dev * STRIP, frame)
            e = eig[:, c, rows, :].reshape(modes * STRIP, frame)
            both = jnp.dot(weights_t[...], high, preferred_element_type=jnp.float32)
            rest = jnp.dot(weights_t[:modes * STRIP], low, preferred_element_type=jnp.float32)
            grad = (both[:modes * STRIP] + both[modes * STRIP:] + rest) * scale
            for k in range(modes):
                group = 2 * k + c
                if share:
                    group = (group // share ^ my_block) * share + group % share
                eigen[q, group, inner, :] = grad[k * STRIP:(k + 1) * STRIP]
            cross[...] += lax.dot_general(
                high, e, (((1,), (1,)), ((), ())), preferred_element_type=jnp.float32
            )
        return carry

    lax.fori_loop(0, frame // STRIP, eigen_strip, 0, unroll=4)
    pending = []

    def start(source, target):
        copy = pltpu.make_async_copy(source, target, out_sem.at[len(pending)])
        copy.start()
        pending.append(copy)

    for h in far_first(shares):
        mine, other = slabs_of(member, h)
        out_eigen[h] = eigen[other].astype(jnp.bfloat16)
        start(out_eigen.at[h], eigen_send[h % 2].at[h // 2])
        start(eigen.at[mine], eigen_keep[h % 2].at[h // 2])

    total = exact(one_hot(by_position[::-1], 1), diagonals(cross[...]))
    coef[...] = lax.dot_general(
        one_hot(by_mode[::-1], 1), total, (((1,), (1,)), ((), ())),
        precision=lax.Precision.HIGHEST, preferred_element_type=jnp.float32,
    ) * (1.0 / frame)

    def drain(j, carry):
        grad_copy(j).wait()
        return carry

    lax.fori_loop(0, 2 * pairs, drain, 0)
    for copy in pending:
        copy.wait()


def positions(offs, scale, indices, pieces, eigenprobes, amps, table, coef_t):
    modes, _, frame, _ = eigenprobes.shape
    pos_dev = amps.shape[0]
    side = pieces[0].shape[2]
    shares = len(offs)
    blocks = side // LANES
    smem = pl.BlockSpec(memory_space=SMEM)
    whole = pl.BlockSpec(memory_space=VMEM)
    anywhere = pl.BlockSpec(memory_space=pl.ANY)
    eigen_half = (shares // 2, 2 * modes, frame // shares, frame)
    eigen_part = (shares // 4,) + eigen_half[1:]
    grads = (pos_dev, 2, frame, frame)
    return pl.pallas_call(
        functools.partial(position_kernel, offs, scale),
        in_specs=[smem] * 3 + [anywhere] * (len(pieces) + 3) + [whole],
        out_specs=[anywhere] * 5 + [whole],
        scratch_shapes=[
            pltpu.VMEM((REACH, 2, side, side), jnp.bfloat16),
            pltpu.VMEM(table.shape, jnp.bfloat16),
            pltpu.VMEM(grads, jnp.float32),
            pltpu.VMEM(amps.shape, jnp.bfloat16),
            pltpu.VMEM(eigenprobes.shape, jnp.bfloat16),
            pltpu.VMEM((REACH, 2, blocks + 1, side, LANES), jnp.float32),
            pltpu.VMEM((2, frame, 2 * frame), jnp.bfloat16),
            pltpu.VMEM((2, 2 * frame, frame), jnp.bfloat16),
            pltpu.VMEM((2, 2 * frame, frame), jnp.float32),
            pltpu.VMEM((2, 2, frame, frame), jnp.float32),
            pltpu.VMEM(grads, jnp.bfloat16),
            pltpu.VMEM(grads, jnp.bfloat16),
            pltpu.VMEM((shares, 2 * modes, frame // shares, frame), jnp.float32),
            pltpu.VMEM(eigen_half, jnp.bfloat16),
            pltpu.VMEM((pos_dev * STRIP, modes * STRIP), jnp.float32),
            pltpu.VMEM((pos_dev * STRIP, 2 * modes * STRIP), jnp.bfloat16),
            pltpu.VMEM((2 * modes * STRIP, pos_dev * STRIP), jnp.bfloat16),
            pltpu.SemaphoreType.DMA((len(pieces),)),
            pltpu.SemaphoreType.DMA,
            pltpu.SemaphoreType.DMA,
            pltpu.SemaphoreType.DMA,
            pltpu.SemaphoreType.DMA((pos_dev,)),
            pltpu.SemaphoreType.DMA((shares,)),
        ],
        out_shape=[
            jax.ShapeDtypeStruct(eigen_part, jnp.bfloat16),
            jax.ShapeDtypeStruct(eigen_part, jnp.bfloat16),
            jax.ShapeDtypeStruct(eigen_part, jnp.float32),
            jax.ShapeDtypeStruct(eigen_part, jnp.float32),
            jax.ShapeDtypeStruct(grads, jnp.float32),
            jax.ShapeDtypeStruct((modes, pos_dev), jnp.float32),
        ],
        compiler_params=pltpu.CompilerParams(vmem_limit_bytes=VMEM_LIMIT),
        name="positions",
    )(*indices, *pieces, eigenprobes, amps, table, coef_t)


def scatter_kernel(shares, tile_list, offsets, group_counts, grads_in, *refs):
    send, keep = refs[:2 * REACH], refs[2 * REACH:4 * REACH]
    grads, acc, out_send, grad_sem, out_sem = refs[4 * REACH:]
    pos_dev, _, frame, _ = grads.shape
    blocks, side = acc.shape[2] - 1, acc.shape[3]
    slab = side // shares
    _, member, alive, place = coordinates(tile_list, offsets, group_counts, pos_dev)

    def grad_copy(j):
        return pltpu.make_async_copy(grads_in.at[j], grads.at[j], grad_sem.at[j])

    def begin(j, carry):
        grad_copy(j).start()
        return carry

    lax.fori_loop(0, alive, begin, 0)

    def clear(i, carry):
        rows = pl.ds(pl.multiple_of(i * LANES, LANES), LANES)
        for section in range(REACH):
            for c in range(2):
                for b in range(blocks + 1):
                    acc[section, c, b, rows, :] = jnp.zeros((LANES, LANES), jnp.float32)
        return carry

    lax.fori_loop(0, side // LANES, clear, 0)
    lane = lax.broadcasted_iota(jnp.int32, (STRIP, LANES), 1)

    def add(j, carry):
        grad_copy(j).wait()
        for m in range(2):
            section, row, col = place(j, m)
            cb, s = col // LANES, col % LANES
            inside = lane >= s
            for i in range(frame // STRIP):
                for c in range(2):
                    low, high = (
                        pltpu.roll(grads[j, c, i * STRIP:(i + 1) * STRIP, b * LANES:(b + 1) * LANES], s, 1)
                        for b in range(2)
                    )
                    for b, value in enumerate(
                        (
                            jnp.where(inside, low, 0.0),
                            jnp.where(inside, high, low),
                            jnp.where(inside, 0.0, high),
                        )
                    ):
                        at = (section, c, cb + b, pl.ds(row + i * STRIP, STRIP), slice(None))
                        acc[at] = acc[at] + value
        return carry

    lax.fori_loop(0, alive, add, 0)
    pending = []

    def start(source, target):
        copy = pltpu.make_async_copy(source, target, out_sem.at[len(pending)])
        copy.start()
        pending.append(copy)

    for section in range(REACH - 1, -1, -1):
        for h in far_first(shares):
            mine, other = (pl.multiple_of(at * slab, slab) for at in slabs_of(member, h))
            start(
                acc.at[section, :, pl.ds(0, blocks), pl.ds(mine, slab), :],
                keep[2 * section + h % 2].at[h // 2],
            )
            for c in range(2):
                for b in range(blocks):
                    out_send[section, h, c, b] = acc[section, c, b, pl.ds(other, slab), :].astype(jnp.bfloat16)
            start(out_send.at[section, h], send[2 * section + h % 2].at[h // 2])
    for copy in pending:
        copy.wait()


def scatter(shares, side, indices, grads):
    blocks = side // LANES
    anywhere = pl.BlockSpec(memory_space=pl.ANY)
    half = (shares // 2, 2, blocks, side // shares, LANES)
    part = (shares // 4,) + half[1:]
    return pl.pallas_call(
        functools.partial(scatter_kernel, shares),
        in_specs=[pl.BlockSpec(memory_space=SMEM)] * 3 + [anywhere],
        out_specs=[anywhere] * (4 * REACH),
        scratch_shapes=[
            pltpu.VMEM(grads.shape, jnp.float32),
            pltpu.VMEM((REACH, 2, blocks + 1, side, LANES), jnp.float32),
            pltpu.VMEM((REACH,) + half, jnp.bfloat16),
            pltpu.SemaphoreType.DMA((grads.shape[0],)),
            pltpu.SemaphoreType.DMA((REACH * shares,)),
        ],
        out_shape=[jax.ShapeDtypeStruct(part, jnp.bfloat16)] * (2 * REACH)
        + [jax.ShapeDtypeStruct(part, jnp.float32)] * (2 * REACH),
        compiler_params=pltpu.CompilerParams(vmem_limit_bytes=20 * 1024 * 1024),
        cost_estimate=pl.CostEstimate(flops=1 << 24, bytes_accessed=16 << 20, transcendentals=0),
        name="scatter",
    )(*indices, grads)


def after(array, *others):
    return lax.optimization_barrier((array,) + others)[0]


def after_all(arrays, *others):
    return lax.optimization_barrier(tuple(arrays) + others)[:len(arrays)]


def halve(keep, send, before_core=(), before_cross=()):
    far = [keep[1], after(swap(after(send[1], *before_core), "probe", 1), *before_cross)]
    terms = [keep[0], swap(send[0], "probe", 1)]
    leaving = None
    bit = 2
    while True:
        sending = sum(term.astype(jnp.float32) for term in far).astype(jnp.bfloat16)
        leaving = sending if leaving is None else leaving
        terms.append(swap(sending, "probe", bit))
        if terms[0].shape[0] == 1:
            return sum(term[0].astype(jnp.float32) for term in terms), leaving, terms[-1]
        pick = lambda term, which: term.reshape((term.shape[0] // 2, 2) + term.shape[1:])[:, which]
        far, terms = [pick(term, 1) for term in terms], [pick(term, 0) for term in terms]
        bit *= 2


def scatter_rows(axis, value):
    me = lax.axis_index(axis)
    total = lax.dynamic_index_in_dim(value, me, 0, False)
    sent = []
    for i in range(1, lax.axis_size(axis)):
        sent.append(lax.dynamic_index_in_dim(value, me ^ i, 0, False).astype(jnp.bfloat16))
        total += swap(sent[-1], axis, i).astype(jnp.float32)
    return total.astype(jnp.bfloat16), sent


def scatter_sum(axis, value):
    terms = [value]
    sent = []
    bit = 1
    while bit < lax.axis_size(axis):
        pick = lambda term, which: term.reshape((term.shape[0] // 2, 2) + term.shape[1:])[:, which]
        sent.append(sum(pick(term, 1).astype(jnp.float32) for term in terms).astype(jnp.bfloat16))
        terms = [pick(term, 0) for term in terms] + [swap(sent[-1], axis, bit)]
        bit *= 2
    return sum(term[0].astype(jnp.float32) for term in terms).astype(jnp.bfloat16), sent


def gather_shares(axis, total, *others):
    held = {0: total}
    bit = lax.axis_size(axis) // 2
    while bit:
        held.update({i ^ bit: swap(piece, axis, bit) for i, piece in held.items()})
        if others:
            held[bit], others = after(held[bit], *others), ()
        bit //= 2
    return [held[i] for i in range(lax.axis_size(axis))]


def place_kernel(axis, *refs):
    pieces, out = refs[:-1], refs[-1]
    me = lax.axis_index(axis)
    for i, piece in enumerate(pieces):
        out[me ^ i] = piece[...].astype(jnp.float32)


def place(axis, held):
    return pl.pallas_call(
        functools.partial(place_kernel, axis),
        in_specs=[pl.BlockSpec(memory_space=VMEM)] * len(held),
        out_specs=pl.BlockSpec(memory_space=VMEM),
        out_shape=jax.ShapeDtypeStruct((len(held),) + held[0].shape, jnp.float32),
        compiler_params=pltpu.CompilerParams(vmem_limit_bytes=8 * 1024 * 1024),
        name="place",
    )(*held)


def finish_kernel(first, second, out):
    blocks = first.shape[1]
    for c in range(2):
        for b in range(blocks):
            out[c, :, b * LANES:(b + 1) * LANES] = first[c, b] + second[c, b].astype(jnp.float32)


def finish(first, second):
    _, blocks, slab, lanes = first.shape
    return pl.pallas_call(
        finish_kernel,
        in_specs=[pl.BlockSpec(memory_space=VMEM)] * 2,
        out_specs=pl.BlockSpec(memory_space=VMEM),
        out_shape=jax.ShapeDtypeStruct((2, slab, blocks * lanes), jnp.float32),
        compiler_params=pltpu.CompilerParams(vmem_limit_bytes=8 * 1024 * 1024),
        name="finish",
    )(first, second)


def on_device(tiles, eigenprobes, coefficients, tile_list, offsets, amplitudes, group_counts):
    modes, _, frame, _ = eigenprobes.shape
    side = tiles.shape[2]
    pos_dev = coefficients.shape[0]
    blocks = lax.axis_size("blk")
    shares = lax.axis_size("probe")
    member = lax.axis_index("probe")
    slab = side // shares
    bits = [1 << i for i in range(shares.bit_length() - 1)]

    offs = [0]
    for bit in reversed(bits):
        offs = offs + [o ^ bit for o in offs]
    quarter = lax.dynamic_slice_in_dim(tiles[0], member * slab, slab, 1)
    near = shift(quarter, "blk", -1)
    held = [[near], [shift(near, "blk", -1)]]
    eig, amps = stage(*after_all((eigenprobes, amplitudes), near))
    held[1][0] = after(held[1][0], eig)
    table, tile, coef_t, lists, corners = stage(
        *after_all((tables(frame), tiles[0], coefficients.T, tile_list.T, offsets.T), held[1][0])
    )
    for bit in reversed(bits):
        for part in held:
            arrived = [swap(piece, "probe", bit) for piece in part]
            if bit > 1:
                arrived[0] = after(arrived[0], eig if part is held[0] else table)
            part += arrived

    indices = (lists, corners, group_counts)
    scale = (pos_dev * blocks * shares) ** (-0.5)
    out = positions(
        tuple(offs), scale, indices, [tile] + held[0] + held[1], eig, amps, table, coef_t
    )
    eigen_send, eigen_keep, grads, coef_rows = out[:2], out[2:4], out[4], out[5]

    eigen, leaving, crossed = halve(eigen_keep, eigen_send)
    out = scatter(shares, side, indices, after(grads, leaving))
    send, keep = ([out[at + 2 * i:at + 2 * i + 2] for i in range(REACH)] for at in (0, 2 * REACH))
    last = REACH - 1
    share = share_of(2 * modes, blocks)
    if share:
        total, sent = scatter_sum("blk", eigen.reshape((blocks, share) + eigen.shape[1:]))
    else:
        total, sent = scatter_rows("blk", eigen.reshape(blocks, -1, frame))
    mine, _, _ = halve(keep[last], send[last], before_core=(crossed,))
    moving = after(mine.astype(jnp.bfloat16), *sent[:1])
    for section in range(last - 1, -1, -1):
        mine, _, _ = halve(keep[section], send[section], before_cross=(moving,))
        arrived = shift(moving, "blk", 1)
        if section > 0:
            moving = (arrived.astype(jnp.float32) + mine).astype(jnp.bfloat16)
    eigen_share = place("blk", gather_shares("blk", total, arrived))
    eigen_share = eigen_share.reshape(modes, 2, frame // shares, frame)
    summed = finish(mine, arrived)
    return (summed[None], eigen_share, coef_rows.T)


def solution(mesh):
    in_specs = (
        P(("recon", "blk"), None, None, None),
        P("recon", None, None, None),
        P(("recon", "blk", "probe"), None),
        P(("recon", "blk", "probe"), None),
        P(("recon", "blk", "probe"), None),
        P(("recon", "blk", "probe"), None, None),
        P(("recon", "blk")),
    )
    out_specs = (
        P(("recon", "blk"), None, "probe", None),
        P("recon", None, "probe", None),
        P(("recon", "blk", "probe"), None),
    )
    return jax.shard_map(
        on_device, mesh=mesh, in_specs=in_specs, out_specs=out_specs, check_vma=False
    )
```

```python
import functools
import math

import jax
import jax.numpy as jnp
import ml_dtypes
import numpy as np
from jax import lax
from jax.experimental import pallas as pl
from jax.experimental.pallas import tpu as pltpu
from jax.sharding import PartitionSpec as P

REACH = 3
LANES = 128
STRIP = 16
VMEM = pltpu.MemorySpace.VMEM
SMEM = pltpu.MemorySpace.SMEM
VMEM_LIMIT = 36 * 1024 * 1024


def tables(frame):
    indices = np.arange(frame)
    angle = (indices[:, None] * indices[None, :] % frame) * (2.0 * math.pi / frame)
    cos_part = np.cos(angle) / math.sqrt(frame)
    sin_part = -np.sin(angle) / math.sqrt(frame)
    forward = np.block([[cos_part, sin_part], [-sin_part, cos_part]])
    forward = forward.astype(np.float32).astype(ml_dtypes.bfloat16)
    return jnp.asarray(np.stack([forward, forward.T]))


def shift(array, axis, by):
    peers = lax.axis_size(axis)
    return lax.ppermute(array, axis, [(i, (i + by) % peers) for i in range(peers)])


def swap(array, axis, bit):
    peers = lax.axis_size(axis)
    return lax.ppermute(array, axis, [(i, i ^ bit) for i in range(peers)])


def slabs_of(member, h):
    pair, core = member >> 1, member & 1
    mine = 2 * (pair ^ h) + core
    return mine, mine ^ 1


def far_first(shares):
    return [*range(1, shares // 2, 2), *range(0, shares // 2, 2)]


def share_of(groups, peers):
    return groups // peers if groups % peers == 0 else 0


def coordinates(tile_list, offsets, group_counts, pos_dev):
    blocks = lax.axis_size("blk")
    my_block, member = lax.axis_index("blk"), lax.axis_index("probe")
    alive = jnp.clip(group_counts[0] - member * pos_dev, 0, pos_dev)

    def place(j, m):
        section = lax.rem(tile_list[m, j] - my_block + blocks, blocks)
        return section, offsets[2 * m, j], offsets[2 * m + 1, j]

    return my_block, member, alive, place


def one_hot(shape, axis):
    return (
        lax.broadcasted_iota(jnp.int32, shape, axis) // STRIP == lax.broadcasted_iota(jnp.int32, shape, 1 - axis)
    ).astype(jnp.float32)


def diagonals(array):
    row = lax.broadcasted_iota(jnp.int32, array.shape, 0)
    col = lax.broadcasted_iota(jnp.int32, array.shape, 1)
    return jnp.where(row % STRIP == col % STRIP, array, 0.0)


def exact(left, right):
    return jnp.dot(left, right, precision=lax.Precision.HIGHEST, preferred_element_type=jnp.float32)


def two_terms(array):
    high = array.astype(jnp.bfloat16)
    return high, (array - high.astype(jnp.float32)).astype(jnp.bfloat16)


def stage_kernel(*refs):
    count = len(refs) // 2
    sem = refs[-1]
    copies = [
        pltpu.make_async_copy(source, target, sem.at[i])
        for i, (source, target) in enumerate(zip(refs[:count], refs[count:2 * count]))
    ]
    for copy in copies:
        copy.start()
    for copy in copies:
        copy.wait()


def stage(*arrays):
    anywhere = pl.BlockSpec(memory_space=pl.ANY)
    return pl.pallas_call(
        stage_kernel,
        in_specs=[anywhere] * len(arrays),
        out_specs=[anywhere] * len(arrays),
        scratch_shapes=[pltpu.SemaphoreType.DMA((len(arrays),))],
        out_shape=[jax.ShapeDtypeStruct(x.shape, x.dtype) for x in arrays],
        compiler_params=pltpu.CompilerParams(vmem_limit_bytes=1024 * 1024),
        name="stage",
    )(*arrays)


def position_kernel(offs, scale, tile_list, offsets, group_counts, *refs):
    shares = len(offs)
    pieces = refs[: 1 + (REACH - 1) * shares]
    eig_in, amps_in, tables_in, coef_in = refs[len(pieces):len(pieces) + 4]
    eigen_send, eigen_keep = refs[len(pieces) + 4:len(pieces) + 6], refs[len(pieces) + 6:len(pieces) + 8]
    grads_out, coef = refs[len(pieces) + 8:len(pieces) + 10]
    (staged, table, probe, amps, eig, obj, ex, mid, far, patch, d_high, d_low, eigen, out_eigen, cross,
     weights, weights_t, piece_sem, table_sem, amps_sem, eig_sem, grad_sem, out_sem) = refs[len(pieces) + 10:]
    pos_dev, _, frame, _ = probe.shape
    modes = eig.shape[0]
    side = staged.shape[2]
    blocks = side // LANES
    slab = side // shares
    my_block, member, alive, place = coordinates(tile_list, offsets, group_counts, pos_dev)
    strips = range(frame // STRIP)

    copies = [pltpu.make_async_copy(pieces[0], staged.at[0], piece_sem.at[0])]
    for section in range(1, REACH):
        for i in range(shares):
            start = pl.multiple_of((member ^ offs[i]) * slab, slab)
            at = 1 + (section - 1) * shares + i
            copies.append(
                pltpu.make_async_copy(
                    pieces[at], staged.at[section, :, pl.ds(start, slab), :], piece_sem.at[at]
                )
            )
    table_copy = pltpu.make_async_copy(tables_in, table, table_sem)
    amps_copy = pltpu.make_async_copy(amps_in, amps, amps_sem)
    eig_copy = pltpu.make_async_copy(eig_in, eig, eig_sem)
    for copy in [eig_copy] + copies + [table_copy, amps_copy]:
        copy.start()

    by_position = (pos_dev * STRIP, pos_dev)
    by_mode = (modes * STRIP, modes)
    tall_t = exact(exact(one_hot(by_mode, 0), coef_in[...]), one_hot(by_position[::-1], 1))
    high, low = two_terms(diagonals(tall_t))
    weights_t[...] = jnp.concatenate([high, low], 0)
    spread = lax.dot_general(
        one_hot(by_position, 0), coef_in[...], (((1,), (1,)), ((), ())),
        precision=lax.Precision.HIGHEST, preferred_element_type=jnp.float32,
    )
    high, low = two_terms(diagonals(exact(spread, one_hot(by_mode[::-1], 1))))
    weights[...] = jnp.concatenate([high, low], 1)
    eig_copy.wait()

    def synth(i, carry):
        rows = pl.ds(pl.multiple_of(i * STRIP, STRIP), STRIP)
        for c in range(2):
            e = eig[:, c, rows, :].reshape(modes * STRIP, frame)
            made = jnp.dot(
                weights[...], jnp.concatenate([e, e], 0), preferred_element_type=jnp.float32
            )
            probe[:, c, rows, :] = made.reshape(pos_dev, STRIP, frame)
        return carry

    lax.fori_loop(0, frame // STRIP, synth, 0, unroll=4)
    for copy in copies:
        copy.wait()

    def widen(i, carry):
        rows = pl.ds(pl.multiple_of(i * LANES, LANES), LANES)
        for section in range(REACH):
            for c in range(2):
                for b in range(blocks):
                    obj[section, c, b, rows, :] = staged[
                        section, c, rows, b * LANES:(b + 1) * LANES
                    ].astype(jnp.float32)
        return carry

    lax.fori_loop(0, side // LANES, widen, 0)
    table_copy.wait()
    amps_copy.wait()

    lane = lax.broadcasted_iota(jnp.int32, (STRIP, LANES), 1)

    def enter(j, slot):
        where = []
        for m in range(2):
            section, row, col = place(j, m)
            s = col % LANES
            where.append((section, row, col // LANES, (LANES - s) % LANES, lane < LANES - s))
        for i in strips:
            rows = slice(i * STRIP, (i + 1) * STRIP)
            parts = []
            for c in range(2):
                total = None
                for section, row, cb, back_by, keep_lane in where:
                    rolled = [
                        pltpu.roll(obj[section, c, cb + b, pl.ds(row + i * STRIP, STRIP), :], back_by, 1)
                        for b in range(3)
                    ]
                    block = [jnp.where(keep_lane, rolled[b], rolled[b + 1]) for b in range(2)]
                    total = block if total is None else [x + y for x, y in zip(total, block)]
                parts.append([0.5 * x for x in total])
            for b in range(2):
                cols = slice(b * LANES, (b + 1) * LANES)
                o_re, o_im = parts[0][b], parts[1][b]
                p_re, p_im = probe[j, 0, rows, cols], probe[j, 1, rows, cols]
                patch[slot, 0, rows, cols] = o_re
                patch[slot, 1, rows, cols] = o_im
                ex[slot, rows, b * LANES:(b + 1) * LANES] = (p_re * o_re - p_im * o_im).astype(jnp.bfloat16)
                ex[slot, rows, frame + b * LANES:frame + (b + 1) * LANES] = (
                    p_re * o_im + p_im * o_re
                ).astype(jnp.bfloat16)

    def transform(slot, way):
        half = jnp.dot(ex[slot], table[way], preferred_element_type=jnp.float32)
        mid[slot, :frame] = half[:, :frame].astype(jnp.bfloat16)
        mid[slot, frame:] = half[:, frame:].astype(jnp.bfloat16)
        far[slot] = jnp.dot(table[1 - way], mid[slot], preferred_element_type=jnp.float32)

    def residual(j, slot, living):
        for i in strips:
            rows = slice(i * STRIP, (i + 1) * STRIP)
            lower = slice(frame + i * STRIP, frame + (i + 1) * STRIP)
            f_re, f_im = far[slot, rows], far[slot, lower]
            factor = 1.0 - amps[j, rows].astype(jnp.float32) * lax.rsqrt(f_re * f_re + f_im * f_im + 1.0)
            if living is not None:
                factor = factor * living
            ex[slot, rows, :frame] = (f_re * factor).astype(jnp.bfloat16)
            ex[slot, rows, frame:] = (f_im * factor).astype(jnp.bfloat16)

    def leave(j, slot):
        for i in strips:
            rows = slice(i * STRIP, (i + 1) * STRIP)
            lower = slice(frame + i * STRIP, frame + (i + 1) * STRIP)
            b_re, b_im = far[slot, rows], far[slot, lower]
            o_re, o_im = patch[slot, 0, rows], patch[slot, 1, rows]
            p_re, p_im = probe[j, 0, rows], probe[j, 1, rows]
            for c, d in enumerate((o_re * b_re + o_im * b_im, o_re * b_im - o_im * b_re)):
                high = d.astype(jnp.bfloat16)
                d_high[j, c, rows] = high
                d_low[j, c, rows] = (d - high.astype(jnp.float32)).astype(jnp.bfloat16)
            probe[j, 0, rows] = 0.5 * (p_re * b_re + p_im * b_im)
            probe[j, 1, rows] = 0.5 * (p_re * b_im - p_im * b_re)

    def grad_copy(j):
        return pltpu.make_async_copy(probe.at[j], grads_out.at[j], grad_sem.at[j])

    def visit(pair, carry):
        first, second = 2 * pair, 2 * pair + 1
        enter(first, 0)
        transform(0, 0)
        enter(second, 1)
        transform(1, 0)
        residual(first, 0, None)
        transform(0, 1)
        residual(second, 1, jnp.where(second < alive, 1.0, 0.0))
        transform(1, 1)
        leave(first, 0)
        leave(second, 1)
        grad_copy(first).start()
        grad_copy(second).start()
        return carry

    pairs = (alive + 1) // 2
    lax.fori_loop(0, pairs, visit, 0)

    def skip(j, carry):
        d_high[j] = jnp.zeros((2, frame, frame), jnp.bfloat16)
        d_low[j] = jnp.zeros((2, frame, frame), jnp.bfloat16)
        return carry

    lax.fori_loop(2 * pairs, pos_dev, skip, 0)

    cross[...] = jnp.zeros_like(cross)
    rows_q = frame // shares
    groups = 2 * modes
    share = share_of(groups, lax.axis_size("blk"))

    def eigen_strip(i, carry):
        rows = pl.ds(pl.multiple_of(i * STRIP, STRIP), STRIP)
        q = i // (rows_q // STRIP)
        inner = pl.ds(pl.multiple_of(i % (rows_q // STRIP) * STRIP, STRIP), STRIP)
        for c in range(2):
            high = d_high[:, c, rows, :].reshape(pos_dev * STRIP, frame)
            low = d_low[:, c, rows, :].reshape(pos_dev * STRIP, frame)
            e = eig[:, c, rows, :].reshape(modes * STRIP, frame)
            both = jnp.dot(weights_t[...], high, preferred_element_type=jnp.float32)
            rest = jnp.dot(weights_t[:modes * STRIP], low, preferred_element_type=jnp.float32)
            grad = (both[:modes * STRIP] + both[modes * STRIP:] + rest) * scale
            for k in range(modes):
                group = 2 * k + c
                if share:
                    group = (group // share ^ my_block) * share + group % share
                eigen[q, group, inner, :] = grad[k * STRIP:(k + 1) * STRIP]
            cross[...] += lax.dot_general(
                high, e, (((1,), (1,)), ((), ())), preferred_element_type=jnp.float32
            )
        return carry

    lax.fori_loop(0, frame // STRIP, eigen_strip, 0, unroll=4)
    pending = []

    def start(source, target):
        copy = pltpu.make_async_copy(source, target, out_sem.at[len(pending)])
        copy.start()
        pending.append(copy)

    for h in far_first(shares):
        mine, other = slabs_of(member, h)
        out_eigen[h] = eigen[other].astype(jnp.bfloat16)
        start(out_eigen.at[h], eigen_send[h % 2].at[h // 2])
        start(eigen.at[mine], eigen_keep[h % 2].at[h // 2])

    total = exact(one_hot(by_position[::-1], 1), diagonals(cross[...]))
    coef[...] = lax.dot_general(
        one_hot(by_mode[::-1], 1), total, (((1,), (1,)), ((), ())),
        precision=lax.Precision.HIGHEST, preferred_element_type=jnp.float32,
    ) * (1.0 / frame)

    def drain(j, carry):
        grad_copy(j).wait()
        return carry

    lax.fori_loop(0, 2 * pairs, drain, 0)
    for copy in pending:
        copy.wait()


def positions(offs, scale, indices, pieces, eigenprobes, amps, table, coef_t):
    modes, _, frame, _ = eigenprobes.shape
    pos_dev = amps.shape[0]
    side = pieces[0].shape[2]
    shares = len(offs)
    blocks = side // LANES
    smem = pl.BlockSpec(memory_space=SMEM)
    whole = pl.BlockSpec(memory_space=VMEM)
    anywhere = pl.BlockSpec(memory_space=pl.ANY)
    eigen_half = (shares // 2, 2 * modes, frame // shares, frame)
    eigen_part = (shares // 4,) + eigen_half[1:]
    grads = (pos_dev, 2, frame, frame)
    return pl.pallas_call(
        functools.partial(position_kernel, offs, scale),
        in_specs=[smem] * 3 + [anywhere] * (len(pieces) + 3) + [whole],
        out_specs=[anywhere] * 5 + [whole],
        scratch_shapes=[
            pltpu.VMEM((REACH, 2, side, side), jnp.bfloat16),
            pltpu.VMEM(table.shape, jnp.bfloat16),
            pltpu.VMEM(grads, jnp.float32),
            pltpu.VMEM(amps.shape, jnp.bfloat16),
            pltpu.VMEM(eigenprobes.shape, jnp.bfloat16),
            pltpu.VMEM((REACH, 2, blocks + 1, side, LANES), jnp.float32),
            pltpu.VMEM((2, frame, 2 * frame), jnp.bfloat16),
            pltpu.VMEM((2, 2 * frame, frame), jnp.bfloat16),
            pltpu.VMEM((2, 2 * frame, frame), jnp.float32),
            pltpu.VMEM((2, 2, frame, frame), jnp.float32),
            pltpu.VMEM(grads, jnp.bfloat16),
            pltpu.VMEM(grads, jnp.bfloat16),
            pltpu.VMEM((shares, 2 * modes, frame // shares, frame), jnp.float32),
            pltpu.VMEM(eigen_half, jnp.bfloat16),
            pltpu.VMEM((pos_dev * STRIP, modes * STRIP), jnp.float32),
            pltpu.VMEM((pos_dev * STRIP, 2 * modes * STRIP), jnp.bfloat16),
            pltpu.VMEM((2 * modes * STRIP, pos_dev * STRIP), jnp.bfloat16),
            pltpu.SemaphoreType.DMA((len(pieces),)),
            pltpu.SemaphoreType.DMA,
            pltpu.SemaphoreType.DMA,
            pltpu.SemaphoreType.DMA,
            pltpu.SemaphoreType.DMA((pos_dev,)),
            pltpu.SemaphoreType.DMA((shares,)),
        ],
        out_shape=[
            jax.ShapeDtypeStruct(eigen_part, jnp.bfloat16),
            jax.ShapeDtypeStruct(eigen_part, jnp.bfloat16),
            jax.ShapeDtypeStruct(eigen_part, jnp.float32),
            jax.ShapeDtypeStruct(eigen_part, jnp.float32),
            jax.ShapeDtypeStruct(grads, jnp.float32),
            jax.ShapeDtypeStruct((modes, pos_dev), jnp.float32),
        ],
        compiler_params=pltpu.CompilerParams(vmem_limit_bytes=VMEM_LIMIT),
        name="positions",
    )(*indices, *pieces, eigenprobes, amps, table, coef_t)


def scatter_kernel(shares, tile_list, offsets, group_counts, grads_in, *refs):
    send, keep = refs[:2 * REACH], refs[2 * REACH:4 * REACH]
    grads, acc, out_send, grad_sem, out_sem = refs[4 * REACH:]
    pos_dev, _, frame, _ = grads.shape
    blocks, side = acc.shape[2] - 1, acc.shape[3]
    slab = side // shares
    _, member, alive, place = coordinates(tile_list, offsets, group_counts, pos_dev)

    def grad_copy(j):
        return pltpu.make_async_copy(grads_in.at[j], grads.at[j], grad_sem.at[j])

    def begin(j, carry):
        grad_copy(j).start()
        return carry

    lax.fori_loop(0, alive, begin, 0)

    def clear(i, carry):
        rows = pl.ds(pl.multiple_of(i * LANES, LANES), LANES)
        for section in range(REACH):
            for c in range(2):
                for b in range(blocks + 1):
                    acc[section, c, b, rows, :] = jnp.zeros((LANES, LANES), jnp.float32)
        return carry

    lax.fori_loop(0, side // LANES, clear, 0)
    lane = lax.broadcasted_iota(jnp.int32, (STRIP, LANES), 1)

    def add(j, carry):
        grad_copy(j).wait()
        for m in range(2):
            section, row, col = place(j, m)
            cb, s = col // LANES, col % LANES
            inside = lane >= s
            for i in range(frame // STRIP):
                for c in range(2):
                    low, high = (
                        pltpu.roll(grads[j, c, i * STRIP:(i + 1) * STRIP, b * LANES:(b + 1) * LANES], s, 1)
                        for b in range(2)
                    )
                    for b, value in enumerate(
                        (
                            jnp.where(inside, low, 0.0),
                            jnp.where(inside, high, low),
                            jnp.where(inside, 0.0, high),
                        )
                    ):
                        at = (section, c, cb + b, pl.ds(row + i * STRIP, STRIP), slice(None))
                        acc[at] = acc[at] + value
        return carry

    lax.fori_loop(0, alive, add, 0)
    pending = []

    def start(source, target):
        copy = pltpu.make_async_copy(source, target, out_sem.at[len(pending)])
        copy.start()
        pending.append(copy)

    for section in range(REACH - 1, -1, -1):
        for h in far_first(shares):
            mine, other = (pl.multiple_of(at * slab, slab) for at in slabs_of(member, h))
            start(
                acc.at[section, :, pl.ds(0, blocks), pl.ds(mine, slab), :],
                keep[2 * section + h % 2].at[h // 2],
            )
            for c in range(2):
                for b in range(blocks):
                    out_send[section, h, c, b] = acc[section, c, b, pl.ds(other, slab), :].astype(jnp.bfloat16)
            start(out_send.at[section, h], send[2 * section + h % 2].at[h // 2])
    for copy in pending:
        copy.wait()


def scatter(shares, side, indices, grads):
    blocks = side // LANES
    anywhere = pl.BlockSpec(memory_space=pl.ANY)
    half = (shares // 2, 2, blocks, side // shares, LANES)
    part = (shares // 4,) + half[1:]
    return pl.pallas_call(
        functools.partial(scatter_kernel, shares),
        in_specs=[pl.BlockSpec(memory_space=SMEM)] * 3 + [anywhere],
        out_specs=[anywhere] * (4 * REACH),
        scratch_shapes=[
            pltpu.VMEM(grads.shape, jnp.float32),
            pltpu.VMEM((REACH, 2, blocks + 1, side, LANES), jnp.float32),
            pltpu.VMEM((REACH,) + half, jnp.bfloat16),
            pltpu.SemaphoreType.DMA((grads.shape[0],)),
            pltpu.SemaphoreType.DMA((REACH * shares,)),
        ],
        out_shape=[jax.ShapeDtypeStruct(part, jnp.bfloat16)] * (2 * REACH)
        + [jax.ShapeDtypeStruct(part, jnp.float32)] * (2 * REACH),
        compiler_params=pltpu.CompilerParams(vmem_limit_bytes=20 * 1024 * 1024),
        cost_estimate=pl.CostEstimate(flops=1 << 24, bytes_accessed=16 << 20, transcendentals=0),
        name="scatter",
    )(*indices, grads)


def after(array, *others):
    return lax.optimization_barrier((array,) + others)[0]


def after_all(arrays, *others):
    return lax.optimization_barrier(tuple(arrays) + others)[:len(arrays)]


def halve(keep, send, before_core=(), before_cross=()):
    far = [keep[1], after(swap(after(send[1], *before_core), "probe", 1), *before_cross)]
    terms = [keep[0], swap(send[0], "probe", 1)]
    leaving = None
    bit = 2
    while True:
        sending = sum(term.astype(jnp.float32) for term in far).astype(jnp.bfloat16)
        leaving = sending if leaving is None else leaving
        terms.append(swap(sending, "probe", bit))
        if terms[0].shape[0] == 1:
            return sum(term[0].astype(jnp.float32) for term in terms), leaving, terms[-1]
        pick = lambda term, which: term.reshape((term.shape[0] // 2, 2) + term.shape[1:])[:, which]
        far, terms = [pick(term, 1) for term in terms], [pick(term, 0) for term in terms]
        bit *= 2


def scatter_sum(axis, value, relative):
    me = lax.axis_index(axis)
    share = (lambda i: value[i]) if relative else (lambda i: lax.dynamic_index_in_dim(value, me ^ i, 0, False))
    total = share(0)
    sent = [share(i).astype(jnp.bfloat16) for i in range(1, lax.axis_size(axis))]
    for i, sending in enumerate(sent, 1):
        total += swap(sending, axis, i).astype(jnp.float32)
    return total.astype(jnp.bfloat16), sent


def place_kernel(axis, *refs):
    pieces, out = refs[:-1], refs[-1]
    me = lax.axis_index(axis)
    for i, piece in enumerate(pieces):
        out[me ^ i] = piece[...].astype(jnp.float32)


def place(axis, held):
    return pl.pallas_call(
        functools.partial(place_kernel, axis),
        in_specs=[pl.BlockSpec(memory_space=VMEM)] * len(held),
        out_specs=pl.BlockSpec(memory_space=VMEM),
        out_shape=jax.ShapeDtypeStruct((len(held),) + held[0].shape, jnp.float32),
        compiler_params=pltpu.CompilerParams(vmem_limit_bytes=8 * 1024 * 1024),
        name="place",
    )(*held)


def finish_kernel(first, second, out):
    blocks = first.shape[1]
    for c in range(2):
        for b in range(blocks):
            out[c, :, b * LANES:(b + 1) * LANES] = first[c, b] + second[c, b].astype(jnp.float32)


def finish(first, second):
    _, blocks, slab, lanes = first.shape
    return pl.pallas_call(
        finish_kernel,
        in_specs=[pl.BlockSpec(memory_space=VMEM)] * 2,
        out_specs=pl.BlockSpec(memory_space=VMEM),
        out_shape=jax.ShapeDtypeStruct((2, slab, blocks * lanes), jnp.float32),
        compiler_params=pltpu.CompilerParams(vmem_limit_bytes=8 * 1024 * 1024),
        name="finish",
    )(first, second)


def on_device(tiles, eigenprobes, coefficients, tile_list, offsets, amplitudes, group_counts):
    modes, _, frame, _ = eigenprobes.shape
    side = tiles.shape[2]
    pos_dev = coefficients.shape[0]
    blocks = lax.axis_size("blk")
    shares = lax.axis_size("probe")
    member = lax.axis_index("probe")
    slab = side // shares
    bits = [1 << i for i in range(shares.bit_length() - 1)]

    offs = [0]
    for bit in reversed(bits):
        offs = offs + [o ^ bit for o in offs]
    quarter = lax.dynamic_slice_in_dim(tiles[0], member * slab, slab, 1)
    near = shift(quarter, "blk", -1)
    held = [[near], [shift(near, "blk", -1)]]
    eig, amps = stage(*after_all((eigenprobes, amplitudes), near))
    held[1][0] = after(held[1][0], eig)
    table, tile, coef_t, lists, corners = stage(
        *after_all((tables(frame), tiles[0], coefficients.T, tile_list.T, offsets.T), held[1][0])
    )
    for bit in reversed(bits):
        for part in held:
            arrived = [swap(piece, "probe", bit) for piece in part]
            if bit > 1:
                arrived[0] = after(arrived[0], eig if part is held[0] else table)
            part += arrived

    indices = (lists, corners, group_counts)
    scale = (pos_dev * blocks * shares) ** (-0.5)
    out = positions(
        tuple(offs), scale, indices, [tile] + held[0] + held[1], eig, amps, table, coef_t
    )
    eigen_send, eigen_keep, grads, coef_rows = out[:2], out[2:4], out[4], out[5]

    eigen, leaving, crossed = halve(eigen_keep, eigen_send)
    out = scatter(shares, side, indices, after(grads, leaving))
    send, keep = ([out[at + 2 * i:at + 2 * i + 2] for i in range(REACH)] for at in (0, 2 * REACH))
    last = REACH - 1
    relative = share_of(2 * modes, blocks) > 0
    total, sent = scatter_sum("blk", eigen.reshape(blocks, -1, frame), relative)
    mine, leaving, _ = halve(keep[last], send[last], before_cross=sent)
    moving = after(mine.astype(jnp.bfloat16), total)
    for section in range(last - 1, -1, -1):
        mine, leaving, _ = halve(keep[section], send[section], before_cross=(moving,))
        if section == last - 1:
            total = after(total, leaving)
        arrived = shift(moving, "blk", 1)
        if section > 0:
            moving = (arrived.astype(jnp.float32) + mine).astype(jnp.bfloat16)
    gathered = [swap(total, "blk", i) for i in range(1, blocks)]
    eigen_share = place("blk", [after(total, arrived)] + gathered)
    eigen_share = eigen_share.reshape(modes, 2, frame // shares, frame)
    summed = finish(mine, arrived)
    return (summed[None], eigen_share, coef_rows.T)


def solution(mesh):
    in_specs = (
        P(("recon", "blk"), None, None, None),
        P("recon", None, None, None),
        P(("recon", "blk", "probe"), None),
        P(("recon", "blk", "probe"), None),
        P(("recon", "blk", "probe"), None),
        P(("recon", "blk", "probe"), None, None),
        P(("recon", "blk")),
    )
    out_specs = (
        P(("recon", "blk"), None, "probe", None),
        P("recon", None, "probe", None),
        P(("recon", "blk", "probe"), None),
    )
    return jax.shard_map(
        on_device, mesh=mesh, in_specs=in_specs, out_specs=out_specs, check_vma=False
    )
```

```python
import functools
import math

import jax
import jax.numpy as jnp
import ml_dtypes
import numpy as np
from jax import lax
from jax.experimental import pallas as pl
from jax.experimental.pallas import tpu as pltpu
from jax.sharding import PartitionSpec as P

REACH = 3
LANES = 128
STRIP = 16
VMEM = pltpu.MemorySpace.VMEM
SMEM = pltpu.MemorySpace.SMEM
VMEM_LIMIT = 36 * 1024 * 1024


def tables(frame):
    indices = np.arange(frame)
    angle = (indices[:, None] * indices[None, :] % frame) * (2.0 * math.pi / frame)
    cos_part = np.cos(angle) / math.sqrt(frame)
    sin_part = -np.sin(angle) / math.sqrt(frame)
    forward = np.block([[cos_part, sin_part], [-sin_part, cos_part]])
    forward = forward.astype(np.float32).astype(ml_dtypes.bfloat16)
    return jnp.asarray(np.stack([forward, forward.T]))


def shift(array, axis, by):
    peers = lax.axis_size(axis)
    return lax.ppermute(array, axis, [(i, (i + by) % peers) for i in range(peers)])


def swap(array, axis, bit):
    peers = lax.axis_size(axis)
    return lax.ppermute(array, axis, [(i, i ^ bit) for i in range(peers)])


def slabs_of(member, h):
    pair, core = member >> 1, member & 1
    mine = 2 * (pair ^ h) + core
    return mine, mine ^ 1


def far_first(shares):
    return [*range(1, shares // 2, 2), *range(0, shares // 2, 2)]


def share_of(groups, peers):
    return groups // peers if groups % peers == 0 else 0


def coordinates(tile_list, offsets, group_counts, pos_dev):
    blocks = lax.axis_size("blk")
    my_block, member = lax.axis_index("blk"), lax.axis_index("probe")
    alive = jnp.clip(group_counts[0] - member * pos_dev, 0, pos_dev)

    def place(j, m):
        section = lax.rem(tile_list[m, j] - my_block + blocks, blocks)
        return section, offsets[2 * m, j], offsets[2 * m + 1, j]

    return my_block, member, alive, place


def one_hot(shape, axis):
    return (
        lax.broadcasted_iota(jnp.int32, shape, axis) // STRIP == lax.broadcasted_iota(jnp.int32, shape, 1 - axis)
    ).astype(jnp.float32)


def diagonals(array):
    row = lax.broadcasted_iota(jnp.int32, array.shape, 0)
    col = lax.broadcasted_iota(jnp.int32, array.shape, 1)
    return jnp.where(row % STRIP == col % STRIP, array, 0.0)


def exact(left, right):
    return jnp.dot(left, right, precision=lax.Precision.HIGHEST, preferred_element_type=jnp.float32)


def two_terms(array):
    high = array.astype(jnp.bfloat16)
    return high, (array - high.astype(jnp.float32)).astype(jnp.bfloat16)


def stage_kernel(*refs):
    count = len(refs) // 2
    sem = refs[-1]
    copies = [
        pltpu.make_async_copy(source, target, sem.at[i])
        for i, (source, target) in enumerate(zip(refs[:count], refs[count:2 * count]))
    ]
    for copy in copies:
        copy.start()
    for copy in copies:
        copy.wait()


def stage(*arrays):
    anywhere = pl.BlockSpec(memory_space=pl.ANY)
    return pl.pallas_call(
        stage_kernel,
        in_specs=[anywhere] * len(arrays),
        out_specs=[anywhere] * len(arrays),
        scratch_shapes=[pltpu.SemaphoreType.DMA((len(arrays),))],
        out_shape=[jax.ShapeDtypeStruct(x.shape, x.dtype) for x in arrays],
        compiler_params=pltpu.CompilerParams(vmem_limit_bytes=1024 * 1024),
        name="stage",
    )(*arrays)


def position_kernel(offs, scale, tile_list, offsets, group_counts, *refs):
    shares = len(offs)
    pieces = refs[: 1 + (REACH - 1) * shares]
    eig_in, amps_in, tables_in, coef_in = refs[len(pieces):len(pieces) + 4]
    eigen_send, eigen_keep = refs[len(pieces) + 4:len(pieces) + 6], refs[len(pieces) + 6:len(pieces) + 8]
    grads_out, coef = refs[len(pieces) + 8:len(pieces) + 10]
    (staged, table, probe, amps, eig, obj, ex, mid, far, patch, d_high, d_low, eigen, out_eigen, cross,
     weights, weights_t, piece_sem, table_sem, amps_sem, eig_sem, grad_sem, out_sem) = refs[len(pieces) + 10:]
    pos_dev, _, frame, _ = probe.shape
    modes = eig.shape[0]
    side = staged.shape[2]
    blocks = side // LANES
    slab = side // shares
    my_block, member, alive, place = coordinates(tile_list, offsets, group_counts, pos_dev)
    strips = range(frame // STRIP)

    copies = [pltpu.make_async_copy(pieces[0], staged.at[0], piece_sem.at[0])]
    for section in range(1, REACH):
        for i in range(shares):
            start = pl.multiple_of((member ^ offs[i]) * slab, slab)
            at = 1 + (section - 1) * shares + i
            copies.append(
                pltpu.make_async_copy(
                    pieces[at], staged.at[section, :, pl.ds(start, slab), :], piece_sem.at[at]
                )
            )
    table_copy = pltpu.make_async_copy(tables_in, table, table_sem)
    amps_copy = pltpu.make_async_copy(amps_in, amps, amps_sem)
    eig_copy = pltpu.make_async_copy(eig_in, eig, eig_sem)
    for copy in [eig_copy] + copies + [table_copy, amps_copy]:
        copy.start()

    by_position = (pos_dev * STRIP, pos_dev)
    by_mode = (modes * STRIP, modes)
    tall_t = exact(exact(one_hot(by_mode, 0), coef_in[...]), one_hot(by_position[::-1], 1))
    high, low = two_terms(diagonals(tall_t))
    weights_t[...] = jnp.concatenate([high, low], 0)
    spread = lax.dot_general(
        one_hot(by_position, 0), coef_in[...], (((1,), (1,)), ((), ())),
        precision=lax.Precision.HIGHEST, preferred_element_type=jnp.float32,
    )
    high, low = two_terms(diagonals(exact(spread, one_hot(by_mode[::-1], 1))))
    weights[...] = jnp.concatenate([high, low], 1)
    eig_copy.wait()

    def synth(i, carry):
        rows = pl.ds(pl.multiple_of(i * STRIP, STRIP), STRIP)
        for c in range(2):
            e = eig[:, c, rows, :].reshape(modes * STRIP, frame)
            made = jnp.dot(
                weights[...], jnp.concatenate([e, e], 0), preferred_element_type=jnp.float32
            )
            probe[:, c, rows, :] = made.reshape(pos_dev, STRIP, frame)
        return carry

    lax.fori_loop(0, frame // STRIP, synth, 0, unroll=4)
    for copy in copies:
        copy.wait()

    def widen(i, carry):
        rows = pl.ds(pl.multiple_of(i * LANES, LANES), LANES)
        for section in range(REACH):
            for c in range(2):
                for b in range(blocks):
                    obj[section, c, b, rows, :] = staged[
                        section, c, rows, b * LANES:(b + 1) * LANES
                    ].astype(jnp.float32)
        return carry

    lax.fori_loop(0, side // LANES, widen, 0)
    table_copy.wait()
    amps_copy.wait()

    lane = lax.broadcasted_iota(jnp.int32, (STRIP, LANES), 1)

    def enter(j, slot):
        where = []
        for m in range(2):
            section, row, col = place(j, m)
            s = col % LANES
            where.append((section, row, col // LANES, (LANES - s) % LANES, lane < LANES - s))
        for i in strips:
            rows = slice(i * STRIP, (i + 1) * STRIP)
            parts = []
            for c in range(2):
                total = None
                for section, row, cb, back_by, keep_lane in where:
                    rolled = [
                        pltpu.roll(obj[section, c, cb + b, pl.ds(row + i * STRIP, STRIP), :], back_by, 1)
                        for b in range(3)
                    ]
                    block = [jnp.where(keep_lane, rolled[b], rolled[b + 1]) for b in range(2)]
                    total = block if total is None else [x + y for x, y in zip(total, block)]
                parts.append([0.5 * x for x in total])
            for b in range(2):
                cols = slice(b * LANES, (b + 1) * LANES)
                o_re, o_im = parts[0][b], parts[1][b]
                p_re, p_im = probe[j, 0, rows, cols], probe[j, 1, rows, cols]
                patch[slot, 0, rows, cols] = o_re
                patch[slot, 1, rows, cols] = o_im
                ex[slot, rows, b * LANES:(b + 1) * LANES] = (p_re * o_re - p_im * o_im).astype(jnp.bfloat16)
                ex[slot, rows, frame + b * LANES:frame + (b + 1) * LANES] = (
                    p_re * o_im + p_im * o_re
                ).astype(jnp.bfloat16)

    def transform(slot, way):
        half = jnp.dot(ex[slot], table[way], preferred_element_type=jnp.float32)
        mid[slot, :frame] = half[:, :frame].astype(jnp.bfloat16)
        mid[slot, frame:] = half[:, frame:].astype(jnp.bfloat16)
        far[slot] = jnp.dot(table[1 - way], mid[slot], preferred_element_type=jnp.float32)

    def residual(j, slot, living):
        for i in strips:
            rows = slice(i * STRIP, (i + 1) * STRIP)
            lower = slice(frame + i * STRIP, frame + (i + 1) * STRIP)
            f_re, f_im = far[slot, rows], far[slot, lower]
            factor = 1.0 - amps[j, rows].astype(jnp.float32) * lax.rsqrt(f_re * f_re + f_im * f_im + 1.0)
            if living is not None:
                factor = factor * living
            ex[slot, rows, :frame] = (f_re * factor).astype(jnp.bfloat16)
            ex[slot, rows, frame:] = (f_im * factor).astype(jnp.bfloat16)

    def leave(j, slot):
        for i in strips:
            rows = slice(i * STRIP, (i + 1) * STRIP)
            lower = slice(frame + i * STRIP, frame + (i + 1) * STRIP)
            b_re, b_im = far[slot, rows], far[slot, lower]
            o_re, o_im = patch[slot, 0, rows], patch[slot, 1, rows]
            p_re, p_im = probe[j, 0, rows], probe[j, 1, rows]
            for c, d in enumerate((o_re * b_re + o_im * b_im, o_re * b_im - o_im * b_re)):
                high = d.astype(jnp.bfloat16)
                d_high[j, c, rows] = high
                d_low[j, c, rows] = (d - high.astype(jnp.float32)).astype(jnp.bfloat16)
            probe[j, 0, rows] = 0.5 * (p_re * b_re + p_im * b_im)
            probe[j, 1, rows] = 0.5 * (p_re * b_im - p_im * b_re)

    def grad_copy(j):
        return pltpu.make_async_copy(probe.at[j], grads_out.at[j], grad_sem.at[j])

    def visit(pair, carry):
        first, second = 2 * pair, 2 * pair + 1
        enter(first, 0)
        transform(0, 0)
        enter(second, 1)
        transform(1, 0)
        residual(first, 0, None)
        transform(0, 1)
        residual(second, 1, jnp.where(second < alive, 1.0, 0.0))
        transform(1, 1)
        leave(first, 0)
        leave(second, 1)
        grad_copy(first).start()
        grad_copy(second).start()
        return carry

    pairs = (alive + 1) // 2
    lax.fori_loop(0, pairs, visit, 0)

    def skip(j, carry):
        d_high[j] = jnp.zeros((2, frame, frame), jnp.bfloat16)
        d_low[j] = jnp.zeros((2, frame, frame), jnp.bfloat16)
        return carry

    lax.fori_loop(2 * pairs, pos_dev, skip, 0)

    cross[...] = jnp.zeros_like(cross)
    rows_q = frame // shares
    groups = 2 * modes
    share = share_of(groups, lax.axis_size("blk"))

    def eigen_strip(i, carry):
        rows = pl.ds(pl.multiple_of(i * STRIP, STRIP), STRIP)
        q = i // (rows_q // STRIP)
        inner = pl.ds(pl.multiple_of(i % (rows_q // STRIP) * STRIP, STRIP), STRIP)
        for c in range(2):
            high = d_high[:, c, rows, :].reshape(pos_dev * STRIP, frame)
            low = d_low[:, c, rows, :].reshape(pos_dev * STRIP, frame)
            e = eig[:, c, rows, :].reshape(modes * STRIP, frame)
            both = jnp.dot(weights_t[...], high, preferred_element_type=jnp.float32)
            rest = jnp.dot(weights_t[:modes * STRIP], low, preferred_element_type=jnp.float32)
            grad = (both[:modes * STRIP] + both[modes * STRIP:] + rest) * scale
            for k in range(modes):
                group = 2 * k + c
                if share:
                    group = (group // share ^ my_block) * share + group % share
                eigen[q, group, inner, :] = grad[k * STRIP:(k + 1) * STRIP]
            cross[...] += lax.dot_general(
                high, e, (((1,), (1,)), ((), ())), preferred_element_type=jnp.float32
            )
        return carry

    lax.fori_loop(0, frame // STRIP, eigen_strip, 0, unroll=4)
    pending = []

    def start(source, target):
        copy = pltpu.make_async_copy(source, target, out_sem.at[len(pending)])
        copy.start()
        pending.append(copy)

    for h in far_first(shares):
        mine, other = slabs_of(member, h)
        out_eigen[h] = eigen[other].astype(jnp.bfloat16)
        start(out_eigen.at[h], eigen_send[h % 2].at[h // 2])
        start(eigen.at[mine], eigen_keep[h % 2].at[h // 2])

    total = exact(one_hot(by_position[::-1], 1), diagonals(cross[...]))
    coef[...] = lax.dot_general(
        one_hot(by_mode[::-1], 1), total, (((1,), (1,)), ((), ())),
        precision=lax.Precision.HIGHEST, preferred_element_type=jnp.float32,
    ) * (1.0 / frame)

    def drain(j, carry):
        grad_copy(j).wait()
        return carry

    lax.fori_loop(0, 2 * pairs, drain, 0)
    for copy in pending:
        copy.wait()


def positions(offs, scale, indices, pieces, eigenprobes, amps, table, coef_t):
    modes, _, frame, _ = eigenprobes.shape
    pos_dev = amps.shape[0]
    side = pieces[0].shape[2]
    shares = len(offs)
    blocks = side // LANES
    smem = pl.BlockSpec(memory_space=SMEM)
    whole = pl.BlockSpec(memory_space=VMEM)
    anywhere = pl.BlockSpec(memory_space=pl.ANY)
    eigen_half = (shares // 2, 2 * modes, frame // shares, frame)
    eigen_part = (shares // 4,) + eigen_half[1:]
    grads = (pos_dev, 2, frame, frame)
    return pl.pallas_call(
        functools.partial(position_kernel, offs, scale),
        in_specs=[smem] * 3 + [anywhere] * (len(pieces) + 3) + [whole],
        out_specs=[anywhere] * 5 + [whole],
        scratch_shapes=[
            pltpu.VMEM((REACH, 2, side, side), jnp.bfloat16),
            pltpu.VMEM(table.shape, jnp.bfloat16),
            pltpu.VMEM(grads, jnp.float32),
            pltpu.VMEM(amps.shape, jnp.bfloat16),
            pltpu.VMEM(eigenprobes.shape, jnp.bfloat16),
            pltpu.VMEM((REACH, 2, blocks + 1, side, LANES), jnp.float32),
            pltpu.VMEM((2, frame, 2 * frame), jnp.bfloat16),
            pltpu.VMEM((2, 2 * frame, frame), jnp.bfloat16),
            pltpu.VMEM((2, 2 * frame, frame), jnp.float32),
            pltpu.VMEM((2, 2, frame, frame), jnp.float32),
            pltpu.VMEM(grads, jnp.bfloat16),
            pltpu.VMEM(grads, jnp.bfloat16),
            pltpu.VMEM((shares, 2 * modes, frame // shares, frame), jnp.float32),
            pltpu.VMEM(eigen_half, jnp.bfloat16),
            pltpu.VMEM((pos_dev * STRIP, modes * STRIP), jnp.float32),
            pltpu.VMEM((pos_dev * STRIP, 2 * modes * STRIP), jnp.bfloat16),
            pltpu.VMEM((2 * modes * STRIP, pos_dev * STRIP), jnp.bfloat16),
            pltpu.SemaphoreType.DMA((len(pieces),)),
            pltpu.SemaphoreType.DMA,
            pltpu.SemaphoreType.DMA,
            pltpu.SemaphoreType.DMA,
            pltpu.SemaphoreType.DMA((pos_dev,)),
            pltpu.SemaphoreType.DMA((shares,)),
        ],
        out_shape=[
            jax.ShapeDtypeStruct(eigen_part, jnp.bfloat16),
            jax.ShapeDtypeStruct(eigen_part, jnp.bfloat16),
            jax.ShapeDtypeStruct(eigen_part, jnp.float32),
            jax.ShapeDtypeStruct(eigen_part, jnp.float32),
            jax.ShapeDtypeStruct(grads, jnp.float32),
            jax.ShapeDtypeStruct((modes, pos_dev), jnp.float32),
        ],
        compiler_params=pltpu.CompilerParams(vmem_limit_bytes=VMEM_LIMIT),
        name="positions",
    )(*indices, *pieces, eigenprobes, amps, table, coef_t)


def scatter_kernel(shares, tile_list, offsets, group_counts, grads_in, *refs):
    send, keep = refs[:2 * REACH], refs[2 * REACH:4 * REACH]
    grads, acc, out_send, grad_sem, out_sem = refs[4 * REACH:]
    pos_dev, _, frame, _ = grads.shape
    blocks, side = acc.shape[2] - 1, acc.shape[3]
    slab = side // shares
    _, member, alive, place = coordinates(tile_list, offsets, group_counts, pos_dev)

    def grad_copy(j):
        return pltpu.make_async_copy(grads_in.at[j], grads.at[j], grad_sem.at[j])

    def begin(j, carry):
        grad_copy(j).start()
        return carry

    lax.fori_loop(0, alive, begin, 0)

    def clear(i, carry):
        rows = pl.ds(pl.multiple_of(i * LANES, LANES), LANES)
        for section in range(REACH):
            for c in range(2):
                for b in range(blocks + 1):
                    acc[section, c, b, rows, :] = jnp.zeros((LANES, LANES), jnp.float32)
        return carry

    lax.fori_loop(0, side // LANES, clear, 0)
    lane = lax.broadcasted_iota(jnp.int32, (STRIP, LANES), 1)

    def add(j, carry):
        grad_copy(j).wait()
        for m in range(2):
            section, row, col = place(j, m)
            cb, s = col // LANES, col % LANES
            inside = lane >= s
            for i in range(frame // STRIP):
                for c in range(2):
                    low, high = (
                        pltpu.roll(grads[j, c, i * STRIP:(i + 1) * STRIP, b * LANES:(b + 1) * LANES], s, 1)
                        for b in range(2)
                    )
                    for b, value in enumerate(
                        (
                            jnp.where(inside, low, 0.0),
                            jnp.where(inside, high, low),
                            jnp.where(inside, 0.0, high),
                        )
                    ):
                        at = (section, c, cb + b, pl.ds(row + i * STRIP, STRIP), slice(None))
                        acc[at] = acc[at] + value
        return carry

    lax.fori_loop(0, alive, add, 0)
    pending = []

    def start(source, target):
        copy = pltpu.make_async_copy(source, target, out_sem.at[len(pending)])
        copy.start()
        pending.append(copy)

    for section in range(REACH - 1, -1, -1):
        for h in far_first(shares):
            mine, other = (pl.multiple_of(at * slab, slab) for at in slabs_of(member, h))
            start(
                acc.at[section, :, pl.ds(0, blocks), pl.ds(mine, slab), :],
                keep[2 * section + h % 2].at[h // 2],
            )
            for c in range(2):
                for b in range(blocks):
                    out_send[section, h, c, b] = acc[section, c, b, pl.ds(other, slab), :].astype(jnp.bfloat16)
            start(out_send.at[section, h], send[2 * section + h % 2].at[h // 2])
    for copy in pending:
        copy.wait()


def scatter(shares, side, indices, grads):
    blocks = side // LANES
    anywhere = pl.BlockSpec(memory_space=pl.ANY)
    half = (shares // 2, 2, blocks, side // shares, LANES)
    part = (shares // 4,) + half[1:]
    return pl.pallas_call(
        functools.partial(scatter_kernel, shares),
        in_specs=[pl.BlockSpec(memory_space=SMEM)] * 3 + [anywhere],
        out_specs=[anywhere] * (4 * REACH),
        scratch_shapes=[
            pltpu.VMEM(grads.shape, jnp.float32),
            pltpu.VMEM((REACH, 2, blocks + 1, side, LANES), jnp.float32),
            pltpu.VMEM((REACH,) + half, jnp.bfloat16),
            pltpu.SemaphoreType.DMA((grads.shape[0],)),
            pltpu.SemaphoreType.DMA((REACH * shares,)),
        ],
        out_shape=[jax.ShapeDtypeStruct(part, jnp.bfloat16)] * (2 * REACH)
        + [jax.ShapeDtypeStruct(part, jnp.float32)] * (2 * REACH),
        compiler_params=pltpu.CompilerParams(vmem_limit_bytes=20 * 1024 * 1024),
        cost_estimate=pl.CostEstimate(flops=1 << 24, bytes_accessed=16 << 20, transcendentals=0),
        name="scatter",
    )(*indices, grads)


def from_next(array, axis):
    last = lax.axis_size(axis) - 1
    around = lax.ppermute(array, axis, [(0, last)])
    short = lax.ppermute(array, axis, [(i, i - 1) for i in range(1, last + 1)])
    return short + around


def after(array, *others):
    return lax.optimization_barrier((array,) + others)[0]


def after_all(arrays, *others):
    return lax.optimization_barrier(tuple(arrays) + others)[:len(arrays)]


def halve(keep, send, before_core=(), before_cross=()):
    far = [keep[1], after(swap(after(send[1], *before_core), "probe", 1), *before_cross)]
    terms = [keep[0], swap(send[0], "probe", 1)]
    leaving = None
    bit = 2
    while True:
        sending = sum(term.astype(jnp.float32) for term in far).astype(jnp.bfloat16)
        leaving = sending if leaving is None else leaving
        terms.append(swap(sending, "probe", bit))
        if terms[0].shape[0] == 1:
            return sum(term[0].astype(jnp.float32) for term in terms), leaving, terms[-1]
        pick = lambda term, which: term.reshape((term.shape[0] // 2, 2) + term.shape[1:])[:, which]
        far, terms = [pick(term, 1) for term in terms], [pick(term, 0) for term in terms]
        bit *= 2


def scatter_sum(axis, value, relative):
    me = lax.axis_index(axis)
    share = (lambda i: value[i]) if relative else (lambda i: lax.dynamic_index_in_dim(value, me ^ i, 0, False))
    total = share(0)
    sent = [share(i).astype(jnp.bfloat16) for i in range(1, lax.axis_size(axis))]
    for i, sending in enumerate(sent, 1):
        total += swap(sending, axis, i).astype(jnp.float32)
    return total.astype(jnp.bfloat16), sent


def place_kernel(axis, *refs):
    pieces, out = refs[:-1], refs[-1]
    me = lax.axis_index(axis)
    for i, piece in enumerate(pieces):
        out[me ^ i] = piece[...].astype(jnp.float32)


def place(axis, held):
    return pl.pallas_call(
        functools.partial(place_kernel, axis),
        in_specs=[pl.BlockSpec(memory_space=VMEM)] * len(held),
        out_specs=pl.BlockSpec(memory_space=VMEM),
        out_shape=jax.ShapeDtypeStruct((len(held),) + held[0].shape, jnp.float32),
        compiler_params=pltpu.CompilerParams(vmem_limit_bytes=8 * 1024 * 1024),
        name="place",
    )(*held)


def finish_kernel(first, second, out):
    blocks = first.shape[1]
    for c in range(2):
        for b in range(blocks):
            out[c, :, b * LANES:(b + 1) * LANES] = first[c, b] + second[c, b].astype(jnp.float32)


def finish(first, second):
    _, blocks, slab, lanes = first.shape
    return pl.pallas_call(
        finish_kernel,
        in_specs=[pl.BlockSpec(memory_space=VMEM)] * 2,
        out_specs=pl.BlockSpec(memory_space=VMEM),
        out_shape=jax.ShapeDtypeStruct((2, slab, blocks * lanes), jnp.float32),
        compiler_params=pltpu.CompilerParams(vmem_limit_bytes=8 * 1024 * 1024),
        name="finish",
    )(first, second)


def on_device(tiles, eigenprobes, coefficients, tile_list, offsets, amplitudes, group_counts):
    modes, _, frame, _ = eigenprobes.shape
    side = tiles.shape[2]
    pos_dev = coefficients.shape[0]
    blocks = lax.axis_size("blk")
    shares = lax.axis_size("probe")
    member = lax.axis_index("probe")
    slab = side // shares
    bits = [1 << i for i in range(shares.bit_length() - 1)]

    offs = [0]
    for bit in reversed(bits):
        offs = offs + [o ^ bit for o in offs]
    quarter = lax.dynamic_slice_in_dim(tiles[0], member * slab, slab, 1)
    near = from_next(quarter, "blk")
    held = [[near], [from_next(near, "blk")]]
    eig, amps = stage(*after_all((eigenprobes, amplitudes), near))
    held[1][0] = after(held[1][0], eig)
    table, tile, coef_t, lists, corners = stage(
        *after_all((tables(frame), tiles[0], coefficients.T, tile_list.T, offsets.T), held[1][0])
    )
    for bit in reversed(bits):
        for part in held:
            arrived = [swap(piece, "probe", bit) for piece in part]
            if bit > 1:
                arrived[0] = after(arrived[0], eig if part is held[0] else table)
            part += arrived

    indices = (lists, corners, group_counts)
    scale = (pos_dev * blocks * shares) ** (-0.5)
    out = positions(
        tuple(offs), scale, indices, [tile] + held[0] + held[1], eig, amps, table, coef_t
    )
    eigen_send, eigen_keep, grads, coef_rows = out[:2], out[2:4], out[4], out[5]

    eigen, leaving, crossed = halve(eigen_keep, eigen_send)
    out = scatter(shares, side, indices, after(grads, leaving))
    send, keep = ([out[at + 2 * i:at + 2 * i + 2] for i in range(REACH)] for at in (0, 2 * REACH))
    last = REACH - 1
    relative = share_of(2 * modes, blocks) > 0
    total, sent = scatter_sum("blk", eigen.reshape(blocks, -1, frame), relative)
    mine, leaving, _ = halve(keep[last], send[last], before_cross=sent)
    moving = after(mine.astype(jnp.bfloat16), total)
    gathered = [swap(total, "blk", i) for i in range(1, blocks)]
    for section in range(last - 1, -1, -1):
        gate = [moving] + (gathered if section == 0 else [])
        mine, _, _ = halve(keep[section], send[section], before_cross=gate)
        arrived = shift(moving, "blk", 1)
        if section > 0:
            moving = (arrived.astype(jnp.float32) + mine).astype(jnp.bfloat16)
    eigen_share = place("blk", [after(total, arrived)] + gathered)
    eigen_share = eigen_share.reshape(modes, 2, frame // shares, frame)
    summed = finish(mine, arrived)
    return (summed[None], eigen_share, coef_rows.T)


def solution(mesh):
    in_specs = (
        P(("recon", "blk"), None, None, None),
        P("recon", None, None, None),
        P(("recon", "blk", "probe"), None),
        P(("recon", "blk", "probe"), None),
        P(("recon", "blk", "probe"), None),
        P(("recon", "blk", "probe"), None, None),
        P(("recon", "blk")),
    )
    out_specs = (
        P(("recon", "blk"), None, "probe", None),
        P("recon", None, "probe", None),
        P(("recon", "blk", "probe"), None),
    )
    return jax.shard_map(
        on_device, mesh=mesh, in_specs=in_specs, out_specs=out_specs, check_vma=False
    )
```

```python
import functools
import math

import jax
import jax.numpy as jnp
import ml_dtypes
import numpy as np
from jax import lax
from jax.experimental import pallas as pl
from jax.experimental.pallas import tpu as pltpu
from jax.sharding import PartitionSpec as P

REACH = 3
LANES = 128
STRIP = 16
VMEM = pltpu.MemorySpace.VMEM
SMEM = pltpu.MemorySpace.SMEM
VMEM_LIMIT = 36 * 1024 * 1024


def tables(frame):
    indices = np.arange(frame)
    angle = (indices[:, None] * indices[None, :] % frame) * (2.0 * math.pi / frame)
    cos_part = np.cos(angle) / math.sqrt(frame)
    sin_part = -np.sin(angle) / math.sqrt(frame)
    forward = np.block([[cos_part, sin_part], [-sin_part, cos_part]])
    forward = forward.astype(np.float32).astype(ml_dtypes.bfloat16)
    return jnp.asarray(np.stack([forward, forward.T]))


def shift(array, axis, by):
    peers = lax.axis_size(axis)
    return lax.ppermute(array, axis, [(i, (i + by) % peers) for i in range(peers)])


def swap(array, axis, bit):
    peers = lax.axis_size(axis)
    return lax.ppermute(array, axis, [(i, i ^ bit) for i in range(peers)])


def slabs_of(member, h):
    pair, core = member >> 1, member & 1
    mine = 2 * (pair ^ h) + core
    return mine, mine ^ 1


def far_first(shares):
    return [*range(1, shares // 2, 2), *range(0, shares // 2, 2)]


def share_of(groups, peers):
    return groups // peers if groups % peers == 0 else 0


def coordinates(tile_list, offsets, group_counts, pos_dev):
    blocks = lax.axis_size("blk")
    my_block, member = lax.axis_index("blk"), lax.axis_index("probe")
    alive = jnp.clip(group_counts[0] - member * pos_dev, 0, pos_dev)

    def place(j, m):
        section = lax.rem(tile_list[m, j] - my_block + blocks, blocks)
        return section, offsets[2 * m, j], offsets[2 * m + 1, j]

    return my_block, member, alive, place


def one_hot(shape, axis):
    return (
        lax.broadcasted_iota(jnp.int32, shape, axis) // STRIP == lax.broadcasted_iota(jnp.int32, shape, 1 - axis)
    ).astype(jnp.float32)


def diagonals(array):
    row = lax.broadcasted_iota(jnp.int32, array.shape, 0)
    col = lax.broadcasted_iota(jnp.int32, array.shape, 1)
    return jnp.where(row % STRIP == col % STRIP, array, 0.0)


def exact(left, right):
    return jnp.dot(left, right, precision=lax.Precision.HIGHEST, preferred_element_type=jnp.float32)


def two_terms(array):
    high = array.astype(jnp.bfloat16)
    return high, (array - high.astype(jnp.float32)).astype(jnp.bfloat16)


def stage_kernel(*refs):
    count = len(refs) // 2
    sem = refs[-1]
    copies = [
        pltpu.make_async_copy(source, target, sem.at[i])
        for i, (source, target) in enumerate(zip(refs[:count], refs[count:2 * count]))
    ]
    for copy in copies:
        copy.start()
    for copy in copies:
        copy.wait()


def stage(*arrays):
    anywhere = pl.BlockSpec(memory_space=pl.ANY)
    return pl.pallas_call(
        stage_kernel,
        in_specs=[anywhere] * len(arrays),
        out_specs=[anywhere] * len(arrays),
        scratch_shapes=[pltpu.SemaphoreType.DMA((len(arrays),))],
        out_shape=[jax.ShapeDtypeStruct(x.shape, x.dtype) for x in arrays],
        compiler_params=pltpu.CompilerParams(vmem_limit_bytes=1024 * 1024),
        name="stage",
    )(*arrays)


def position_kernel(offs, scale, tile_list, offsets, group_counts, *refs):
    shares = len(offs)
    pieces = refs[: 1 + 2 * (REACH - 1) * shares]
    eig_in, amps_in, tables_in, coef_in = refs[len(pieces):len(pieces) + 4]
    eigen_send, eigen_keep = refs[len(pieces) + 4:len(pieces) + 6], refs[len(pieces) + 6:len(pieces) + 8]
    grads_out, coef = refs[len(pieces) + 8:len(pieces) + 10]
    (staged, table, probe, amps, eig, obj, ex, mid, far, patch, d_high, d_low, eigen, out_eigen, cross,
     weights, weights_t, piece_sem, table_sem, amps_sem, eig_sem, grad_sem, out_sem) = refs[len(pieces) + 10:]
    pos_dev, _, frame, _ = probe.shape
    modes = eig.shape[0]
    side = staged.shape[2]
    blocks = side // LANES
    slab = side // shares
    my_block, member, alive, place = coordinates(tile_list, offsets, group_counts, pos_dev)
    strips = range(frame // STRIP)

    copies = [pltpu.make_async_copy(pieces[0], staged.at[0], piece_sem.at[0])]
    for section in range(1, REACH):
        for i in range(shares):
            start = pl.multiple_of((member ^ offs[i]) * slab, slab)
            for c in range(2):
                at = len(copies)
                copies.append(
                    pltpu.make_async_copy(
                        pieces[at], staged.at[section, c, pl.ds(start, slab), :], piece_sem.at[at]
                    )
                )
    table_copy = pltpu.make_async_copy(tables_in, table, table_sem)
    amps_copy = pltpu.make_async_copy(amps_in, amps, amps_sem)
    eig_copy = pltpu.make_async_copy(eig_in, eig, eig_sem)
    for copy in [eig_copy] + copies + [table_copy, amps_copy]:
        copy.start()

    by_position = (pos_dev * STRIP, pos_dev)
    by_mode = (modes * STRIP, modes)
    tall_t = exact(exact(one_hot(by_mode, 0), coef_in[...]), one_hot(by_position[::-1], 1))
    high, low = two_terms(diagonals(tall_t))
    weights_t[...] = jnp.concatenate([high, low], 0)
    spread = lax.dot_general(
        one_hot(by_position, 0), coef_in[...], (((1,), (1,)), ((), ())),
        precision=lax.Precision.HIGHEST, preferred_element_type=jnp.float32,
    )
    high, low = two_terms(diagonals(exact(spread, one_hot(by_mode[::-1], 1))))
    weights[...] = jnp.concatenate([high, low], 1)
    eig_copy.wait()

    def synth(i, carry):
        rows = pl.ds(pl.multiple_of(i * STRIP, STRIP), STRIP)
        for c in range(2):
            e = eig[:, c, rows, :].reshape(modes * STRIP, frame)
            made = jnp.dot(
                weights[...], jnp.concatenate([e, e], 0), preferred_element_type=jnp.float32
            )
            probe[:, c, rows, :] = made.reshape(pos_dev, STRIP, frame)
        return carry

    lax.fori_loop(0, frame // STRIP, synth, 0, unroll=4)
    for copy in copies:
        copy.wait()

    def widen(i, carry):
        rows = pl.ds(pl.multiple_of(i * LANES, LANES), LANES)
        for section in range(REACH):
            for c in range(2):
                for b in range(blocks):
                    obj[section, c, b, rows, :] = staged[
                        section, c, rows, b * LANES:(b + 1) * LANES
                    ].astype(jnp.float32)
        return carry

    lax.fori_loop(0, side // LANES, widen, 0)
    table_copy.wait()
    amps_copy.wait()

    lane = lax.broadcasted_iota(jnp.int32, (STRIP, LANES), 1)

    def enter(j, slot):
        where = []
        for m in range(2):
            section, row, col = place(j, m)
            s = col % LANES
            where.append((section, row, col // LANES, (LANES - s) % LANES, lane < LANES - s))
        for i in strips:
            rows = slice(i * STRIP, (i + 1) * STRIP)
            parts = []
            for c in range(2):
                total = None
                for section, row, cb, back_by, keep_lane in where:
                    rolled = [
                        pltpu.roll(obj[section, c, cb + b, pl.ds(row + i * STRIP, STRIP), :], back_by, 1)
                        for b in range(3)
                    ]
                    block = [jnp.where(keep_lane, rolled[b], rolled[b + 1]) for b in range(2)]
                    total = block if total is None else [x + y for x, y in zip(total, block)]
                parts.append([0.5 * x for x in total])
            for b in range(2):
                cols = slice(b * LANES, (b + 1) * LANES)
                o_re, o_im = parts[0][b], parts[1][b]
                p_re, p_im = probe[j, 0, rows, cols], probe[j, 1, rows, cols]
                patch[slot, 0, rows, cols] = o_re
                patch[slot, 1, rows, cols] = o_im
                ex[slot, rows, b * LANES:(b + 1) * LANES] = (p_re * o_re - p_im * o_im).astype(jnp.bfloat16)
                ex[slot, rows, frame + b * LANES:frame + (b + 1) * LANES] = (
                    p_re * o_im + p_im * o_re
                ).astype(jnp.bfloat16)

    def transform(slot, way):
        half = jnp.dot(ex[slot], table[way], preferred_element_type=jnp.float32)
        mid[slot, :frame] = half[:, :frame].astype(jnp.bfloat16)
        mid[slot, frame:] = half[:, frame:].astype(jnp.bfloat16)
        far[slot] = jnp.dot(table[1 - way], mid[slot], preferred_element_type=jnp.float32)

    def residual(j, slot, living):
        for i in strips:
            rows = slice(i * STRIP, (i + 1) * STRIP)
            lower = slice(frame + i * STRIP, frame + (i + 1) * STRIP)
            f_re, f_im = far[slot, rows], far[slot, lower]
            factor = 1.0 - amps[j, rows].astype(jnp.float32) * lax.rsqrt(f_re * f_re + f_im * f_im + 1.0)
            if living is not None:
                factor = factor * living
            ex[slot, rows, :frame] = (f_re * factor).astype(jnp.bfloat16)
            ex[slot, rows, frame:] = (f_im * factor).astype(jnp.bfloat16)

    def leave(j, slot):
        for i in strips:
            rows = slice(i * STRIP, (i + 1) * STRIP)
            lower = slice(frame + i * STRIP, frame + (i + 1) * STRIP)
            b_re, b_im = far[slot, rows], far[slot, lower]
            o_re, o_im = patch[slot, 0, rows], patch[slot, 1, rows]
            p_re, p_im = probe[j, 0, rows], probe[j, 1, rows]
            for c, d in enumerate((o_re * b_re + o_im * b_im, o_re * b_im - o_im * b_re)):
                high = d.astype(jnp.bfloat16)
                d_high[j, c, rows] = high
                d_low[j, c, rows] = (d - high.astype(jnp.float32)).astype(jnp.bfloat16)
            probe[j, 0, rows] = 0.5 * (p_re * b_re + p_im * b_im)
            probe[j, 1, rows] = 0.5 * (p_re * b_im - p_im * b_re)

    def grad_copy(j):
        return pltpu.make_async_copy(probe.at[j], grads_out.at[j], grad_sem.at[j])

    def visit(pair, carry):
        first, second = 2 * pair, 2 * pair + 1
        enter(first, 0)
        transform(0, 0)
        enter(second, 1)
        transform(1, 0)
        residual(first, 0, None)
        transform(0, 1)
        residual(second, 1, jnp.where(second < alive, 1.0, 0.0))
        transform(1, 1)
        leave(first, 0)
        leave(second, 1)
        grad_copy(first).start()
        grad_copy(second).start()
        return carry

    pairs = (alive + 1) // 2
    lax.fori_loop(0, pairs, visit, 0)

    def skip(j, carry):
        d_high[j] = jnp.zeros((2, frame, frame), jnp.bfloat16)
        d_low[j] = jnp.zeros((2, frame, frame), jnp.bfloat16)
        return carry

    lax.fori_loop(2 * pairs, pos_dev, skip, 0)

    cross[...] = jnp.zeros_like(cross)
    rows_q = frame // shares
    groups = 2 * modes
    share = share_of(groups, lax.axis_size("blk"))

    def eigen_strip(i, carry):
        rows = pl.ds(pl.multiple_of(i * STRIP, STRIP), STRIP)
        q = i // (rows_q // STRIP)
        inner = pl.ds(pl.multiple_of(i % (rows_q // STRIP) * STRIP, STRIP), STRIP)
        for c in range(2):
            high = d_high[:, c, rows, :].reshape(pos_dev * STRIP, frame)
            low = d_low[:, c, rows, :].reshape(pos_dev * STRIP, frame)
            e = eig[:, c, rows, :].reshape(modes * STRIP, frame)
            both = jnp.dot(weights_t[...], high, preferred_element_type=jnp.float32)
            rest = jnp.dot(weights_t[:modes * STRIP], low, preferred_element_type=jnp.float32)
            grad = (both[:modes * STRIP] + both[modes * STRIP:] + rest) * scale
            for k in range(modes):
                group = 2 * k + c
                if share:
                    group = (group // share ^ my_block) * share + group % share
                eigen[q, group, inner, :] = grad[k * STRIP:(k + 1) * STRIP]
            cross[...] += lax.dot_general(
                high, e, (((1,), (1,)), ((), ())), preferred_element_type=jnp.float32
            )
        return carry

    lax.fori_loop(0, frame // STRIP, eigen_strip, 0, unroll=4)
    pending = []

    def start(source, target):
        copy = pltpu.make_async_copy(source, target, out_sem.at[len(pending)])
        copy.start()
        pending.append(copy)

    for h in far_first(shares):
        mine, other = slabs_of(member, h)
        out_eigen[h] = eigen[other].astype(jnp.bfloat16)
        start(out_eigen.at[h], eigen_send[h % 2].at[h // 2])
        start(eigen.at[mine], eigen_keep[h % 2].at[h // 2])

    total = exact(one_hot(by_position[::-1], 1), diagonals(cross[...]))
    coef[...] = lax.dot_general(
        one_hot(by_mode[::-1], 1), total, (((1,), (1,)), ((), ())),
        precision=lax.Precision.HIGHEST, preferred_element_type=jnp.float32,
    ) * (1.0 / frame)

    def drain(j, carry):
        grad_copy(j).wait()
        return carry

    lax.fori_loop(0, 2 * pairs, drain, 0)
    for copy in pending:
        copy.wait()


def positions(offs, scale, indices, pieces, eigenprobes, amps, table, coef_t):
    modes, _, frame, _ = eigenprobes.shape
    pos_dev = amps.shape[0]
    side = pieces[0].shape[2]
    shares = len(offs)
    blocks = side // LANES
    smem = pl.BlockSpec(memory_space=SMEM)
    whole = pl.BlockSpec(memory_space=VMEM)
    anywhere = pl.BlockSpec(memory_space=pl.ANY)
    eigen_half = (shares // 2, 2 * modes, frame // shares, frame)
    eigen_part = (shares // 4,) + eigen_half[1:]
    grads = (pos_dev, 2, frame, frame)
    return pl.pallas_call(
        functools.partial(position_kernel, offs, scale),
        in_specs=[smem] * 3 + [anywhere] * (len(pieces) + 3) + [whole],
        out_specs=[anywhere] * 5 + [whole],
        scratch_shapes=[
            pltpu.VMEM((REACH, 2, side, side), jnp.bfloat16),
            pltpu.VMEM(table.shape, jnp.bfloat16),
            pltpu.VMEM(grads, jnp.float32),
            pltpu.VMEM(amps.shape, jnp.bfloat16),
            pltpu.VMEM(eigenprobes.shape, jnp.bfloat16),
            pltpu.VMEM((REACH, 2, blocks + 1, side, LANES), jnp.float32),
            pltpu.VMEM((2, frame, 2 * frame), jnp.bfloat16),
            pltpu.VMEM((2, 2 * frame, frame), jnp.bfloat16),
            pltpu.VMEM((2, 2 * frame, frame), jnp.float32),
            pltpu.VMEM((2, 2, frame, frame), jnp.float32),
            pltpu.VMEM(grads, jnp.bfloat16),
            pltpu.VMEM(grads, jnp.bfloat16),
            pltpu.VMEM((shares, 2 * modes, frame // shares, frame), jnp.float32),
            pltpu.VMEM(eigen_half, jnp.bfloat16),
            pltpu.VMEM((pos_dev * STRIP, modes * STRIP), jnp.float32),
            pltpu.VMEM((pos_dev * STRIP, 2 * modes * STRIP), jnp.bfloat16),
            pltpu.VMEM((2 * modes * STRIP, pos_dev * STRIP), jnp.bfloat16),
            pltpu.SemaphoreType.DMA((len(pieces),)),
            pltpu.SemaphoreType.DMA,
            pltpu.SemaphoreType.DMA,
            pltpu.SemaphoreType.DMA,
            pltpu.SemaphoreType.DMA((pos_dev,)),
            pltpu.SemaphoreType.DMA((shares,)),
        ],
        out_shape=[
            jax.ShapeDtypeStruct(eigen_part, jnp.bfloat16),
            jax.ShapeDtypeStruct(eigen_part, jnp.bfloat16),
            jax.ShapeDtypeStruct(eigen_part, jnp.float32),
            jax.ShapeDtypeStruct(eigen_part, jnp.float32),
            jax.ShapeDtypeStruct(grads, jnp.float32),
            jax.ShapeDtypeStruct((modes, pos_dev), jnp.float32),
        ],
        compiler_params=pltpu.CompilerParams(vmem_limit_bytes=VMEM_LIMIT),
        name="positions",
    )(*indices, *pieces, eigenprobes, amps, table, coef_t)


def scatter_kernel(shares, tile_list, offsets, group_counts, grads_in, *refs):
    send, keep = refs[:2 * REACH], refs[2 * REACH:4 * REACH]
    grads, acc, out_send, grad_sem, out_sem = refs[4 * REACH:]
    pos_dev, _, frame, _ = grads.shape
    blocks, side = acc.shape[2] - 1, acc.shape[3]
    slab = side // shares
    _, member, alive, place = coordinates(tile_list, offsets, group_counts, pos_dev)

    def grad_copy(j):
        return pltpu.make_async_copy(grads_in.at[j], grads.at[j], grad_sem.at[j])

    def begin(j, carry):
        grad_copy(j).start()
        return carry

    lax.fori_loop(0, alive, begin, 0)

    def clear(i, carry):
        rows = pl.ds(pl.multiple_of(i * LANES, LANES), LANES)
        for section in range(REACH):
            for c in range(2):
                for b in range(blocks + 1):
                    acc[section, c, b, rows, :] = jnp.zeros((LANES, LANES), jnp.float32)
        return carry

    lax.fori_loop(0, side // LANES, clear, 0)
    lane = lax.broadcasted_iota(jnp.int32, (STRIP, LANES), 1)

    def add(j, carry):
        grad_copy(j).wait()
        for m in range(2):
            section, row, col = place(j, m)
            cb, s = col // LANES, col % LANES
            inside = lane >= s
            for i in range(frame // STRIP):
                for c in range(2):
                    low, high = (
                        pltpu.roll(grads[j, c, i * STRIP:(i + 1) * STRIP, b * LANES:(b + 1) * LANES], s, 1)
                        for b in range(2)
                    )
                    for b, value in enumerate(
                        (
                            jnp.where(inside, low, 0.0),
                            jnp.where(inside, high, low),
                            jnp.where(inside, 0.0, high),
                        )
                    ):
                        at = (section, c, cb + b, pl.ds(row + i * STRIP, STRIP), slice(None))
                        acc[at] = acc[at] + value
        return carry

    lax.fori_loop(0, alive, add, 0)
    pending = []

    def start(source, target):
        copy = pltpu.make_async_copy(source, target, out_sem.at[len(pending)])
        copy.start()
        pending.append(copy)

    for section in range(REACH - 1, -1, -1):
        for h in far_first(shares):
            mine, other = (pl.multiple_of(at * slab, slab) for at in slabs_of(member, h))
            start(
                acc.at[section, :, pl.ds(0, blocks), pl.ds(mine, slab), :],
                keep[2 * section + h % 2].at[h // 2],
            )
            for c in range(2):
                for b in range(blocks):
                    out_send[section, h, c, b] = acc[section, c, b, pl.ds(other, slab), :].astype(jnp.bfloat16)
            start(out_send.at[section, h], send[2 * section + h % 2].at[h // 2])
    for copy in pending:
        copy.wait()


def scatter(shares, side, indices, grads):
    blocks = side // LANES
    anywhere = pl.BlockSpec(memory_space=pl.ANY)
    half = (shares // 2, 2, blocks, side // shares, LANES)
    part = (shares // 4,) + half[1:]
    return pl.pallas_call(
        functools.partial(scatter_kernel, shares),
        in_specs=[pl.BlockSpec(memory_space=SMEM)] * 3 + [anywhere],
        out_specs=[anywhere] * (4 * REACH),
        scratch_shapes=[
            pltpu.VMEM(grads.shape, jnp.float32),
            pltpu.VMEM((REACH, 2, blocks + 1, side, LANES), jnp.float32),
            pltpu.VMEM((REACH,) + half, jnp.bfloat16),
            pltpu.SemaphoreType.DMA((grads.shape[0],)),
            pltpu.SemaphoreType.DMA((REACH * shares,)),
        ],
        out_shape=[jax.ShapeDtypeStruct(part, jnp.bfloat16)] * (2 * REACH)
        + [jax.ShapeDtypeStruct(part, jnp.float32)] * (2 * REACH),
        compiler_params=pltpu.CompilerParams(vmem_limit_bytes=20 * 1024 * 1024),
        cost_estimate=pl.CostEstimate(flops=1 << 24, bytes_accessed=16 << 20, transcendentals=0),
        name="scatter",
    )(*indices, grads)


def after(array, *others):
    return lax.optimization_barrier((array,) + others)[0]


def after_all(arrays, *others):
    return lax.optimization_barrier(tuple(arrays) + others)[:len(arrays)]


def halve(keep, send, before_core=(), before_cross=()):
    far = [keep[1], after(swap(after(send[1], *before_core), "probe", 1), *before_cross)]
    terms = [keep[0], swap(send[0], "probe", 1)]
    leaving = None
    bit = 2
    while True:
        sending = sum(term.astype(jnp.float32) for term in far).astype(jnp.bfloat16)
        leaving = sending if leaving is None else leaving
        terms.append(swap(sending, "probe", bit))
        if terms[0].shape[0] == 1:
            return sum(term[0].astype(jnp.float32) for term in terms), leaving, terms[-1]
        pick = lambda term, which: term.reshape((term.shape[0] // 2, 2) + term.shape[1:])[:, which]
        far, terms = [pick(term, 1) for term in terms], [pick(term, 0) for term in terms]
        bit *= 2


def scatter_sum(axis, value, relative):
    me = lax.axis_index(axis)
    share = (lambda i: value[i]) if relative else (lambda i: lax.dynamic_index_in_dim(value, me ^ i, 0, False))
    total = share(0)
    sent = [share(i).astype(jnp.bfloat16) for i in range(1, lax.axis_size(axis))]
    for i, sending in enumerate(sent, 1):
        total += swap(sending, axis, i).astype(jnp.float32)
    return total.astype(jnp.bfloat16), sent


def place_kernel(axis, *refs):
    pieces, out = refs[:-1], refs[-1]
    me = lax.axis_index(axis)
    for i, piece in enumerate(pieces):
        out[me ^ i] = piece[...].astype(jnp.float32)


def place(axis, held):
    return pl.pallas_call(
        functools.partial(place_kernel, axis),
        in_specs=[pl.BlockSpec(memory_space=VMEM)] * len(held),
        out_specs=pl.BlockSpec(memory_space=VMEM),
        out_shape=jax.ShapeDtypeStruct((len(held),) + held[0].shape, jnp.float32),
        compiler_params=pltpu.CompilerParams(vmem_limit_bytes=8 * 1024 * 1024),
        name="place",
    )(*held)


def finish_kernel(first, second, out):
    blocks = first.shape[1]
    for c in range(2):
        for b in range(blocks):
            out[c, :, b * LANES:(b + 1) * LANES] = first[c, b] + second[c, b].astype(jnp.float32)


def finish(first, second):
    _, blocks, slab, lanes = first.shape
    return pl.pallas_call(
        finish_kernel,
        in_specs=[pl.BlockSpec(memory_space=VMEM)] * 2,
        out_specs=pl.BlockSpec(memory_space=VMEM),
        out_shape=jax.ShapeDtypeStruct((2, slab, blocks * lanes), jnp.float32),
        compiler_params=pltpu.CompilerParams(vmem_limit_bytes=8 * 1024 * 1024),
        name="finish",
    )(first, second)


def on_device(tiles, eigenprobes, coefficients, tile_list, offsets, amplitudes, group_counts):
    modes, _, frame, _ = eigenprobes.shape
    side = tiles.shape[2]
    pos_dev = coefficients.shape[0]
    blocks = lax.axis_size("blk")
    shares = lax.axis_size("probe")
    member = lax.axis_index("probe")
    slab = side // shares
    bits = [1 << i for i in range(shares.bit_length() - 1)]

    offs = [0]
    for bit in reversed(bits):
        offs = offs + [o ^ bit for o in offs]
    (eig,) = stage(eigenprobes)
    moving = [
        lax.dynamic_slice(tiles, (0, c, member * slab, 0), (1, 1, slab, side)).reshape(slab, side)
        for c in range(2)
    ]
    held = []
    for section in range(1, REACH):
        moving = [shift(part, "blk", -1) for part in moving]
        if section == 1:
            moving[0] = after(moving[0], eig)
        held.append([[part] for part in moving])
    amps, table, tile, coef_t, lists, corners = stage(
        *after_all((amplitudes, tables(frame), tiles[0], coefficients.T, tile_list.T, offsets.T), *moving)
    )
    for bit in reversed(bits):
        for section in held:
            for c, part in enumerate(section):
                arrived = [swap(piece, "probe", bit) for piece in part]
                if bit > 1 and c == 1 and section is held[-1]:
                    arrived[0] = after(arrived[0], table)
                part += arrived
    pieces = [tile] + [part[i] for section in held for i in range(shares) for part in section]

    indices = (lists, corners, group_counts)
    scale = (pos_dev * blocks * shares) ** (-0.5)
    out = positions(
        tuple(offs), scale, indices, pieces, eig, amps, table, coef_t
    )
    eigen_send, eigen_keep, grads, coef_rows = out[:2], out[2:4], out[4], out[5]

    eigen, leaving, crossed = halve(eigen_keep, eigen_send)
    out = scatter(shares, side, indices, after(grads, leaving))
    send, keep = ([out[at + 2 * i:at + 2 * i + 2] for i in range(REACH)] for at in (0, 2 * REACH))
    last = REACH - 1
    relative = share_of(2 * modes, blocks) > 0
    total, sent = scatter_sum("blk", eigen.reshape(blocks, -1, frame), relative)
    mine, leaving, _ = halve(keep[last], send[last], before_cross=sent)
    moving = after(mine.astype(jnp.bfloat16), total)
    gathered = [swap(total, "blk", i) for i in range(1, blocks)]
    gate = moving
    for section in range(last - 1, -1, -1):
        mine, _, gate = halve(keep[section], send[section], before_cross=(gate,))
        arrived = shift(moving, "blk", 1)
        if section > 0:
            moving = (arrived.astype(jnp.float32) + mine).astype(jnp.bfloat16)
        if section == 1:
            moving = after(moving, *gathered)
    eigen_share = place("blk", [after(total, arrived)] + gathered)
    eigen_share = eigen_share.reshape(modes, 2, frame // shares, frame)
    summed = finish(mine, arrived)
    return (summed[None], eigen_share, coef_rows.T)


def solution(mesh):
    in_specs = (
        P(("recon", "blk"), None, None, None),
        P("recon", None, None, None),
        P(("recon", "blk", "probe"), None),
        P(("recon", "blk", "probe"), None),
        P(("recon", "blk", "probe"), None),
        P(("recon", "blk", "probe"), None, None),
        P(("recon", "blk")),
    )
    out_specs = (
        P(("recon", "blk"), None, "probe", None),
        P("recon", None, "probe", None),
        P(("recon", "blk", "probe"), None),
    )
    return jax.shard_map(
        on_device, mesh=mesh, in_specs=in_specs, out_specs=out_specs, check_vma=False
    )
```

```python
import functools
import math

import jax
import jax.numpy as jnp
import ml_dtypes
import numpy as np
from jax import lax
from jax.experimental import pallas as pl
from jax.experimental.pallas import tpu as pltpu
from jax.sharding import PartitionSpec as P

REACH = 3
LANES = 128
STRIP = 16
VMEM = pltpu.MemorySpace.VMEM
SMEM = pltpu.MemorySpace.SMEM
VMEM_LIMIT = 36 * 1024 * 1024


def tables(frame):
    indices = np.arange(frame)
    angle = (indices[:, None] * indices[None, :] % frame) * (2.0 * math.pi / frame)
    cos_part = np.cos(angle) / math.sqrt(frame)
    sin_part = -np.sin(angle) / math.sqrt(frame)
    forward = np.block([[cos_part, sin_part], [-sin_part, cos_part]])
    forward = forward.astype(np.float32).astype(ml_dtypes.bfloat16)
    return jnp.asarray(np.stack([forward, forward.T]))


def shift(array, axis, by):
    peers = lax.axis_size(axis)
    return lax.ppermute(array, axis, [(i, (i + by) % peers) for i in range(peers)])


def swap(array, axis, bit):
    peers = lax.axis_size(axis)
    return lax.ppermute(array, axis, [(i, i ^ bit) for i in range(peers)])


def slabs_of(member, h):
    pair, core = member >> 1, member & 1
    mine = 2 * (pair ^ h) + core
    return mine, mine ^ 1


def far_first(shares):
    return [*range(1, shares // 2, 2), *range(0, shares // 2, 2)]


def coordinates(tile_list, offsets, group_counts, pos_dev):
    blocks = lax.axis_size("blk")
    my_block, member = lax.axis_index("blk"), lax.axis_index("probe")
    alive = jnp.clip(group_counts[0] - member * pos_dev, 0, pos_dev)

    def place(j, m):
        section = lax.rem(tile_list[m, j] - my_block + blocks, blocks)
        return section, offsets[2 * m, j], offsets[2 * m + 1, j]

    return my_block, member, alive, place


def one_hot(shape, axis):
    return (
        lax.broadcasted_iota(jnp.int32, shape, axis) // STRIP == lax.broadcasted_iota(jnp.int32, shape, 1 - axis)
    ).astype(jnp.float32)


def diagonals(array):
    row = lax.broadcasted_iota(jnp.int32, array.shape, 0)
    col = lax.broadcasted_iota(jnp.int32, array.shape, 1)
    return jnp.where(row % STRIP == col % STRIP, array, 0.0)


def exact(left, right):
    return jnp.dot(left, right, precision=lax.Precision.HIGHEST, preferred_element_type=jnp.float32)


def two_terms(array):
    high = array.astype(jnp.bfloat16)
    return high, (array - high.astype(jnp.float32)).astype(jnp.bfloat16)


def stage_kernel(*refs):
    count = len(refs) // 2
    sem = refs[-1]
    copies = [
        pltpu.make_async_copy(source, target, sem.at[i])
        for i, (source, target) in enumerate(zip(refs[:count], refs[count:2 * count]))
    ]
    for copy in copies:
        copy.start()
    for copy in copies:
        copy.wait()


def stage(*arrays):
    anywhere = pl.BlockSpec(memory_space=pl.ANY)
    return pl.pallas_call(
        stage_kernel,
        in_specs=[anywhere] * len(arrays),
        out_specs=[anywhere] * len(arrays),
        scratch_shapes=[pltpu.SemaphoreType.DMA((len(arrays),))],
        out_shape=[jax.ShapeDtypeStruct(x.shape, x.dtype) for x in arrays],
        compiler_params=pltpu.CompilerParams(vmem_limit_bytes=1024 * 1024),
        name="stage",
    )(*arrays)


def position_kernel(offs, scale, tile_list, offsets, group_counts, *refs):
    shares = len(offs)
    pieces = refs[: 1 + (REACH - 1) * shares]
    eig_in, amps_in, tables_in, coef_in = refs[len(pieces):len(pieces) + 4]
    eigen_send, eigen_keep = refs[len(pieces) + 4:len(pieces) + 6], refs[len(pieces) + 6:len(pieces) + 8]
    grads_out, coef = refs[len(pieces) + 8:len(pieces) + 10]
    (staged, table, probe, amps, eig, obj, ex, mid, far, patch, d_high, d_low, eigen, out_eigen, cross,
     weights, weights_t, piece_sem, table_sem, amps_sem, eig_sem, grad_sem, out_sem) = refs[len(pieces) + 10:]
    pos_dev, _, frame, _ = probe.shape
    modes = eig.shape[0]
    side = staged.shape[2]
    blocks = side // LANES
    slab = side // shares
    my_block, member, alive, place = coordinates(tile_list, offsets, group_counts, pos_dev)
    strips = range(frame // STRIP)

    copies = [pltpu.make_async_copy(pieces[0], staged.at[0], piece_sem.at[0])]
    for section in range(1, REACH):
        for i in range(shares):
            start = pl.multiple_of((member ^ offs[i]) * slab, slab)
            at = 1 + (section - 1) * shares + i
            copies.append(
                pltpu.make_async_copy(
                    pieces[at], staged.at[section, :, pl.ds(start, slab), :], piece_sem.at[at]
                )
            )
    table_copy = pltpu.make_async_copy(tables_in, table, table_sem)
    amps_copy = pltpu.make_async_copy(amps_in, amps, amps_sem)
    eig_copy = pltpu.make_async_copy(eig_in, eig, eig_sem)
    for copy in [eig_copy] + copies + [table_copy, amps_copy]:
        copy.start()

    by_position = (pos_dev * STRIP, pos_dev)
    by_mode = (modes * STRIP, modes)
    tall_t = exact(exact(one_hot(by_mode, 0), coef_in[...]), one_hot(by_position[::-1], 1))
    high, low = two_terms(diagonals(tall_t))
    weights_t[...] = jnp.concatenate([high, low], 0)
    spread = lax.dot_general(
        one_hot(by_position, 0), coef_in[...], (((1,), (1,)), ((), ())),
        precision=lax.Precision.HIGHEST, preferred_element_type=jnp.float32,
    )
    high, low = two_terms(diagonals(exact(spread, one_hot(by_mode[::-1], 1))))
    weights[...] = jnp.concatenate([high, low], 1)
    eig_copy.wait()

    def synth(i, carry):
        rows = pl.ds(pl.multiple_of(i * STRIP, STRIP), STRIP)
        for c in range(2):
            e = eig[:, c, rows, :].reshape(modes * STRIP, frame)
            made = jnp.dot(
                weights[...], jnp.concatenate([e, e], 0), preferred_element_type=jnp.float32
            )
            probe[:, c, rows, :] = made.reshape(pos_dev, STRIP, frame)
        return carry

    lax.fori_loop(0, frame // STRIP, synth, 0, unroll=4)
    for copy in copies:
        copy.wait()

    def widen(i, carry):
        rows = pl.ds(pl.multiple_of(i * LANES, LANES), LANES)
        for section in range(REACH):
            for c in range(2):
                for b in range(blocks):
                    obj[section, c, b, rows, :] = staged[
                        section, c, rows, b * LANES:(b + 1) * LANES
                    ].astype(jnp.float32)
        return carry

    lax.fori_loop(0, side // LANES, widen, 0)
    table_copy.wait()
    amps_copy.wait()

    lane = lax.broadcasted_iota(jnp.int32, (STRIP, LANES), 1)

    def enter(j, slot):
        where = []
        for m in range(2):
            section, row, col = place(j, m)
            s = col % LANES
            where.append((section, row, col // LANES, (LANES - s) % LANES, lane < LANES - s))
        for i in strips:
            rows = slice(i * STRIP, (i + 1) * STRIP)
            parts = []
            for c in range(2):
                total = None
                for section, row, cb, back_by, keep_lane in where:
                    rolled = [
                        pltpu.roll(obj[section, c, cb + b, pl.ds(row + i * STRIP, STRIP), :], back_by, 1)
                        for b in range(3)
                    ]
                    block = [jnp.where(keep_lane, rolled[b], rolled[b + 1]) for b in range(2)]
                    total = block if total is None else [x + y for x, y in zip(total, block)]
                parts.append([0.5 * x for x in total])
            for b in range(2):
                cols = slice(b * LANES, (b + 1) * LANES)
                o_re, o_im = parts[0][b], parts[1][b]
                p_re, p_im = probe[j, 0, rows, cols], probe[j, 1, rows, cols]
                patch[slot, 0, rows, cols] = o_re
                patch[slot, 1, rows, cols] = o_im
                ex[slot, rows, b * LANES:(b + 1) * LANES] = (p_re * o_re - p_im * o_im).astype(jnp.bfloat16)
                ex[slot, rows, frame + b * LANES:frame + (b + 1) * LANES] = (
                    p_re * o_im + p_im * o_re
                ).astype(jnp.bfloat16)

    def transform(slot, way):
        half = jnp.dot(ex[slot], table[way], preferred_element_type=jnp.float32)
        mid[slot, :frame] = half[:, :frame].astype(jnp.bfloat16)
        mid[slot, frame:] = half[:, frame:].astype(jnp.bfloat16)
        far[slot] = jnp.dot(table[1 - way], mid[slot], preferred_element_type=jnp.float32)

    def residual(j, slot, living):
        for i in strips:
            rows = slice(i * STRIP, (i + 1) * STRIP)
            lower = slice(frame + i * STRIP, frame + (i + 1) * STRIP)
            f_re, f_im = far[slot, rows], far[slot, lower]
            factor = 1.0 - amps[j, rows].astype(jnp.float32) * lax.rsqrt(f_re * f_re + f_im * f_im + 1.0)
            if living is not None:
                factor = factor * living
            ex[slot, rows, :frame] = (f_re * factor).astype(jnp.bfloat16)
            ex[slot, rows, frame:] = (f_im * factor).astype(jnp.bfloat16)

    def leave(j, slot):
        for i in strips:
            rows = slice(i * STRIP, (i + 1) * STRIP)
            lower = slice(frame + i * STRIP, frame + (i + 1) * STRIP)
            b_re, b_im = far[slot, rows], far[slot, lower]
            o_re, o_im = patch[slot, 0, rows], patch[slot, 1, rows]
            p_re, p_im = probe[j, 0, rows], probe[j, 1, rows]
            for c, d in enumerate((o_re * b_re + o_im * b_im, o_re * b_im - o_im * b_re)):
                high = d.astype(jnp.bfloat16)
                d_high[j, c, rows] = high
                d_low[j, c, rows] = (d - high.astype(jnp.float32)).astype(jnp.bfloat16)
            probe[j, 0, rows] = 0.5 * (p_re * b_re + p_im * b_im)
            probe[j, 1, rows] = 0.5 * (p_re * b_im - p_im * b_re)

    def grad_copy(j):
        return pltpu.make_async_copy(probe.at[j], grads_out.at[j], grad_sem.at[j])

    def visit(pair, carry):
        first, second = 2 * pair, 2 * pair + 1
        enter(first, 0)
        transform(0, 0)
        enter(second, 1)
        transform(1, 0)
        residual(first, 0, None)
        transform(0, 1)
        residual(second, 1, jnp.where(second < alive, 1.0, 0.0))
        transform(1, 1)
        leave(first, 0)
        leave(second, 1)
        grad_copy(first).start()
        grad_copy(second).start()
        return carry

    pairs = (alive + 1) // 2
    lax.fori_loop(0, pairs, visit, 0)

    def skip(j, carry):
        d_high[j] = jnp.zeros((2, frame, frame), jnp.bfloat16)
        d_low[j] = jnp.zeros((2, frame, frame), jnp.bfloat16)
        return carry

    lax.fori_loop(2 * pairs, pos_dev, skip, 0)

    cross[...] = jnp.zeros_like(cross)
    rows_q = frame // shares

    def eigen_strip(i, carry):
        rows = pl.ds(pl.multiple_of(i * STRIP, STRIP), STRIP)
        q = i // (rows_q // STRIP)
        inner = pl.ds(pl.multiple_of(i % (rows_q // STRIP) * STRIP, STRIP), STRIP)
        for c in range(2):
            high = d_high[:, c, rows, :].reshape(pos_dev * STRIP, frame)
            low = d_low[:, c, rows, :].reshape(pos_dev * STRIP, frame)
            e = eig[:, c, rows, :].reshape(modes * STRIP, frame)
            both = jnp.dot(weights_t[...], high, preferred_element_type=jnp.float32)
            rest = jnp.dot(weights_t[:modes * STRIP], low, preferred_element_type=jnp.float32)
            grad = (both[:modes * STRIP] + both[modes * STRIP:] + rest) * scale
            for k in range(modes):
                eigen[q, 2 * k + c, inner, :] = grad[k * STRIP:(k + 1) * STRIP]
            cross[...] += lax.dot_general(
                high, e, (((1,), (1,)), ((), ())), preferred_element_type=jnp.float32
            )
        return carry

    lax.fori_loop(0, frame // STRIP, eigen_strip, 0, unroll=4)
    pending = []

    def start(source, target):
        copy = pltpu.make_async_copy(source, target, out_sem.at[len(pending)])
        copy.start()
        pending.append(copy)

    for h in far_first(shares):
        mine, other = slabs_of(member, h)
        out_eigen[h] = eigen[other].astype(jnp.bfloat16)
        start(out_eigen.at[h], eigen_send[h % 2].at[h // 2])
        start(eigen.at[mine], eigen_keep[h % 2].at[h // 2])

    total = exact(one_hot(by_position[::-1], 1), diagonals(cross[...]))
    coef[...] = lax.dot_general(
        one_hot(by_mode[::-1], 1), total, (((1,), (1,)), ((), ())),
        precision=lax.Precision.HIGHEST, preferred_element_type=jnp.float32,
    ) * (1.0 / frame)

    def drain(j, carry):
        grad_copy(j).wait()
        return carry

    lax.fori_loop(0, 2 * pairs, drain, 0)
    for copy in pending:
        copy.wait()


def positions(offs, scale, indices, pieces, eigenprobes, amps, table, coef_t):
    modes, _, frame, _ = eigenprobes.shape
    pos_dev = amps.shape[0]
    side = pieces[0].shape[2]
    shares = len(offs)
    blocks = side // LANES
    smem = pl.BlockSpec(memory_space=SMEM)
    whole = pl.BlockSpec(memory_space=VMEM)
    anywhere = pl.BlockSpec(memory_space=pl.ANY)
    eigen_half = (shares // 2, 2 * modes, frame // shares, frame)
    eigen_part = (shares // 4,) + eigen_half[1:]
    grads = (pos_dev, 2, frame, frame)
    return pl.pallas_call(
        functools.partial(position_kernel, offs, scale),
        in_specs=[smem] * 3 + [anywhere] * (len(pieces) + 3) + [whole],
        out_specs=[anywhere] * 5 + [whole],
        scratch_shapes=[
            pltpu.VMEM((REACH, 2, side, side), jnp.bfloat16),
            pltpu.VMEM(table.shape, jnp.bfloat16),
            pltpu.VMEM(grads, jnp.float32),
            pltpu.VMEM(amps.shape, jnp.bfloat16),
            pltpu.VMEM(eigenprobes.shape, jnp.bfloat16),
            pltpu.VMEM((REACH, 2, blocks + 1, side, LANES), jnp.float32),
            pltpu.VMEM((2, frame, 2 * frame), jnp.bfloat16),
            pltpu.VMEM((2, 2 * frame, frame), jnp.bfloat16),
            pltpu.VMEM((2, 2 * frame, frame), jnp.float32),
            pltpu.VMEM((2, 2, frame, frame), jnp.float32),
            pltpu.VMEM(grads, jnp.bfloat16),
            pltpu.VMEM(grads, jnp.bfloat16),
            pltpu.VMEM((shares, 2 * modes, frame // shares, frame), jnp.float32),
            pltpu.VMEM(eigen_half, jnp.bfloat16),
            pltpu.VMEM((pos_dev * STRIP, modes * STRIP), jnp.float32),
            pltpu.VMEM((pos_dev * STRIP, 2 * modes * STRIP), jnp.bfloat16),
            pltpu.VMEM((2 * modes * STRIP, pos_dev * STRIP), jnp.bfloat16),
            pltpu.SemaphoreType.DMA((len(pieces),)),
            pltpu.SemaphoreType.DMA,
            pltpu.SemaphoreType.DMA,
            pltpu.SemaphoreType.DMA,
            pltpu.SemaphoreType.DMA((pos_dev,)),
            pltpu.SemaphoreType.DMA((shares,)),
        ],
        out_shape=[
            jax.ShapeDtypeStruct(eigen_part, jnp.bfloat16),
            jax.ShapeDtypeStruct(eigen_part, jnp.bfloat16),
            jax.ShapeDtypeStruct(eigen_part, jnp.float32),
            jax.ShapeDtypeStruct(eigen_part, jnp.float32),
            jax.ShapeDtypeStruct(grads, jnp.float32),
            jax.ShapeDtypeStruct((modes, pos_dev), jnp.float32),
        ],
        compiler_params=pltpu.CompilerParams(vmem_limit_bytes=VMEM_LIMIT),
        name="positions",
    )(*indices, *pieces, eigenprobes, amps, table, coef_t)


def scatter_kernel(shares, tile_list, offsets, group_counts, grads_in, *refs):
    send, keep = refs[:2 * REACH], refs[2 * REACH:4 * REACH]
    grads, acc, out_send, grad_sem, out_sem = refs[4 * REACH:]
    pos_dev, _, frame, _ = grads.shape
    blocks, side = acc.shape[2] - 1, acc.shape[3]
    slab = side // shares
    _, member, alive, place = coordinates(tile_list, offsets, group_counts, pos_dev)

    def grad_copy(j):
        return pltpu.make_async_copy(grads_in.at[j], grads.at[j], grad_sem.at[j])

    def begin(j, carry):
        grad_copy(j).start()
        return carry

    lax.fori_loop(0, alive, begin, 0)

    def clear(i, carry):
        rows = pl.ds(pl.multiple_of(i * LANES, LANES), LANES)
        for section in range(REACH):
            for c in range(2):
                for b in range(blocks + 1):
                    acc[section, c, b, rows, :] = jnp.zeros((LANES, LANES), jnp.float32)
        return carry

    lax.fori_loop(0, side // LANES, clear, 0)
    lane = lax.broadcasted_iota(jnp.int32, (STRIP, LANES), 1)

    def add(j, carry):
        grad_copy(j).wait()
        for m in range(2):
            section, row, col = place(j, m)
            cb, s = col // LANES, col % LANES
            inside = lane >= s
            for i in range(frame // STRIP):
                for c in range(2):
                    low, high = (
                        pltpu.roll(grads[j, c, i * STRIP:(i + 1) * STRIP, b * LANES:(b + 1) * LANES], s, 1)
                        for b in range(2)
                    )
                    for b, value in enumerate(
                        (
                            jnp.where(inside, low, 0.0),
                            jnp.where(inside, high, low),
                            jnp.where(inside, 0.0, high),
                        )
                    ):
                        at = (section, c, cb + b, pl.ds(row + i * STRIP, STRIP), slice(None))
                        acc[at] = acc[at] + value
        return carry

    lax.fori_loop(0, alive, add, 0)
    pending = []

    def start(source, target):
        copy = pltpu.make_async_copy(source, target, out_sem.at[len(pending)])
        copy.start()
        pending.append(copy)

    for section in range(REACH - 1, -1, -1):
        for h in far_first(shares):
            mine, other = (pl.multiple_of(at * slab, slab) for at in slabs_of(member, h))
            start(
                acc.at[section, :, pl.ds(0, blocks), pl.ds(mine, slab), :],
                keep[2 * section + h % 2].at[h // 2],
            )
            for c in range(2):
                for b in range(blocks):
                    out_send[section, h, c, b] = acc[section, c, b, pl.ds(other, slab), :].astype(jnp.bfloat16)
            start(out_send.at[section, h], send[2 * section + h % 2].at[h // 2])
    for copy in pending:
        copy.wait()


def scatter(shares, side, indices, grads):
    blocks = side // LANES
    anywhere = pl.BlockSpec(memory_space=pl.ANY)
    half = (shares // 2, 2, blocks, side // shares, LANES)
    part = (shares // 4,) + half[1:]
    return pl.pallas_call(
        functools.partial(scatter_kernel, shares),
        in_specs=[pl.BlockSpec(memory_space=SMEM)] * 3 + [anywhere],
        out_specs=[anywhere] * (4 * REACH),
        scratch_shapes=[
            pltpu.VMEM(grads.shape, jnp.float32),
            pltpu.VMEM((REACH, 2, blocks + 1, side, LANES), jnp.float32),
            pltpu.VMEM((REACH,) + half, jnp.bfloat16),
            pltpu.SemaphoreType.DMA((grads.shape[0],)),
            pltpu.SemaphoreType.DMA((REACH * shares,)),
        ],
        out_shape=[jax.ShapeDtypeStruct(part, jnp.bfloat16)] * (2 * REACH)
        + [jax.ShapeDtypeStruct(part, jnp.float32)] * (2 * REACH),
        compiler_params=pltpu.CompilerParams(vmem_limit_bytes=20 * 1024 * 1024),
        cost_estimate=pl.CostEstimate(flops=1 << 24, bytes_accessed=16 << 20, transcendentals=0),
        name="scatter",
    )(*indices, grads)


def after(array, *others):
    return lax.optimization_barrier((array,) + others)[0]


def after_all(arrays, *others):
    return lax.optimization_barrier(tuple(arrays) + others)[:len(arrays)]


def halve(keep, send, before_core=(), before_cross=()):
    far = [keep[1], after(swap(after(send[1], *before_core), "probe", 1), *before_cross)]
    terms = [keep[0], swap(send[0], "probe", 1)]
    leaving = None
    bit = 2
    while True:
        sending = sum(term.astype(jnp.float32) for term in far).astype(jnp.bfloat16)
        leaving = sending if leaving is None else leaving
        terms.append(swap(sending, "probe", bit))
        if terms[0].shape[0] == 1:
            return sum(term[0].astype(jnp.float32) for term in terms), leaving, terms[-1]
        pick = lambda term, which: term.reshape((term.shape[0] // 2, 2) + term.shape[1:])[:, which]
        far, terms = [pick(term, 1) for term in terms], [pick(term, 0) for term in terms]
        bit *= 2


def sum_over(axis, value):
    peers = lax.axis_size(axis)
    shares = lax.all_to_all(value.astype(jnp.bfloat16), axis, 0, 0)
    total = jnp.sum(shares.astype(jnp.float32), 0).astype(jnp.bfloat16)

    def gather(*others):
        copies = jnp.broadcast_to(after(total, *others), (peers,) + total.shape)
        return lax.all_to_all(copies, axis, 0, 0).astype(jnp.float32)

    return total, gather


def finish_kernel(first, second, out):
    blocks = first.shape[1]
    for c in range(2):
        for b in range(blocks):
            out[c, :, b * LANES:(b + 1) * LANES] = first[c, b] + second[c, b].astype(jnp.float32)


def finish(first, second):
    _, blocks, slab, lanes = first.shape
    return pl.pallas_call(
        finish_kernel,
        in_specs=[pl.BlockSpec(memory_space=VMEM)] * 2,
        out_specs=pl.BlockSpec(memory_space=VMEM),
        out_shape=jax.ShapeDtypeStruct((2, slab, blocks * lanes), jnp.float32),
        compiler_params=pltpu.CompilerParams(vmem_limit_bytes=8 * 1024 * 1024),
        name="finish",
    )(first, second)


def on_device(tiles, eigenprobes, coefficients, tile_list, offsets, amplitudes, group_counts):
    modes, _, frame, _ = eigenprobes.shape
    side = tiles.shape[2]
    pos_dev = coefficients.shape[0]
    blocks = lax.axis_size("blk")
    shares = lax.axis_size("probe")
    member = lax.axis_index("probe")
    slab = side // shares
    bits = [1 << i for i in range(shares.bit_length() - 1)]

    offs = [0]
    for bit in reversed(bits):
        offs = offs + [o ^ bit for o in offs]
    quarter = lax.dynamic_slice_in_dim(tiles[0], member * slab, slab, 1)
    near = shift(quarter, "blk", -1)
    held = [[near], [shift(near, "blk", -1)]]
    eig, amps = stage(*after_all((eigenprobes, amplitudes), near))
    held[1][0] = after(held[1][0], eig)
    table, tile, coef_t, lists, corners = stage(
        *after_all((tables(frame), tiles[0], coefficients.T, tile_list.T, offsets.T), held[1][0])
    )
    for bit in reversed(bits):
        for part in held:
            arrived = [swap(piece, "probe", bit) for piece in part]
            if bit > 1:
                arrived[0] = after(arrived[0], eig if part is held[0] else table)
            part += arrived

    indices = (lists, corners, group_counts)
    scale = (pos_dev * blocks * shares) ** (-0.5)
    out = positions(
        tuple(offs), scale, indices, [tile] + held[0] + held[1], eig, amps, table, coef_t
    )
    eigen_send, eigen_keep, grads, coef_rows = out[:2], out[2:4], out[4], out[5]

    eigen, leaving, crossed = halve(eigen_keep, eigen_send)
    out = scatter(shares, side, indices, after(grads, leaving))
    send, keep = ([out[at + 2 * i:at + 2 * i + 2] for i in range(REACH)] for at in (0, 2 * REACH))
    last = REACH - 1
    mine, leaving, _ = halve(keep[last], send[last], before_cross=(crossed,))
    total, gather = sum_over("blk", after(eigen, leaving).reshape(blocks, -1, frame))
    moving = after(mine.astype(jnp.bfloat16), total)
    gate = moving
    for section in range(last - 1, -1, -1):
        mine, gate, _ = halve(keep[section], send[section], before_cross=(gate,))
        arrived = shift(moving, "blk", 1)
        if section > 0:
            moving = (arrived.astype(jnp.float32) + mine).astype(jnp.bfloat16)
    eigen_share = gather(gate).reshape(modes, 2, frame // shares, frame)
    summed = finish(mine, arrived)
    return (summed[None], eigen_share, coef_rows.T)


def solution(mesh):
    in_specs = (
        P(("recon", "blk"), None, None, None),
        P("recon", None, None, None),
        P(("recon", "blk", "probe"), None),
        P(("recon", "blk", "probe"), None),
        P(("recon", "blk", "probe"), None),
        P(("recon", "blk", "probe"), None, None),
        P(("recon", "blk")),
    )
    out_specs = (
        P(("recon", "blk"), None, "probe", None),
        P("recon", None, "probe", None),
        P(("recon", "blk", "probe"), None),
    )
    return jax.shard_map(
        on_device, mesh=mesh, in_specs=in_specs, out_specs=out_specs, check_vma=False
    )
```

```python
import functools
import math

import jax
import jax.numpy as jnp
import ml_dtypes
import numpy as np
from jax import lax
from jax.experimental import pallas as pl
from jax.experimental.pallas import tpu as pltpu
from jax.sharding import PartitionSpec as P

REACH = 3
LANES = 128
STRIP = 16
VMEM = pltpu.MemorySpace.VMEM
SMEM = pltpu.MemorySpace.SMEM
VMEM_LIMIT = 36 * 1024 * 1024


def tables(frame):
    indices = np.arange(frame)
    angle = (indices[:, None] * indices[None, :] % frame) * (2.0 * math.pi / frame)
    cos_part = np.cos(angle) / math.sqrt(frame)
    sin_part = -np.sin(angle) / math.sqrt(frame)
    forward = np.block([[cos_part, sin_part], [-sin_part, cos_part]])
    forward = forward.astype(np.float32).astype(ml_dtypes.bfloat16)
    return jnp.asarray(np.stack([forward, forward.T]))


def shift(array, axis, by):
    peers = lax.axis_size(axis)
    return lax.ppermute(array, axis, [(i, (i + by) % peers) for i in range(peers)])


def swap(array, axis, bit):
    peers = lax.axis_size(axis)
    return lax.ppermute(array, axis, [(i, i ^ bit) for i in range(peers)])


def slabs_of(member, h):
    pair, core = member >> 1, member & 1
    mine = 2 * (pair ^ h) + core
    return mine, mine ^ 1


def far_first(shares):
    return [*range(1, shares // 2, 2), *range(0, shares // 2, 2)]


def coordinates(tile_list, offsets, group_counts, pos_dev):
    blocks = lax.axis_size("blk")
    my_block, member = lax.axis_index("blk"), lax.axis_index("probe")
    alive = jnp.clip(group_counts[0] - member * pos_dev, 0, pos_dev)

    def place(j, m):
        section = lax.rem(tile_list[m, j] - my_block + blocks, blocks)
        return section, offsets[2 * m, j], offsets[2 * m + 1, j]

    return my_block, member, alive, place


def one_hot(shape, axis):
    return (
        lax.broadcasted_iota(jnp.int32, shape, axis) // STRIP == lax.broadcasted_iota(jnp.int32, shape, 1 - axis)
    ).astype(jnp.float32)


def diagonals(array):
    row = lax.broadcasted_iota(jnp.int32, array.shape, 0)
    col = lax.broadcasted_iota(jnp.int32, array.shape, 1)
    return jnp.where(row % STRIP == col % STRIP, array, 0.0)


def exact(left, right):
    return jnp.dot(left, right, precision=lax.Precision.HIGHEST, preferred_element_type=jnp.float32)


def two_terms(array):
    high = array.astype(jnp.bfloat16)
    return high, (array - high.astype(jnp.float32)).astype(jnp.bfloat16)


def stage_kernel(*refs):
    count = len(refs) // 2
    sem = refs[-1]
    copies = [
        pltpu.make_async_copy(source, target, sem.at[i])
        for i, (source, target) in enumerate(zip(refs[:count], refs[count:2 * count]))
    ]
    for copy in copies:
        copy.start()
    for copy in copies:
        copy.wait()


def stage(*arrays):
    anywhere = pl.BlockSpec(memory_space=pl.ANY)
    return pl.pallas_call(
        stage_kernel,
        in_specs=[anywhere] * len(arrays),
        out_specs=[anywhere] * len(arrays),
        scratch_shapes=[pltpu.SemaphoreType.DMA((len(arrays),))],
        out_shape=[jax.ShapeDtypeStruct(x.shape, x.dtype) for x in arrays],
        compiler_params=pltpu.CompilerParams(vmem_limit_bytes=1024 * 1024),
        name="stage",
    )(*arrays)


def position_kernel(offs, scale, tile_list, offsets, group_counts, *refs):
    shares = len(offs)
    pieces = refs[: 1 + (REACH - 1) * shares]
    eig_in, amps_in, tables_in, coef_in = refs[len(pieces):len(pieces) + 4]
    eigen_send, eigen_keep = refs[len(pieces) + 4:len(pieces) + 6], refs[len(pieces) + 6:len(pieces) + 8]
    grads_out, coef = refs[len(pieces) + 8:len(pieces) + 10]
    (staged, table, probe, amps, eig, obj, ex, mid, far, patch, d_high, d_low, eigen, out_eigen, cross,
     weights, weights_t, piece_sem, table_sem, amps_sem, eig_sem, grad_sem, out_sem) = refs[len(pieces) + 10:]
    pos_dev, _, frame, _ = probe.shape
    modes = eig.shape[0]
    side = staged.shape[2]
    blocks = side // LANES
    slab = side // shares
    my_block, member, alive, place = coordinates(tile_list, offsets, group_counts, pos_dev)
    strips = range(frame // STRIP)

    copies = [pltpu.make_async_copy(pieces[0], staged.at[0], piece_sem.at[0])]
    for section in range(1, REACH):
        for i in range(shares):
            start = pl.multiple_of((member ^ offs[i]) * slab, slab)
            at = 1 + (section - 1) * shares + i
            copies.append(
                pltpu.make_async_copy(
                    pieces[at], staged.at[section, :, pl.ds(start, slab), :], piece_sem.at[at]
                )
            )
    table_copy = pltpu.make_async_copy(tables_in, table, table_sem)
    amps_copy = pltpu.make_async_copy(amps_in, amps, amps_sem)
    eig_copy = pltpu.make_async_copy(eig_in, eig, eig_sem)
    for copy in [eig_copy] + copies + [table_copy, amps_copy]:
        copy.start()

    by_position = (pos_dev * STRIP, pos_dev)
    by_mode = (modes * STRIP, modes)
    tall_t = exact(exact(one_hot(by_mode, 0), coef_in[...]), one_hot(by_position[::-1], 1))
    high, low = two_terms(diagonals(tall_t))
    weights_t[...] = jnp.concatenate([high, low], 0)
    spread = lax.dot_general(
        one_hot(by_position, 0), coef_in[...], (((1,), (1,)), ((), ())),
        precision=lax.Precision.HIGHEST, preferred_element_type=jnp.float32,
    )
    high, low = two_terms(diagonals(exact(spread, one_hot(by_mode[::-1], 1))))
    weights[...] = jnp.concatenate([high, low], 1)
    eig_copy.wait()

    def synth(i, carry):
        rows = pl.ds(pl.multiple_of(i * STRIP, STRIP), STRIP)
        for c in range(2):
            e = eig[:, c, rows, :].reshape(modes * STRIP, frame)
            made = jnp.dot(
                weights[...], jnp.concatenate([e, e], 0), preferred_element_type=jnp.float32
            )
            probe[:, c, rows, :] = made.reshape(pos_dev, STRIP, frame)
        return carry

    lax.fori_loop(0, frame // STRIP, synth, 0, unroll=4)
    for copy in copies:
        copy.wait()

    def widen(i, carry):
        rows = pl.ds(pl.multiple_of(i * LANES, LANES), LANES)
        for section in range(REACH):
            for c in range(2):
                for b in range(blocks):
                    obj[section, c, b, rows, :] = staged[
                        section, c, rows, b * LANES:(b + 1) * LANES
                    ].astype(jnp.float32)
        return carry

    lax.fori_loop(0, side // LANES, widen, 0)
    table_copy.wait()
    amps_copy.wait()

    lane = lax.broadcasted_iota(jnp.int32, (STRIP, LANES), 1)

    def enter(j, slot):
        where = []
        for m in range(2):
            section, row, col = place(j, m)
            s = col % LANES
            where.append((section, row, col // LANES, (LANES - s) % LANES, lane < LANES - s))
        for i in strips:
            rows = slice(i * STRIP, (i + 1) * STRIP)
            parts = []
            for c in range(2):
                total = None
                for section, row, cb, back_by, keep_lane in where:
                    rolled = [
                        pltpu.roll(obj[section, c, cb + b, pl.ds(row + i * STRIP, STRIP), :], back_by, 1)
                        for b in range(3)
                    ]
                    block = [jnp.where(keep_lane, rolled[b], rolled[b + 1]) for b in range(2)]
                    total = block if total is None else [x + y for x, y in zip(total, block)]
                parts.append([0.5 * x for x in total])
            for b in range(2):
                cols = slice(b * LANES, (b + 1) * LANES)
                o_re, o_im = parts[0][b], parts[1][b]
                p_re, p_im = probe[j, 0, rows, cols], probe[j, 1, rows, cols]
                patch[slot, 0, rows, cols] = o_re
                patch[slot, 1, rows, cols] = o_im
                ex[slot, rows, b * LANES:(b + 1) * LANES] = (p_re * o_re - p_im * o_im).astype(jnp.bfloat16)
                ex[slot, rows, frame + b * LANES:frame + (b + 1) * LANES] = (
                    p_re * o_im + p_im * o_re
                ).astype(jnp.bfloat16)

    def transform(slot, way):
        half = jnp.dot(ex[slot], table[way], preferred_element_type=jnp.float32)
        mid[slot, :frame] = half[:, :frame].astype(jnp.bfloat16)
        mid[slot, frame:] = half[:, frame:].astype(jnp.bfloat16)
        far[slot] = jnp.dot(table[1 - way], mid[slot], preferred_element_type=jnp.float32)

    def residual(j, slot, living):
        for i in strips:
            rows = slice(i * STRIP, (i + 1) * STRIP)
            lower = slice(frame + i * STRIP, frame + (i + 1) * STRIP)
            f_re, f_im = far[slot, rows], far[slot, lower]
            factor = 1.0 - amps[j, rows].astype(jnp.float32) * lax.rsqrt(f_re * f_re + f_im * f_im + 1.0)
            if living is not None:
                factor = factor * living
            ex[slot, rows, :frame] = (f_re * factor).astype(jnp.bfloat16)
            ex[slot, rows, frame:] = (f_im * factor).astype(jnp.bfloat16)

    def leave(j, slot):
        for i in strips:
            rows = slice(i * STRIP, (i + 1) * STRIP)
            lower = slice(frame + i * STRIP, frame + (i + 1) * STRIP)
            b_re, b_im = far[slot, rows], far[slot, lower]
            o_re, o_im = patch[slot, 0, rows], patch[slot, 1, rows]
            p_re, p_im = probe[j, 0, rows], probe[j, 1, rows]
            for c, d in enumerate((o_re * b_re + o_im * b_im, o_re * b_im - o_im * b_re)):
                high = d.astype(jnp.bfloat16)
                d_high[j, c, rows] = high
                d_low[j, c, rows] = (d - high.astype(jnp.float32)).astype(jnp.bfloat16)
            probe[j, 0, rows] = 0.5 * (p_re * b_re + p_im * b_im)
            probe[j, 1, rows] = 0.5 * (p_re * b_im - p_im * b_re)

    def grad_copy(j):
        return pltpu.make_async_copy(probe.at[j], grads_out.at[j], grad_sem.at[j])

    def visit(pair, carry):
        first, second = 2 * pair, 2 * pair + 1
        enter(first, 0)
        transform(0, 0)
        enter(second, 1)
        transform(1, 0)
        residual(first, 0, None)
        transform(0, 1)
        residual(second, 1, jnp.where(second < alive, 1.0, 0.0))
        transform(1, 1)
        leave(first, 0)
        leave(second, 1)
        grad_copy(first).start()
        grad_copy(second).start()
        return carry

    pairs = (alive + 1) // 2
    lax.fori_loop(0, pairs, visit, 0)

    def skip(j, carry):
        d_high[j] = jnp.zeros((2, frame, frame), jnp.bfloat16)
        d_low[j] = jnp.zeros((2, frame, frame), jnp.bfloat16)
        return carry

    lax.fori_loop(2 * pairs, pos_dev, skip, 0)

    cross[...] = jnp.zeros_like(cross)
    rows_q = frame // shares

    def eigen_strip(i, carry):
        rows = pl.ds(pl.multiple_of(i * STRIP, STRIP), STRIP)
        q = i // (rows_q // STRIP)
        inner = pl.ds(pl.multiple_of(i % (rows_q // STRIP) * STRIP, STRIP), STRIP)
        for c in range(2):
            high = d_high[:, c, rows, :].reshape(pos_dev * STRIP, frame)
            low = d_low[:, c, rows, :].reshape(pos_dev * STRIP, frame)
            e = eig[:, c, rows, :].reshape(modes * STRIP, frame)
            both = jnp.dot(weights_t[...], high, preferred_element_type=jnp.float32)
            rest = jnp.dot(weights_t[:modes * STRIP], low, preferred_element_type=jnp.float32)
            grad = (both[:modes * STRIP] + both[modes * STRIP:] + rest) * scale
            for k in range(modes):
                eigen[q, 2 * k + c, inner, :] = grad[k * STRIP:(k + 1) * STRIP]
            cross[...] += lax.dot_general(
                high, e, (((1,), (1,)), ((), ())), preferred_element_type=jnp.float32
            )
        return carry

    lax.fori_loop(0, frame // STRIP, eigen_strip, 0, unroll=4)
    pending = []

    def start(source, target):
        copy = pltpu.make_async_copy(source, target, out_sem.at[len(pending)])
        copy.start()
        pending.append(copy)

    for h in far_first(shares):
        mine, other = slabs_of(member, h)
        out_eigen[h] = eigen[other].astype(jnp.bfloat16)
        start(out_eigen.at[h], eigen_send[h % 2].at[h // 2])
        start(eigen.at[mine], eigen_keep[h % 2].at[h // 2])

    total = exact(one_hot(by_position[::-1], 1), diagonals(cross[...]))
    coef[...] = lax.dot_general(
        one_hot(by_mode[::-1], 1), total, (((1,), (1,)), ((), ())),
        precision=lax.Precision.HIGHEST, preferred_element_type=jnp.float32,
    ) * (1.0 / frame)

    def drain(j, carry):
        grad_copy(j).wait()
        return carry

    lax.fori_loop(0, 2 * pairs, drain, 0)
    for copy in pending:
        copy.wait()


def positions(offs, scale, indices, pieces, eigenprobes, amps, table, coef_t):
    modes, _, frame, _ = eigenprobes.shape
    pos_dev = amps.shape[0]
    side = pieces[0].shape[2]
    shares = len(offs)
    blocks = side // LANES
    smem = pl.BlockSpec(memory_space=SMEM)
    whole = pl.BlockSpec(memory_space=VMEM)
    anywhere = pl.BlockSpec(memory_space=pl.ANY)
    eigen_half = (shares // 2, 2 * modes, frame // shares, frame)
    eigen_part = (shares // 4,) + eigen_half[1:]
    grads = (pos_dev, 2, frame, frame)
    return pl.pallas_call(
        functools.partial(position_kernel, offs, scale),
        in_specs=[smem] * 3 + [anywhere] * (len(pieces) + 3) + [whole],
        out_specs=[anywhere] * 5 + [whole],
        scratch_shapes=[
            pltpu.VMEM((REACH, 2, side, side), jnp.bfloat16),
            pltpu.VMEM(table.shape, jnp.bfloat16),
            pltpu.VMEM(grads, jnp.float32),
            pltpu.VMEM(amps.shape, jnp.bfloat16),
            pltpu.VMEM(eigenprobes.shape, jnp.bfloat16),
            pltpu.VMEM((REACH, 2, blocks + 1, side, LANES), jnp.float32),
            pltpu.VMEM((2, frame, 2 * frame), jnp.bfloat16),
            pltpu.VMEM((2, 2 * frame, frame), jnp.bfloat16),
            pltpu.VMEM((2, 2 * frame, frame), jnp.float32),
            pltpu.VMEM((2, 2, frame, frame), jnp.float32),
            pltpu.VMEM(grads, jnp.bfloat16),
            pltpu.VMEM(grads, jnp.bfloat16),
            pltpu.VMEM((shares, 2 * modes, frame // shares, frame), jnp.float32),
            pltpu.VMEM(eigen_half, jnp.bfloat16),
            pltpu.VMEM((pos_dev * STRIP, modes * STRIP), jnp.float32),
            pltpu.VMEM((pos_dev * STRIP, 2 * modes * STRIP), jnp.bfloat16),
            pltpu.VMEM((2 * modes * STRIP, pos_dev * STRIP), jnp.bfloat16),
            pltpu.SemaphoreType.DMA((len(pieces),)),
            pltpu.SemaphoreType.DMA,
            pltpu.SemaphoreType.DMA,
            pltpu.SemaphoreType.DMA,
            pltpu.SemaphoreType.DMA((pos_dev,)),
            pltpu.SemaphoreType.DMA((shares,)),
        ],
        out_shape=[
            jax.ShapeDtypeStruct(eigen_part, jnp.bfloat16),
            jax.ShapeDtypeStruct(eigen_part, jnp.bfloat16),
            jax.ShapeDtypeStruct(eigen_part, jnp.float32),
            jax.ShapeDtypeStruct(eigen_part, jnp.float32),
            jax.ShapeDtypeStruct(grads, jnp.float32),
            jax.ShapeDtypeStruct((modes, pos_dev), jnp.float32),
        ],
        compiler_params=pltpu.CompilerParams(vmem_limit_bytes=VMEM_LIMIT),
        name="positions",
    )(*indices, *pieces, eigenprobes, amps, table, coef_t)


def scatter_kernel(shares, tile_list, offsets, group_counts, grads_in, *refs):
    send, keep = refs[:2 * REACH], refs[2 * REACH:4 * REACH]
    grads, acc, out_send, grad_sem, out_sem = refs[4 * REACH:]
    pos_dev, _, frame, _ = grads.shape
    blocks, side = acc.shape[2] - 1, acc.shape[3]
    slab = side // shares
    _, member, alive, place = coordinates(tile_list, offsets, group_counts, pos_dev)

    def grad_copy(j):
        return pltpu.make_async_copy(grads_in.at[j], grads.at[j], grad_sem.at[j])

    def begin(j, carry):
        grad_copy(j).start()
        return carry

    lax.fori_loop(0, alive, begin, 0)

    def clear(i, carry):
        rows = pl.ds(pl.multiple_of(i * LANES, LANES), LANES)
        for section in range(REACH):
            for c in range(2):
                for b in range(blocks + 1):
                    acc[section, c, b, rows, :] = jnp.zeros((LANES, LANES), jnp.float32)
        return carry

    lax.fori_loop(0, side // LANES, clear, 0)
    lane = lax.broadcasted_iota(jnp.int32, (STRIP, LANES), 1)

    def add(j, carry):
        grad_copy(j).wait()
        for m in range(2):
            section, row, col = place(j, m)
            cb, s = col // LANES, col % LANES
            inside = lane >= s
            for i in range(frame // STRIP):
                for c in range(2):
                    low, high = (
                        pltpu.roll(grads[j, c, i * STRIP:(i + 1) * STRIP, b * LANES:(b + 1) * LANES], s, 1)
                        for b in range(2)
                    )
                    for b, value in enumerate(
                        (
                            jnp.where(inside, low, 0.0),
                            jnp.where(inside, high, low),
                            jnp.where(inside, 0.0, high),
                        )
                    ):
                        at = (section, c, cb + b, pl.ds(row + i * STRIP, STRIP), slice(None))
                        acc[at] = acc[at] + value
        return carry

    lax.fori_loop(0, alive, add, 0)
    pending = []

    def start(source, target):
        copy = pltpu.make_async_copy(source, target, out_sem.at[len(pending)])
        copy.start()
        pending.append(copy)

    for section in range(REACH - 1, -1, -1):
        for h in far_first(shares):
            mine, other = (pl.multiple_of(at * slab, slab) for at in slabs_of(member, h))
            start(
                acc.at[section, :, pl.ds(0, blocks), pl.ds(mine, slab), :],
                keep[2 * section + h % 2].at[h // 2],
            )
            for c in range(2):
                for b in range(blocks):
                    out_send[section, h, c, b] = acc[section, c, b, pl.ds(other, slab), :].astype(jnp.bfloat16)
            start(out_send.at[section, h], send[2 * section + h % 2].at[h // 2])
    for copy in pending:
        copy.wait()


def scatter(shares, side, indices, grads):
    blocks = side // LANES
    anywhere = pl.BlockSpec(memory_space=pl.ANY)
    half = (shares // 2, 2, blocks, side // shares, LANES)
    part = (shares // 4,) + half[1:]
    return pl.pallas_call(
        functools.partial(scatter_kernel, shares),
        in_specs=[pl.BlockSpec(memory_space=SMEM)] * 3 + [anywhere],
        out_specs=[anywhere] * (4 * REACH),
        scratch_shapes=[
            pltpu.VMEM(grads.shape, jnp.float32),
            pltpu.VMEM((REACH, 2, blocks + 1, side, LANES), jnp.float32),
            pltpu.VMEM((REACH,) + half, jnp.bfloat16),
            pltpu.SemaphoreType.DMA((grads.shape[0],)),
            pltpu.SemaphoreType.DMA((REACH * shares,)),
        ],
        out_shape=[jax.ShapeDtypeStruct(part, jnp.bfloat16)] * (2 * REACH)
        + [jax.ShapeDtypeStruct(part, jnp.float32)] * (2 * REACH),
        compiler_params=pltpu.CompilerParams(vmem_limit_bytes=20 * 1024 * 1024),
        cost_estimate=pl.CostEstimate(flops=1 << 24, bytes_accessed=16 << 20, transcendentals=0),
        name="scatter",
    )(*indices, grads)


def after(array, *others):
    return lax.optimization_barrier((array,) + others)[0]


def after_all(arrays, *others):
    return lax.optimization_barrier(tuple(arrays) + others)[:len(arrays)]


def halve(keep, send, before_core=(), before_cross=()):
    far = [keep[1], after(swap(after(send[1], *before_core), "probe", 1), *before_cross)]
    terms = [keep[0], swap(send[0], "probe", 1)]
    leaving = None
    bit = 2
    while True:
        sending = sum(term.astype(jnp.float32) for term in far).astype(jnp.bfloat16)
        leaving = sending if leaving is None else leaving
        terms.append(swap(sending, "probe", bit))
        if terms[0].shape[0] == 1:
            return sum(term[0].astype(jnp.float32) for term in terms), leaving, terms[-1]
        pick = lambda term, which: term.reshape((term.shape[0] // 2, 2) + term.shape[1:])[:, which]
        far, terms = [pick(term, 1) for term in terms], [pick(term, 0) for term in terms]
        bit *= 2


def add_up_kernel(shares, out):
    total = shares[0].astype(jnp.float32)
    for i in range(1, shares.shape[0]):
        total += shares[i].astype(jnp.float32)
    total = total.astype(jnp.bfloat16)
    for i in range(out.shape[0]):
        out[i] = total


def widen_kernel(array, out):
    out[...] = array[...].astype(jnp.float32)


def small_call(kernel, array, kind, name):
    return pl.pallas_call(
        kernel,
        in_specs=[pl.BlockSpec(memory_space=VMEM)],
        out_specs=pl.BlockSpec(memory_space=VMEM),
        out_shape=jax.ShapeDtypeStruct(array.shape, kind),
        compiler_params=pltpu.CompilerParams(vmem_limit_bytes=8 * 1024 * 1024),
        name=name,
    )(array)


def finish_kernel(first, second, out):
    blocks = first.shape[1]
    for c in range(2):
        for b in range(blocks):
            out[c, :, b * LANES:(b + 1) * LANES] = first[c, b] + second[c, b].astype(jnp.float32)


def finish(first, second):
    _, blocks, slab, lanes = first.shape
    return pl.pallas_call(
        finish_kernel,
        in_specs=[pl.BlockSpec(memory_space=VMEM)] * 2,
        out_specs=pl.BlockSpec(memory_space=VMEM),
        out_shape=jax.ShapeDtypeStruct((2, slab, blocks * lanes), jnp.float32),
        compiler_params=pltpu.CompilerParams(vmem_limit_bytes=8 * 1024 * 1024),
        name="finish",
    )(first, second)


def on_device(tiles, eigenprobes, coefficients, tile_list, offsets, amplitudes, group_counts):
    modes, _, frame, _ = eigenprobes.shape
    side = tiles.shape[2]
    pos_dev = coefficients.shape[0]
    blocks = lax.axis_size("blk")
    shares = lax.axis_size("probe")
    member = lax.axis_index("probe")
    slab = side // shares
    bits = [1 << i for i in range(shares.bit_length() - 1)]

    offs = [0]
    for bit in reversed(bits):
        offs = offs + [o ^ bit for o in offs]
    quarter = lax.dynamic_slice_in_dim(tiles[0], member * slab, slab, 1)
    near = shift(quarter, "blk", -1)
    held = [[near], [shift(near, "blk", -1)]]
    eig, amps = stage(*after_all((eigenprobes, amplitudes), near))
    held[1][0] = after(held[1][0], eig)
    table, tile, coef_t, lists, corners = stage(
        *after_all((tables(frame), tiles[0], coefficients.T, tile_list.T, offsets.T), held[1][0])
    )
    for bit in reversed(bits):
        for part in held:
            arrived = [swap(piece, "probe", bit) for piece in part]
            if bit > 1:
                arrived[0] = after(arrived[0], eig if part is held[0] else table)
            part += arrived

    indices = (lists, corners, group_counts)
    scale = (pos_dev * blocks * shares) ** (-0.5)
    out = positions(
        tuple(offs), scale, indices, [tile] + held[0] + held[1], eig, amps, table, coef_t
    )
    eigen_send, eigen_keep, grads, coef_rows = out[:2], out[2:4], out[4], out[5]

    eigen, leaving, crossed = halve(eigen_keep, eigen_send)
    out = scatter(shares, side, indices, after(grads, leaving))
    send, keep = ([out[at + 2 * i:at + 2 * i + 2] for i in range(REACH)] for at in (0, 2 * REACH))
    last = REACH - 1
    mine, leaving, _ = halve(keep[last], send[last], before_cross=(crossed,))
    scattered = after(eigen, leaving).reshape(blocks, -1, frame).astype(jnp.bfloat16)
    scattered = lax.all_to_all(scattered, "blk", 0, 0)
    moving = mine.astype(jnp.bfloat16)
    gate = moving
    for section in range(last - 1, -1, -1):
        mine, _, gate = halve(keep[section], send[section], before_cross=(gate,))
        if section == last - 1:
            scattered = after(scattered, gate)
        arrived = shift(moving, "blk", 1)
        if section > 0:
            moving = (arrived.astype(jnp.float32) + mine).astype(jnp.bfloat16)
    copies = small_call(add_up_kernel, scattered, jnp.bfloat16, "add_up")
    gathered = lax.all_to_all(copies, "blk", 0, 0)
    eigen_share = small_call(widen_kernel, gathered, jnp.float32, "widen")
    eigen_share = eigen_share.reshape(modes, 2, frame // shares, frame)
    summed = finish(mine, arrived)
    return (summed[None], eigen_share, coef_rows.T)


def solution(mesh):
    in_specs = (
        P(("recon", "blk"), None, None, None),
        P("recon", None, None, None),
        P(("recon", "blk", "probe"), None),
        P(("recon", "blk", "probe"), None),
        P(("recon", "blk", "probe"), None),
        P(("recon", "blk", "probe"), None, None),
        P(("recon", "blk")),
    )
    out_specs = (
        P(("recon", "blk"), None, "probe", None),
        P("recon", None, "probe", None),
        P(("recon", "blk", "probe"), None),
    )
    return jax.shard_map(
        on_device, mesh=mesh, in_specs=in_specs, out_specs=out_specs, check_vma=False
    )
```

```python
import functools
import math

import jax
import jax.numpy as jnp
import ml_dtypes
import numpy as np
from jax import lax
from jax.experimental import pallas as pl
from jax.experimental.pallas import tpu as pltpu
from jax.sharding import PartitionSpec as P

REACH = 3
LANES = 128
STRIP = 16
VMEM = pltpu.MemorySpace.VMEM
SMEM = pltpu.MemorySpace.SMEM
VMEM_LIMIT = 36 * 1024 * 1024


def tables(frame):
    indices = np.arange(frame)
    angle = (indices[:, None] * indices[None, :] % frame) * (2.0 * math.pi / frame)
    cos_part = np.cos(angle) / math.sqrt(frame)
    sin_part = -np.sin(angle) / math.sqrt(frame)
    forward = np.block([[cos_part, sin_part], [-sin_part, cos_part]])
    forward = forward.astype(np.float32).astype(ml_dtypes.bfloat16)
    return jnp.asarray(np.stack([forward, forward.T]))


def shift(array, axis, by):
    peers = lax.axis_size(axis)
    return lax.ppermute(array, axis, [(i, (i + by) % peers) for i in range(peers)])


def swap(array, axis, bit):
    peers = lax.axis_size(axis)
    return lax.ppermute(array, axis, [(i, i ^ bit) for i in range(peers)])


def slabs_of(member, h):
    pair, core = member >> 1, member & 1
    mine = 2 * (pair ^ h) + core
    return mine, mine ^ 1


def far_first(shares):
    return [*range(1, shares // 2, 2), *range(0, shares // 2, 2)]


def coordinates(tile_list, offsets, group_counts, pos_dev):
    blocks = lax.axis_size("blk")
    my_block, member = lax.axis_index("blk"), lax.axis_index("probe")
    alive = jnp.clip(group_counts[0] - member * pos_dev, 0, pos_dev)

    def place(j, m):
        section = lax.rem(tile_list[m, j] - my_block + blocks, blocks)
        return section, offsets[2 * m, j], offsets[2 * m + 1, j]

    return my_block, member, alive, place


def one_hot(shape, axis):
    return (
        lax.broadcasted_iota(jnp.int32, shape, axis) // STRIP == lax.broadcasted_iota(jnp.int32, shape, 1 - axis)
    ).astype(jnp.float32)


def diagonals(array):
    row = lax.broadcasted_iota(jnp.int32, array.shape, 0)
    col = lax.broadcasted_iota(jnp.int32, array.shape, 1)
    return jnp.where(row % STRIP == col % STRIP, array, 0.0)


def exact(left, right):
    return jnp.dot(left, right, precision=lax.Precision.HIGHEST, preferred_element_type=jnp.float32)


def two_terms(array):
    high = array.astype(jnp.bfloat16)
    return high, (array - high.astype(jnp.float32)).astype(jnp.bfloat16)


def stage_kernel(*refs):
    count = len(refs) // 2
    sem = refs[-1]
    copies = [
        pltpu.make_async_copy(source, target, sem.at[i])
        for i, (source, target) in enumerate(zip(refs[:count], refs[count:2 * count]))
    ]
    for copy in copies:
        copy.start()
    for copy in copies:
        copy.wait()


def stage(*arrays):
    anywhere = pl.BlockSpec(memory_space=pl.ANY)
    return pl.pallas_call(
        stage_kernel,
        in_specs=[anywhere] * len(arrays),
        out_specs=[anywhere] * len(arrays),
        scratch_shapes=[pltpu.SemaphoreType.DMA((len(arrays),))],
        out_shape=[jax.ShapeDtypeStruct(x.shape, x.dtype) for x in arrays],
        compiler_params=pltpu.CompilerParams(vmem_limit_bytes=1024 * 1024),
        name="stage",
    )(*arrays)


def position_kernel(offs, scale, tile_list, offsets, group_counts, *refs):
    shares = len(offs)
    pieces = refs[: 1 + (REACH - 1) * shares]
    eig_in, amps_in, tables_in, coef_in = refs[len(pieces):len(pieces) + 4]
    eigen_send, eigen_keep, grads_out, coef = refs[len(pieces) + 4:len(pieces) + 8]
    (staged, table, probe, amps, eig, obj, ex, mid, far, patch, d_high, d_low, eigen, out_eigen, cross,
     weights, weights_t, piece_sem, table_sem, amps_sem, eig_sem, grad_sem, out_sem) = refs[len(pieces) + 8:]
    pos_dev, _, frame, _ = probe.shape
    modes = eig.shape[0]
    side = staged.shape[2]
    blocks = side // LANES
    slab = side // shares
    my_block, member, alive, place = coordinates(tile_list, offsets, group_counts, pos_dev)
    strips = range(frame // STRIP)

    copies = [pltpu.make_async_copy(pieces[0], staged.at[0], piece_sem.at[0])]
    for section in range(1, REACH):
        for i in range(shares):
            start = pl.multiple_of((member ^ offs[i]) * slab, slab)
            at = 1 + (section - 1) * shares + i
            copies.append(
                pltpu.make_async_copy(
                    pieces[at], staged.at[section, :, pl.ds(start, slab), :], piece_sem.at[at]
                )
            )
    table_copy = pltpu.make_async_copy(tables_in, table, table_sem)
    amps_copy = pltpu.make_async_copy(amps_in, amps, amps_sem)
    eig_copy = pltpu.make_async_copy(eig_in, eig, eig_sem)
    for copy in [eig_copy] + copies + [table_copy, amps_copy]:
        copy.start()

    by_position = (pos_dev * STRIP, pos_dev)
    by_mode = (modes * STRIP, modes)
    tall_t = exact(exact(one_hot(by_mode, 0), coef_in[...]), one_hot(by_position[::-1], 1))
    high, low = two_terms(diagonals(tall_t))
    weights_t[...] = jnp.concatenate([high, low], 0)
    spread = lax.dot_general(
        one_hot(by_position, 0), coef_in[...], (((1,), (1,)), ((), ())),
        precision=lax.Precision.HIGHEST, preferred_element_type=jnp.float32,
    )
    high, low = two_terms(diagonals(exact(spread, one_hot(by_mode[::-1], 1))))
    weights[...] = jnp.concatenate([high, low], 1)
    eig_copy.wait()

    def synth(i, carry):
        rows = pl.ds(pl.multiple_of(i * STRIP, STRIP), STRIP)
        for c in range(2):
            e = eig[:, c, rows, :].reshape(modes * STRIP, frame)
            made = jnp.dot(
                weights[...], jnp.concatenate([e, e], 0), preferred_element_type=jnp.float32
            )
            probe[:, c, rows, :] = made.reshape(pos_dev, STRIP, frame)
        return carry

    lax.fori_loop(0, frame // STRIP, synth, 0, unroll=4)
    for copy in copies:
        copy.wait()

    def widen(i, carry):
        rows = pl.ds(pl.multiple_of(i * LANES, LANES), LANES)
        for section in range(REACH):
            for c in range(2):
                for b in range(blocks):
                    obj[section, c, b, rows, :] = staged[
                        section, c, rows, b * LANES:(b + 1) * LANES
                    ].astype(jnp.float32)
        return carry

    lax.fori_loop(0, side // LANES, widen, 0)
    table_copy.wait()
    amps_copy.wait()

    lane = lax.broadcasted_iota(jnp.int32, (STRIP, LANES), 1)

    def enter(j, slot):
        where = []
        for m in range(2):
            section, row, col = place(j, m)
            s = col % LANES
            where.append((section, row, col // LANES, (LANES - s) % LANES, lane < LANES - s))
        for i in strips:
            rows = slice(i * STRIP, (i + 1) * STRIP)
            parts = []
            for c in range(2):
                total = None
                for section, row, cb, back_by, keep_lane in where:
                    rolled = [
                        pltpu.roll(obj[section, c, cb + b, pl.ds(row + i * STRIP, STRIP), :], back_by, 1)
                        for b in range(3)
                    ]
                    block = [jnp.where(keep_lane, rolled[b], rolled[b + 1]) for b in range(2)]
                    total = block if total is None else [x + y for x, y in zip(total, block)]
                parts.append([0.5 * x for x in total])
            for b in range(2):
                cols = slice(b * LANES, (b + 1) * LANES)
                o_re, o_im = parts[0][b], parts[1][b]
                p_re, p_im = probe[j, 0, rows, cols], probe[j, 1, rows, cols]
                patch[slot, 0, rows, cols] = o_re
                patch[slot, 1, rows, cols] = o_im
                ex[slot, rows, b * LANES:(b + 1) * LANES] = (p_re * o_re - p_im * o_im).astype(jnp.bfloat16)
                ex[slot, rows, frame + b * LANES:frame + (b + 1) * LANES] = (
                    p_re * o_im + p_im * o_re
                ).astype(jnp.bfloat16)

    def transform(slot, way):
        half = jnp.dot(ex[slot], table[way], preferred_element_type=jnp.float32)
        mid[slot, :frame] = half[:, :frame].astype(jnp.bfloat16)
        mid[slot, frame:] = half[:, frame:].astype(jnp.bfloat16)
        far[slot] = jnp.dot(table[1 - way], mid[slot], preferred_element_type=jnp.float32)

    def residual(j, slot, living):
        for i in strips:
            rows = slice(i * STRIP, (i + 1) * STRIP)
            lower = slice(frame + i * STRIP, frame + (i + 1) * STRIP)
            f_re, f_im = far[slot, rows], far[slot, lower]
            factor = 1.0 - amps[j, rows].astype(jnp.float32) * lax.rsqrt(f_re * f_re + f_im * f_im + 1.0)
            if living is not None:
                factor = factor * living
            ex[slot, rows, :frame] = (f_re * factor).astype(jnp.bfloat16)
            ex[slot, rows, frame:] = (f_im * factor).astype(jnp.bfloat16)

    def leave(j, slot):
        for i in strips:
            rows = slice(i * STRIP, (i + 1) * STRIP)
            lower = slice(frame + i * STRIP, frame + (i + 1) * STRIP)
            b_re, b_im = far[slot, rows], far[slot, lower]
            o_re, o_im = patch[slot, 0, rows], patch[slot, 1, rows]
            p_re, p_im = probe[j, 0, rows], probe[j, 1, rows]
            for c, d in enumerate((o_re * b_re + o_im * b_im, o_re * b_im - o_im * b_re)):
                high = d.astype(jnp.bfloat16)
                d_high[j, c, rows] = high
                d_low[j, c, rows] = (d - high.astype(jnp.float32)).astype(jnp.bfloat16)
            probe[j, 0, rows] = 0.5 * (p_re * b_re + p_im * b_im)
            probe[j, 1, rows] = 0.5 * (p_re * b_im - p_im * b_re)

    def grad_copy(j):
        return pltpu.make_async_copy(probe.at[j], grads_out.at[j], grad_sem.at[j])

    def visit(pair, carry):
        first, second = 2 * pair, 2 * pair + 1
        enter(first, 0)
        transform(0, 0)
        enter(second, 1)
        transform(1, 0)
        residual(first, 0, None)
        transform(0, 1)
        residual(second, 1, jnp.where(second < alive, 1.0, 0.0))
        transform(1, 1)
        leave(first, 0)
        leave(second, 1)
        grad_copy(first).start()
        grad_copy(second).start()
        return carry

    pairs = (alive + 1) // 2
    lax.fori_loop(0, pairs, visit, 0)

    def skip(j, carry):
        d_high[j] = jnp.zeros((2, frame, frame), jnp.bfloat16)
        d_low[j] = jnp.zeros((2, frame, frame), jnp.bfloat16)
        return carry

    lax.fori_loop(2 * pairs, pos_dev, skip, 0)

    cross[...] = jnp.zeros_like(cross)
    rows_q = frame // shares

    def eigen_strip(i, carry):
        rows = pl.ds(pl.multiple_of(i * STRIP, STRIP), STRIP)
        q = i // (rows_q // STRIP)
        inner = pl.ds(pl.multiple_of(i % (rows_q // STRIP) * STRIP, STRIP), STRIP)
        for c in range(2):
            high = d_high[:, c, rows, :].reshape(pos_dev * STRIP, frame)
            low = d_low[:, c, rows, :].reshape(pos_dev * STRIP, frame)
            e = eig[:, c, rows, :].reshape(modes * STRIP, frame)
            both = jnp.dot(weights_t[...], high, preferred_element_type=jnp.float32)
            rest = jnp.dot(weights_t[:modes * STRIP], low, preferred_element_type=jnp.float32)
            grad = (both[:modes * STRIP] + both[modes * STRIP:] + rest) * scale
            for k in range(modes):
                eigen[q, 2 * k + c, inner, :] = grad[k * STRIP:(k + 1) * STRIP]
            cross[...] += lax.dot_general(
                high, e, (((1,), (1,)), ((), ())), preferred_element_type=jnp.float32
            )
        return carry

    lax.fori_loop(0, frame // STRIP, eigen_strip, 0, unroll=4)
    pending = []

    def start(source, target):
        copy = pltpu.make_async_copy(source, target, out_sem.at[len(pending)])
        copy.start()
        pending.append(copy)

    parts, _, share = out_eigen.shape[:3]
    for h in range(shares // 2):
        mine, other = slabs_of(member, h)
        for i in range(parts):
            of_part = pl.ds(i * share, share)
            out_eigen[i, h] = eigen[other, of_part].astype(jnp.bfloat16)
            start(eigen.at[mine, of_part], eigen_keep.at[i, h])
    start(out_eigen, eigen_send)

    total = exact(one_hot(by_position[::-1], 1), diagonals(cross[...]))
    coef[...] = lax.dot_general(
        one_hot(by_mode[::-1], 1), total, (((1,), (1,)), ((), ())),
        precision=lax.Precision.HIGHEST, preferred_element_type=jnp.float32,
    ) * (1.0 / frame)

    def drain(j, carry):
        grad_copy(j).wait()
        return carry

    lax.fori_loop(0, 2 * pairs, drain, 0)
    for copy in pending:
        copy.wait()


def positions(offs, scale, indices, pieces, eigenprobes, amps, table, coef_t):
    modes, _, frame, _ = eigenprobes.shape
    pos_dev = amps.shape[0]
    side = pieces[0].shape[2]
    shares = len(offs)
    blocks = side // LANES
    smem = pl.BlockSpec(memory_space=SMEM)
    whole = pl.BlockSpec(memory_space=VMEM)
    anywhere = pl.BlockSpec(memory_space=pl.ANY)
    peers = lax.axis_size("blk")
    parts = peers if 2 * modes % peers == 0 else 1
    eigen_half = (parts, shares // 2, 2 * modes // parts, frame // shares, frame)
    grads = (pos_dev, 2, frame, frame)
    return pl.pallas_call(
        functools.partial(position_kernel, offs, scale),
        in_specs=[smem] * 3 + [anywhere] * (len(pieces) + 3) + [whole],
        out_specs=[anywhere] * 3 + [whole],
        scratch_shapes=[
            pltpu.VMEM((REACH, 2, side, side), jnp.bfloat16),
            pltpu.VMEM(table.shape, jnp.bfloat16),
            pltpu.VMEM(grads, jnp.float32),
            pltpu.VMEM(amps.shape, jnp.bfloat16),
            pltpu.VMEM(eigenprobes.shape, jnp.bfloat16),
            pltpu.VMEM((REACH, 2, blocks + 1, side, LANES), jnp.float32),
            pltpu.VMEM((2, frame, 2 * frame), jnp.bfloat16),
            pltpu.VMEM((2, 2 * frame, frame), jnp.bfloat16),
            pltpu.VMEM((2, 2 * frame, frame), jnp.float32),
            pltpu.VMEM((2, 2, frame, frame), jnp.float32),
            pltpu.VMEM(grads, jnp.bfloat16),
            pltpu.VMEM(grads, jnp.bfloat16),
            pltpu.VMEM((shares, 2 * modes, frame // shares, frame), jnp.float32),
            pltpu.VMEM(eigen_half, jnp.bfloat16),
            pltpu.VMEM((pos_dev * STRIP, modes * STRIP), jnp.float32),
            pltpu.VMEM((pos_dev * STRIP, 2 * modes * STRIP), jnp.bfloat16),
            pltpu.VMEM((2 * modes * STRIP, pos_dev * STRIP), jnp.bfloat16),
            pltpu.SemaphoreType.DMA((len(pieces),)),
            pltpu.SemaphoreType.DMA,
            pltpu.SemaphoreType.DMA,
            pltpu.SemaphoreType.DMA,
            pltpu.SemaphoreType.DMA((pos_dev,)),
            pltpu.SemaphoreType.DMA((parts * (shares // 2) + 1,)),
        ],
        out_shape=[
            jax.ShapeDtypeStruct(eigen_half, jnp.bfloat16),
            jax.ShapeDtypeStruct(eigen_half, jnp.float32),
            jax.ShapeDtypeStruct(grads, jnp.float32),
            jax.ShapeDtypeStruct((modes, pos_dev), jnp.float32),
        ],
        compiler_params=pltpu.CompilerParams(vmem_limit_bytes=VMEM_LIMIT),
        name="positions",
    )(*indices, *pieces, eigenprobes, amps, table, coef_t)


def scatter_kernel(shares, tile_list, offsets, group_counts, grads_in, *refs):
    send, keep = refs[:2 * REACH], refs[2 * REACH:4 * REACH]
    grads, acc, out_send, grad_sem, out_sem = refs[4 * REACH:]
    pos_dev, _, frame, _ = grads.shape
    blocks, side = acc.shape[2] - 1, acc.shape[3]
    slab = side // shares
    _, member, alive, place = coordinates(tile_list, offsets, group_counts, pos_dev)

    def grad_copy(j):
        return pltpu.make_async_copy(grads_in.at[j], grads.at[j], grad_sem.at[j])

    def begin(j, carry):
        grad_copy(j).start()
        return carry

    lax.fori_loop(0, alive, begin, 0)

    def clear(i, carry):
        rows = pl.ds(pl.multiple_of(i * LANES, LANES), LANES)
        for section in range(REACH):
            for c in range(2):
                for b in range(blocks + 1):
                    acc[section, c, b, rows, :] = jnp.zeros((LANES, LANES), jnp.float32)
        return carry

    lax.fori_loop(0, side // LANES, clear, 0)
    lane = lax.broadcasted_iota(jnp.int32, (STRIP, LANES), 1)

    def add(j, carry):
        grad_copy(j).wait()
        for m in range(2):
            section, row, col = place(j, m)
            cb, s = col // LANES, col % LANES
            inside = lane >= s
            for i in range(frame // STRIP):
                for c in range(2):
                    low, high = (
                        pltpu.roll(grads[j, c, i * STRIP:(i + 1) * STRIP, b * LANES:(b + 1) * LANES], s, 1)
                        for b in range(2)
                    )
                    for b, value in enumerate(
                        (
                            jnp.where(inside, low, 0.0),
                            jnp.where(inside, high, low),
                            jnp.where(inside, 0.0, high),
                        )
                    ):
                        at = (section, c, cb + b, pl.ds(row + i * STRIP, STRIP), slice(None))
                        acc[at] = acc[at] + value
        return carry

    lax.fori_loop(0, alive, add, 0)
    pending = []

    def start(source, target):
        copy = pltpu.make_async_copy(source, target, out_sem.at[len(pending)])
        copy.start()
        pending.append(copy)

    for section in range(REACH - 1, -1, -1):
        for h in far_first(shares):
            mine, other = (pl.multiple_of(at * slab, slab) for at in slabs_of(member, h))
            start(
                acc.at[section, :, pl.ds(0, blocks), pl.ds(mine, slab), :],
                keep[2 * section + h % 2].at[h // 2],
            )
            for c in range(2):
                for b in range(blocks):
                    out_send[section, h, c, b] = acc[section, c, b, pl.ds(other, slab), :].astype(jnp.bfloat16)
            start(out_send.at[section, h], send[2 * section + h % 2].at[h // 2])
    for copy in pending:
        copy.wait()


def scatter(shares, side, indices, grads):
    blocks = side // LANES
    anywhere = pl.BlockSpec(memory_space=pl.ANY)
    half = (shares // 2, 2, blocks, side // shares, LANES)
    part = (shares // 4,) + half[1:]
    return pl.pallas_call(
        functools.partial(scatter_kernel, shares),
        in_specs=[pl.BlockSpec(memory_space=SMEM)] * 3 + [anywhere],
        out_specs=[anywhere] * (4 * REACH),
        scratch_shapes=[
            pltpu.VMEM(grads.shape, jnp.float32),
            pltpu.VMEM((REACH, 2, blocks + 1, side, LANES), jnp.float32),
            pltpu.VMEM((REACH,) + half, jnp.bfloat16),
            pltpu.SemaphoreType.DMA((grads.shape[0],)),
            pltpu.SemaphoreType.DMA((REACH * shares,)),
        ],
        out_shape=[jax.ShapeDtypeStruct(part, jnp.bfloat16)] * (2 * REACH)
        + [jax.ShapeDtypeStruct(part, jnp.float32)] * (2 * REACH),
        compiler_params=pltpu.CompilerParams(vmem_limit_bytes=20 * 1024 * 1024),
        cost_estimate=pl.CostEstimate(flops=1 << 24, bytes_accessed=16 << 20, transcendentals=0),
        name="scatter",
    )(*indices, grads)


def after(array, *others):
    return lax.optimization_barrier((array,) + others)[0]


def after_all(arrays, *others):
    return lax.optimization_barrier(tuple(arrays) + others)[:len(arrays)]


def cross(far, terms):
    leaving = None
    bit = 2
    while True:
        sending = sum(term.astype(jnp.float32) for term in far).astype(jnp.bfloat16)
        leaving = sending if leaving is None else leaving
        terms = terms + [swap(sending, "probe", bit)]
        if terms[0].shape[0] == 1:
            return [term[0] for term in terms], leaving, terms[-1]
        far, terms = halves(terms)
        bit *= 2


def halves(terms):
    pick = lambda term, which: term.reshape((term.shape[0] // 2, 2) + term.shape[1:])[:, which]
    return [pick(term, 1) for term in terms], [pick(term, 0) for term in terms]


def halve(keep, send, *before_cross):
    far = [keep[1], after(swap(send[1], "probe", 1), *before_cross)]
    terms, leaving, arrived = cross(far, [keep[0], swap(send[0], "probe", 1)])
    return sum(term.astype(jnp.float32) for term in terms), leaving, arrived


def add_up_kernel(shares, out):
    total = shares[0].astype(jnp.float32)
    for i in range(1, shares.shape[0]):
        total += shares[i].astype(jnp.float32)
    out[...] = total


def copies_kernel(first, second, out):
    total = (first[...].astype(jnp.float32) + second[...].astype(jnp.float32)).astype(jnp.bfloat16)
    for i in range(out.shape[0]):
        out[i] = total


def widen_kernel(array, out):
    out[...] = array[...].astype(jnp.float32)


def small_call(kernel, shape, kind, name, *arrays):
    return pl.pallas_call(
        kernel,
        in_specs=[pl.BlockSpec(memory_space=VMEM)] * len(arrays),
        out_specs=pl.BlockSpec(memory_space=VMEM),
        out_shape=jax.ShapeDtypeStruct(shape, kind),
        compiler_params=pltpu.CompilerParams(vmem_limit_bytes=8 * 1024 * 1024),
        name=name,
    )(*arrays)


def finish_kernel(first, second, out):
    blocks = first.shape[1]
    for c in range(2):
        for b in range(blocks):
            out[c, :, b * LANES:(b + 1) * LANES] = first[c, b] + second[c, b].astype(jnp.float32)


def finish(first, second):
    _, blocks, slab, lanes = first.shape
    return pl.pallas_call(
        finish_kernel,
        in_specs=[pl.BlockSpec(memory_space=VMEM)] * 2,
        out_specs=pl.BlockSpec(memory_space=VMEM),
        out_shape=jax.ShapeDtypeStruct((2, slab, blocks * lanes), jnp.float32),
        compiler_params=pltpu.CompilerParams(vmem_limit_bytes=8 * 1024 * 1024),
        name="finish",
    )(first, second)


def on_device(tiles, eigenprobes, coefficients, tile_list, offsets, amplitudes, group_counts):
    modes, _, frame, _ = eigenprobes.shape
    side = tiles.shape[2]
    pos_dev = coefficients.shape[0]
    blocks = lax.axis_size("blk")
    shares = lax.axis_size("probe")
    member = lax.axis_index("probe")
    slab = side // shares
    bits = [1 << i for i in range(shares.bit_length() - 1)]

    offs = [0]
    for bit in reversed(bits):
        offs = offs + [o ^ bit for o in offs]
    quarter = lax.dynamic_slice_in_dim(tiles[0], member * slab, slab, 1)
    near = shift(quarter, "blk", -1)
    held = [[near], [shift(near, "blk", -1)]]
    eig, amps = stage(*after_all((eigenprobes, amplitudes), near))
    held[1][0] = after(held[1][0], eig)
    table, tile, coef_t, lists, corners = stage(
        *after_all((tables(frame), tiles[0], coefficients.T, tile_list.T, offsets.T), held[1][0])
    )
    for bit in reversed(bits):
        for part in held:
            arrived = [swap(piece, "probe", bit) for piece in part]
            if bit > 1:
                arrived[0] = after(arrived[0], eig if part is held[0] else table)
            part += arrived

    indices = (lists, corners, group_counts)
    scale = (pos_dev * blocks * shares) ** (-0.5)
    out = positions(
        tuple(offs), scale, indices, [tile] + held[0] + held[1], eig, amps, table, coef_t
    )
    eigen_send, eigen_keep, grads, coef_rows = out

    partial = (eigen_keep + swap(eigen_send, "probe", 1).astype(jnp.float32)).astype(jnp.bfloat16)
    if partial.shape[0] == blocks:
        partial = partial.reshape(blocks, shares // 2, -1, frame)
    else:
        partial = jnp.moveaxis(partial.reshape(shares // 2, blocks, -1, frame), 1, 0)
    scattered = lax.all_to_all(partial, "blk", 0, 0)
    out = scatter(shares, side, indices, after(grads, partial))
    send, keep = ([out[at + 2 * i:at + 2 * i + 2] for i in range(REACH)] for at in (0, 2 * REACH))
    last = REACH - 1
    mine, _, _ = halve(keep[last], send[last])
    moving = mine.astype(jnp.bfloat16)
    gate = moving
    for section in range(last - 1, -1, -1):
        mine, leaving, gate = halve(keep[section], send[section], gate)
        if section == last - 1:
            scattered = after(scattered, leaving)
        arrived = shift(moving, "blk", 1)
        if section > 0:
            moving = (arrived.astype(jnp.float32) + mine).astype(jnp.bfloat16)
    total = small_call(add_up_kernel, scattered.shape[1:], jnp.float32, "add_up", scattered)
    terms, _, _ = cross(*halves([total]))
    first = sum(terms[:-1]) if len(terms) > 2 else terms[0]
    copies = small_call(
        copies_kernel, (blocks,) + first.shape, jnp.bfloat16, "copies", first, terms[-1]
    )
    gathered = lax.all_to_all(copies, "blk", 0, 0)
    eigen_share = small_call(widen_kernel, gathered.shape, jnp.float32, "widen", gathered)
    eigen_share = eigen_share.reshape(modes, 2, frame // shares, frame)
    summed = finish(mine, arrived)
    return (summed[None], eigen_share, coef_rows.T)


def solution(mesh):
    in_specs = (
        P(("recon", "blk"), None, None, None),
        P("recon", None, None, None),
        P(("recon", "blk", "probe"), None),
        P(("recon", "blk", "probe"), None),
        P(("recon", "blk", "probe"), None),
        P(("recon", "blk", "probe"), None, None),
        P(("recon", "blk")),
    )
    out_specs = (
        P(("recon", "blk"), None, "probe", None),
        P("recon", None, "probe", None),
        P(("recon", "blk", "probe"), None),
    )
    return jax.shard_map(
        on_device, mesh=mesh, in_specs=in_specs, out_specs=out_specs, check_vma=False
    )
```

```python
import functools
import math

import jax
import jax.numpy as jnp
import ml_dtypes
import numpy as np
from jax import lax
from jax.experimental import pallas as pl
from jax.experimental.pallas import tpu as pltpu
from jax.sharding import PartitionSpec as P

REACH = 3
LANES = 128
STRIP = 16
VMEM = pltpu.MemorySpace.VMEM
SMEM = pltpu.MemorySpace.SMEM
VMEM_LIMIT = 36 * 1024 * 1024


def tables(frame):
    indices = np.arange(frame)
    angle = (indices[:, None] * indices[None, :] % frame) * (2.0 * math.pi / frame)
    cos_part = np.cos(angle) / math.sqrt(frame)
    sin_part = -np.sin(angle) / math.sqrt(frame)
    forward = np.block([[cos_part, sin_part], [-sin_part, cos_part]])
    forward = forward.astype(np.float32).astype(ml_dtypes.bfloat16)
    return jnp.asarray(np.stack([forward, forward.T]))


def shift(array, axis, by):
    peers = lax.axis_size(axis)
    return lax.ppermute(array, axis, [(i, (i + by) % peers) for i in range(peers)])


def swap(array, axis, bit):
    peers = lax.axis_size(axis)
    return lax.ppermute(array, axis, [(i, i ^ bit) for i in range(peers)])


def slabs_of(member, h):
    pair, core = member >> 1, member & 1
    mine = 2 * (pair ^ h) + core
    return mine, mine ^ 1


def far_first(shares):
    return [*range(1, shares // 2, 2), *range(0, shares // 2, 2)]


def share_of(groups, peers):
    return groups // peers if groups % peers == 0 else 0


def coordinates(tile_list, offsets, group_counts, pos_dev):
    blocks = lax.axis_size("blk")
    my_block, member = lax.axis_index("blk"), lax.axis_index("probe")
    alive = jnp.clip(group_counts[0] - member * pos_dev, 0, pos_dev)

    def place(j, m):
        section = lax.rem(tile_list[m, j] - my_block + blocks, blocks)
        return section, offsets[2 * m, j], offsets[2 * m + 1, j]

    return my_block, member, alive, place


def one_hot(shape, axis):
    return (
        lax.broadcasted_iota(jnp.int32, shape, axis) // STRIP == lax.broadcasted_iota(jnp.int32, shape, 1 - axis)
    ).astype(jnp.float32)


def diagonals(array):
    row = lax.broadcasted_iota(jnp.int32, array.shape, 0)
    col = lax.broadcasted_iota(jnp.int32, array.shape, 1)
    return jnp.where(row % STRIP == col % STRIP, array, 0.0)


def exact(left, right):
    return jnp.dot(left, right, precision=lax.Precision.HIGHEST, preferred_element_type=jnp.float32)


def two_terms(array):
    high = array.astype(jnp.bfloat16)
    return high, (array - high.astype(jnp.float32)).astype(jnp.bfloat16)


def stage_kernel(*refs):
    count = len(refs) // 2
    sem = refs[-1]
    copies = [
        pltpu.make_async_copy(source, target, sem.at[i])
        for i, (source, target) in enumerate(zip(refs[:count], refs[count:2 * count]))
    ]
    for copy in copies:
        copy.start()
    for copy in copies:
        copy.wait()


def stage(*arrays):
    anywhere = pl.BlockSpec(memory_space=pl.ANY)
    return pl.pallas_call(
        stage_kernel,
        in_specs=[anywhere] * len(arrays),
        out_specs=[anywhere] * len(arrays),
        scratch_shapes=[pltpu.SemaphoreType.DMA((len(arrays),))],
        out_shape=[jax.ShapeDtypeStruct(x.shape, x.dtype) for x in arrays],
        compiler_params=pltpu.CompilerParams(vmem_limit_bytes=1024 * 1024),
        name="stage",
    )(*arrays)


def position_kernel(offs, scale, tile_list, offsets, group_counts, *refs):
    shares = len(offs)
    pieces = refs[: 1 + (REACH - 1) * shares]
    eig_in, amps_in, tables_in, coef_in = refs[len(pieces):len(pieces) + 4]
    eigen_send, eigen_keep = refs[len(pieces) + 4:len(pieces) + 6], refs[len(pieces) + 6:len(pieces) + 8]
    grads_out, coef = refs[len(pieces) + 8:len(pieces) + 10]
    (staged, table, probe, amps, eig, obj, ex, mid, far, patch, d_high, d_low, eigen, out_eigen, cross,
     weights, weights_t, piece_sem, table_sem, amps_sem, eig_sem, grad_sem, out_sem) = refs[len(pieces) + 10:]
    pos_dev, _, frame, _ = probe.shape
    modes = eig.shape[0]
    side = staged.shape[2]
    blocks = side // LANES
    slab = side // shares
    my_block, member, alive, place = coordinates(tile_list, offsets, group_counts, pos_dev)
    strips = range(frame // STRIP)

    copies = [pltpu.make_async_copy(pieces[0], staged.at[0], piece_sem.at[0])]
    for section in range(1, REACH):
        for i in range(shares):
            start = pl.multiple_of((member ^ offs[i]) * slab, slab)
            at = 1 + (section - 1) * shares + i
            copies.append(
                pltpu.make_async_copy(
                    pieces[at], staged.at[section, :, pl.ds(start, slab), :], piece_sem.at[at]
                )
            )
    table_copy = pltpu.make_async_copy(tables_in, table, table_sem)
    amps_copy = pltpu.make_async_copy(amps_in, amps, amps_sem)
    eig_copy = pltpu.make_async_copy(eig_in, eig, eig_sem)
    for copy in [eig_copy] + copies + [table_copy, amps_copy]:
        copy.start()

    by_position = (pos_dev * STRIP, pos_dev)
    by_mode = (modes * STRIP, modes)
    tall_t = exact(exact(one_hot(by_mode, 0), coef_in[...]), one_hot(by_position[::-1], 1))
    high, low = two_terms(diagonals(tall_t))
    weights_t[...] = jnp.concatenate([high, low], 0)
    spread = lax.dot_general(
        one_hot(by_position, 0), coef_in[...], (((1,), (1,)), ((), ())),
        precision=lax.Precision.HIGHEST, preferred_element_type=jnp.float32,
    )
    high, low = two_terms(diagonals(0.5 * exact(spread, one_hot(by_mode[::-1], 1))))
    weights[...] = jnp.concatenate([high, low], 1)
    eig_copy.wait()

    def synth(i, carry):
        rows = pl.ds(pl.multiple_of(i * STRIP, STRIP), STRIP)
        for c in range(2):
            e = eig[:, c, rows, :].reshape(modes * STRIP, frame)
            made = jnp.dot(
                weights[...], jnp.concatenate([e, e], 0), preferred_element_type=jnp.float32
            )
            probe[:, c, rows, :] = made.reshape(pos_dev, STRIP, frame)
        return carry

    lax.fori_loop(0, frame // STRIP, synth, 0, unroll=4)
    for copy in copies:
        copy.wait()

    def widen(i, carry):
        rows = pl.ds(pl.multiple_of(i * LANES, LANES), LANES)
        for section in range(REACH):
            for c in range(2):
                for b in range(blocks):
                    obj[section, c, b, rows, :] = staged[
                        section, c, rows, b * LANES:(b + 1) * LANES
                    ].astype(jnp.float32)
        return carry

    lax.fori_loop(0, side // LANES, widen, 0)
    table_copy.wait()
    amps_copy.wait()

    lane = lax.broadcasted_iota(jnp.int32, (STRIP, LANES), 1)

    def enter(j, slot):
        where = []
        for m in range(2):
            section, row, col = place(j, m)
            s = col % LANES
            where.append((section, row, col // LANES, (LANES - s) % LANES, lane < LANES - s))
        for i in strips:
            rows = slice(i * STRIP, (i + 1) * STRIP)
            parts = []
            for c in range(2):
                total = None
                for section, row, cb, back_by, keep_lane in where:
                    rolled = [
                        pltpu.roll(obj[section, c, cb + b, pl.ds(row + i * STRIP, STRIP), :], back_by, 1)
                        for b in range(3)
                    ]
                    block = [jnp.where(keep_lane, rolled[b], rolled[b + 1]) for b in range(2)]
                    total = block if total is None else [x + y for x, y in zip(total, block)]
                parts.append(total)
            for b in range(2):
                cols = slice(b * LANES, (b + 1) * LANES)
                o_re, o_im = parts[0][b], parts[1][b]
                p_re, p_im = probe[j, 0, rows, cols], probe[j, 1, rows, cols]
                patch[slot, 0, rows, cols] = o_re
                patch[slot, 1, rows, cols] = o_im
                ex[slot, rows, b * LANES:(b + 1) * LANES] = (p_re * o_re - p_im * o_im).astype(jnp.bfloat16)
                ex[slot, rows, frame + b * LANES:frame + (b + 1) * LANES] = (
                    p_re * o_im + p_im * o_re
                ).astype(jnp.bfloat16)

    def transform(slot, way):
        half = jnp.dot(ex[slot], table[way], preferred_element_type=jnp.float32)
        mid[slot, :frame] = half[:, :frame].astype(jnp.bfloat16)
        mid[slot, frame:] = half[:, frame:].astype(jnp.bfloat16)
        far[slot] = jnp.dot(table[1 - way], mid[slot], preferred_element_type=jnp.float32)

    def residual(j, slot, living):
        for i in strips:
            rows = slice(i * STRIP, (i + 1) * STRIP)
            lower = slice(frame + i * STRIP, frame + (i + 1) * STRIP)
            f_re, f_im = far[slot, rows], far[slot, lower]
            factor = 1.0 - amps[j, rows].astype(jnp.float32) * lax.rsqrt(f_re * f_re + f_im * f_im + 1.0)
            if living is not None:
                factor = factor * living
            ex[slot, rows, :frame] = (f_re * factor).astype(jnp.bfloat16)
            ex[slot, rows, frame:] = (f_im * factor).astype(jnp.bfloat16)

    def leave(j, slot):
        for i in strips:
            rows = slice(i * STRIP, (i + 1) * STRIP)
            lower = slice(frame + i * STRIP, frame + (i + 1) * STRIP)
            b_re, b_im = far[slot, rows], far[slot, lower]
            o_re, o_im = patch[slot, 0, rows], patch[slot, 1, rows]
            p_re, p_im = probe[j, 0, rows], probe[j, 1, rows]
            for c, d in enumerate((o_re * b_re + o_im * b_im, o_re * b_im - o_im * b_re)):
                high = d.astype(jnp.bfloat16)
                d_high[j, c, rows] = high
                d_low[j, c, rows] = (d - high.astype(jnp.float32)).astype(jnp.bfloat16)
            probe[j, 0, rows] = p_re * b_re + p_im * b_im
            probe[j, 1, rows] = p_re * b_im - p_im * b_re

    def grad_copy(j):
        return pltpu.make_async_copy(probe.at[j], grads_out.at[j], grad_sem.at[j])

    def visit(pair, carry):
        first, second = 2 * pair, 2 * pair + 1
        enter(first, 0)
        transform(0, 0)
        enter(second, 1)
        transform(1, 0)
        residual(first, 0, None)
        transform(0, 1)
        residual(second, 1, jnp.where(second < alive, 1.0, 0.0))
        transform(1, 1)
        leave(first, 0)
        leave(second, 1)
        grad_copy(first).start()
        grad_copy(second).start()
        return carry

    pairs = (alive + 1) // 2
    lax.fori_loop(0, pairs, visit, 0)

    def skip(j, carry):
        d_high[j] = jnp.zeros((2, frame, frame), jnp.bfloat16)
        d_low[j] = jnp.zeros((2, frame, frame), jnp.bfloat16)
        return carry

    lax.fori_loop(2 * pairs, pos_dev, skip, 0)

    cross[...] = jnp.zeros_like(cross)
    rows_q = frame // shares
    groups = 2 * modes
    share = share_of(groups, lax.axis_size("blk"))

    def eigen_strip(i, carry):
        rows = pl.ds(pl.multiple_of(i * STRIP, STRIP), STRIP)
        q = i // (rows_q // STRIP)
        inner = pl.ds(pl.multiple_of(i % (rows_q // STRIP) * STRIP, STRIP), STRIP)
        for c in range(2):
            high = d_high[:, c, rows, :].reshape(pos_dev * STRIP, frame)
            low = d_low[:, c, rows, :].reshape(pos_dev * STRIP, frame)
            e = eig[:, c, rows, :].reshape(modes * STRIP, frame)
            both = jnp.dot(weights_t[...], high, preferred_element_type=jnp.float32)
            rest = jnp.dot(weights_t[:modes * STRIP], low, preferred_element_type=jnp.float32)
            grad = (both[:modes * STRIP] + both[modes * STRIP:] + rest) * (0.5 * scale)
            for k in range(modes):
                group = 2 * k + c
                if share:
                    group = (group // share ^ my_block) * share + group % share
                eigen[q, group, inner, :] = grad[k * STRIP:(k + 1) * STRIP]
            cross[...] += lax.dot_general(
                high, e, (((1,), (1,)), ((), ())), preferred_element_type=jnp.float32
            )
        return carry

    lax.fori_loop(0, frame // STRIP, eigen_strip, 0, unroll=4)
    pending = []

    def start(source, target):
        copy = pltpu.make_async_copy(source, target, out_sem.at[len(pending)])
        copy.start()
        pending.append(copy)

    for h in far_first(shares):
        mine, other = slabs_of(member, h)
        out_eigen[h] = eigen[other].astype(jnp.bfloat16)
        start(out_eigen.at[h], eigen_send[h % 2].at[h // 2])
        start(eigen.at[mine], eigen_keep[h % 2].at[h // 2])

    total = exact(one_hot(by_position[::-1], 1), diagonals(cross[...]))
    coef[...] = lax.dot_general(
        one_hot(by_mode[::-1], 1), total, (((1,), (1,)), ((), ())),
        precision=lax.Precision.HIGHEST, preferred_element_type=jnp.float32,
    ) * (0.5 / frame)

    def drain(j, carry):
        grad_copy(j).wait()
        return carry

    lax.fori_loop(0, 2 * pairs, drain, 0)
    for copy in pending:
        copy.wait()


def positions(offs, scale, indices, pieces, eigenprobes, amps, table, coef_t):
    modes, _, frame, _ = eigenprobes.shape
    pos_dev = amps.shape[0]
    side = pieces[0].shape[2]
    shares = len(offs)
    blocks = side // LANES
    smem = pl.BlockSpec(memory_space=SMEM)
    whole = pl.BlockSpec(memory_space=VMEM)
    anywhere = pl.BlockSpec(memory_space=pl.ANY)
    eigen_half = (shares // 2, 2 * modes, frame // shares, frame)
    eigen_part = (shares // 4,) + eigen_half[1:]
    grads = (pos_dev, 2, frame, frame)
    return pl.pallas_call(
        functools.partial(position_kernel, offs, scale),
        in_specs=[smem] * 3 + [anywhere] * (len(pieces) + 3) + [whole],
        out_specs=[anywhere] * 5 + [whole],
        scratch_shapes=[
            pltpu.VMEM((REACH, 2, side, side), jnp.bfloat16),
            pltpu.VMEM(table.shape, jnp.bfloat16),
            pltpu.VMEM(grads, jnp.float32),
            pltpu.VMEM(amps.shape, jnp.bfloat16),
            pltpu.VMEM(eigenprobes.shape, jnp.bfloat16),
            pltpu.VMEM((REACH, 2, blocks + 1, side, LANES), jnp.float32),
            pltpu.VMEM((2, frame, 2 * frame), jnp.bfloat16),
            pltpu.VMEM((2, 2 * frame, frame), jnp.bfloat16),
            pltpu.VMEM((2, 2 * frame, frame), jnp.float32),
            pltpu.VMEM((2, 2, frame, frame), jnp.float32),
            pltpu.VMEM(grads, jnp.bfloat16),
            pltpu.VMEM(grads, jnp.bfloat16),
            pltpu.VMEM((shares, 2 * modes, frame // shares, frame), jnp.float32),
            pltpu.VMEM(eigen_half, jnp.bfloat16),
            pltpu.VMEM((pos_dev * STRIP, modes * STRIP), jnp.float32),
            pltpu.VMEM((pos_dev * STRIP, 2 * modes * STRIP), jnp.bfloat16),
            pltpu.VMEM((2 * modes * STRIP, pos_dev * STRIP), jnp.bfloat16),
            pltpu.SemaphoreType.DMA((len(pieces),)),
            pltpu.SemaphoreType.DMA,
            pltpu.SemaphoreType.DMA,
            pltpu.SemaphoreType.DMA,
            pltpu.SemaphoreType.DMA((pos_dev,)),
            pltpu.SemaphoreType.DMA((shares,)),
        ],
        out_shape=[
            jax.ShapeDtypeStruct(eigen_part, jnp.bfloat16),
            jax.ShapeDtypeStruct(eigen_part, jnp.bfloat16),
            jax.ShapeDtypeStruct(eigen_part, jnp.float32),
            jax.ShapeDtypeStruct(eigen_part, jnp.float32),
            jax.ShapeDtypeStruct(grads, jnp.float32),
            jax.ShapeDtypeStruct((modes, pos_dev), jnp.float32),
        ],
        compiler_params=pltpu.CompilerParams(vmem_limit_bytes=VMEM_LIMIT),
        name="positions",
    )(*indices, *pieces, eigenprobes, amps, table, coef_t)


def scatter_kernel(shares, tile_list, offsets, group_counts, grads_in, *refs):
    send, keep = refs[:2 * REACH], refs[2 * REACH:4 * REACH]
    grads, acc, out_send, grad_sem, out_sem = refs[4 * REACH:]
    pos_dev, _, frame, _ = grads.shape
    blocks, side = acc.shape[2] - 1, acc.shape[3]
    slab = side // shares
    _, member, alive, place = coordinates(tile_list, offsets, group_counts, pos_dev)

    def grad_copy(j):
        return pltpu.make_async_copy(grads_in.at[j], grads.at[j], grad_sem.at[j])

    def begin(j, carry):
        grad_copy(j).start()
        return carry

    lax.fori_loop(0, alive, begin, 0)

    def clear(i, carry):
        rows = pl.ds(pl.multiple_of(i * LANES, LANES), LANES)
        for section in range(REACH):
            for c in range(2):
                for b in range(blocks + 1):
                    acc[section, c, b, rows, :] = jnp.zeros((LANES, LANES), jnp.float32)
        return carry

    lax.fori_loop(0, side // LANES, clear, 0)
    lane = lax.broadcasted_iota(jnp.int32, (STRIP, LANES), 1)

    def add(j, carry):
        grad_copy(j).wait()
        for m in range(2):
            section, row, col = place(j, m)
            cb, s = col // LANES, col % LANES
            inside = lane >= s
            for i in range(frame // STRIP):
                for c in range(2):
                    low, high = (
                        pltpu.roll(grads[j, c, i * STRIP:(i + 1) * STRIP, b * LANES:(b + 1) * LANES], s, 1)
                        for b in range(2)
                    )
                    for b, value in enumerate(
                        (
                            jnp.where(inside, low, 0.0),
                            jnp.where(inside, high, low),
                            jnp.where(inside, 0.0, high),
                        )
                    ):
                        at = (section, c, cb + b, pl.ds(row + i * STRIP, STRIP), slice(None))
                        acc[at] = acc[at] + value
        return carry

    lax.fori_loop(0, alive, add, 0)
    pending = []

    def start(source, target):
        copy = pltpu.make_async_copy(source, target, out_sem.at[len(pending)])
        copy.start()
        pending.append(copy)

    for section in range(REACH - 1, -1, -1):
        for h in far_first(shares):
            mine, other = (pl.multiple_of(at * slab, slab) for at in slabs_of(member, h))
            start(
                acc.at[section, :, pl.ds(0, blocks), pl.ds(mine, slab), :],
                keep[2 * section + h % 2].at[h // 2],
            )
            for c in range(2):
                for b in range(blocks):
                    out_send[section, h, c, b] = acc[section, c, b, pl.ds(other, slab), :].astype(jnp.bfloat16)
            start(out_send.at[section, h], send[2 * section + h % 2].at[h // 2])
    for copy in pending:
        copy.wait()


def scatter(shares, side, indices, grads):
    blocks = side // LANES
    anywhere = pl.BlockSpec(memory_space=pl.ANY)
    half = (shares // 2, 2, blocks, side // shares, LANES)
    part = (shares // 4,) + half[1:]
    return pl.pallas_call(
        functools.partial(scatter_kernel, shares),
        in_specs=[pl.BlockSpec(memory_space=SMEM)] * 3 + [anywhere],
        out_specs=[anywhere] * (4 * REACH),
        scratch_shapes=[
            pltpu.VMEM(grads.shape, jnp.float32),
            pltpu.VMEM((REACH, 2, blocks + 1, side, LANES), jnp.float32),
            pltpu.VMEM((REACH,) + half, jnp.bfloat16),
            pltpu.SemaphoreType.DMA((grads.shape[0],)),
            pltpu.SemaphoreType.DMA((REACH * shares,)),
        ],
        out_shape=[jax.ShapeDtypeStruct(part, jnp.bfloat16)] * (2 * REACH)
        + [jax.ShapeDtypeStruct(part, jnp.float32)] * (2 * REACH),
        compiler_params=pltpu.CompilerParams(vmem_limit_bytes=20 * 1024 * 1024),
        cost_estimate=pl.CostEstimate(flops=1 << 24, bytes_accessed=16 << 20, transcendentals=0),
        name="scatter",
    )(*indices, grads)


def after(array, *others):
    return lax.optimization_barrier((array,) + others)[0]


def after_all(arrays, *others):
    return lax.optimization_barrier(tuple(arrays) + others)[:len(arrays)]


def halve(keep, send, before_core=(), before_cross=()):
    far = [keep[1], after(swap(after(send[1], *before_core), "probe", 1), *before_cross)]
    terms = [keep[0], swap(send[0], "probe", 1)]
    leaving = None
    bit = 2
    while True:
        sending = sum(term.astype(jnp.float32) for term in far).astype(jnp.bfloat16)
        leaving = sending if leaving is None else leaving
        terms.append(swap(sending, "probe", bit))
        if terms[0].shape[0] == 1:
            return sum(term[0].astype(jnp.float32) for term in terms), leaving, terms[-1]
        pick = lambda term, which: term.reshape((term.shape[0] // 2, 2) + term.shape[1:])[:, which]
        far, terms = [pick(term, 1) for term in terms], [pick(term, 0) for term in terms]
        bit *= 2


def add_up_kernel(own, *refs):
    arrived, out = refs[:-1], refs[-1]
    total = own[...]
    for term in arrived:
        total += term[...].astype(jnp.float32)
    total = total.astype(jnp.bfloat16)
    for i in range(out.shape[0]):
        out[i] = total


def widen_kernel(array, out):
    out[...] = array[...].astype(jnp.float32)


def small_call(kernel, shape, kind, name, *arrays):
    return pl.pallas_call(
        kernel,
        in_specs=[pl.BlockSpec(memory_space=VMEM)] * len(arrays),
        out_specs=pl.BlockSpec(memory_space=VMEM),
        out_shape=jax.ShapeDtypeStruct(shape, kind),
        compiler_params=pltpu.CompilerParams(vmem_limit_bytes=8 * 1024 * 1024),
        name=name,
    )(*arrays)


def scatter_sum(axis, value, relative):
    peers, me = lax.axis_size(axis), lax.axis_index(axis)
    share = (lambda i: value[i]) if relative else (lambda i: lax.dynamic_index_in_dim(value, me ^ i, 0, False))
    sent = [share(i).astype(jnp.bfloat16) for i in range(1, peers)]
    arrived = [swap(sending, axis, i) for i, sending in enumerate(sent, 1)]
    total = small_call(
        add_up_kernel, (peers,) + value.shape[1:], jnp.bfloat16, "add_up", share(0), *arrived
    )
    return total, sent


def finish_kernel(first, second, out):
    blocks = first.shape[1]
    for c in range(2):
        for b in range(blocks):
            out[c, :, b * LANES:(b + 1) * LANES] = first[c, b] + second[c, b].astype(jnp.float32)


def finish(first, second):
    _, blocks, slab, lanes = first.shape
    return pl.pallas_call(
        finish_kernel,
        in_specs=[pl.BlockSpec(memory_space=VMEM)] * 2,
        out_specs=pl.BlockSpec(memory_space=VMEM),
        out_shape=jax.ShapeDtypeStruct((2, slab, blocks * lanes), jnp.float32),
        compiler_params=pltpu.CompilerParams(vmem_limit_bytes=8 * 1024 * 1024),
        name="finish",
    )(first, second)


def on_device(tiles, eigenprobes, coefficients, tile_list, offsets, amplitudes, group_counts):
    modes, _, frame, _ = eigenprobes.shape
    side = tiles.shape[2]
    pos_dev = coefficients.shape[0]
    blocks = lax.axis_size("blk")
    shares = lax.axis_size("probe")
    member = lax.axis_index("probe")
    slab = side // shares
    bits = [1 << i for i in range(shares.bit_length() - 1)]

    offs = [0]
    for bit in reversed(bits):
        offs = offs + [o ^ bit for o in offs]
    quarter = lax.dynamic_slice_in_dim(tiles[0], member * slab, slab, 1)
    near = shift(quarter, "blk", -1)
    held = [[near], [shift(near, "blk", -1)]]
    eig, amps = stage(*after_all((eigenprobes, amplitudes), near))
    held[1][0] = after(held[1][0], eig)
    table, tile, coef_t, lists, corners = stage(
        *after_all((tables(frame), tiles[0], coefficients.T, tile_list.T, offsets.T), held[1][0])
    )
    for bit in reversed(bits):
        for part in held:
            arrived = [swap(piece, "probe", bit) for piece in part]
            if bit > 1:
                arrived[0] = after(arrived[0], eig if part is held[0] else table)
            part += arrived

    indices = (lists, corners, group_counts)
    scale = (pos_dev * blocks * shares) ** (-0.5)
    out = positions(
        tuple(offs), scale, indices, [tile] + held[0] + held[1], eig, amps, table, coef_t
    )
    eigen_send, eigen_keep, grads, coef_rows = out[:2], out[2:4], out[4], out[5]

    eigen, leaving, crossed = halve(eigen_keep, eigen_send)
    out = scatter(shares, side, indices, after(grads, leaving))
    send, keep = ([out[at + 2 * i:at + 2 * i + 2] for i in range(REACH)] for at in (0, 2 * REACH))
    last = REACH - 1
    relative = share_of(2 * modes, blocks) > 0
    total, sent = scatter_sum("blk", eigen.reshape(blocks, -1, frame), relative)
    mine, leaving, _ = halve(keep[last], send[last], before_cross=sent)
    moving = after(mine.astype(jnp.bfloat16), total)
    gate = moving
    for section in range(last - 1, -1, -1):
        mine, leaving, gate = halve(keep[section], send[section], before_cross=(gate,))
        if section == last - 1:
            total = after(total, leaving)
        arrived = shift(moving, "blk", 1)
        if section > 0:
            moving = (arrived.astype(jnp.float32) + mine).astype(jnp.bfloat16)
    gathered = lax.all_to_all(total, "blk", 0, 0)
    eigen_share = small_call(widen_kernel, gathered.shape, jnp.float32, "widen", gathered)
    eigen_share = eigen_share.reshape(modes, 2, frame // shares, frame)
    summed = finish(mine, arrived)
    return (summed[None], eigen_share, coef_rows.T)


def solution(mesh):
    in_specs = (
        P(("recon", "blk"), None, None, None),
        P("recon", None, None, None),
        P(("recon", "blk", "probe"), None),
        P(("recon", "blk", "probe"), None),
        P(("recon", "blk", "probe"), None),
        P(("recon", "blk", "probe"), None, None),
        P(("recon", "blk")),
    )
    out_specs = (
        P(("recon", "blk"), None, "probe", None),
        P("recon", None, "probe", None),
        P(("recon", "blk", "probe"), None),
    )
    return jax.shard_map(
        on_device, mesh=mesh, in_specs=in_specs, out_specs=out_specs, check_vma=False
    )
```

```python
import functools
import math

import jax
import jax.numpy as jnp
import ml_dtypes
import numpy as np
from jax import lax
from jax.experimental import pallas as pl
from jax.experimental.pallas import tpu as pltpu
from jax.sharding import PartitionSpec as P

REACH = 3
LANES = 128
STRIP = 16
VMEM = pltpu.MemorySpace.VMEM
SMEM = pltpu.MemorySpace.SMEM
VMEM_LIMIT = 36 * 1024 * 1024


def tables(frame):
    indices = np.arange(frame)
    angle = (indices[:, None] * indices[None, :] % frame) * (2.0 * math.pi / frame)
    cos_part = np.cos(angle) / math.sqrt(frame)
    sin_part = -np.sin(angle) / math.sqrt(frame)
    forward = np.block([[cos_part, sin_part], [-sin_part, cos_part]])
    forward = forward.astype(np.float32).astype(ml_dtypes.bfloat16)
    return jnp.asarray(np.stack([forward, forward.T]))


def shift(array, axis, by):
    peers = lax.axis_size(axis)
    return lax.ppermute(array, axis, [(i, (i + by) % peers) for i in range(peers)])


def swap(array, axis, bit):
    peers = lax.axis_size(axis)
    return lax.ppermute(array, axis, [(i, i ^ bit) for i in range(peers)])


def slabs_of(member, h):
    pair, core = member >> 1, member & 1
    mine = 2 * (pair ^ h) + core
    return mine, mine ^ 1


def far_first(shares):
    return [*range(1, shares // 2, 2), *range(0, shares // 2, 2)]


def share_of(groups, peers):
    return groups // peers if groups % peers == 0 else 0


def coordinates(tile_list, offsets, group_counts, pos_dev):
    blocks = lax.axis_size("blk")
    my_block, member = lax.axis_index("blk"), lax.axis_index("probe")
    alive = jnp.clip(group_counts[0] - member * pos_dev, 0, pos_dev)

    def place(j, m):
        section = lax.rem(tile_list[m, j] - my_block + blocks, blocks)
        return section, offsets[2 * m, j], offsets[2 * m + 1, j]

    return my_block, member, alive, place


def one_hot(shape, axis):
    return (
        lax.broadcasted_iota(jnp.int32, shape, axis) // STRIP == lax.broadcasted_iota(jnp.int32, shape, 1 - axis)
    ).astype(jnp.float32)


def diagonals(array):
    row = lax.broadcasted_iota(jnp.int32, array.shape, 0)
    col = lax.broadcasted_iota(jnp.int32, array.shape, 1)
    return jnp.where(row % STRIP == col % STRIP, array, 0.0)


def exact(left, right):
    return jnp.dot(left, right, precision=lax.Precision.HIGHEST, preferred_element_type=jnp.float32)


def two_terms(array):
    high = array.astype(jnp.bfloat16)
    return high, (array - high.astype(jnp.float32)).astype(jnp.bfloat16)


def stage_kernel(*refs):
    count = len(refs) // 2
    sem = refs[-1]
    copies = [
        pltpu.make_async_copy(source, target, sem.at[i])
        for i, (source, target) in enumerate(zip(refs[:count], refs[count:2 * count]))
    ]
    for copy in copies:
        copy.start()
    for copy in copies:
        copy.wait()


def stage(*arrays):
    anywhere = pl.BlockSpec(memory_space=pl.ANY)
    return pl.pallas_call(
        stage_kernel,
        in_specs=[anywhere] * len(arrays),
        out_specs=[anywhere] * len(arrays),
        scratch_shapes=[pltpu.SemaphoreType.DMA((len(arrays),))],
        out_shape=[jax.ShapeDtypeStruct(x.shape, x.dtype) for x in arrays],
        compiler_params=pltpu.CompilerParams(vmem_limit_bytes=1024 * 1024),
        name="stage",
    )(*arrays)


def position_kernel(offs, scale, tile_list, offsets, group_counts, *refs):
    shares = len(offs)
    pieces = refs[: 1 + (REACH - 1) * shares]
    eig_in, amps_in, tables_in, coef_in = refs[len(pieces):len(pieces) + 4]
    eigen_send, eigen_keep = refs[len(pieces) + 4:len(pieces) + 6], refs[len(pieces) + 6:len(pieces) + 8]
    grads_out, coef = refs[len(pieces) + 8:len(pieces) + 10]
    (staged, table, probe, amps, eig, obj, ex, mid, far, patch, d_high, d_low, eigen, out_eigen, cross,
     weights, weights_t, piece_sem, table_sem, amps_sem, eig_sem, grad_sem, out_sem) = refs[len(pieces) + 10:]
    pos_dev, _, frame, _ = probe.shape
    modes = eig.shape[0]
    side = staged.shape[2]
    blocks = side // LANES
    slab = side // shares
    my_block, member, alive, place = coordinates(tile_list, offsets, group_counts, pos_dev)
    strips = range(frame // STRIP)

    copies = [pltpu.make_async_copy(pieces[0], staged.at[0], piece_sem.at[0])]
    for section in range(1, REACH):
        for i in range(shares):
            start = pl.multiple_of((member ^ offs[i]) * slab, slab)
            at = 1 + (section - 1) * shares + i
            copies.append(
                pltpu.make_async_copy(
                    pieces[at], staged.at[section, :, pl.ds(start, slab), :], piece_sem.at[at]
                )
            )
    table_copy = pltpu.make_async_copy(tables_in, table, table_sem)
    amps_copy = pltpu.make_async_copy(amps_in, amps, amps_sem)
    eig_copy = pltpu.make_async_copy(eig_in, eig, eig_sem)
    for copy in [eig_copy] + copies + [table_copy, amps_copy]:
        copy.start()

    by_position = (pos_dev * STRIP, pos_dev)
    by_mode = (modes * STRIP, modes)
    tall_t = exact(exact(one_hot(by_mode, 0), coef_in[...]), one_hot(by_position[::-1], 1))
    high, low = two_terms(diagonals(tall_t))
    weights_t[...] = jnp.concatenate([high, low], 0)
    spread = lax.dot_general(
        one_hot(by_position, 0), coef_in[...], (((1,), (1,)), ((), ())),
        precision=lax.Precision.HIGHEST, preferred_element_type=jnp.float32,
    )
    high, low = two_terms(diagonals(0.5 * exact(spread, one_hot(by_mode[::-1], 1))))
    weights[...] = jnp.concatenate([high, low], 1)
    eig_copy.wait()

    def synth(i, carry):
        rows = pl.ds(pl.multiple_of(i * STRIP, STRIP), STRIP)
        for c in range(2):
            e = eig[:, c, rows, :].reshape(modes * STRIP, frame)
            made = jnp.dot(
                weights[...], jnp.concatenate([e, e], 0), preferred_element_type=jnp.float32
            )
            probe[:, c, rows, :] = made.reshape(pos_dev, STRIP, frame)
        return carry

    lax.fori_loop(0, frame // STRIP, synth, 0, unroll=4)
    for copy in copies:
        copy.wait()

    def widen(i, carry):
        rows = pl.ds(pl.multiple_of(i * LANES, LANES), LANES)
        for section in range(REACH):
            for c in range(2):
                for b in range(blocks):
                    obj[section, c, b, rows, :] = staged[
                        section, c, rows, b * LANES:(b + 1) * LANES
                    ].astype(jnp.float32)
        return carry

    lax.fori_loop(0, side // LANES, widen, 0)
    table_copy.wait()
    amps_copy.wait()

    lane = lax.broadcasted_iota(jnp.int32, (STRIP, LANES), 1)

    def enter(j, slot):
        where = []
        for m in range(2):
            section, row, col = place(j, m)
            s = col % LANES
            where.append((section, row, col // LANES, (LANES - s) % LANES, lane < LANES - s))
        for i in strips:
            rows = slice(i * STRIP, (i + 1) * STRIP)
            parts = []
            for c in range(2):
                total = None
                for section, row, cb, back_by, keep_lane in where:
                    rolled = [
                        pltpu.roll(obj[section, c, cb + b, pl.ds(row + i * STRIP, STRIP), :], back_by, 1)
                        for b in range(3)
                    ]
                    block = [jnp.where(keep_lane, rolled[b], rolled[b + 1]) for b in range(2)]
                    total = block if total is None else [x + y for x, y in zip(total, block)]
                parts.append(total)
            for b in range(2):
                cols = slice(b * LANES, (b + 1) * LANES)
                o_re, o_im = parts[0][b], parts[1][b]
                p_re, p_im = probe[j, 0, rows, cols], probe[j, 1, rows, cols]
                patch[slot, 0, rows, cols] = o_re
                patch[slot, 1, rows, cols] = o_im
                ex[slot, rows, b * LANES:(b + 1) * LANES] = (p_re * o_re - p_im * o_im).astype(jnp.bfloat16)
                ex[slot, rows, frame + b * LANES:frame + (b + 1) * LANES] = (
                    p_re * o_im + p_im * o_re
                ).astype(jnp.bfloat16)

    def transform(slot, way):
        half = jnp.dot(ex[slot], table[way], preferred_element_type=jnp.float32)
        mid[slot, :frame] = half[:, :frame].astype(jnp.bfloat16)
        mid[slot, frame:] = half[:, frame:].astype(jnp.bfloat16)
        far[slot] = jnp.dot(table[1 - way], mid[slot], preferred_element_type=jnp.float32)

    def residual(j, slot, living):
        for i in strips:
            rows = slice(i * STRIP, (i + 1) * STRIP)
            lower = slice(frame + i * STRIP, frame + (i + 1) * STRIP)
            f_re, f_im = far[slot, rows], far[slot, lower]
            factor = 1.0 - amps[j, rows].astype(jnp.float32) * lax.rsqrt(f_re * f_re + f_im * f_im + 1.0)
            if living is not None:
                factor = factor * living
            ex[slot, rows, :frame] = (f_re * factor).astype(jnp.bfloat16)
            ex[slot, rows, frame:] = (f_im * factor).astype(jnp.bfloat16)

    def leave(j, slot):
        for i in strips:
            rows = slice(i * STRIP, (i + 1) * STRIP)
            lower = slice(frame + i * STRIP, frame + (i + 1) * STRIP)
            b_re, b_im = far[slot, rows], far[slot, lower]
            o_re, o_im = patch[slot, 0, rows], patch[slot, 1, rows]
            p_re, p_im = probe[j, 0, rows], probe[j, 1, rows]
            for c, d in enumerate((o_re * b_re + o_im * b_im, o_re * b_im - o_im * b_re)):
                high = d.astype(jnp.bfloat16)
                d_high[j, c, rows] = high
                d_low[j, c, rows] = (d - high.astype(jnp.float32)).astype(jnp.bfloat16)
            probe[j, 0, rows] = p_re * b_re + p_im * b_im
            probe[j, 1, rows] = p_re * b_im - p_im * b_re

    def grad_copy(j):
        return pltpu.make_async_copy(probe.at[j], grads_out.at[j], grad_sem.at[j])

    def visit(pair, carry):
        first, second = 2 * pair, 2 * pair + 1
        enter(first, 0)
        transform(0, 0)
        enter(second, 1)
        transform(1, 0)
        residual(first, 0, None)
        transform(0, 1)
        residual(second, 1, jnp.where(second < alive, 1.0, 0.0))
        transform(1, 1)
        leave(first, 0)
        leave(second, 1)
        grad_copy(first).start()
        grad_copy(second).start()
        return carry

    pairs = (alive + 1) // 2
    lax.fori_loop(0, pairs, visit, 0)

    def skip(j, carry):
        d_high[j] = jnp.zeros((2, frame, frame), jnp.bfloat16)
        d_low[j] = jnp.zeros((2, frame, frame), jnp.bfloat16)
        return carry

    lax.fori_loop(2 * pairs, pos_dev, skip, 0)

    cross[...] = jnp.zeros_like(cross)
    rows_q = frame // shares
    groups = 2 * modes
    share = share_of(groups, lax.axis_size("blk"))

    def eigen_strip(i, carry):
        rows = pl.ds(pl.multiple_of(i * STRIP, STRIP), STRIP)
        q = i // (rows_q // STRIP)
        inner = pl.ds(pl.multiple_of(i % (rows_q // STRIP) * STRIP, STRIP), STRIP)
        for c in range(2):
            high = d_high[:, c, rows, :].reshape(pos_dev * STRIP, frame)
            low = d_low[:, c, rows, :].reshape(pos_dev * STRIP, frame)
            e = eig[:, c, rows, :].reshape(modes * STRIP, frame)
            both = jnp.dot(weights_t[...], high, preferred_element_type=jnp.float32)
            rest = jnp.dot(weights_t[:modes * STRIP], low, preferred_element_type=jnp.float32)
            grad = (both[:modes * STRIP] + both[modes * STRIP:] + rest) * (0.5 * scale)
            for k in range(modes):
                group = 2 * k + c
                if share:
                    group = (group // share ^ my_block) * share + group % share
                eigen[q, group, inner, :] = grad[k * STRIP:(k + 1) * STRIP]
            cross[...] += lax.dot_general(
                high, e, (((1,), (1,)), ((), ())), preferred_element_type=jnp.float32
            )
        return carry

    lax.fori_loop(0, frame // STRIP, eigen_strip, 0, unroll=4)
    pending = []

    def start(source, target):
        copy = pltpu.make_async_copy(source, target, out_sem.at[len(pending)])
        copy.start()
        pending.append(copy)

    for h in far_first(shares):
        mine, other = slabs_of(member, h)
        out_eigen[h] = eigen[other].astype(jnp.bfloat16)
        start(out_eigen.at[h], eigen_send[h % 2].at[h // 2])
        start(eigen.at[mine], eigen_keep[h % 2].at[h // 2])

    total = exact(one_hot(by_position[::-1], 1), diagonals(cross[...]))
    coef[...] = lax.dot_general(
        one_hot(by_mode[::-1], 1), total, (((1,), (1,)), ((), ())),
        precision=lax.Precision.HIGHEST, preferred_element_type=jnp.float32,
    ) * (0.5 / frame)

    def drain(j, carry):
        grad_copy(j).wait()
        return carry

    lax.fori_loop(0, 2 * pairs, drain, 0)
    for copy in pending:
        copy.wait()


def positions(offs, scale, indices, pieces, eigenprobes, amps, table, coef_t):
    modes, _, frame, _ = eigenprobes.shape
    pos_dev = amps.shape[0]
    side = pieces[0].shape[2]
    shares = len(offs)
    blocks = side // LANES
    smem = pl.BlockSpec(memory_space=SMEM)
    whole = pl.BlockSpec(memory_space=VMEM)
    anywhere = pl.BlockSpec(memory_space=pl.ANY)
    eigen_half = (shares // 2, 2 * modes, frame // shares, frame)
    eigen_part = (shares // 4,) + eigen_half[1:]
    grads = (pos_dev, 2, frame, frame)
    return pl.pallas_call(
        functools.partial(position_kernel, offs, scale),
        in_specs=[smem] * 3 + [anywhere] * (len(pieces) + 3) + [whole],
        out_specs=[anywhere] * 5 + [whole],
        scratch_shapes=[
            pltpu.VMEM((REACH, 2, side, side), jnp.bfloat16),
            pltpu.VMEM(table.shape, jnp.bfloat16),
            pltpu.VMEM(grads, jnp.float32),
            pltpu.VMEM(amps.shape, jnp.bfloat16),
            pltpu.VMEM(eigenprobes.shape, jnp.bfloat16),
            pltpu.VMEM((REACH, 2, blocks + 1, side, LANES), jnp.float32),
            pltpu.VMEM((2, frame, 2 * frame), jnp.bfloat16),
            pltpu.VMEM((2, 2 * frame, frame), jnp.bfloat16),
            pltpu.VMEM((2, 2 * frame, frame), jnp.float32),
            pltpu.VMEM((2, 2, frame, frame), jnp.float32),
            pltpu.VMEM(grads, jnp.bfloat16),
            pltpu.VMEM(grads, jnp.bfloat16),
            pltpu.VMEM((shares, 2 * modes, frame // shares, frame), jnp.float32),
            pltpu.VMEM(eigen_half, jnp.bfloat16),
            pltpu.VMEM((pos_dev * STRIP, modes * STRIP), jnp.float32),
            pltpu.VMEM((pos_dev * STRIP, 2 * modes * STRIP), jnp.bfloat16),
            pltpu.VMEM((2 * modes * STRIP, pos_dev * STRIP), jnp.bfloat16),
            pltpu.SemaphoreType.DMA((len(pieces),)),
            pltpu.SemaphoreType.DMA,
            pltpu.SemaphoreType.DMA,
            pltpu.SemaphoreType.DMA,
            pltpu.SemaphoreType.DMA((pos_dev,)),
            pltpu.SemaphoreType.DMA((shares,)),
        ],
        out_shape=[
            jax.ShapeDtypeStruct(eigen_part, jnp.bfloat16),
            jax.ShapeDtypeStruct(eigen_part, jnp.bfloat16),
            jax.ShapeDtypeStruct(eigen_part, jnp.float32),
            jax.ShapeDtypeStruct(eigen_part, jnp.float32),
            jax.ShapeDtypeStruct(grads, jnp.float32),
            jax.ShapeDtypeStruct((modes, pos_dev), jnp.float32),
        ],
        compiler_params=pltpu.CompilerParams(vmem_limit_bytes=VMEM_LIMIT),
        name="positions",
    )(*indices, *pieces, eigenprobes, amps, table, coef_t)


def scatter_kernel(shares, tile_list, offsets, group_counts, grads_in, *refs):
    send, keep = refs[:2 * REACH], refs[2 * REACH:4 * REACH]
    grads, acc, out_send, grad_sem, out_sem = refs[4 * REACH:]
    pos_dev, _, frame, _ = grads.shape
    blocks, side = acc.shape[2] - 1, acc.shape[3]
    slab = side // shares
    _, member, alive, place = coordinates(tile_list, offsets, group_counts, pos_dev)

    def grad_copy(j):
        return pltpu.make_async_copy(grads_in.at[j], grads.at[j], grad_sem.at[j])

    def begin(j, carry):
        grad_copy(j).start()
        return carry

    lax.fori_loop(0, alive, begin, 0)

    def clear(i, carry):
        rows = pl.ds(pl.multiple_of(i * LANES, LANES), LANES)
        for section in range(REACH):
            for c in range(2):
                for b in range(blocks + 1):
                    acc[section, c, b, rows, :] = jnp.zeros((LANES, LANES), jnp.float32)
        return carry

    lax.fori_loop(0, side // LANES, clear, 0)
    lane = lax.broadcasted_iota(jnp.int32, (STRIP, LANES), 1)

    def add(j, carry):
        grad_copy(j).wait()
        for m in range(2):
            section, row, col = place(j, m)
            cb, s = col // LANES, col % LANES
            inside = lane >= s
            for i in range(frame // STRIP):
                for c in range(2):
                    low, high = (
                        pltpu.roll(grads[j, c, i * STRIP:(i + 1) * STRIP, b * LANES:(b + 1) * LANES], s, 1)
                        for b in range(2)
                    )
                    for b, value in enumerate(
                        (
                            jnp.where(inside, low, 0.0),
                            jnp.where(inside, high, low),
                            jnp.where(inside, 0.0, high),
                        )
                    ):
                        at = (section, c, cb + b, pl.ds(row + i * STRIP, STRIP), slice(None))
                        acc[at] = acc[at] + value
        return carry

    lax.fori_loop(0, alive, add, 0)
    pending = []

    def start(source, target):
        copy = pltpu.make_async_copy(source, target, out_sem.at[len(pending)])
        copy.start()
        pending.append(copy)

    for section in range(REACH - 1, -1, -1):
        for h in far_first(shares):
            mine, other = (pl.multiple_of(at * slab, slab) for at in slabs_of(member, h))
            start(
                acc.at[section, :, pl.ds(0, blocks), pl.ds(mine, slab), :],
                keep[2 * section + h % 2].at[h // 2],
            )
            for c in range(2):
                for b in range(blocks):
                    out_send[section, h, c, b] = acc[section, c, b, pl.ds(other, slab), :].astype(jnp.bfloat16)
            start(out_send.at[section, h], send[2 * section + h % 2].at[h // 2])
    for copy in pending:
        copy.wait()


def scatter(shares, side, indices, grads):
    blocks = side // LANES
    anywhere = pl.BlockSpec(memory_space=pl.ANY)
    half = (shares // 2, 2, blocks, side // shares, LANES)
    part = (shares // 4,) + half[1:]
    return pl.pallas_call(
        functools.partial(scatter_kernel, shares),
        in_specs=[pl.BlockSpec(memory_space=SMEM)] * 3 + [anywhere],
        out_specs=[anywhere] * (4 * REACH),
        scratch_shapes=[
            pltpu.VMEM(grads.shape, jnp.float32),
            pltpu.VMEM((REACH, 2, blocks + 1, side, LANES), jnp.float32),
            pltpu.VMEM((REACH,) + half, jnp.bfloat16),
            pltpu.SemaphoreType.DMA((grads.shape[0],)),
            pltpu.SemaphoreType.DMA((REACH * shares,)),
        ],
        out_shape=[jax.ShapeDtypeStruct(part, jnp.bfloat16)] * (2 * REACH)
        + [jax.ShapeDtypeStruct(part, jnp.float32)] * (2 * REACH),
        compiler_params=pltpu.CompilerParams(vmem_limit_bytes=20 * 1024 * 1024),
        cost_estimate=pl.CostEstimate(flops=1 << 24, bytes_accessed=16 << 20, transcendentals=0),
        name="scatter",
    )(*indices, grads)


def after(array, *others):
    return lax.optimization_barrier((array,) + others)[0]


def after_all(arrays, *others):
    return lax.optimization_barrier(tuple(arrays) + others)[:len(arrays)]


def halve(keep, send, before_core=(), before_cross=()):
    far = [keep[1], after(swap(after(send[1], *before_core), "probe", 1), *before_cross)]
    terms = [keep[0], swap(send[0], "probe", 1)]
    leaving = None
    bit = 2
    while True:
        sending = sum(term.astype(jnp.float32) for term in far).astype(jnp.bfloat16)
        leaving = sending if leaving is None else leaving
        terms.append(swap(sending, "probe", bit))
        if terms[0].shape[0] == 1:
            return sum(term[0].astype(jnp.float32) for term in terms), leaving, terms[-1]
        pick = lambda term, which: term.reshape((term.shape[0] // 2, 2) + term.shape[1:])[:, which]
        far, terms = [pick(term, 1) for term in terms], [pick(term, 0) for term in terms]
        bit *= 2


def add_up_kernel(own, *refs):
    arrived, out = refs[:-1], refs[-1]
    total = own[...]
    for term in arrived:
        total += term[...].astype(jnp.float32)
    out[...] = total.astype(jnp.bfloat16)


def place_kernel(axis, offs, *refs):
    pieces, out = refs[:-1], refs[-1]
    me = lax.axis_index(axis)
    each = pieces[0].shape[0]
    for i, off in enumerate(offs):
        out[me ^ off] = pieces[i // each][i % each].astype(jnp.float32)


def small_call(kernel, shape, kind, name, *arrays):
    return pl.pallas_call(
        kernel,
        in_specs=[pl.BlockSpec(memory_space=VMEM)] * len(arrays),
        out_specs=pl.BlockSpec(memory_space=VMEM),
        out_shape=jax.ShapeDtypeStruct(shape, kind),
        compiler_params=pltpu.CompilerParams(vmem_limit_bytes=8 * 1024 * 1024),
        name=name,
    )(*arrays)


def gather_shares(axis, held):
    offs, first = [0], None
    bit = lax.axis_size(axis) // 2
    while True:
        arrived = swap(held, axis, bit)
        first = arrived if first is None else first
        offs = offs + [o ^ bit for o in offs]
        if bit == 1:
            return [held, arrived], offs, first
        held = jnp.concatenate([held, arrived], 0)
        bit //= 2


def scatter_sum(axis, value, relative):
    peers, me = lax.axis_size(axis), lax.axis_index(axis)
    share = (lambda i: value[i]) if relative else (lambda i: lax.dynamic_index_in_dim(value, me ^ i, 0, False))
    sent = [share(i).astype(jnp.bfloat16) for i in range(1, peers)]
    arrived = [swap(sending, axis, i) for i, sending in enumerate(sent, 1)]
    total = small_call(
        add_up_kernel, value.shape[1:], jnp.bfloat16, "add_up", share(0), *arrived
    )
    return total, sent


def finish_kernel(first, second, out):
    blocks = first.shape[1]
    for c in range(2):
        for b in range(blocks):
            out[c, :, b * LANES:(b + 1) * LANES] = first[c, b] + second[c, b].astype(jnp.float32)


def finish(first, second):
    _, blocks, slab, lanes = first.shape
    return pl.pallas_call(
        finish_kernel,
        in_specs=[pl.BlockSpec(memory_space=VMEM)] * 2,
        out_specs=pl.BlockSpec(memory_space=VMEM),
        out_shape=jax.ShapeDtypeStruct((2, slab, blocks * lanes), jnp.float32),
        compiler_params=pltpu.CompilerParams(vmem_limit_bytes=8 * 1024 * 1024),
        name="finish",
    )(first, second)


def on_device(tiles, eigenprobes, coefficients, tile_list, offsets, amplitudes, group_counts):
    modes, _, frame, _ = eigenprobes.shape
    side = tiles.shape[2]
    pos_dev = coefficients.shape[0]
    blocks = lax.axis_size("blk")
    shares = lax.axis_size("probe")
    member = lax.axis_index("probe")
    slab = side // shares
    bits = [1 << i for i in range(shares.bit_length() - 1)]

    offs = [0]
    for bit in reversed(bits):
        offs = offs + [o ^ bit for o in offs]
    quarter = lax.dynamic_slice_in_dim(tiles[0], member * slab, slab, 1)
    near = shift(quarter, "blk", -1)
    held = [[near], [shift(near, "blk", -1)]]
    eig, amps = stage(*after_all((eigenprobes, amplitudes), near))
    held[1][0] = after(held[1][0], eig)
    table, tile, coef_t, lists, corners = stage(
        *after_all((tables(frame), tiles[0], coefficients.T, tile_list.T, offsets.T), held[1][0])
    )
    for bit in reversed(bits):
        for part in held:
            arrived = [swap(piece, "probe", bit) for piece in part]
            if bit > 1:
                arrived[0] = after(arrived[0], eig if part is held[0] else table)
            part += arrived

    indices = (lists, corners, group_counts)
    scale = (pos_dev * blocks * shares) ** (-0.5)
    out = positions(
        tuple(offs), scale, indices, [tile] + held[0] + held[1], eig, amps, table, coef_t
    )
    eigen_send, eigen_keep, grads, coef_rows = out[:2], out[2:4], out[4], out[5]

    eigen, leaving, crossed = halve(eigen_keep, eigen_send)
    out = scatter(shares, side, indices, after(grads, leaving))
    send, keep = ([out[at + 2 * i:at + 2 * i + 2] for i in range(REACH)] for at in (0, 2 * REACH))
    last = REACH - 1
    relative = share_of(2 * modes, blocks) > 0
    total, sent = scatter_sum("blk", eigen.reshape(blocks, -1, frame), relative)
    mine, leaving, _ = halve(keep[last], send[last], before_cross=sent)
    moving = after(mine.astype(jnp.bfloat16), total)
    gate = moving
    for section in range(last - 1, -1, -1):
        mine, leaving, gate = halve(keep[section], send[section], before_cross=(gate,))
        if section == last - 1:
            pieces, order, first = gather_shares("blk", after(total, leaving)[None])
        arrived = shift(moving, "blk", 1)
        if section > 0:
            moving = (arrived.astype(jnp.float32) + mine).astype(jnp.bfloat16)
            gate = after(moving, first)
    eigen_share = small_call(
        functools.partial(place_kernel, "blk", order), (blocks,) + total.shape, jnp.float32, "place", *pieces
    )
    eigen_share = eigen_share.reshape(modes, 2, frame // shares, frame)
    summed = finish(mine, arrived)
    return (summed[None], eigen_share, coef_rows.T)


def solution(mesh):
    in_specs = (
        P(("recon", "blk"), None, None, None),
        P("recon", None, None, None),
        P(("recon", "blk", "probe"), None),
        P(("recon", "blk", "probe"), None),
        P(("recon", "blk", "probe"), None),
        P(("recon", "blk", "probe"), None, None),
        P(("recon", "blk")),
    )
    out_specs = (
        P(("recon", "blk"), None, "probe", None),
        P("recon", None, "probe", None),
        P(("recon", "blk", "probe"), None),
    )
    return jax.shard_map(
        on_device, mesh=mesh, in_specs=in_specs, out_specs=out_specs, check_vma=False
    )
```

```python
import functools
import math

import jax
import jax.numpy as jnp
import ml_dtypes
import numpy as np
from jax import lax
from jax.experimental import pallas as pl
from jax.experimental.pallas import tpu as pltpu
from jax.sharding import PartitionSpec as P

REACH = 3
LANES = 128
STRIP = 16
VMEM = pltpu.MemorySpace.VMEM
SMEM = pltpu.MemorySpace.SMEM
VMEM_LIMIT = 36 * 1024 * 1024


def tables(frame):
    indices = np.arange(frame)
    angle = (indices[:, None] * indices[None, :] % frame) * (2.0 * math.pi / frame)
    cos_part = np.cos(angle) / math.sqrt(frame)
    sin_part = -np.sin(angle) / math.sqrt(frame)
    forward = np.block([[cos_part, sin_part], [-sin_part, cos_part]])
    forward = forward.astype(np.float32).astype(ml_dtypes.bfloat16)
    return jnp.asarray(np.stack([forward, forward.T]))


def shift(array, axis, by):
    peers = lax.axis_size(axis)
    return lax.ppermute(array, axis, [(i, (i + by) % peers) for i in range(peers)])


def swap(array, axis, bit):
    peers = lax.axis_size(axis)
    return lax.ppermute(array, axis, [(i, i ^ bit) for i in range(peers)])


def slabs_of(member, h):
    pair, core = member >> 1, member & 1
    mine = 2 * (pair ^ h) + core
    return mine, mine ^ 1


def far_first(shares):
    return [*range(1, shares // 2, 2), *range(0, shares // 2, 2)]


def share_of(groups, peers):
    return groups // peers if groups % peers == 0 else 0


def coordinates(tile_list, offsets, group_counts, pos_dev):
    blocks = lax.axis_size("blk")
    my_block, member = lax.axis_index("blk"), lax.axis_index("probe")
    alive = jnp.clip(group_counts[0] - member * pos_dev, 0, pos_dev)

    def place(j, m):
        section = lax.rem(tile_list[m, j] - my_block + blocks, blocks)
        return section, offsets[2 * m, j], offsets[2 * m + 1, j]

    return my_block, member, alive, place


def one_hot(shape, axis):
    return (
        lax.broadcasted_iota(jnp.int32, shape, axis) // STRIP == lax.broadcasted_iota(jnp.int32, shape, 1 - axis)
    ).astype(jnp.float32)


def diagonals(array):
    row = lax.broadcasted_iota(jnp.int32, array.shape, 0)
    col = lax.broadcasted_iota(jnp.int32, array.shape, 1)
    return jnp.where(row % STRIP == col % STRIP, array, 0.0)


def exact(left, right):
    return jnp.dot(left, right, precision=lax.Precision.HIGHEST, preferred_element_type=jnp.float32)


def two_terms(array):
    high = array.astype(jnp.bfloat16)
    return high, (array - high.astype(jnp.float32)).astype(jnp.bfloat16)


def stage_kernel(*refs):
    count = len(refs) // 2
    sem = refs[-1]
    copies = [
        pltpu.make_async_copy(source, target, sem.at[i])
        for i, (source, target) in enumerate(zip(refs[:count], refs[count:2 * count]))
    ]
    for copy in copies:
        copy.start()
    for copy in copies:
        copy.wait()


def stage(*arrays):
    anywhere = pl.BlockSpec(memory_space=pl.ANY)
    return pl.pallas_call(
        stage_kernel,
        in_specs=[anywhere] * len(arrays),
        out_specs=[anywhere] * len(arrays),
        scratch_shapes=[pltpu.SemaphoreType.DMA((len(arrays),))],
        out_shape=[jax.ShapeDtypeStruct(x.shape, x.dtype) for x in arrays],
        compiler_params=pltpu.CompilerParams(vmem_limit_bytes=1024 * 1024),
        name="stage",
    )(*arrays)


def position_kernel(offs, scale, tile_list, offsets, group_counts, *refs):
    shares = len(offs)
    pieces = refs[: 1 + (REACH - 1) * shares]
    eig_in, amps_in, tables_in, coef_in = refs[len(pieces):len(pieces) + 4]
    eigen_send, eigen_keep = refs[len(pieces) + 4:len(pieces) + 6], refs[len(pieces) + 6:len(pieces) + 8]
    grads_out, coef = refs[len(pieces) + 8:len(pieces) + 10]
    (staged, table, probe, amps, eig, obj, ex, mid, far, patch, dprobe, eigen, out_eigen, cross,
     weights, weights_t, piece_sem, table_sem, amps_sem, eig_sem, grad_sem, out_sem) = refs[len(pieces) + 10:]
    pos_dev, _, frame, _ = probe.shape
    modes = eig.shape[0]
    side = staged.shape[2]
    blocks = side // LANES
    slab = side // shares
    my_block, member, alive, place = coordinates(tile_list, offsets, group_counts, pos_dev)
    strips = range(frame // STRIP)

    copies = [pltpu.make_async_copy(pieces[0], staged.at[0], piece_sem.at[0])]
    for section in range(1, REACH):
        for i in range(shares):
            start = pl.multiple_of((member ^ offs[i]) * slab, slab)
            at = 1 + (section - 1) * shares + i
            copies.append(
                pltpu.make_async_copy(
                    pieces[at], staged.at[section, :, pl.ds(start, slab), :], piece_sem.at[at]
                )
            )
    table_copy = pltpu.make_async_copy(tables_in, table, table_sem)
    amps_copy = pltpu.make_async_copy(amps_in, amps, amps_sem)
    eig_copy = pltpu.make_async_copy(eig_in, eig, eig_sem)
    for copy in [eig_copy] + copies + [table_copy, amps_copy]:
        copy.start()

    by_position = (pos_dev * STRIP, pos_dev)
    by_mode = (modes * STRIP, modes)
    tall_t = exact(exact(one_hot(by_mode, 0), coef_in[...]), one_hot(by_position[::-1], 1))
    high, low = two_terms(diagonals(tall_t))
    weights_t[...] = jnp.concatenate([high, low], 0)
    spread = lax.dot_general(
        one_hot(by_position, 0), coef_in[...], (((1,), (1,)), ((), ())),
        precision=lax.Precision.HIGHEST, preferred_element_type=jnp.float32,
    )
    high, low = two_terms(diagonals(0.5 * exact(spread, one_hot(by_mode[::-1], 1))))
    weights[...] = jnp.concatenate([high, low], 1)
    eig_copy.wait()

    def synth(i, carry):
        rows = pl.ds(pl.multiple_of(i * STRIP, STRIP), STRIP)
        for c in range(2):
            e = eig[:, c, rows, :].reshape(modes * STRIP, frame)
            made = jnp.dot(
                weights[...], jnp.concatenate([e, e], 0), preferred_element_type=jnp.float32
            )
            probe[:, c, rows, :] = made.reshape(pos_dev, STRIP, frame)
        return carry

    lax.fori_loop(0, frame // STRIP, synth, 0, unroll=8)
    for copy in copies:
        copy.wait()

    def widen(i, carry):
        rows = pl.ds(pl.multiple_of(i * LANES, LANES), LANES)
        for section in range(REACH):
            for c in range(2):
                for b in range(blocks):
                    obj[section, c, b, rows, :] = staged[
                        section, c, rows, b * LANES:(b + 1) * LANES
                    ].astype(jnp.float32)
        return carry

    lax.fori_loop(0, side // LANES, widen, 0)
    table_copy.wait()
    amps_copy.wait()

    lane = lax.broadcasted_iota(jnp.int32, (STRIP, LANES), 1)

    def enter(j, slot):
        where = []
        for m in range(2):
            section, row, col = place(j, m)
            s = col % LANES
            where.append((section, row, col // LANES, (LANES - s) % LANES, lane < LANES - s))
        for i in strips:
            rows = slice(i * STRIP, (i + 1) * STRIP)
            parts = []
            for c in range(2):
                total = None
                for section, row, cb, back_by, keep_lane in where:
                    rolled = [
                        pltpu.roll(obj[section, c, cb + b, pl.ds(row + i * STRIP, STRIP), :], back_by, 1)
                        for b in range(3)
                    ]
                    block = [jnp.where(keep_lane, rolled[b], rolled[b + 1]) for b in range(2)]
                    total = block if total is None else [x + y for x, y in zip(total, block)]
                parts.append(total)
            for b in range(2):
                cols = slice(b * LANES, (b + 1) * LANES)
                o_re, o_im = parts[0][b], parts[1][b]
                p_re, p_im = probe[j, 0, rows, cols], probe[j, 1, rows, cols]
                patch[slot, 0, rows, cols] = o_re
                patch[slot, 1, rows, cols] = o_im
                ex[slot, rows, b * LANES:(b + 1) * LANES] = (p_re * o_re - p_im * o_im).astype(jnp.bfloat16)
                ex[slot, rows, frame + b * LANES:frame + (b + 1) * LANES] = (
                    p_re * o_im + p_im * o_re
                ).astype(jnp.bfloat16)

    def transform(slot, way):
        half = jnp.dot(ex[slot], table[way], preferred_element_type=jnp.float32)
        mid[slot, :frame] = half[:, :frame].astype(jnp.bfloat16)
        mid[slot, frame:] = half[:, frame:].astype(jnp.bfloat16)
        far[slot] = jnp.dot(table[1 - way], mid[slot], preferred_element_type=jnp.float32)

    def residual(j, slot, living):
        for i in strips:
            rows = slice(i * STRIP, (i + 1) * STRIP)
            lower = slice(frame + i * STRIP, frame + (i + 1) * STRIP)
            f_re, f_im = far[slot, rows], far[slot, lower]
            factor = 1.0 - amps[j, rows].astype(jnp.float32) * lax.rsqrt(f_re * f_re + f_im * f_im + 1.0)
            if living is not None:
                factor = factor * living
            ex[slot, rows, :frame] = (f_re * factor).astype(jnp.bfloat16)
            ex[slot, rows, frame:] = (f_im * factor).astype(jnp.bfloat16)

    def leave(j, slot):
        for i in strips:
            rows = slice(i * STRIP, (i + 1) * STRIP)
            lower = slice(frame + i * STRIP, frame + (i + 1) * STRIP)
            b_re, b_im = far[slot, rows], far[slot, lower]
            o_re, o_im = patch[slot, 0, rows], patch[slot, 1, rows]
            p_re, p_im = probe[j, 0, rows], probe[j, 1, rows]
            for c, d in enumerate((o_re * b_re + o_im * b_im, o_re * b_im - o_im * b_re)):
                dprobe[j, c, rows] = d.astype(jnp.bfloat16)
            probe[j, 0, rows] = p_re * b_re + p_im * b_im
            probe[j, 1, rows] = p_re * b_im - p_im * b_re

    def grad_copy(j):
        return pltpu.make_async_copy(probe.at[j], grads_out.at[j], grad_sem.at[j])

    def visit(pair, carry):
        first, second = 2 * pair, 2 * pair + 1
        enter(first, 0)
        transform(0, 0)
        enter(second, 1)
        transform(1, 0)
        residual(first, 0, None)
        transform(0, 1)
        residual(second, 1, jnp.where(second < alive, 1.0, 0.0))
        transform(1, 1)
        leave(first, 0)
        leave(second, 1)
        grad_copy(first).start()
        grad_copy(second).start()
        return carry

    pairs = (alive + 1) // 2
    lax.fori_loop(0, pairs, visit, 0)

    def skip(j, carry):
        dprobe[j] = jnp.zeros((2, frame, frame), jnp.bfloat16)
        return carry

    lax.fori_loop(2 * pairs, pos_dev, skip, 0)

    cross[...] = jnp.zeros_like(cross)
    rows_q = frame // shares
    groups = 2 * modes
    share = share_of(groups, lax.axis_size("blk"))

    def eigen_strip(i, carry):
        rows = pl.ds(pl.multiple_of(i * STRIP, STRIP), STRIP)
        q = i // (rows_q // STRIP)
        inner = pl.ds(pl.multiple_of(i % (rows_q // STRIP) * STRIP, STRIP), STRIP)
        for c in range(2):
            d = dprobe[:, c, rows, :].reshape(pos_dev * STRIP, frame)
            e = eig[:, c, rows, :].reshape(modes * STRIP, frame)
            both = jnp.dot(weights_t[...], d, preferred_element_type=jnp.float32)
            grad = (both[:modes * STRIP] + both[modes * STRIP:]) * (0.5 * scale)
            for k in range(modes):
                group = 2 * k + c
                if share:
                    group = (group // share ^ my_block) * share + group % share
                eigen[q, group, inner, :] = grad[k * STRIP:(k + 1) * STRIP]
            cross[...] += lax.dot_general(
                d, e, (((1,), (1,)), ((), ())), preferred_element_type=jnp.float32
            )
        return carry

    lax.fori_loop(0, frame // STRIP, eigen_strip, 0, unroll=8)
    pending = []

    def start(source, target):
        copy = pltpu.make_async_copy(source, target, out_sem.at[len(pending)])
        copy.start()
        pending.append(copy)

    for h in far_first(shares):
        mine, other = slabs_of(member, h)
        out_eigen[h] = eigen[other].astype(jnp.bfloat16)
        start(out_eigen.at[h], eigen_send[h % 2].at[h // 2])
        start(eigen.at[mine], eigen_keep[h % 2].at[h // 2])

    total = exact(one_hot(by_position[::-1], 1), diagonals(cross[...]))
    coef[...] = lax.dot_general(
        one_hot(by_mode[::-1], 1), total, (((1,), (1,)), ((), ())),
        precision=lax.Precision.HIGHEST, preferred_element_type=jnp.float32,
    ) * (0.5 / frame)

    def drain(j, carry):
        grad_copy(j).wait()
        return carry

    lax.fori_loop(0, 2 * pairs, drain, 0)
    for copy in pending:
        copy.wait()


def positions(offs, scale, indices, pieces, eigenprobes, amps, table, coef_t):
    modes, _, frame, _ = eigenprobes.shape
    pos_dev = amps.shape[0]
    side = pieces[0].shape[2]
    shares = len(offs)
    blocks = side // LANES
    smem = pl.BlockSpec(memory_space=SMEM)
    whole = pl.BlockSpec(memory_space=VMEM)
    anywhere = pl.BlockSpec(memory_space=pl.ANY)
    eigen_half = (shares // 2, 2 * modes, frame // shares, frame)
    eigen_part = (shares // 4,) + eigen_half[1:]
    grads = (pos_dev, 2, frame, frame)
    return pl.pallas_call(
        functools.partial(position_kernel, offs, scale),
        in_specs=[smem] * 3 + [anywhere] * (len(pieces) + 3) + [whole],
        out_specs=[anywhere] * 5 + [whole],
        scratch_shapes=[
            pltpu.VMEM((REACH, 2, side, side), jnp.bfloat16),
            pltpu.VMEM(table.shape, jnp.bfloat16),
            pltpu.VMEM(grads, jnp.float32),
            pltpu.VMEM(amps.shape, jnp.bfloat16),
            pltpu.VMEM(eigenprobes.shape, jnp.bfloat16),
            pltpu.VMEM((REACH, 2, blocks + 1, side, LANES), jnp.float32),
            pltpu.VMEM((2, frame, 2 * frame), jnp.bfloat16),
            pltpu.VMEM((2, 2 * frame, frame), jnp.bfloat16),
            pltpu.VMEM((2, 2 * frame, frame), jnp.float32),
            pltpu.VMEM((2, 2, frame, frame), jnp.float32),
            pltpu.VMEM(grads, jnp.bfloat16),
            pltpu.VMEM((shares, 2 * modes, frame // shares, frame), jnp.float32),
            pltpu.VMEM(eigen_half, jnp.bfloat16),
            pltpu.VMEM((pos_dev * STRIP, modes * STRIP), jnp.float32),
            pltpu.VMEM((pos_dev * STRIP, 2 * modes * STRIP), jnp.bfloat16),
            pltpu.VMEM((2 * modes * STRIP, pos_dev * STRIP), jnp.bfloat16),
            pltpu.SemaphoreType.DMA((len(pieces),)),
            pltpu.SemaphoreType.DMA,
            pltpu.SemaphoreType.DMA,
            pltpu.SemaphoreType.DMA,
            pltpu.SemaphoreType.DMA((pos_dev,)),
            pltpu.SemaphoreType.DMA((shares,)),
        ],
        out_shape=[
            jax.ShapeDtypeStruct(eigen_part, jnp.bfloat16),
            jax.ShapeDtypeStruct(eigen_part, jnp.bfloat16),
            jax.ShapeDtypeStruct(eigen_part, jnp.float32),
            jax.ShapeDtypeStruct(eigen_part, jnp.float32),
            jax.ShapeDtypeStruct(grads, jnp.float32),
            jax.ShapeDtypeStruct((modes, pos_dev), jnp.float32),
        ],
        compiler_params=pltpu.CompilerParams(vmem_limit_bytes=VMEM_LIMIT),
        name="positions",
    )(*indices, *pieces, eigenprobes, amps, table, coef_t)


def scatter_kernel(shares, tile_list, offsets, group_counts, grads_in, *refs):
    send, keep = refs[:2 * REACH], refs[2 * REACH:4 * REACH]
    grads, acc, out_send, grad_sem, out_sem = refs[4 * REACH:]
    pos_dev, _, frame, _ = grads.shape
    blocks, side = acc.shape[2] - 1, acc.shape[3]
    slab = side // shares
    _, member, alive, place = coordinates(tile_list, offsets, group_counts, pos_dev)

    def grad_copy(j):
        return pltpu.make_async_copy(grads_in.at[j], grads.at[j], grad_sem.at[j])

    def begin(j, carry):
        grad_copy(j).start()
        return carry

    lax.fori_loop(0, alive, begin, 0)

    def clear(i, carry):
        rows = pl.ds(pl.multiple_of(i * LANES, LANES), LANES)
        for section in range(REACH):
            for c in range(2):
                for b in range(blocks + 1):
                    acc[section, c, b, rows, :] = jnp.zeros((LANES, LANES), jnp.float32)
        return carry

    lax.fori_loop(0, side // LANES, clear, 0)
    lane = lax.broadcasted_iota(jnp.int32, (STRIP, LANES), 1)

    def add(j, carry):
        grad_copy(j).wait()
        for m in range(2):
            section, row, col = place(j, m)
            cb, s = col // LANES, col % LANES
            inside = lane >= s
            for i in range(frame // STRIP):
                for c in range(2):
                    low, high = (
                        pltpu.roll(grads[j, c, i * STRIP:(i + 1) * STRIP, b * LANES:(b + 1) * LANES], s, 1)
                        for b in range(2)
                    )
                    for b, value in enumerate(
                        (
                            jnp.where(inside, low, 0.0),
                            jnp.where(inside, high, low),
                            jnp.where(inside, 0.0, high),
                        )
                    ):
                        at = (section, c, cb + b, pl.ds(row + i * STRIP, STRIP), slice(None))
                        acc[at] = acc[at] + value
        return carry

    lax.fori_loop(0, alive, add, 0)
    pending = []

    def start(source, target):
        copy = pltpu.make_async_copy(source, target, out_sem.at[len(pending)])
        copy.start()
        pending.append(copy)

    for section in range(REACH - 1, -1, -1):
        for h in far_first(shares):
            mine, other = (pl.multiple_of(at * slab, slab) for at in slabs_of(member, h))
            start(
                acc.at[section, :, pl.ds(0, blocks), pl.ds(mine, slab), :],
                keep[2 * section + h % 2].at[h // 2],
            )
            for c in range(2):
                for b in range(blocks):
                    out_send[section, h, c, b] = acc[section, c, b, pl.ds(other, slab), :].astype(jnp.bfloat16)
            start(out_send.at[section, h], send[2 * section + h % 2].at[h // 2])
    for copy in pending:
        copy.wait()


def scatter(shares, side, indices, grads):
    blocks = side // LANES
    anywhere = pl.BlockSpec(memory_space=pl.ANY)
    half = (shares // 2, 2, blocks, side // shares, LANES)
    part = (shares // 4,) + half[1:]
    return pl.pallas_call(
        functools.partial(scatter_kernel, shares),
        in_specs=[pl.BlockSpec(memory_space=SMEM)] * 3 + [anywhere],
        out_specs=[anywhere] * (4 * REACH),
        scratch_shapes=[
            pltpu.VMEM(grads.shape, jnp.float32),
            pltpu.VMEM((REACH, 2, blocks + 1, side, LANES), jnp.float32),
            pltpu.VMEM((REACH,) + half, jnp.bfloat16),
            pltpu.SemaphoreType.DMA((grads.shape[0],)),
            pltpu.SemaphoreType.DMA((REACH * shares,)),
        ],
        out_shape=[jax.ShapeDtypeStruct(part, jnp.bfloat16)] * (2 * REACH)
        + [jax.ShapeDtypeStruct(part, jnp.float32)] * (2 * REACH),
        compiler_params=pltpu.CompilerParams(vmem_limit_bytes=20 * 1024 * 1024),
        cost_estimate=pl.CostEstimate(flops=1 << 24, bytes_accessed=16 << 20, transcendentals=0),
        name="scatter",
    )(*indices, grads)


def after(array, *others):
    return lax.optimization_barrier((array,) + others)[0]


def after_all(arrays, *others):
    return lax.optimization_barrier(tuple(arrays) + others)[:len(arrays)]


def halve(keep, send, before_core=(), before_cross=()):
    far = [keep[1], after(swap(after(send[1], *before_core), "probe", 1), *before_cross)]
    terms = [keep[0], swap(send[0], "probe", 1)]
    leaving = None
    bit = 2
    while True:
        sending = sum(term.astype(jnp.float32) for term in far).astype(jnp.bfloat16)
        leaving = sending if leaving is None else leaving
        terms.append(swap(sending, "probe", bit))
        if terms[0].shape[0] == 1:
            return sum(term[0].astype(jnp.float32) for term in terms), leaving, terms[-1]
        pick = lambda term, which: term.reshape((term.shape[0] // 2, 2) + term.shape[1:])[:, which]
        far, terms = [pick(term, 1) for term in terms], [pick(term, 0) for term in terms]
        bit *= 2


def add_up_kernel(own, *refs):
    arrived, out = refs[:-1], refs[-1]
    total = own[...]
    for term in arrived:
        total += term[...].astype(jnp.float32)
    total = total.astype(jnp.bfloat16)
    for i in range(out.shape[0]):
        out[i] = total


def widen_kernel(array, out):
    out[...] = array[...].astype(jnp.float32)


def small_call(kernel, shape, kind, name, *arrays):
    return pl.pallas_call(
        kernel,
        in_specs=[pl.BlockSpec(memory_space=VMEM)] * len(arrays),
        out_specs=pl.BlockSpec(memory_space=VMEM),
        out_shape=jax.ShapeDtypeStruct(shape, kind),
        compiler_params=pltpu.CompilerParams(vmem_limit_bytes=8 * 1024 * 1024),
        name=name,
    )(*arrays)


def scatter_sum(axis, value, relative):
    peers, me = lax.axis_size(axis), lax.axis_index(axis)
    share = (lambda i: value[i]) if relative else (lambda i: lax.dynamic_index_in_dim(value, me ^ i, 0, False))
    sent = [share(i).astype(jnp.bfloat16) for i in range(1, peers)]
    arrived = [swap(sending, axis, i) for i, sending in enumerate(sent, 1)]
    total = small_call(
        add_up_kernel, (peers,) + value.shape[1:], jnp.bfloat16, "add_up", share(0), *arrived
    )
    return total, sent


def finish_kernel(first, second, out):
    blocks = first.shape[1]
    for c in range(2):
        for b in range(blocks):
            out[c, :, b * LANES:(b + 1) * LANES] = first[c, b] + second[c, b].astype(jnp.float32)


def finish(first, second):
    _, blocks, slab, lanes = first.shape
    return pl.pallas_call(
        finish_kernel,
        in_specs=[pl.BlockSpec(memory_space=VMEM)] * 2,
        out_specs=pl.BlockSpec(memory_space=VMEM),
        out_shape=jax.ShapeDtypeStruct((2, slab, blocks * lanes), jnp.float32),
        compiler_params=pltpu.CompilerParams(vmem_limit_bytes=8 * 1024 * 1024),
        name="finish",
    )(first, second)


def on_device(tiles, eigenprobes, coefficients, tile_list, offsets, amplitudes, group_counts):
    modes, _, frame, _ = eigenprobes.shape
    side = tiles.shape[2]
    pos_dev = coefficients.shape[0]
    blocks = lax.axis_size("blk")
    shares = lax.axis_size("probe")
    member = lax.axis_index("probe")
    slab = side // shares
    bits = [1 << i for i in range(shares.bit_length() - 1)]

    offs = [0]
    for bit in reversed(bits):
        offs = offs + [o ^ bit for o in offs]
    quarter = lax.dynamic_slice_in_dim(tiles[0], member * slab, slab, 1)
    near = shift(quarter, "blk", -1)
    held = [[near], [shift(near, "blk", -1)]]
    eig, amps = stage(*after_all((eigenprobes, amplitudes), near))
    held[1][0] = after(held[1][0], eig)
    table, tile, coef_t, lists, corners = stage(
        *after_all((tables(frame), tiles[0], coefficients.T, tile_list.T, offsets.T), held[1][0])
    )
    for bit in reversed(bits):
        for part in held:
            arrived = [swap(piece, "probe", bit) for piece in part]
            if bit > 1:
                arrived[0] = after(arrived[0], eig if part is held[0] else table)
            part += arrived

    indices = (lists, corners, group_counts)
    scale = (pos_dev * blocks * shares) ** (-0.5)
    out = positions(
        tuple(offs), scale, indices, [tile] + held[0] + held[1], eig, amps, table, coef_t
    )
    eigen_send, eigen_keep, grads, coef_rows = out[:2], out[2:4], out[4], out[5]

    eigen, leaving, crossed = halve(eigen_keep, eigen_send)
    out = scatter(shares, side, indices, after(grads, leaving))
    send, keep = ([out[at + 2 * i:at + 2 * i + 2] for i in range(REACH)] for at in (0, 2 * REACH))
    last = REACH - 1
    relative = share_of(2 * modes, blocks) > 0
    total, sent = scatter_sum("blk", eigen.reshape(blocks, -1, frame), relative)
    mine, leaving, _ = halve(keep[last], send[last], before_cross=sent)
    moving = after(mine.astype(jnp.bfloat16), total)
    gate = moving
    for section in range(last - 1, -1, -1):
        mine, leaving, gate = halve(keep[section], send[section], before_cross=(gate,))
        if section == last - 1:
            total = after(total, leaving)
        arrived = shift(moving, "blk", 1)
        if section > 0:
            moving = (arrived.astype(jnp.float32) + mine).astype(jnp.bfloat16)
    gathered = lax.all_to_all(total, "blk", 0, 0)
    eigen_share = small_call(widen_kernel, gathered.shape, jnp.float32, "widen", gathered)
    eigen_share = eigen_share.reshape(modes, 2, frame // shares, frame)
    summed = finish(mine, arrived)
    return (summed[None], eigen_share, coef_rows.T)


def solution(mesh):
    in_specs = (
        P(("recon", "blk"), None, None, None),
        P("recon", None, None, None),
        P(("recon", "blk", "probe"), None),
        P(("recon", "blk", "probe"), None),
        P(("recon", "blk", "probe"), None),
        P(("recon", "blk", "probe"), None, None),
        P(("recon", "blk")),
    )
    out_specs = (
        P(("recon", "blk"), None, "probe", None),
        P("recon", None, "probe", None),
        P(("recon", "blk", "probe"), None),
    )
    return jax.shard_map(
        on_device, mesh=mesh, in_specs=in_specs, out_specs=out_specs, check_vma=False
    )
```

```python
import functools
import math

import jax
import jax.numpy as jnp
import ml_dtypes
import numpy as np
from jax import lax
from jax.experimental import pallas as pl
from jax.experimental.pallas import tpu as pltpu
from jax.sharding import PartitionSpec as P

REACH = 3
LANES = 128
STRIP = 16
VMEM = pltpu.MemorySpace.VMEM
SMEM = pltpu.MemorySpace.SMEM
VMEM_LIMIT = 36 * 1024 * 1024


def tables(frame):
    indices = np.arange(frame)
    angle = (indices[:, None] * indices[None, :] % frame) * (2.0 * math.pi / frame)
    cos_part = np.cos(angle) / math.sqrt(frame)
    sin_part = -np.sin(angle) / math.sqrt(frame)
    forward = np.block([[cos_part, sin_part], [-sin_part, cos_part]])
    forward = forward.astype(np.float32).astype(ml_dtypes.bfloat16)
    return jnp.asarray(np.stack([forward, forward.T]))


def shift(array, axis, by):
    peers = lax.axis_size(axis)
    return lax.ppermute(array, axis, [(i, (i + by) % peers) for i in range(peers)])


def swap(array, axis, bit):
    peers = lax.axis_size(axis)
    return lax.ppermute(array, axis, [(i, i ^ bit) for i in range(peers)])


def slabs_of(member, h):
    pair, core = member >> 1, member & 1
    mine = 2 * (pair ^ h) + core
    return mine, mine ^ 1


def far_first(shares):
    return [*range(1, shares // 2, 2), *range(0, shares // 2, 2)]


def share_of(groups, peers):
    return groups // peers if groups % peers == 0 else 0


def coordinates(tile_list, offsets, group_counts, pos_dev):
    blocks = lax.axis_size("blk")
    my_block, member = lax.axis_index("blk"), lax.axis_index("probe")
    alive = jnp.clip(group_counts[0] - member * pos_dev, 0, pos_dev)

    def place(j, m):
        section = lax.rem(tile_list[m, j] - my_block + blocks, blocks)
        return section, offsets[2 * m, j], offsets[2 * m + 1, j]

    return my_block, member, alive, place


def one_hot(shape, axis):
    return (
        lax.broadcasted_iota(jnp.int32, shape, axis) // STRIP == lax.broadcasted_iota(jnp.int32, shape, 1 - axis)
    ).astype(jnp.float32)


def diagonals(array):
    row = lax.broadcasted_iota(jnp.int32, array.shape, 0)
    col = lax.broadcasted_iota(jnp.int32, array.shape, 1)
    return jnp.where(row % STRIP == col % STRIP, array, 0.0)


def exact(left, right):
    return jnp.dot(left, right, precision=lax.Precision.HIGHEST, preferred_element_type=jnp.float32)


def two_terms(array):
    high = array.astype(jnp.bfloat16)
    return high, (array - high.astype(jnp.float32)).astype(jnp.bfloat16)


def stage_kernel(*refs):
    count = len(refs) // 2
    move(refs[:count], refs[count:2 * count], refs[-1])()


def move(sources, targets, sem):
    copies = [
        pltpu.make_async_copy(source, target, sem.at[i])
        for i, (source, target) in enumerate(zip(sources, targets))
    ]
    for copy in copies:
        copy.start()

    def finish():
        for copy in copies:
            copy.wait()

    return finish


def stage(*arrays):
    anywhere = pl.BlockSpec(memory_space=pl.ANY)
    return pl.pallas_call(
        stage_kernel,
        in_specs=[anywhere] * len(arrays),
        out_specs=[anywhere] * len(arrays),
        scratch_shapes=[pltpu.SemaphoreType.DMA((len(arrays),))],
        out_shape=[jax.ShapeDtypeStruct(x.shape, x.dtype) for x in arrays],
        compiler_params=pltpu.CompilerParams(vmem_limit_bytes=1024 * 1024),
        name="stage",
    )(*arrays)


def weights_kernel(coef_in, *refs):
    count = (len(refs) - 3) // 2
    weights, weights_t = refs[count:count + 2]
    finish = move(refs[:count], refs[count + 2:-1], refs[-1])
    modes, pos_dev = coef_in.shape
    by_position = (pos_dev * STRIP, pos_dev)
    by_mode = (modes * STRIP, modes)
    tall_t = exact(exact(one_hot(by_mode, 0), coef_in[...]), one_hot(by_position[::-1], 1))
    high, low = two_terms(diagonals(tall_t))
    weights_t[...] = jnp.concatenate([high, low], 0)
    spread = lax.dot_general(
        one_hot(by_position, 0), coef_in[...], (((1,), (1,)), ((), ())),
        precision=lax.Precision.HIGHEST, preferred_element_type=jnp.float32,
    )
    high, low = two_terms(diagonals(0.5 * exact(spread, one_hot(by_mode[::-1], 1))))
    weights[...] = jnp.concatenate([high, low], 1)
    finish()


def expand(coef_t, *arrays):
    modes, pos_dev = coef_t.shape
    whole = pl.BlockSpec(memory_space=VMEM)
    anywhere = pl.BlockSpec(memory_space=pl.ANY)
    return pl.pallas_call(
        weights_kernel,
        in_specs=[whole] + [anywhere] * len(arrays),
        out_specs=[whole] * 2 + [anywhere] * len(arrays),
        scratch_shapes=[pltpu.SemaphoreType.DMA((len(arrays),))],
        out_shape=[
            jax.ShapeDtypeStruct((pos_dev * STRIP, 2 * modes * STRIP), jnp.bfloat16),
            jax.ShapeDtypeStruct((2 * modes * STRIP, pos_dev * STRIP), jnp.bfloat16),
        ]
        + [jax.ShapeDtypeStruct(x.shape, x.dtype) for x in arrays],
        compiler_params=pltpu.CompilerParams(vmem_limit_bytes=4 * 1024 * 1024),
        name="expand",
    )(coef_t, *arrays)


def position_kernel(offs, scale, tile_list, offsets, group_counts, *refs):
    shares = len(offs)
    pieces = refs[: 1 + (REACH - 1) * shares]
    eig_in, amps_in, tables_in, weights, weights_t = refs[len(pieces):len(pieces) + 5]
    eigen_send, eigen_keep = refs[len(pieces) + 5:len(pieces) + 7], refs[len(pieces) + 7:len(pieces) + 9]
    grads_out, coef = refs[len(pieces) + 9:len(pieces) + 11]
    (staged, table, probe, amps, eig, obj, ex, mid, far, patch, dprobe, eigen, out_eigen, cross,
     piece_sem, table_sem, amps_sem, eig_sem, grad_sem, out_sem) = refs[len(pieces) + 11:]
    pos_dev, _, frame, _ = probe.shape
    modes = eig.shape[0]
    side = staged.shape[2]
    blocks = side // LANES
    slab = side // shares
    my_block, member, alive, place = coordinates(tile_list, offsets, group_counts, pos_dev)
    strips = range(frame // STRIP)

    copies = [pltpu.make_async_copy(pieces[0], staged.at[0], piece_sem.at[0])]
    for section in range(1, REACH):
        for i in range(shares):
            start = pl.multiple_of((member ^ offs[i]) * slab, slab)
            at = 1 + (section - 1) * shares + i
            copies.append(
                pltpu.make_async_copy(
                    pieces[at], staged.at[section, :, pl.ds(start, slab), :], piece_sem.at[at]
                )
            )
    table_copy = pltpu.make_async_copy(tables_in, table, table_sem)
    amps_copy = pltpu.make_async_copy(amps_in, amps, amps_sem)
    eig_copy = pltpu.make_async_copy(eig_in, eig, eig_sem)
    for copy in [eig_copy] + copies + [table_copy, amps_copy]:
        copy.start()

    eig_copy.wait()

    def synth(i, carry):
        rows = pl.ds(pl.multiple_of(i * STRIP, STRIP), STRIP)
        for c in range(2):
            e = eig[:, c, rows, :].reshape(modes * STRIP, frame)
            made = jnp.dot(
                weights[...], jnp.concatenate([e, e], 0), preferred_element_type=jnp.float32
            )
            probe[:, c, rows, :] = made.reshape(pos_dev, STRIP, frame)
        return carry

    lax.fori_loop(0, frame // STRIP, synth, 0, unroll=8)
    for copy in copies:
        copy.wait()

    def widen(i, carry):
        rows = pl.ds(pl.multiple_of(i * LANES, LANES), LANES)
        for section in range(REACH):
            for c in range(2):
                for b in range(blocks):
                    obj[section, c, b, rows, :] = staged[
                        section, c, rows, b * LANES:(b + 1) * LANES
                    ].astype(jnp.float32)
        return carry

    lax.fori_loop(0, side // LANES, widen, 0)
    table_copy.wait()
    amps_copy.wait()

    lane = lax.broadcasted_iota(jnp.int32, (STRIP, LANES), 1)

    def enter(j, slot):
        where = []
        for m in range(2):
            section, row, col = place(j, m)
            s = col % LANES
            where.append((section, row, col // LANES, (LANES - s) % LANES, lane < LANES - s))
        for i in strips:
            rows = slice(i * STRIP, (i + 1) * STRIP)
            parts = []
            for c in range(2):
                total = None
                for section, row, cb, back_by, keep_lane in where:
                    rolled = [
                        pltpu.roll(obj[section, c, cb + b, pl.ds(row + i * STRIP, STRIP), :], back_by, 1)
                        for b in range(3)
                    ]
                    block = [jnp.where(keep_lane, rolled[b], rolled[b + 1]) for b in range(2)]
                    total = block if total is None else [x + y for x, y in zip(total, block)]
                parts.append(total)
            for b in range(2):
                cols = slice(b * LANES, (b + 1) * LANES)
                o_re, o_im = parts[0][b], parts[1][b]
                p_re, p_im = probe[j, 0, rows, cols], probe[j, 1, rows, cols]
                patch[slot, 0, rows, cols] = o_re
                patch[slot, 1, rows, cols] = o_im
                ex[slot, rows, b * LANES:(b + 1) * LANES] = (p_re * o_re - p_im * o_im).astype(jnp.bfloat16)
                ex[slot, rows, frame + b * LANES:frame + (b + 1) * LANES] = (
                    p_re * o_im + p_im * o_re
                ).astype(jnp.bfloat16)

    def transform(slot, way):
        half = jnp.dot(ex[slot], table[way], preferred_element_type=jnp.float32)
        mid[slot, :frame] = half[:, :frame].astype(jnp.bfloat16)
        mid[slot, frame:] = half[:, frame:].astype(jnp.bfloat16)
        far[slot] = jnp.dot(table[1 - way], mid[slot], preferred_element_type=jnp.float32)

    def residual(j, slot, living):
        for i in strips:
            rows = slice(i * STRIP, (i + 1) * STRIP)
            lower = slice(frame + i * STRIP, frame + (i + 1) * STRIP)
            f_re, f_im = far[slot, rows], far[slot, lower]
            factor = 1.0 - amps[j, rows].astype(jnp.float32) * lax.rsqrt(f_re * f_re + f_im * f_im + 1.0)
            if living is not None:
                factor = factor * living
            ex[slot, rows, :frame] = (f_re * factor).astype(jnp.bfloat16)
            ex[slot, rows, frame:] = (f_im * factor).astype(jnp.bfloat16)

    def leave(j, slot):
        for i in strips:
            rows = slice(i * STRIP, (i + 1) * STRIP)
            lower = slice(frame + i * STRIP, frame + (i + 1) * STRIP)
            b_re, b_im = far[slot, rows], far[slot, lower]
            o_re, o_im = patch[slot, 0, rows], patch[slot, 1, rows]
            p_re, p_im = probe[j, 0, rows], probe[j, 1, rows]
            for c, d in enumerate((o_re * b_re + o_im * b_im, o_re * b_im - o_im * b_re)):
                dprobe[j, c, rows] = d.astype(jnp.bfloat16)
            probe[j, 0, rows] = p_re * b_re + p_im * b_im
            probe[j, 1, rows] = p_re * b_im - p_im * b_re

    def grad_copy(j):
        return pltpu.make_async_copy(probe.at[j], grads_out.at[j], grad_sem.at[j])

    def visit(pair, carry):
        first, second = 2 * pair, 2 * pair + 1
        enter(first, 0)
        transform(0, 0)
        enter(second, 1)
        transform(1, 0)
        residual(first, 0, None)
        transform(0, 1)
        residual(second, 1, jnp.where(second < alive, 1.0, 0.0))
        transform(1, 1)
        leave(first, 0)
        leave(second, 1)
        grad_copy(first).start()
        grad_copy(second).start()
        return carry

    pairs = (alive + 1) // 2
    lax.fori_loop(0, pairs, visit, 0)

    def skip(j, carry):
        dprobe[j] = jnp.zeros((2, frame, frame), jnp.bfloat16)
        return carry

    lax.fori_loop(2 * pairs, pos_dev, skip, 0)

    cross[...] = jnp.zeros_like(cross)
    rows_q = frame // shares
    groups = 2 * modes
    share = share_of(groups, lax.axis_size("blk"))

    def eigen_strip(i, carry):
        rows = pl.ds(pl.multiple_of(i * STRIP, STRIP), STRIP)
        q = i // (rows_q // STRIP)
        inner = pl.ds(pl.multiple_of(i % (rows_q // STRIP) * STRIP, STRIP), STRIP)
        for c in range(2):
            d = dprobe[:, c, rows, :].reshape(pos_dev * STRIP, frame)
            e = eig[:, c, rows, :].reshape(modes * STRIP, frame)
            both = jnp.dot(weights_t[...], d, preferred_element_type=jnp.float32)
            grad = (both[:modes * STRIP] + both[modes * STRIP:]) * (0.5 * scale)
            for k in range(modes):
                group = 2 * k + c
                if share:
                    group = (group // share ^ my_block) * share + group % share
                eigen[q, group, inner, :] = grad[k * STRIP:(k + 1) * STRIP]
            cross[...] += lax.dot_general(
                d, e, (((1,), (1,)), ((), ())), preferred_element_type=jnp.float32
            )
        return carry

    lax.fori_loop(0, frame // STRIP, eigen_strip, 0, unroll=8)
    pending = []

    def start(source, target):
        copy = pltpu.make_async_copy(source, target, out_sem.at[len(pending)])
        copy.start()
        pending.append(copy)

    for h in far_first(shares):
        mine, other = slabs_of(member, h)
        out_eigen[h] = eigen[other].astype(jnp.bfloat16)
        start(out_eigen.at[h], eigen_send[h % 2].at[h // 2])
        start(eigen.at[mine], eigen_keep[h % 2].at[h // 2])

    by_position = (pos_dev * STRIP, pos_dev)
    by_mode = (modes * STRIP, modes)
    total = exact(one_hot(by_position[::-1], 1), diagonals(cross[...]))
    coef[...] = lax.dot_general(
        one_hot(by_mode[::-1], 1), total, (((1,), (1,)), ((), ())),
        precision=lax.Precision.HIGHEST, preferred_element_type=jnp.float32,
    ) * (0.5 / frame)

    def drain(j, carry):
        grad_copy(j).wait()
        return carry

    lax.fori_loop(0, 2 * pairs, drain, 0)
    for copy in pending:
        copy.wait()


def positions(offs, scale, indices, pieces, eigenprobes, amps, table, weights, weights_t):
    modes, _, frame, _ = eigenprobes.shape
    pos_dev = amps.shape[0]
    side = pieces[0].shape[2]
    shares = len(offs)
    blocks = side // LANES
    smem = pl.BlockSpec(memory_space=SMEM)
    whole = pl.BlockSpec(memory_space=VMEM)
    anywhere = pl.BlockSpec(memory_space=pl.ANY)
    eigen_half = (shares // 2, 2 * modes, frame // shares, frame)
    eigen_part = (shares // 4,) + eigen_half[1:]
    grads = (pos_dev, 2, frame, frame)
    return pl.pallas_call(
        functools.partial(position_kernel, offs, scale),
        in_specs=[smem] * 3 + [anywhere] * (len(pieces) + 3) + [whole] * 2,
        out_specs=[anywhere] * 5 + [whole],
        scratch_shapes=[
            pltpu.VMEM((REACH, 2, side, side), jnp.bfloat16),
            pltpu.VMEM(table.shape, jnp.bfloat16),
            pltpu.VMEM(grads, jnp.float32),
            pltpu.VMEM(amps.shape, jnp.bfloat16),
            pltpu.VMEM(eigenprobes.shape, jnp.bfloat16),
            pltpu.VMEM((REACH, 2, blocks + 1, side, LANES), jnp.float32),
            pltpu.VMEM((2, frame, 2 * frame), jnp.bfloat16),
            pltpu.VMEM((2, 2 * frame, frame), jnp.bfloat16),
            pltpu.VMEM((2, 2 * frame, frame), jnp.float32),
            pltpu.VMEM((2, 2, frame, frame), jnp.float32),
            pltpu.VMEM(grads, jnp.bfloat16),
            pltpu.VMEM((shares, 2 * modes, frame // shares, frame), jnp.float32),
            pltpu.VMEM(eigen_half, jnp.bfloat16),
            pltpu.VMEM((pos_dev * STRIP, modes * STRIP), jnp.float32),
            pltpu.SemaphoreType.DMA((len(pieces),)),
            pltpu.SemaphoreType.DMA,
            pltpu.SemaphoreType.DMA,
            pltpu.SemaphoreType.DMA,
            pltpu.SemaphoreType.DMA((pos_dev,)),
            pltpu.SemaphoreType.DMA((shares,)),
        ],
        out_shape=[
            jax.ShapeDtypeStruct(eigen_part, jnp.bfloat16),
            jax.ShapeDtypeStruct(eigen_part, jnp.bfloat16),
            jax.ShapeDtypeStruct(eigen_part, jnp.float32),
            jax.ShapeDtypeStruct(eigen_part, jnp.float32),
            jax.ShapeDtypeStruct(grads, jnp.float32),
            jax.ShapeDtypeStruct((modes, pos_dev), jnp.float32),
        ],
        compiler_params=pltpu.CompilerParams(vmem_limit_bytes=VMEM_LIMIT),
        name="positions",
    )(*indices, *pieces, eigenprobes, amps, table, weights, weights_t)


def scatter_kernel(shares, tile_list, offsets, group_counts, grads_in, *refs):
    send, keep = refs[:2 * REACH], refs[2 * REACH:4 * REACH]
    grads, acc, out_send, grad_sem, out_sem = refs[4 * REACH:]
    pos_dev, _, frame, _ = grads.shape
    blocks, side = acc.shape[2] - 1, acc.shape[3]
    slab = side // shares
    _, member, alive, place = coordinates(tile_list, offsets, group_counts, pos_dev)

    def grad_copy(j):
        return pltpu.make_async_copy(grads_in.at[j], grads.at[j], grad_sem.at[j])

    def begin(j, carry):
        grad_copy(j).start()
        return carry

    lax.fori_loop(0, alive, begin, 0)

    def clear(i, carry):
        rows = pl.ds(pl.multiple_of(i * LANES, LANES), LANES)
        for section in range(REACH):
            for c in range(2):
                for b in range(blocks + 1):
                    acc[section, c, b, rows, :] = jnp.zeros((LANES, LANES), jnp.float32)
        return carry

    lax.fori_loop(0, side // LANES, clear, 0)
    lane = lax.broadcasted_iota(jnp.int32, (STRIP, LANES), 1)

    def add(j, carry):
        grad_copy(j).wait()
        for m in range(2):
            section, row, col = place(j, m)
            cb, s = col // LANES, col % LANES
            inside = lane >= s
            for i in range(frame // STRIP):
                for c in range(2):
                    low, high = (
                        pltpu.roll(grads[j, c, i * STRIP:(i + 1) * STRIP, b * LANES:(b + 1) * LANES], s, 1)
                        for b in range(2)
                    )
                    for b, value in enumerate(
                        (
                            jnp.where(inside, low, 0.0),
                            jnp.where(inside, high, low),
                            jnp.where(inside, 0.0, high),
                        )
                    ):
                        at = (section, c, cb + b, pl.ds(row + i * STRIP, STRIP), slice(None))
                        acc[at] = acc[at] + value
        return carry

    lax.fori_loop(0, alive, add, 0)
    pending = []

    def start(source, target):
        copy = pltpu.make_async_copy(source, target, out_sem.at[len(pending)])
        copy.start()
        pending.append(copy)

    for section in range(REACH - 1, -1, -1):
        for h in far_first(shares):
            mine, other = (pl.multiple_of(at * slab, slab) for at in slabs_of(member, h))
            start(
                acc.at[section, :, pl.ds(0, blocks), pl.ds(mine, slab), :],
                keep[2 * section + h % 2].at[h // 2],
            )
            for c in range(2):
                for b in range(blocks):
                    out_send[section, h, c, b] = acc[section, c, b, pl.ds(other, slab), :].astype(jnp.bfloat16)
            start(out_send.at[section, h], send[2 * section + h % 2].at[h // 2])
    for copy in pending:
        copy.wait()


def scatter(shares, side, indices, grads):
    blocks = side // LANES
    anywhere = pl.BlockSpec(memory_space=pl.ANY)
    half = (shares // 2, 2, blocks, side // shares, LANES)
    part = (shares // 4,) + half[1:]
    return pl.pallas_call(
        functools.partial(scatter_kernel, shares),
        in_specs=[pl.BlockSpec(memory_space=SMEM)] * 3 + [anywhere],
        out_specs=[anywhere] * (4 * REACH),
        scratch_shapes=[
            pltpu.VMEM(grads.shape, jnp.float32),
            pltpu.VMEM((REACH, 2, blocks + 1, side, LANES), jnp.float32),
            pltpu.VMEM((REACH,) + half, jnp.bfloat16),
            pltpu.SemaphoreType.DMA((grads.shape[0],)),
            pltpu.SemaphoreType.DMA((REACH * shares,)),
        ],
        out_shape=[jax.ShapeDtypeStruct(part, jnp.bfloat16)] * (2 * REACH)
        + [jax.ShapeDtypeStruct(part, jnp.float32)] * (2 * REACH),
        compiler_params=pltpu.CompilerParams(vmem_limit_bytes=20 * 1024 * 1024),
        cost_estimate=pl.CostEstimate(flops=1 << 24, bytes_accessed=16 << 20, transcendentals=0),
        name="scatter",
    )(*indices, grads)


def after(array, *others):
    return lax.optimization_barrier((array,) + others)[0]


def after_all(arrays, *others):
    return lax.optimization_barrier(tuple(arrays) + others)[:len(arrays)]


def halve(keep, send, before_core=(), before_cross=()):
    far = [keep[1], after(swap(after(send[1], *before_core), "probe", 1), *before_cross)]
    terms = [keep[0], swap(send[0], "probe", 1)]
    leaving = None
    bit = 2
    while True:
        sending = sum(term.astype(jnp.float32) for term in far).astype(jnp.bfloat16)
        leaving = sending if leaving is None else leaving
        terms.append(swap(sending, "probe", bit))
        if terms[0].shape[0] == 1:
            return sum(term[0].astype(jnp.float32) for term in terms), leaving, terms[-1]
        pick = lambda term, which: term.reshape((term.shape[0] // 2, 2) + term.shape[1:])[:, which]
        far, terms = [pick(term, 1) for term in terms], [pick(term, 0) for term in terms]
        bit *= 2


def add_up_kernel(own, *refs):
    arrived, out = refs[:-1], refs[-1]
    total = own[...]
    for term in arrived:
        total += term[...].astype(jnp.float32)
    total = total.astype(jnp.bfloat16)
    for i in range(out.shape[0]):
        out[i] = total


def widen_kernel(array, out):
    out[...] = array[...].astype(jnp.float32)


def small_call(kernel, shape, kind, name, *arrays):
    return pl.pallas_call(
        kernel,
        in_specs=[pl.BlockSpec(memory_space=VMEM)] * len(arrays),
        out_specs=pl.BlockSpec(memory_space=VMEM),
        out_shape=jax.ShapeDtypeStruct(shape, kind),
        compiler_params=pltpu.CompilerParams(vmem_limit_bytes=8 * 1024 * 1024),
        name=name,
    )(*arrays)


def scatter_sum(axis, value, relative):
    peers, me = lax.axis_size(axis), lax.axis_index(axis)
    share = (lambda i: value[i]) if relative else (lambda i: lax.dynamic_index_in_dim(value, me ^ i, 0, False))
    sent = [share(i).astype(jnp.bfloat16) for i in range(1, peers)]
    arrived = [swap(sending, axis, i) for i, sending in enumerate(sent, 1)]
    total = small_call(
        add_up_kernel, (peers,) + value.shape[1:], jnp.bfloat16, "add_up", share(0), *arrived
    )
    return total, sent


def finish_kernel(first, second, out):
    blocks = first.shape[1]
    for c in range(2):
        for b in range(blocks):
            out[c, :, b * LANES:(b + 1) * LANES] = first[c, b] + second[c, b].astype(jnp.float32)


def finish(first, second):
    _, blocks, slab, lanes = first.shape
    return pl.pallas_call(
        finish_kernel,
        in_specs=[pl.BlockSpec(memory_space=VMEM)] * 2,
        out_specs=pl.BlockSpec(memory_space=VMEM),
        out_shape=jax.ShapeDtypeStruct((2, slab, blocks * lanes), jnp.float32),
        compiler_params=pltpu.CompilerParams(vmem_limit_bytes=8 * 1024 * 1024),
        name="finish",
    )(first, second)


def on_device(tiles, eigenprobes, coefficients, tile_list, offsets, amplitudes, group_counts):
    modes, _, frame, _ = eigenprobes.shape
    side = tiles.shape[2]
    pos_dev = coefficients.shape[0]
    blocks = lax.axis_size("blk")
    shares = lax.axis_size("probe")
    member = lax.axis_index("probe")
    slab = side // shares
    bits = [1 << i for i in range(shares.bit_length() - 1)]

    offs = [0]
    for bit in reversed(bits):
        offs = offs + [o ^ bit for o in offs]
    quarter = lax.dynamic_slice_in_dim(tiles[0], member * slab, slab, 1)
    near = shift(quarter, "blk", -1)
    held = [[near], [shift(near, "blk", -1)]]
    eig, amps = stage(*after_all((eigenprobes, amplitudes), near))
    held[1][0] = after(held[1][0], eig)
    weights, weights_t, table, tile, lists, corners = expand(
        *after_all((coefficients.T, tables(frame), tiles[0], tile_list.T, offsets.T), held[1][0])
    )
    for bit in reversed(bits):
        for part in held:
            arrived = [swap(piece, "probe", bit) for piece in part]
            if bit > 1:
                arrived[0] = after(arrived[0], eig if part is held[0] else table)
            part += arrived

    indices = (lists, corners, group_counts)
    scale = (pos_dev * blocks * shares) ** (-0.5)
    out = positions(
        tuple(offs), scale, indices, [tile] + held[0] + held[1], eig, amps, table, weights, weights_t
    )
    eigen_send, eigen_keep, grads, coef_rows = out[:2], out[2:4], out[4], out[5]

    eigen, leaving, crossed = halve(eigen_keep, eigen_send)
    out = scatter(shares, side, indices, after(grads, leaving))
    send, keep = ([out[at + 2 * i:at + 2 * i + 2] for i in range(REACH)] for at in (0, 2 * REACH))
    last = REACH - 1
    relative = share_of(2 * modes, blocks) > 0
    total, sent = scatter_sum("blk", eigen.reshape(blocks, -1, frame), relative)
    mine, leaving, _ = halve(keep[last], send[last], before_cross=sent)
    moving = after(mine.astype(jnp.bfloat16), *sent)
    gate = moving
    for section in range(last - 1, -1, -1):
        mine, leaving, gate = halve(keep[section], send[section], before_cross=(gate,))
        if section == last - 1:
            total = after(total, leaving)
        arrived = shift(moving, "blk", 1)
        if section > 0:
            moving = (arrived.astype(jnp.float32) + mine).astype(jnp.bfloat16)
    gathered = lax.all_to_all(total, "blk", 0, 0)
    eigen_share = small_call(widen_kernel, gathered.shape, jnp.float32, "widen", gathered)
    eigen_share = eigen_share.reshape(modes, 2, frame // shares, frame)
    summed = finish(mine, arrived)
    return (summed[None], eigen_share, coef_rows.T)


def solution(mesh):
    in_specs = (
        P(("recon", "blk"), None, None, None),
        P("recon", None, None, None),
        P(("recon", "blk", "probe"), None),
        P(("recon", "blk", "probe"), None),
        P(("recon", "blk", "probe"), None),
        P(("recon", "blk", "probe"), None, None),
        P(("recon", "blk")),
    )
    out_specs = (
        P(("recon", "blk"), None, "probe", None),
        P("recon", None, "probe", None),
        P(("recon", "blk", "probe"), None),
    )
    return jax.shard_map(
        on_device, mesh=mesh, in_specs=in_specs, out_specs=out_specs, check_vma=False
    )
```

```python
import functools
import math

import jax
import jax.numpy as jnp
import ml_dtypes
import numpy as np
from jax import lax
from jax.experimental import pallas as pl
from jax.experimental.pallas import tpu as pltpu
from jax.sharding import PartitionSpec as P

REACH = 3
LANES = 128
STRIP = 16
VMEM = pltpu.MemorySpace.VMEM
SMEM = pltpu.MemorySpace.SMEM
VMEM_LIMIT = 36 * 1024 * 1024


def tables(frame):
    indices = np.arange(frame)
    angle = (indices[:, None] * indices[None, :] % frame) * (2.0 * math.pi / frame)
    cos_part = np.cos(angle) / math.sqrt(frame)
    sin_part = -np.sin(angle) / math.sqrt(frame)
    forward = np.block([[cos_part, sin_part], [-sin_part, cos_part]])
    forward = forward.astype(np.float32).astype(ml_dtypes.bfloat16)
    return jnp.asarray(np.stack([forward, forward.T]))


def shift(array, axis, by):
    peers = lax.axis_size(axis)
    return lax.ppermute(array, axis, [(i, (i + by) % peers) for i in range(peers)])


def swap(array, axis, bit):
    peers = lax.axis_size(axis)
    return lax.ppermute(array, axis, [(i, i ^ bit) for i in range(peers)])


def slabs_of(member, h):
    pair, core = member >> 1, member & 1
    mine = 2 * (pair ^ h) + core
    return mine, mine ^ 1


def far_first(shares):
    return [*range(1, shares // 2, 2), *range(0, shares // 2, 2)]


def share_of(groups, peers):
    return groups // peers if groups % peers == 0 else 0


def coordinates(tile_list, offsets, group_counts, pos_dev):
    blocks = lax.axis_size("blk")
    my_block, member = lax.axis_index("blk"), lax.axis_index("probe")
    alive = jnp.clip(group_counts[0] - member * pos_dev, 0, pos_dev)

    def place(j, m):
        section = lax.rem(tile_list[m, j] - my_block + blocks, blocks)
        return section, offsets[2 * m, j], offsets[2 * m + 1, j]

    return my_block, member, alive, place


def one_hot(shape, axis):
    return (
        lax.broadcasted_iota(jnp.int32, shape, axis) // STRIP == lax.broadcasted_iota(jnp.int32, shape, 1 - axis)
    ).astype(jnp.float32)


def diagonals(array):
    row = lax.broadcasted_iota(jnp.int32, array.shape, 0)
    col = lax.broadcasted_iota(jnp.int32, array.shape, 1)
    return jnp.where(row % STRIP == col % STRIP, array, 0.0)


def exact(left, right):
    return jnp.dot(left, right, precision=lax.Precision.HIGHEST, preferred_element_type=jnp.float32)


def two_terms(array):
    high = array.astype(jnp.bfloat16)
    return high, (array - high.astype(jnp.float32)).astype(jnp.bfloat16)


def stage_kernel(*refs):
    count = len(refs) // 2
    move(refs[:count], refs[count:2 * count], refs[-1])()


def move(sources, targets, sem):
    copies = [
        pltpu.make_async_copy(source, target, sem.at[i])
        for i, (source, target) in enumerate(zip(sources, targets))
    ]
    for copy in copies:
        copy.start()

    def finish():
        for copy in copies:
            copy.wait()

    return finish


def stage(*arrays):
    anywhere = pl.BlockSpec(memory_space=pl.ANY)
    return pl.pallas_call(
        stage_kernel,
        in_specs=[anywhere] * len(arrays),
        out_specs=[anywhere] * len(arrays),
        scratch_shapes=[pltpu.SemaphoreType.DMA((len(arrays),))],
        out_shape=[jax.ShapeDtypeStruct(x.shape, x.dtype) for x in arrays],
        compiler_params=pltpu.CompilerParams(vmem_limit_bytes=1024 * 1024),
        name="stage",
    )(*arrays)


def weights_kernel(coef_in, *refs):
    count = (len(refs) - 3) // 2
    weights, weights_t = refs[count:count + 2]
    finish = move(refs[:count], refs[count + 2:-1], refs[-1])
    modes, pos_dev = coef_in.shape
    by_position = (pos_dev * STRIP, pos_dev)
    by_mode = (modes * STRIP, modes)
    tall_t = exact(exact(one_hot(by_mode, 0), coef_in[...]), one_hot(by_position[::-1], 1))
    high, low = two_terms(diagonals(tall_t))
    weights_t[...] = jnp.concatenate([high, low], 0)
    spread = lax.dot_general(
        one_hot(by_position, 0), coef_in[...], (((1,), (1,)), ((), ())),
        precision=lax.Precision.HIGHEST, preferred_element_type=jnp.float32,
    )
    high, low = two_terms(diagonals(0.5 * exact(spread, one_hot(by_mode[::-1], 1))))
    weights[...] = jnp.concatenate([high, low], 1)
    finish()


def expand(coef_t, *arrays):
    modes, pos_dev = coef_t.shape
    whole = pl.BlockSpec(memory_space=VMEM)
    anywhere = pl.BlockSpec(memory_space=pl.ANY)
    return pl.pallas_call(
        weights_kernel,
        in_specs=[whole] + [anywhere] * len(arrays),
        out_specs=[whole] * 2 + [anywhere] * len(arrays),
        scratch_shapes=[pltpu.SemaphoreType.DMA((len(arrays),))],
        out_shape=[
            jax.ShapeDtypeStruct((pos_dev * STRIP, 2 * modes * STRIP), jnp.bfloat16),
            jax.ShapeDtypeStruct((2 * modes * STRIP, pos_dev * STRIP), jnp.bfloat16),
        ]
        + [jax.ShapeDtypeStruct(x.shape, x.dtype) for x in arrays],
        compiler_params=pltpu.CompilerParams(vmem_limit_bytes=4 * 1024 * 1024),
        name="expand",
    )(coef_t, *arrays)


def position_kernel(offs, scale, tile_list, offsets, group_counts, *refs):
    shares = len(offs)
    pieces = refs[: 1 + (REACH - 1) * shares]
    eig_in, amps_in, tables_in, weights, weights_t = refs[len(pieces):len(pieces) + 5]
    eigen_send, eigen_keep = refs[len(pieces) + 5:len(pieces) + 7], refs[len(pieces) + 7:len(pieces) + 9]
    grads_out, coef = refs[len(pieces) + 9:len(pieces) + 11]
    (staged, table, probe, amps, eig, obj, ex, mid, far, patch, dprobe, eigen, out_eigen, cross,
     piece_sem, table_sem, amps_sem, eig_sem, grad_sem, out_sem) = refs[len(pieces) + 11:]
    pos_dev, _, frame, _ = probe.shape
    modes = eig.shape[0]
    side = staged.shape[2]
    blocks = side // LANES
    slab = side // shares
    my_block, member, alive, place = coordinates(tile_list, offsets, group_counts, pos_dev)
    strips = range(frame // STRIP)

    copies = [pltpu.make_async_copy(pieces[0], staged.at[0], piece_sem.at[0])]
    for section in range(1, REACH):
        for i in range(shares):
            start = pl.multiple_of((member ^ offs[i]) * slab, slab)
            at = 1 + (section - 1) * shares + i
            copies.append(
                pltpu.make_async_copy(
                    pieces[at], staged.at[section, :, pl.ds(start, slab), :], piece_sem.at[at]
                )
            )
    table_copy = pltpu.make_async_copy(tables_in, table, table_sem)
    amps_copy = pltpu.make_async_copy(amps_in, amps, amps_sem)
    eig_copy = pltpu.make_async_copy(eig_in, eig, eig_sem)
    for copy in [eig_copy] + copies + [table_copy, amps_copy]:
        copy.start()

    eig_copy.wait()

    def synth(i, carry):
        rows = pl.ds(pl.multiple_of(i * STRIP, STRIP), STRIP)
        for c in range(2):
            e = eig[:, c, rows, :].reshape(modes * STRIP, frame)
            made = jnp.dot(
                weights[...], jnp.concatenate([e, e], 0), preferred_element_type=jnp.float32
            )
            probe[:, c, rows, :] = made.reshape(pos_dev, STRIP, frame)
        return carry

    lax.fori_loop(0, frame // STRIP, synth, 0, unroll=8)
    for copy in copies:
        copy.wait()

    def widen(i, carry):
        rows = pl.ds(pl.multiple_of(i * LANES, LANES), LANES)
        for section in range(REACH):
            for c in range(2):
                for b in range(blocks):
                    obj[section, c, b, rows, :] = staged[
                        section, c, rows, b * LANES:(b + 1) * LANES
                    ].astype(jnp.float32)
        return carry

    lax.fori_loop(0, side // LANES, widen, 0)
    table_copy.wait()
    amps_copy.wait()

    lane = lax.broadcasted_iota(jnp.int32, (STRIP, LANES), 1)

    def enter(j, slot):
        where = []
        for m in range(2):
            section, row, col = place(j, m)
            s = col % LANES
            where.append((section, row, col // LANES, (LANES - s) % LANES, lane < LANES - s))
        for i in strips:
            rows = slice(i * STRIP, (i + 1) * STRIP)
            parts = []
            for c in range(2):
                total = None
                for section, row, cb, back_by, keep_lane in where:
                    rolled = [
                        pltpu.roll(obj[section, c, cb + b, pl.ds(row + i * STRIP, STRIP), :], back_by, 1)
                        for b in range(3)
                    ]
                    block = [jnp.where(keep_lane, rolled[b], rolled[b + 1]) for b in range(2)]
                    total = block if total is None else [x + y for x, y in zip(total, block)]
                parts.append(total)
            for b in range(2):
                cols = slice(b * LANES, (b + 1) * LANES)
                o_re, o_im = parts[0][b], parts[1][b]
                p_re, p_im = probe[j, 0, rows, cols], probe[j, 1, rows, cols]
                patch[slot, 0, rows, cols] = o_re
                patch[slot, 1, rows, cols] = o_im
                ex[slot, rows, b * LANES:(b + 1) * LANES] = (p_re * o_re - p_im * o_im).astype(jnp.bfloat16)
                ex[slot, rows, frame + b * LANES:frame + (b + 1) * LANES] = (
                    p_re * o_im + p_im * o_re
                ).astype(jnp.bfloat16)

    def transform(slot, way):
        half = jnp.dot(ex[slot], table[way], preferred_element_type=jnp.float32)
        mid[slot, :frame] = half[:, :frame].astype(jnp.bfloat16)
        mid[slot, frame:] = half[:, frame:].astype(jnp.bfloat16)
        far[slot] = jnp.dot(table[1 - way], mid[slot], preferred_element_type=jnp.float32)

    def residual(j, slot, living):
        for i in strips:
            rows = slice(i * STRIP, (i + 1) * STRIP)
            lower = slice(frame + i * STRIP, frame + (i + 1) * STRIP)
            f_re, f_im = far[slot, rows], far[slot, lower]
            factor = 1.0 - amps[j, rows].astype(jnp.float32) * lax.rsqrt(f_re * f_re + f_im * f_im + 1.0)
            if living is not None:
                factor = factor * living
            ex[slot, rows, :frame] = (f_re * factor).astype(jnp.bfloat16)
            ex[slot, rows, frame:] = (f_im * factor).astype(jnp.bfloat16)

    def leave(j, slot):
        for i in strips:
            rows = slice(i * STRIP, (i + 1) * STRIP)
            lower = slice(frame + i * STRIP, frame + (i + 1) * STRIP)
            b_re, b_im = far[slot, rows], far[slot, lower]
            o_re, o_im = patch[slot, 0, rows], patch[slot, 1, rows]
            p_re, p_im = probe[j, 0, rows], probe[j, 1, rows]
            for c, d in enumerate((o_re * b_re + o_im * b_im, o_re * b_im - o_im * b_re)):
                dprobe[j, c, rows] = d.astype(jnp.bfloat16)
            probe[j, 0, rows] = p_re * b_re + p_im * b_im
            probe[j, 1, rows] = p_re * b_im - p_im * b_re

    def grad_copy(j):
        return pltpu.make_async_copy(probe.at[j], grads_out.at[j], grad_sem.at[j])

    def visit(pair, carry):
        first, second = 2 * pair, 2 * pair + 1
        enter(first, 0)
        transform(0, 0)
        enter(second, 1)
        transform(1, 0)
        residual(first, 0, None)
        transform(0, 1)
        residual(second, 1, jnp.where(second < alive, 1.0, 0.0))
        transform(1, 1)
        leave(first, 0)
        leave(second, 1)
        grad_copy(first).start()
        grad_copy(second).start()
        return carry

    pairs = (alive + 1) // 2
    lax.fori_loop(0, pairs, visit, 0)

    def skip(j, carry):
        dprobe[j] = jnp.zeros((2, frame, frame), jnp.bfloat16)
        return carry

    lax.fori_loop(2 * pairs, pos_dev, skip, 0)

    cross[...] = jnp.zeros_like(cross)
    rows_q = frame // shares
    groups = 2 * modes
    share = share_of(groups, lax.axis_size("blk"))

    def eigen_strip(i, carry):
        rows = pl.ds(pl.multiple_of(i * STRIP, STRIP), STRIP)
        q = i // (rows_q // STRIP)
        inner = pl.ds(pl.multiple_of(i % (rows_q // STRIP) * STRIP, STRIP), STRIP)
        for c in range(2):
            d = dprobe[:, c, rows, :].reshape(pos_dev * STRIP, frame)
            e = eig[:, c, rows, :].reshape(modes * STRIP, frame)
            both = jnp.dot(weights_t[...], d, preferred_element_type=jnp.float32)
            grad = (both[:modes * STRIP] + both[modes * STRIP:]) * (0.5 * scale)
            for k in range(modes):
                group = 2 * k + c
                if share:
                    group = (group // share ^ my_block) * share + group % share
                eigen[q, group, inner, :] = grad[k * STRIP:(k + 1) * STRIP]
            cross[...] += lax.dot_general(
                d, e, (((1,), (1,)), ((), ())), preferred_element_type=jnp.float32
            )
        return carry

    lax.fori_loop(0, frame // STRIP, eigen_strip, 0, unroll=8)
    pending = []

    def start(source, target):
        copy = pltpu.make_async_copy(source, target, out_sem.at[len(pending)])
        copy.start()
        pending.append(copy)

    for h in far_first(shares):
        mine, other = slabs_of(member, h)
        out_eigen[h] = eigen[other].astype(jnp.bfloat16)
        start(out_eigen.at[h], eigen_send[h % 2].at[h // 2])
        start(eigen.at[mine], eigen_keep[h % 2].at[h // 2])

    by_position = (pos_dev * STRIP, pos_dev)
    by_mode = (modes * STRIP, modes)
    total = exact(one_hot(by_position[::-1], 1), diagonals(cross[...]))
    coef[...] = lax.dot_general(
        one_hot(by_mode[::-1], 1), total, (((1,), (1,)), ((), ())),
        precision=lax.Precision.HIGHEST, preferred_element_type=jnp.float32,
    ) * (0.5 / frame)

    def drain(j, carry):
        grad_copy(j).wait()
        return carry

    lax.fori_loop(0, 2 * pairs, drain, 0)
    for copy in pending:
        copy.wait()


def positions(offs, scale, indices, pieces, eigenprobes, amps, table, weights, weights_t):
    modes, _, frame, _ = eigenprobes.shape
    pos_dev = amps.shape[0]
    side = pieces[0].shape[2]
    shares = len(offs)
    blocks = side // LANES
    smem = pl.BlockSpec(memory_space=SMEM)
    whole = pl.BlockSpec(memory_space=VMEM)
    anywhere = pl.BlockSpec(memory_space=pl.ANY)
    eigen_half = (shares // 2, 2 * modes, frame // shares, frame)
    eigen_part = (shares // 4,) + eigen_half[1:]
    grads = (pos_dev, 2, frame, frame)
    return pl.pallas_call(
        functools.partial(position_kernel, offs, scale),
        in_specs=[smem] * 3 + [anywhere] * (len(pieces) + 3) + [whole] * 2,
        out_specs=[anywhere] * 5 + [whole],
        scratch_shapes=[
            pltpu.VMEM((REACH, 2, side, side), jnp.bfloat16),
            pltpu.VMEM(table.shape, jnp.bfloat16),
            pltpu.VMEM(grads, jnp.float32),
            pltpu.VMEM(amps.shape, jnp.bfloat16),
            pltpu.VMEM(eigenprobes.shape, jnp.bfloat16),
            pltpu.VMEM((REACH, 2, blocks + 1, side, LANES), jnp.float32),
            pltpu.VMEM((2, frame, 2 * frame), jnp.bfloat16),
            pltpu.VMEM((2, 2 * frame, frame), jnp.bfloat16),
            pltpu.VMEM((2, 2 * frame, frame), jnp.float32),
            pltpu.VMEM((2, 2, frame, frame), jnp.float32),
            pltpu.VMEM(grads, jnp.bfloat16),
            pltpu.VMEM((shares, 2 * modes, frame // shares, frame), jnp.float32),
            pltpu.VMEM(eigen_half, jnp.bfloat16),
            pltpu.VMEM((pos_dev * STRIP, modes * STRIP), jnp.float32),
            pltpu.SemaphoreType.DMA((len(pieces),)),
            pltpu.SemaphoreType.DMA,
            pltpu.SemaphoreType.DMA,
            pltpu.SemaphoreType.DMA,
            pltpu.SemaphoreType.DMA((pos_dev,)),
            pltpu.SemaphoreType.DMA((shares,)),
        ],
        out_shape=[
            jax.ShapeDtypeStruct(eigen_part, jnp.bfloat16),
            jax.ShapeDtypeStruct(eigen_part, jnp.bfloat16),
            jax.ShapeDtypeStruct(eigen_part, jnp.float32),
            jax.ShapeDtypeStruct(eigen_part, jnp.float32),
            jax.ShapeDtypeStruct(grads, jnp.float32),
            jax.ShapeDtypeStruct((modes, pos_dev), jnp.float32),
        ],
        compiler_params=pltpu.CompilerParams(vmem_limit_bytes=VMEM_LIMIT),
        name="positions",
    )(*indices, *pieces, eigenprobes, amps, table, weights, weights_t)


def scatter_kernel(shares, tile_list, offsets, group_counts, grads_in, *refs):
    send, keep = refs[:2 * REACH], refs[2 * REACH:4 * REACH]
    grads, acc, out_send, grad_sem, out_sem = refs[4 * REACH:]
    pos_dev, _, frame, _ = grads.shape
    blocks, side = acc.shape[2] - 1, acc.shape[3]
    slab = side // shares
    _, member, alive, place = coordinates(tile_list, offsets, group_counts, pos_dev)

    def grad_copy(j):
        return pltpu.make_async_copy(grads_in.at[j], grads.at[j], grad_sem.at[j])

    def begin(j, carry):
        grad_copy(j).start()
        return carry

    lax.fori_loop(0, alive, begin, 0)

    def clear(i, carry):
        rows = pl.ds(pl.multiple_of(i * LANES, LANES), LANES)
        for section in range(REACH):
            for c in range(2):
                for b in range(blocks + 1):
                    acc[section, c, b, rows, :] = jnp.zeros((LANES, LANES), jnp.float32)
        return carry

    lax.fori_loop(0, side // LANES, clear, 0)
    lane = lax.broadcasted_iota(jnp.int32, (STRIP, LANES), 1)

    def add(j, carry):
        grad_copy(j).wait()
        for m in range(2):
            section, row, col = place(j, m)
            cb, s = col // LANES, col % LANES
            inside = lane >= s
            for i in range(frame // STRIP):
                for c in range(2):
                    low, high = (
                        pltpu.roll(grads[j, c, i * STRIP:(i + 1) * STRIP, b * LANES:(b + 1) * LANES], s, 1)
                        for b in range(2)
                    )
                    for b, value in enumerate(
                        (
                            jnp.where(inside, low, 0.0),
                            jnp.where(inside, high, low),
                            jnp.where(inside, 0.0, high),
                        )
                    ):
                        at = (section, c, cb + b, pl.ds(row + i * STRIP, STRIP), slice(None))
                        acc[at] = acc[at] + value
        return carry

    lax.fori_loop(0, alive, add, 0)
    pending = []

    def start(source, target):
        copy = pltpu.make_async_copy(source, target, out_sem.at[len(pending)])
        copy.start()
        pending.append(copy)

    for section in range(REACH - 1, -1, -1):
        for h in far_first(shares):
            mine, other = (pl.multiple_of(at * slab, slab) for at in slabs_of(member, h))
            start(
                acc.at[section, :, pl.ds(0, blocks), pl.ds(mine, slab), :],
                keep[2 * section + h % 2].at[h // 2],
            )
            for c in range(2):
                for b in range(blocks):
                    out_send[section, h, c, b] = acc[section, c, b, pl.ds(other, slab), :].astype(jnp.bfloat16)
            start(out_send.at[section, h], send[2 * section + h % 2].at[h // 2])
    for copy in pending:
        copy.wait()


def scatter(shares, side, indices, grads):
    blocks = side // LANES
    anywhere = pl.BlockSpec(memory_space=pl.ANY)
    half = (shares // 2, 2, blocks, side // shares, LANES)
    part = (shares // 4,) + half[1:]
    return pl.pallas_call(
        functools.partial(scatter_kernel, shares),
        in_specs=[pl.BlockSpec(memory_space=SMEM)] * 3 + [anywhere],
        out_specs=[anywhere] * (4 * REACH),
        scratch_shapes=[
            pltpu.VMEM(grads.shape, jnp.float32),
            pltpu.VMEM((REACH, 2, blocks + 1, side, LANES), jnp.float32),
            pltpu.VMEM((REACH,) + half, jnp.bfloat16),
            pltpu.SemaphoreType.DMA((grads.shape[0],)),
            pltpu.SemaphoreType.DMA((REACH * shares,)),
        ],
        out_shape=[jax.ShapeDtypeStruct(part, jnp.bfloat16)] * (2 * REACH)
        + [jax.ShapeDtypeStruct(part, jnp.float32)] * (2 * REACH),
        compiler_params=pltpu.CompilerParams(vmem_limit_bytes=20 * 1024 * 1024),
        cost_estimate=pl.CostEstimate(flops=1 << 24, bytes_accessed=16 << 20, transcendentals=0),
        name="scatter",
    )(*indices, grads)


def after(array, *others):
    return lax.optimization_barrier((array,) + others)[0]


def after_all(arrays, *others):
    return lax.optimization_barrier(tuple(arrays) + others)[:len(arrays)]


def halve(keep, send, before_core=(), before_cross=()):
    far = [keep[1], after(swap(after(send[1], *before_core), "probe", 1), *before_cross)]
    terms = [keep[0], swap(send[0], "probe", 1)]
    leaving = None
    bit = 2
    while True:
        sending = sum(term.astype(jnp.float32) for term in far).astype(jnp.bfloat16)
        leaving = sending if leaving is None else leaving
        terms.append(swap(sending, "probe", bit))
        if terms[0].shape[0] == 1:
            return sum(term[0].astype(jnp.float32) for term in terms), leaving, terms[-1]
        pick = lambda term, which: term.reshape((term.shape[0] // 2, 2) + term.shape[1:])[:, which]
        far, terms = [pick(term, 1) for term in terms], [pick(term, 0) for term in terms]
        bit *= 2


def add_up_kernel(own, *refs):
    arrived, out = refs[:-1], refs[-1]
    total = own[...]
    for term in arrived:
        total += term[...].astype(jnp.float32)
    total = total.astype(jnp.bfloat16)
    for i in range(out.shape[0]):
        out[i] = total


def widen_kernel(array, out):
    out[...] = array[...].astype(jnp.float32)


def small_call(kernel, shape, kind, name, *arrays):
    return pl.pallas_call(
        kernel,
        in_specs=[pl.BlockSpec(memory_space=VMEM)] * len(arrays),
        out_specs=pl.BlockSpec(memory_space=VMEM),
        out_shape=jax.ShapeDtypeStruct(shape, kind),
        compiler_params=pltpu.CompilerParams(vmem_limit_bytes=8 * 1024 * 1024),
        name=name,
    )(*arrays)


def scatter_sum(axis, value, relative):
    peers, me = lax.axis_size(axis), lax.axis_index(axis)
    share = (lambda i: value[i]) if relative else (lambda i: lax.dynamic_index_in_dim(value, me ^ i, 0, False))
    sent = [share(i).astype(jnp.bfloat16) for i in range(1, peers)]
    arrived = [swap(sending, axis, i) for i, sending in enumerate(sent, 1)]
    total = small_call(
        add_up_kernel, (peers,) + value.shape[1:], jnp.bfloat16, "add_up", share(0), *arrived
    )
    return total, sent


def finish_kernel(first, second, out):
    blocks = first.shape[1]
    for c in range(2):
        for b in range(blocks):
            out[c, :, b * LANES:(b + 1) * LANES] = first[c, b] + second[c, b].astype(jnp.float32)


def finish(first, second):
    _, blocks, slab, lanes = first.shape
    return pl.pallas_call(
        finish_kernel,
        in_specs=[pl.BlockSpec(memory_space=VMEM)] * 2,
        out_specs=pl.BlockSpec(memory_space=VMEM),
        out_shape=jax.ShapeDtypeStruct((2, slab, blocks * lanes), jnp.float32),
        compiler_params=pltpu.CompilerParams(vmem_limit_bytes=8 * 1024 * 1024),
        name="finish",
    )(first, second)


def on_device(tiles, eigenprobes, coefficients, tile_list, offsets, amplitudes, group_counts):
    modes, _, frame, _ = eigenprobes.shape
    side = tiles.shape[2]
    pos_dev = coefficients.shape[0]
    blocks = lax.axis_size("blk")
    shares = lax.axis_size("probe")
    member = lax.axis_index("probe")
    slab = side // shares
    bits = [1 << i for i in range(shares.bit_length() - 1)]

    offs = [0]
    for bit in reversed(bits):
        offs = offs + [o ^ bit for o in offs]
    quarter = lax.dynamic_slice_in_dim(tiles[0], member * slab, slab, 1)
    near = shift(quarter, "blk", -1)
    held = [[near], [shift(near, "blk", -1)]]
    eig, amps = stage(*after_all((eigenprobes, amplitudes), near))
    held[1][0] = after(held[1][0], eig)
    weights, weights_t, table, tile, lists, corners = expand(
        *after_all((coefficients.T, tables(frame), tiles[0], tile_list.T, offsets.T), held[1][0])
    )
    for bit in reversed(bits):
        for part in held:
            arrived = [swap(piece, "probe", bit) for piece in part]
            if bit > 1:
                arrived[0] = after(arrived[0], eig if part is held[0] else table)
            part += arrived

    indices = (lists, corners, group_counts)
    scale = (pos_dev * blocks * shares) ** (-0.5)
    out = positions(
        tuple(offs), scale, indices, [tile] + held[0] + held[1], eig, amps, table, weights, weights_t
    )
    eigen_send, eigen_keep, grads, coef_rows = out[:2], out[2:4], out[4], out[5]

    eigen, leaving, crossed = halve(eigen_keep, eigen_send)
    out = scatter(shares, side, indices, after(grads, leaving))
    send, keep = ([out[at + 2 * i:at + 2 * i + 2] for i in range(REACH)] for at in (0, 2 * REACH))
    last = REACH - 1
    relative = share_of(2 * modes, blocks) > 0
    total, sent = scatter_sum("blk", eigen.reshape(blocks, -1, frame), relative)
    mine, leaving, _ = halve(keep[last], send[last], before_cross=sent)
    moving = after(mine.astype(jnp.bfloat16), total)
    gate = moving
    for section in range(last - 1, -1, -1):
        mine, leaving, gate = halve(keep[section], send[section], before_cross=(gate,))
        if section == last - 1:
            total = after(total, leaving)
        arrived = shift(moving, "blk", 1)
        if section > 0:
            moving = (arrived.astype(jnp.float32) + mine).astype(jnp.bfloat16)
    gathered = lax.all_to_all(total, "blk", 0, 0)
    eigen_share = small_call(widen_kernel, gathered.shape, jnp.float32, "widen", gathered)
    eigen_share = eigen_share.reshape(modes, 2, frame // shares, frame)
    summed = finish(mine, arrived)
    return (summed[None], eigen_share, coef_rows.T)


def solution(mesh):
    in_specs = (
        P(("recon", "blk"), None, None, None),
        P("recon", None, None, None),
        P(("recon", "blk", "probe"), None),
        P(("recon", "blk", "probe"), None),
        P(("recon", "blk", "probe"), None),
        P(("recon", "blk", "probe"), None, None),
        P(("recon", "blk")),
    )
    out_specs = (
        P(("recon", "blk"), None, "probe", None),
        P("recon", None, "probe", None),
        P(("recon", "blk", "probe"), None),
    )
    return jax.shard_map(
        on_device, mesh=mesh, in_specs=in_specs, out_specs=out_specs, check_vma=False
    )
```

```python
import functools
import math

import jax
import jax.numpy as jnp
import ml_dtypes
import numpy as np
from jax import lax
from jax.experimental import pallas as pl
from jax.experimental.pallas import tpu as pltpu
from jax.sharding import PartitionSpec as P

REACH = 3
LANES = 128
STRIP = 16
VMEM = pltpu.MemorySpace.VMEM
SMEM = pltpu.MemorySpace.SMEM
VMEM_LIMIT = 36 * 1024 * 1024


def tables(frame):
    indices = np.arange(frame)
    angle = (indices[:, None] * indices[None, :] % frame) * (2.0 * math.pi / frame)
    cos_part = np.cos(angle) / math.sqrt(frame)
    sin_part = -np.sin(angle) / math.sqrt(frame)
    forward = np.block([[cos_part, sin_part], [-sin_part, cos_part]])
    forward = forward.astype(np.float32).astype(ml_dtypes.bfloat16)
    return jnp.asarray(np.stack([forward, forward.T]))


def shift(array, axis, by):
    peers = lax.axis_size(axis)
    return lax.ppermute(array, axis, [(i, (i + by) % peers) for i in range(peers)])


def swap(array, axis, bit):
    peers = lax.axis_size(axis)
    return lax.ppermute(array, axis, [(i, i ^ bit) for i in range(peers)])


def slabs_of(member, h):
    pair, core = member >> 1, member & 1
    mine = 2 * (pair ^ h) + core
    return mine, mine ^ 1


def far_first(shares):
    return [*range(1, shares // 2, 2), *range(0, shares // 2, 2)]


def share_of(groups, peers):
    return groups // peers if groups % peers == 0 else 0


def coordinates(tile_list, offsets, group_counts, pos_dev):
    blocks = lax.axis_size("blk")
    my_block, member = lax.axis_index("blk"), lax.axis_index("probe")
    alive = jnp.clip(group_counts[0] - member * pos_dev, 0, pos_dev)

    def place(j, m):
        section = lax.rem(tile_list[m, j] - my_block + blocks, blocks)
        return section, offsets[2 * m, j], offsets[2 * m + 1, j]

    return my_block, member, alive, place


def one_hot(shape, axis):
    return (
        lax.broadcasted_iota(jnp.int32, shape, axis) // STRIP == lax.broadcasted_iota(jnp.int32, shape, 1 - axis)
    ).astype(jnp.float32)


def diagonals(array):
    row = lax.broadcasted_iota(jnp.int32, array.shape, 0)
    col = lax.broadcasted_iota(jnp.int32, array.shape, 1)
    return jnp.where(row % STRIP == col % STRIP, array, 0.0)


def exact(left, right):
    return jnp.dot(left, right, precision=lax.Precision.HIGHEST, preferred_element_type=jnp.float32)


def two_terms(array):
    high = array.astype(jnp.bfloat16)
    return high, (array - high.astype(jnp.float32)).astype(jnp.bfloat16)


def stage_kernel(*refs):
    count = len(refs) // 2
    move(refs[:count], refs[count:2 * count], refs[-1])()


def move(sources, targets, sem):
    copies = [
        pltpu.make_async_copy(source, target, sem.at[i])
        for i, (source, target) in enumerate(zip(sources, targets))
    ]
    for copy in copies:
        copy.start()

    def finish():
        for copy in copies:
            copy.wait()

    return finish


def stage(*arrays):
    anywhere = pl.BlockSpec(memory_space=pl.ANY)
    return pl.pallas_call(
        stage_kernel,
        in_specs=[anywhere] * len(arrays),
        out_specs=[anywhere] * len(arrays),
        scratch_shapes=[pltpu.SemaphoreType.DMA((len(arrays),))],
        out_shape=[jax.ShapeDtypeStruct(x.shape, x.dtype) for x in arrays],
        compiler_params=pltpu.CompilerParams(vmem_limit_bytes=1024 * 1024),
        name="stage",
    )(*arrays)


def weights_kernel(coef_in, *refs):
    count = (len(refs) - 3) // 2
    weights, weights_t = refs[count:count + 2]
    finish = move(refs[:count], refs[count + 2:-1], refs[-1])
    modes, pos_dev = coef_in.shape
    by_position = (pos_dev * STRIP, pos_dev)
    by_mode = (modes * STRIP, modes)
    tall_t = exact(exact(one_hot(by_mode, 0), coef_in[...]), one_hot(by_position[::-1], 1))
    high, low = two_terms(diagonals(tall_t))
    weights_t[...] = jnp.concatenate([high, low], 0)
    spread = lax.dot_general(
        one_hot(by_position, 0), coef_in[...], (((1,), (1,)), ((), ())),
        precision=lax.Precision.HIGHEST, preferred_element_type=jnp.float32,
    )
    high, low = two_terms(diagonals(0.5 * exact(spread, one_hot(by_mode[::-1], 1))))
    weights[...] = jnp.concatenate([high, low], 1)
    finish()


def expand(coef_t, *arrays):
    modes, pos_dev = coef_t.shape
    whole = pl.BlockSpec(memory_space=VMEM)
    anywhere = pl.BlockSpec(memory_space=pl.ANY)
    return pl.pallas_call(
        weights_kernel,
        in_specs=[whole] + [anywhere] * len(arrays),
        out_specs=[whole] * 2 + [anywhere] * len(arrays),
        scratch_shapes=[pltpu.SemaphoreType.DMA((len(arrays),))],
        out_shape=[
            jax.ShapeDtypeStruct((pos_dev * STRIP, 2 * modes * STRIP), jnp.bfloat16),
            jax.ShapeDtypeStruct((2 * modes * STRIP, pos_dev * STRIP), jnp.bfloat16),
        ]
        + [jax.ShapeDtypeStruct(x.shape, x.dtype) for x in arrays],
        compiler_params=pltpu.CompilerParams(vmem_limit_bytes=4 * 1024 * 1024),
        name="expand",
    )(coef_t, *arrays)


def position_kernel(offs, scale, tile_list, offsets, group_counts, *refs):
    shares = len(offs)
    pieces = refs[: 1 + (REACH - 1) * shares]
    eig_in, amps_in, tables_in, weights, weights_t = refs[len(pieces):len(pieces) + 5]
    eigen_send, eigen_keep = refs[len(pieces) + 5:len(pieces) + 7], refs[len(pieces) + 7:len(pieces) + 9]
    grads_out, coef = refs[len(pieces) + 9:len(pieces) + 11]
    (staged, table, probe, amps, eig, obj, ex, mid, far, patch, dprobe, eigen, out_eigen, cross,
     piece_sem, table_sem, amps_sem, eig_sem, grad_sem, out_sem) = refs[len(pieces) + 11:]
    pos_dev, _, frame, _ = probe.shape
    modes = eig.shape[0]
    side = staged.shape[2]
    blocks = side // LANES
    slab = side // shares
    my_block, member, alive, place = coordinates(tile_list, offsets, group_counts, pos_dev)
    strips = range(frame // STRIP)

    copies = [pltpu.make_async_copy(pieces[0], staged.at[0], piece_sem.at[0])]
    for section in range(1, REACH):
        for i in range(shares):
            start = pl.multiple_of((member ^ offs[i]) * slab, slab)
            at = 1 + (section - 1) * shares + i
            copies.append(
                pltpu.make_async_copy(
                    pieces[at], staged.at[section, :, pl.ds(start, slab), :], piece_sem.at[at]
                )
            )
    table_copy = pltpu.make_async_copy(tables_in, table, table_sem)
    amps_copy = pltpu.make_async_copy(amps_in, amps, amps_sem)
    eig_copy = pltpu.make_async_copy(eig_in, eig, eig_sem)
    for copy in [eig_copy] + copies + [table_copy, amps_copy]:
        copy.start()

    eig_copy.wait()

    def synth(i, carry):
        rows = pl.ds(pl.multiple_of(i * STRIP, STRIP), STRIP)
        e = jnp.concatenate([eig[:, c, rows, :].reshape(modes * STRIP, frame) for c in range(2)], 1)
        made = jnp.dot(weights[...], jnp.concatenate([e, e], 0), preferred_element_type=jnp.float32)
        for c in range(2):
            probe[:, c, rows, :] = made[:, c * frame:(c + 1) * frame].reshape(pos_dev, STRIP, frame)
        return carry

    lax.fori_loop(0, frame // STRIP, synth, 0, unroll=16)
    for copy in copies:
        copy.wait()

    def widen(i, carry):
        rows = pl.ds(pl.multiple_of(i * LANES, LANES), LANES)
        for section in range(REACH):
            for c in range(2):
                for b in range(blocks):
                    obj[section, c, b, rows, :] = staged[
                        section, c, rows, b * LANES:(b + 1) * LANES
                    ].astype(jnp.float32)
        return carry

    lax.fori_loop(0, side // LANES, widen, 0)
    table_copy.wait()
    amps_copy.wait()

    lane = lax.broadcasted_iota(jnp.int32, (STRIP, LANES), 1)

    def enter(j, slot):
        where = []
        for m in range(2):
            section, row, col = place(j, m)
            s = col % LANES
            where.append((section, row, col // LANES, (LANES - s) % LANES, lane < LANES - s))
        for i in strips:
            rows = slice(i * STRIP, (i + 1) * STRIP)
            parts = []
            for c in range(2):
                total = None
                for section, row, cb, back_by, keep_lane in where:
                    rolled = [
                        pltpu.roll(obj[section, c, cb + b, pl.ds(row + i * STRIP, STRIP), :], back_by, 1)
                        for b in range(3)
                    ]
                    block = [jnp.where(keep_lane, rolled[b], rolled[b + 1]) for b in range(2)]
                    total = block if total is None else [x + y for x, y in zip(total, block)]
                parts.append(total)
            for b in range(2):
                cols = slice(b * LANES, (b + 1) * LANES)
                o_re, o_im = parts[0][b], parts[1][b]
                p_re, p_im = probe[j, 0, rows, cols], probe[j, 1, rows, cols]
                patch[slot, 0, rows, cols] = o_re
                patch[slot, 1, rows, cols] = o_im
                ex[slot, rows, b * LANES:(b + 1) * LANES] = (p_re * o_re - p_im * o_im).astype(jnp.bfloat16)
                ex[slot, rows, frame + b * LANES:frame + (b + 1) * LANES] = (
                    p_re * o_im + p_im * o_re
                ).astype(jnp.bfloat16)

    def transform(slot, way):
        half = jnp.dot(ex[slot], table[way], preferred_element_type=jnp.float32)
        mid[slot, :frame] = half[:, :frame].astype(jnp.bfloat16)
        mid[slot, frame:] = half[:, frame:].astype(jnp.bfloat16)
        far[slot] = jnp.dot(table[1 - way], mid[slot], preferred_element_type=jnp.float32)

    def residual(j, slot, living):
        for i in strips:
            rows = slice(i * STRIP, (i + 1) * STRIP)
            lower = slice(frame + i * STRIP, frame + (i + 1) * STRIP)
            f_re, f_im = far[slot, rows], far[slot, lower]
            factor = 1.0 - amps[j, rows].astype(jnp.float32) * lax.rsqrt(f_re * f_re + f_im * f_im + 1.0)
            if living is not None:
                factor = factor * living
            ex[slot, rows, :frame] = (f_re * factor).astype(jnp.bfloat16)
            ex[slot, rows, frame:] = (f_im * factor).astype(jnp.bfloat16)

    def leave(j, slot):
        for i in strips:
            rows = slice(i * STRIP, (i + 1) * STRIP)
            lower = slice(frame + i * STRIP, frame + (i + 1) * STRIP)
            b_re, b_im = far[slot, rows], far[slot, lower]
            o_re, o_im = patch[slot, 0, rows], patch[slot, 1, rows]
            p_re, p_im = probe[j, 0, rows], probe[j, 1, rows]
            for c, d in enumerate((o_re * b_re + o_im * b_im, o_re * b_im - o_im * b_re)):
                dprobe[j, c, rows] = d.astype(jnp.bfloat16)
            probe[j, 0, rows] = p_re * b_re + p_im * b_im
            probe[j, 1, rows] = p_re * b_im - p_im * b_re

    def grad_copy(j):
        return pltpu.make_async_copy(probe.at[j], grads_out.at[j], grad_sem.at[j])

    def visit(pair, carry):
        first, second = 2 * pair, 2 * pair + 1
        enter(first, 0)
        transform(0, 0)
        enter(second, 1)
        transform(1, 0)
        residual(first, 0, None)
        transform(0, 1)
        residual(second, 1, jnp.where(second < alive, 1.0, 0.0))
        transform(1, 1)
        leave(first, 0)
        leave(second, 1)
        grad_copy(first).start()
        grad_copy(second).start()
        return carry

    pairs = (alive + 1) // 2
    lax.fori_loop(0, pairs, visit, 0)

    def skip(j, carry):
        dprobe[j] = jnp.zeros((2, frame, frame), jnp.bfloat16)
        return carry

    lax.fori_loop(2 * pairs, pos_dev, skip, 0)

    cross[...] = jnp.zeros_like(cross)
    rows_q = frame // shares
    groups = 2 * modes
    share = share_of(groups, lax.axis_size("blk"))

    def eigen_strip(i, carry):
        rows = pl.ds(pl.multiple_of(i * STRIP, STRIP), STRIP)
        q = i // (rows_q // STRIP)
        inner = pl.ds(pl.multiple_of(i % (rows_q // STRIP) * STRIP, STRIP), STRIP)
        d = jnp.concatenate([dprobe[:, c, rows, :].reshape(pos_dev * STRIP, frame) for c in range(2)], 1)
        e = jnp.concatenate([eig[:, c, rows, :].reshape(modes * STRIP, frame) for c in range(2)], 1)
        both = jnp.dot(weights_t[...], d, preferred_element_type=jnp.float32)
        grad = (both[:modes * STRIP] + both[modes * STRIP:]) * (0.5 * scale)
        for c in range(2):
            for k in range(modes):
                group = 2 * k + c
                if share:
                    group = (group // share ^ my_block) * share + group % share
                eigen[q, group, inner, :] = grad[k * STRIP:(k + 1) * STRIP, c * frame:(c + 1) * frame]
        cross[...] += lax.dot_general(d, e, (((1,), (1,)), ((), ())), preferred_element_type=jnp.float32)
        return carry

    lax.fori_loop(0, frame // STRIP, eigen_strip, 0, unroll=16)
    pending = []

    def start(source, target):
        copy = pltpu.make_async_copy(source, target, out_sem.at[len(pending)])
        copy.start()
        pending.append(copy)

    for h in far_first(shares):
        mine, other = slabs_of(member, h)
        out_eigen[h] = eigen[other].astype(jnp.bfloat16)
        start(out_eigen.at[h], eigen_send[h % 2].at[h // 2])
        start(eigen.at[mine], eigen_keep[h % 2].at[h // 2])

    by_position = (pos_dev * STRIP, pos_dev)
    by_mode = (modes * STRIP, modes)
    total = exact(one_hot(by_position[::-1], 1), diagonals(cross[...]))
    coef[...] = lax.dot_general(
        one_hot(by_mode[::-1], 1), total, (((1,), (1,)), ((), ())),
        precision=lax.Precision.HIGHEST, preferred_element_type=jnp.float32,
    ) * (0.5 / frame)

    def drain(j, carry):
        grad_copy(j).wait()
        return carry

    lax.fori_loop(0, 2 * pairs, drain, 0)
    for copy in pending:
        copy.wait()


def positions(offs, scale, indices, pieces, eigenprobes, amps, table, weights, weights_t):
    modes, _, frame, _ = eigenprobes.shape
    pos_dev = amps.shape[0]
    side = pieces[0].shape[2]
    shares = len(offs)
    blocks = side // LANES
    smem = pl.BlockSpec(memory_space=SMEM)
    whole = pl.BlockSpec(memory_space=VMEM)
    anywhere = pl.BlockSpec(memory_space=pl.ANY)
    eigen_half = (shares // 2, 2 * modes, frame // shares, frame)
    eigen_part = (shares // 4,) + eigen_half[1:]
    grads = (pos_dev, 2, frame, frame)
    return pl.pallas_call(
        functools.partial(position_kernel, offs, scale),
        in_specs=[smem] * 3 + [anywhere] * (len(pieces) + 3) + [whole] * 2,
        out_specs=[anywhere] * 5 + [whole],
        scratch_shapes=[
            pltpu.VMEM((REACH, 2, side, side), jnp.bfloat16),
            pltpu.VMEM(table.shape, jnp.bfloat16),
            pltpu.VMEM(grads, jnp.float32),
            pltpu.VMEM(amps.shape, jnp.bfloat16),
            pltpu.VMEM(eigenprobes.shape, jnp.bfloat16),
            pltpu.VMEM((REACH, 2, blocks + 1, side, LANES), jnp.float32),
            pltpu.VMEM((2, frame, 2 * frame), jnp.bfloat16),
            pltpu.VMEM((2, 2 * frame, frame), jnp.bfloat16),
            pltpu.VMEM((2, 2 * frame, frame), jnp.float32),
            pltpu.VMEM((2, 2, frame, frame), jnp.float32),
            pltpu.VMEM(grads, jnp.bfloat16),
            pltpu.VMEM((shares, 2 * modes, frame // shares, frame), jnp.float32),
            pltpu.VMEM(eigen_half, jnp.bfloat16),
            pltpu.VMEM((pos_dev * STRIP, modes * STRIP), jnp.float32),
            pltpu.SemaphoreType.DMA((len(pieces),)),
            pltpu.SemaphoreType.DMA,
            pltpu.SemaphoreType.DMA,
            pltpu.SemaphoreType.DMA,
            pltpu.SemaphoreType.DMA((pos_dev,)),
            pltpu.SemaphoreType.DMA((shares,)),
        ],
        out_shape=[
            jax.ShapeDtypeStruct(eigen_part, jnp.bfloat16),
            jax.ShapeDtypeStruct(eigen_part, jnp.bfloat16),
            jax.ShapeDtypeStruct(eigen_part, jnp.float32),
            jax.ShapeDtypeStruct(eigen_part, jnp.float32),
            jax.ShapeDtypeStruct(grads, jnp.float32),
            jax.ShapeDtypeStruct((modes, pos_dev), jnp.float32),
        ],
        compiler_params=pltpu.CompilerParams(vmem_limit_bytes=VMEM_LIMIT),
        name="positions",
    )(*indices, *pieces, eigenprobes, amps, table, weights, weights_t)


def scatter_kernel(shares, tile_list, offsets, group_counts, grads_in, *refs):
    send, keep = refs[:2 * REACH], refs[2 * REACH:4 * REACH]
    grads, acc, out_send, grad_sem, out_sem = refs[4 * REACH:]
    pos_dev, _, frame, _ = grads.shape
    blocks, side = acc.shape[2] - 1, acc.shape[3]
    slab = side // shares
    _, member, alive, place = coordinates(tile_list, offsets, group_counts, pos_dev)

    def grad_copy(j):
        return pltpu.make_async_copy(grads_in.at[j], grads.at[j], grad_sem.at[j])

    def begin(j, carry):
        grad_copy(j).start()
        return carry

    lax.fori_loop(0, alive, begin, 0)

    def clear(i, carry):
        rows = pl.ds(pl.multiple_of(i * LANES, LANES), LANES)
        for section in range(REACH):
            for c in range(2):
                for b in range(blocks + 1):
                    acc[section, c, b, rows, :] = jnp.zeros((LANES, LANES), jnp.float32)
        return carry

    lax.fori_loop(0, side // LANES, clear, 0)
    lane = lax.broadcasted_iota(jnp.int32, (STRIP, LANES), 1)

    def add(j, carry):
        grad_copy(j).wait()
        for m in range(2):
            section, row, col = place(j, m)
            cb, s = col // LANES, col % LANES
            inside = lane >= s
            for i in range(frame // STRIP):
                for c in range(2):
                    low, high = (
                        pltpu.roll(grads[j, c, i * STRIP:(i + 1) * STRIP, b * LANES:(b + 1) * LANES], s, 1)
                        for b in range(2)
                    )
                    for b, value in enumerate(
                        (
                            jnp.where(inside, low, 0.0),
                            jnp.where(inside, high, low),
                            jnp.where(inside, 0.0, high),
                        )
                    ):
                        at = (section, c, cb + b, pl.ds(row + i * STRIP, STRIP), slice(None))
                        acc[at] = acc[at] + value
        return carry

    lax.fori_loop(0, alive, add, 0)
    pending = []

    def start(source, target):
        copy = pltpu.make_async_copy(source, target, out_sem.at[len(pending)])
        copy.start()
        pending.append(copy)

    for section in range(REACH - 1, -1, -1):
        for h in far_first(shares):
            mine, other = (pl.multiple_of(at * slab, slab) for at in slabs_of(member, h))
            start(
                acc.at[section, :, pl.ds(0, blocks), pl.ds(mine, slab), :],
                keep[2 * section + h % 2].at[h // 2],
            )
            for c in range(2):
                for b in range(blocks):
                    out_send[section, h, c, b] = acc[section, c, b, pl.ds(other, slab), :].astype(jnp.bfloat16)
            start(out_send.at[section, h], send[2 * section + h % 2].at[h // 2])
    for copy in pending:
        copy.wait()


def scatter(shares, side, indices, grads):
    blocks = side // LANES
    anywhere = pl.BlockSpec(memory_space=pl.ANY)
    half = (shares // 2, 2, blocks, side // shares, LANES)
    part = (shares // 4,) + half[1:]
    return pl.pallas_call(
        functools.partial(scatter_kernel, shares),
        in_specs=[pl.BlockSpec(memory_space=SMEM)] * 3 + [anywhere],
        out_specs=[anywhere] * (4 * REACH),
        scratch_shapes=[
            pltpu.VMEM(grads.shape, jnp.float32),
            pltpu.VMEM((REACH, 2, blocks + 1, side, LANES), jnp.float32),
            pltpu.VMEM((REACH,) + half, jnp.bfloat16),
            pltpu.SemaphoreType.DMA((grads.shape[0],)),
            pltpu.SemaphoreType.DMA((REACH * shares,)),
        ],
        out_shape=[jax.ShapeDtypeStruct(part, jnp.bfloat16)] * (2 * REACH)
        + [jax.ShapeDtypeStruct(part, jnp.float32)] * (2 * REACH),
        compiler_params=pltpu.CompilerParams(vmem_limit_bytes=20 * 1024 * 1024),
        cost_estimate=pl.CostEstimate(flops=1 << 24, bytes_accessed=16 << 20, transcendentals=0),
        name="scatter",
    )(*indices, grads)


def after(array, *others):
    return lax.optimization_barrier((array,) + others)[0]


def after_all(arrays, *others):
    return lax.optimization_barrier(tuple(arrays) + others)[:len(arrays)]


def halve(keep, send, before_core=(), before_cross=()):
    far = [keep[1], after(swap(after(send[1], *before_core), "probe", 1), *before_cross)]
    terms = [keep[0], swap(send[0], "probe", 1)]
    leaving = None
    bit = 2
    while True:
        sending = sum(term.astype(jnp.float32) for term in far).astype(jnp.bfloat16)
        leaving = sending if leaving is None else leaving
        terms.append(swap(sending, "probe", bit))
        if terms[0].shape[0] == 1:
            return sum(term[0].astype(jnp.float32) for term in terms), leaving, terms[-1]
        pick = lambda term, which: term.reshape((term.shape[0] // 2, 2) + term.shape[1:])[:, which]
        far, terms = [pick(term, 1) for term in terms], [pick(term, 0) for term in terms]
        bit *= 2


def add_up_kernel(own, *refs):
    arrived, out = refs[:-1], refs[-1]
    total = own[...]
    for term in arrived:
        total += term[...].astype(jnp.float32)
    total = total.astype(jnp.bfloat16)
    for i in range(out.shape[0]):
        out[i] = total


def widen_kernel(array, out):
    out[...] = array[...].astype(jnp.float32)


def small_call(kernel, shape, kind, name, *arrays):
    return pl.pallas_call(
        kernel,
        in_specs=[pl.BlockSpec(memory_space=VMEM)] * len(arrays),
        out_specs=pl.BlockSpec(memory_space=VMEM),
        out_shape=jax.ShapeDtypeStruct(shape, kind),
        compiler_params=pltpu.CompilerParams(vmem_limit_bytes=8 * 1024 * 1024),
        name=name,
    )(*arrays)


def scatter_sum(axis, value, relative):
    peers, me = lax.axis_size(axis), lax.axis_index(axis)
    share = (lambda i: value[i]) if relative else (lambda i: lax.dynamic_index_in_dim(value, me ^ i, 0, False))
    sent = [share(i).astype(jnp.bfloat16) for i in range(1, peers)]
    arrived = [swap(sending, axis, i) for i, sending in enumerate(sent, 1)]
    total = small_call(
        add_up_kernel, (peers,) + value.shape[1:], jnp.bfloat16, "add_up", share(0), *arrived
    )
    return total, sent


def finish_kernel(first, second, out):
    blocks = first.shape[1]
    for c in range(2):
        for b in range(blocks):
            out[c, :, b * LANES:(b + 1) * LANES] = first[c, b] + second[c, b].astype(jnp.float32)


def finish(first, second):
    _, blocks, slab, lanes = first.shape
    return pl.pallas_call(
        finish_kernel,
        in_specs=[pl.BlockSpec(memory_space=VMEM)] * 2,
        out_specs=pl.BlockSpec(memory_space=VMEM),
        out_shape=jax.ShapeDtypeStruct((2, slab, blocks * lanes), jnp.float32),
        compiler_params=pltpu.CompilerParams(vmem_limit_bytes=8 * 1024 * 1024),
        name="finish",
    )(first, second)


def on_device(tiles, eigenprobes, coefficients, tile_list, offsets, amplitudes, group_counts):
    modes, _, frame, _ = eigenprobes.shape
    side = tiles.shape[2]
    pos_dev = coefficients.shape[0]
    blocks = lax.axis_size("blk")
    shares = lax.axis_size("probe")
    member = lax.axis_index("probe")
    slab = side // shares
    bits = [1 << i for i in range(shares.bit_length() - 1)]

    offs = [0]
    for bit in reversed(bits):
        offs = offs + [o ^ bit for o in offs]
    quarter = lax.dynamic_slice_in_dim(tiles[0], member * slab, slab, 1)
    near = shift(quarter, "blk", -1)
    held = [[near], [shift(near, "blk", -1)]]
    eig, amps = stage(*after_all((eigenprobes, amplitudes), near))
    held[1][0] = after(held[1][0], eig)
    weights, weights_t, table, tile, lists, corners = expand(
        *after_all((coefficients.T, tables(frame), tiles[0], tile_list.T, offsets.T), held[1][0])
    )
    for bit in reversed(bits):
        for part in held:
            arrived = [swap(piece, "probe", bit) for piece in part]
            if bit > 1:
                arrived[0] = after(arrived[0], eig if part is held[0] else table)
            part += arrived

    indices = (lists, corners, group_counts)
    scale = (pos_dev * blocks * shares) ** (-0.5)
    out = positions(
        tuple(offs), scale, indices, [tile] + held[0] + held[1], eig, amps, table, weights, weights_t
    )
    eigen_send, eigen_keep, grads, coef_rows = out[:2], out[2:4], out[4], out[5]

    eigen, leaving, crossed = halve(eigen_keep, eigen_send)
    out = scatter(shares, side, indices, after(grads, leaving))
    send, keep = ([out[at + 2 * i:at + 2 * i + 2] for i in range(REACH)] for at in (0, 2 * REACH))
    last = REACH - 1
    relative = share_of(2 * modes, blocks) > 0
    total, sent = scatter_sum("blk", eigen.reshape(blocks, -1, frame), relative)
    mine, leaving, _ = halve(keep[last], send[last], before_cross=sent)
    moving = after(mine.astype(jnp.bfloat16), total)
    gate = moving
    for section in range(last - 1, -1, -1):
        mine, leaving, gate = halve(keep[section], send[section], before_cross=(gate,))
        if section == last - 1:
            total = after(total, leaving)
        arrived = shift(moving, "blk", 1)
        if section > 0:
            moving = (arrived.astype(jnp.float32) + mine).astype(jnp.bfloat16)
    gathered = lax.all_to_all(total, "blk", 0, 0)
    eigen_share = small_call(widen_kernel, gathered.shape, jnp.float32, "widen", gathered)
    eigen_share = eigen_share.reshape(modes, 2, frame // shares, frame)
    summed = finish(mine, arrived)
    return (summed[None], eigen_share, coef_rows.T)


def solution(mesh):
    in_specs = (
        P(("recon", "blk"), None, None, None),
        P("recon", None, None, None),
        P(("recon", "blk", "probe"), None),
        P(("recon", "blk", "probe"), None),
        P(("recon", "blk", "probe"), None),
        P(("recon", "blk", "probe"), None, None),
        P(("recon", "blk")),
    )
    out_specs = (
        P(("recon", "blk"), None, "probe", None),
        P("recon", None, "probe", None),
        P(("recon", "blk", "probe"), None),
    )
    return jax.shard_map(
        on_device, mesh=mesh, in_specs=in_specs, out_specs=out_specs, check_vma=False
    )
```
